32 devices in a mesh: outer: 4 (over y, core), inner: 8 (over z, x).
Axes of the slice: x: 2, y: 2, z: 4, core: 2. Of those that a mesh axis runs over, the one named last changes fastest.
Arguments:
- layer_input: bfloat16 [1024, 256, 192], P(('outer', 'inner')), may hold values from -6 to 6
- out_grad: bfloat16 [1024, 256, 192], P(('outer', 'inner')), may hold values from -6 to 6
- mix_weight: bfloat16 [256, 128], replicated, may hold values from -0.375 to 0.375
- lift_weight: bfloat16 [128, 192], replicated, may hold values from -0.5 to 0.5
- linear_weight: bfloat16 [256, 256], replicated, may hold values from -0.375 to 0.375
- row_ids: int32 [1024, 256], P(('outer', 'inner')), may hold values from 0 to 16383, as said below
- row_home: int32 [16384], replicated, may hold values from 0 to 16383, as said below
- table: float32 [16384, 192], P('inner'), may hold values from -0.6 to 0.6
- row_accum: float32 [16384], P('inner'), may hold values from 1 to 100
Outputs:
- new_table: float32 [16384, 192], P('inner')
- new_accum: float32 [16384], P('inner')
- mix_grad: float32 [256, 128], replicated
- lift_grad: float32 [128, 192], replicated
- linear_grad: float32 [256, 256], replicated
The draws below stay inside these ranges and needn't reach their ends.
Inputs may be any that keep to these rules, and one draw needn't show every extreme that they name: row_home is a permutation: hashed row i is stored at position row_home[i], held by inner index row_home[i] // 2048. In each aligned block of 16 samples (all their features together), every inner index is the owner, row_home[row_ids] // 2048, of exactly 512 lookups. The same row may be named many times.
All inputs are finite; a program needn't handle non-finite values.
Results may differ from the reference program's by a relative error of at most 0.0041.
Values may be sent and summed in bfloat16 or wider, within the bound.
No kernel may reach another device: no remote copies, remote signals or barrier semaphores. Data moves between devices by JAX's collectives and lax.ppermute only.
A program may use at most 64 MiB of HBM per device.

```python
import math
import jax
import jax.numpy as jnp
from jax import lax

FEATS = 256
D = 192
RANK = 128
SAMP_DEV = 32
ROWS_DEV = 2048
BATCH = 1024
ROWS = 16384
N_INNER = 8


def shared_rows(key):
    base = jax.random.fold_in(key, 911)
    k_perm, k_owner, k_first, k_second, k_third = jax.random.split(base, 5)
    row_home = jax.random.permutation(k_perm, ROWS).astype(jnp.int32)
    inverse = jnp.zeros((ROWS,), jnp.int32).at[row_home].set(jnp.arange(ROWS, dtype=jnp.int32))
    per_half = SAMP_DEV // 2 * FEATS
    blocks = BATCH // (SAMP_DEV // 2)
    pattern = jnp.arange(per_half, dtype=jnp.int32) % N_INNER
    owner_keys = jax.random.split(k_owner, blocks)
    owners = jax.vmap(lambda sub_key: jax.random.permutation(sub_key, pattern))(owner_keys)
    shape_all = (blocks, per_half)
    local_rows = jnp.minimum(jax.random.randint(k_first, shape_all, 0, ROWS_DEV), jax.random.randint(k_second, shape_all, 0, ROWS_DEV))
    local_rows = jnp.minimum(local_rows, jax.random.randint(k_third, shape_all, 0, ROWS_DEV))
    places = (owners * ROWS_DEV + local_rows).astype(jnp.int32)
    row_ids = jnp.take(inverse, places.reshape(-1), axis=0).reshape(BATCH, FEATS)
    return (row_ids.astype(jnp.int32), row_home)


def draw_row_ids(key, part):
    return shared_rows(key)[0]


def draw_row_home(key, part):
    return shared_rows(key)[1]


def levels(key, dims, cuts, least, top_value):
    factor_of, own = 1.0, jax.random.fold_in(key, 6)
    for axis_at, parts in cuts:
        draws = jnp.exp(jax.random.uniform(jax.random.fold_in(own, axis_at), (parts,), jnp.float32, least / len(cuts), top_value / len(cuts)))
        factor_of = factor_of * jnp.repeat(draws, dims[axis_at] // parts).reshape([-1 if axis == axis_at else 1 for axis in range(len(dims))])
    return factor_of


def bell_draw(own_key, dims, scale, reach, cuts=(), kind=jnp.bfloat16):
    entries = scale * jax.random.normal(own_key, dims, jnp.float32)
    if cuts:
        entries = entries * levels(own_key, dims, cuts, -0.22, 0.18)
    return jnp.clip(entries, -reach, reach).astype(kind)


def setup_inputs(seed: int = 0) -> dict:
    splits = jax.random.split(jax.random.key(seed), 10)
    layer_input = bell_draw(splits[0], (BATCH, FEATS, D), 1.0, 6.0, ((0, 32),))
    out_grad = bell_draw(splits[1], (BATCH, FEATS, D), 1.0, 6.0, ((0, 32),))
    mix_weight = bell_draw(splits[2], (FEATS, RANK), FEATS ** -0.5, 0.375)
    lift_weight = bell_draw(splits[3], (RANK, D), RANK ** -0.5, 0.5)
    linear_weight = bell_draw(splits[4], (FEATS, FEATS), FEATS ** -0.5, 0.375)
    row_ids = draw_row_ids(jax.random.fold_in(splits[9], 71), 0)
    row_home = draw_row_home(jax.random.fold_in(splits[9], 71), 0)
    table = bell_draw(splits[7], (ROWS, D), 0.1, 0.6, ((0, 8),), jnp.float32)
    row_accum = jnp.clip(jnp.exp(math.log(100.0) - 4.6051702 * jax.random.uniform(splits[8], (ROWS,), jnp.float32) ** levels(splits[8], (ROWS,), ((0, 8),), -0.2, 0.2)), 1.0, 100.0)
    return {"layer_input": layer_input, "out_grad": out_grad, "mix_weight": mix_weight, "lift_weight": lift_weight, "linear_weight": linear_weight, "row_ids": row_ids, "row_home": row_home, "table": table, "row_accum": row_accum}


LEARN_RATE = 0.5

def to_half(values):
    return lax.optimization_barrier(values.astype(jnp.bfloat16)).astype(jnp.float32)

def reference(layer_input, out_grad, mix_weight, lift_weight, linear_weight, row_ids, row_home, table, row_accum):
    scaling = 1.0 / math.sqrt(D)
    blocks = BATCH // SAMP_DEV
    inputs_all = layer_input.reshape(blocks, SAMP_DEV, FEATS, D)
    grads_all = out_grad.reshape(blocks, SAMP_DEV, FEATS, D)
    places_all = jnp.take(row_home, row_ids.reshape(-1), axis=0).astype(jnp.int32).reshape(blocks, SAMP_DEV * FEATS)
    mixing = mix_weight.astype(jnp.float32)
    lifting = lift_weight.astype(jnp.float32)
    linear = linear_weight.astype(jnp.float32)

    def step(carry, item):
        g_mix, g_lift, g_linear, g_table = carry
        inputs_blk, grads_blk, places = item
        inputs = inputs_blk.astype(jnp.float32)
        cotangent = grads_blk.astype(jnp.float32)
        compressed = to_half(jnp.einsum('bfd,fk->bdk', inputs, mixing))
        products = to_half(jnp.einsum('bfd,bdk->bfk', inputs, compressed) * scaling)
        d_products = to_half(jnp.einsum('bfd,kd->bfk', cotangent, lifting))
        d_compressed = to_half(jnp.einsum('bfd,bfk->bdk', inputs, d_products) * scaling)
        d_inputs = cotangent + jnp.einsum('fg,bfd->bgd', linear, cotangent)
        d_inputs = d_inputs + scaling * jnp.einsum('bfk,bdk->bfd', d_products, compressed)
        d_inputs = d_inputs + jnp.einsum('fk,bdk->bfd', mixing, d_compressed)
        g_mix = g_mix + jnp.einsum('bfd,bdk->fk', inputs, d_compressed)
        g_lift = g_lift + jnp.einsum('bfk,bfd->kd', products, cotangent)
        g_linear = g_linear + jnp.einsum('bfd,bgd->fg', cotangent, inputs)
        rounded = to_half(d_inputs).reshape(-1, D)
        g_table = g_table.at[places].add(rounded)
        return ((g_mix, g_lift, g_linear, g_table), None)
    start = (jnp.zeros((FEATS, RANK), jnp.float32), jnp.zeros((RANK, D), jnp.float32), jnp.zeros((FEATS, FEATS), jnp.float32), jnp.zeros((ROWS, D), jnp.float32))
    (g_mix, g_lift, g_linear, g_table), unused = lax.scan(step, start, (inputs_all, grads_all, places_all))
    new_accum = row_accum + lax.optimization_barrier(jnp.mean(g_table * g_table, axis=1))
    new_table = table - LEARN_RATE * g_table / jnp.sqrt(new_accum)[:, None]
    return (new_table, new_accum, g_mix / BATCH, g_lift / BATCH, g_linear / BATCH)
```

```python
import functools
import math

import jax
import jax.numpy as jnp
from jax import lax
from jax.experimental import pallas as pl
from jax.experimental.pallas import tpu as pltpu
from jax.sharding import PartitionSpec as P

LEARN_RATE = 0.5


def interaction_grads(inputs, cotangent, mix_weight, lift_weight, linear_weight, scaling):
    compressed = jnp.einsum(
        "bfd,fk->bdk", inputs, mix_weight, preferred_element_type=jnp.float32
    ).astype(jnp.bfloat16)
    products = (
        jnp.einsum("bfd,bdk->bfk", inputs, compressed, preferred_element_type=jnp.float32) * scaling
    ).astype(jnp.bfloat16)
    d_products = jnp.einsum(
        "bfd,kd->bfk", cotangent, lift_weight, preferred_element_type=jnp.float32
    ).astype(jnp.bfloat16)
    d_compressed = (
        jnp.einsum("bfd,bfk->bdk", inputs, d_products, preferred_element_type=jnp.float32) * scaling
    ).astype(jnp.bfloat16)
    d_inputs = cotangent.astype(jnp.float32)
    d_inputs = d_inputs + jnp.einsum(
        "fg,bfd->bgd", linear_weight, cotangent, preferred_element_type=jnp.float32
    )
    d_inputs = d_inputs + scaling * jnp.einsum(
        "bfk,bdk->bfd", d_products, compressed, preferred_element_type=jnp.float32
    )
    d_inputs = d_inputs + jnp.einsum(
        "fk,bdk->bfd", mix_weight, d_compressed, preferred_element_type=jnp.float32
    )
    g_mix = jnp.einsum("bfd,bdk->fk", inputs, d_compressed, preferred_element_type=jnp.float32)
    g_lift = jnp.einsum("bfk,bfd->kd", products, cotangent, preferred_element_type=jnp.float32)
    g_linear = jnp.einsum("bfd,bgd->fg", cotangent, inputs, preferred_element_type=jnp.float32)
    rows_out = d_inputs.astype(jnp.bfloat16).reshape(-1, d_inputs.shape[2])
    return (rows_out, (g_mix, g_lift, g_linear))


def adagrad(weights, history, gradient):
    updated = history + jnp.mean(gradient * gradient, axis=1)
    return (weights - LEARN_RATE * gradient / jnp.sqrt(updated)[:, None], updated)


def owner_ranks(owner_of, owners):
    lookups = owner_of.shape[0]
    width = math.gcd(lookups, 128)
    groups = lookups // width
    hot = (owner_of[:, None] == jnp.arange(owners, dtype=jnp.int32)[None, :]).astype(jnp.bfloat16)
    hot = hot.reshape(groups, width, owners)
    lower = (jnp.arange(width)[:, None] > jnp.arange(width)[None, :]).astype(jnp.bfloat16)
    within = jnp.einsum("ij,gjo->gio", lower, hot, preferred_element_type=jnp.float32)
    totals = jnp.sum(hot.astype(jnp.float32), axis=1)
    before = jnp.cumsum(totals, axis=0) - totals
    counted = jnp.sum(hot.astype(jnp.float32) * (within + before[:, None, :]), axis=2)
    return counted.reshape(-1).astype(jnp.int32)


def add_rows(collected, slots, values):
    count = values.shape[0]
    table_rows = collected.shape[0]
    width = math.gcd(count, 2048)
    columns = jnp.arange(table_rows, dtype=jnp.int32)
    for block_index in range(count // width):
        start = block_index * width
        hot = (slots[start : start + width, None] == columns[None, :]).astype(jnp.bfloat16)
        collected = collected + jnp.einsum(
            "lr,ld->rd", hot, values[start : start + width], preferred_element_type=jnp.float32
        )
    return collected


def routed_rows(
    layer_input,
    out_grad,
    mix_weight,
    lift_weight,
    linear_weight,
    row_ids,
    row_home,
    table,
    row_accum,
):
    owners = lax.axis_size("inner")
    sample_count, feature_count, embed_width = layer_input.shape
    table_rows = table.shape[0]
    half_samples = sample_count // 2
    lookups = sample_count * feature_count
    per_owner = lookups // (2 * owners)
    scaling = 1.0 / math.sqrt(embed_width)
    placed = jnp.take(row_home, row_ids.reshape(-1), axis=0)
    owner_of = placed // table_rows
    target = owner_of * (2 * per_owner) + owner_ranks(owner_of, owners)
    ordering = jnp.zeros((lookups,), jnp.int32).at[target].set(jnp.arange(lookups, dtype=jnp.int32))
    ordering = ordering.reshape(owners, 2, per_owner)
    local_rows = (
        jnp.zeros((lookups,), jnp.int32)
        .at[target]
        .set(placed % table_rows)
        .reshape(owners, 2 * per_owner)
    )
    arrived_rows = lax.all_to_all(
        local_rows, "inner", split_axis=0, concat_axis=0, tiled=True
    ).reshape(owners, 2, per_owner)
    collected = jnp.zeros((table_rows, embed_width), jnp.float32)
    totals = None
    for half_index in range(2):
        first_sample = half_index * half_samples
        rows_out, partial_value = interaction_grads(
            layer_input[first_sample : first_sample + half_samples],
            out_grad[first_sample : first_sample + half_samples],
            mix_weight,
            lift_weight,
            linear_weight,
            scaling,
        )
        picked = ordering[:, half_index, :] - half_index * half_samples * feature_count
        outgoing = jnp.take(rows_out, picked.reshape(-1), axis=0).reshape(
            owners, per_owner, embed_width
        )
        incoming = lax.all_to_all(outgoing, "inner", split_axis=0, concat_axis=0, tiled=True)
        collected = add_rows(
            collected, arrived_rows[:, half_index, :].reshape(-1), incoming.reshape(-1, embed_width)
        )
        if totals is None:
            totals = partial_value
        else:
            totals = tuple((earlier + later for earlier, later in zip(totals, partial_value)))
    batch_total = sample_count * lax.axis_size("outer") * owners
    summed = lax.psum((totals[0], totals[1], totals[2]), ("outer", "inner"))
    mix_grad = summed[0] / batch_total
    lift_grad = summed[1] / batch_total
    linear_grad = summed[2] / batch_total
    complete = lax.psum(collected, "outer")
    new_table, new_accum = adagrad(table, row_accum, complete)
    return (new_table, new_accum, mix_grad, lift_grad, linear_grad)


def matmul(left, right):
    return jnp.dot(left, right, preferred_element_type=jnp.float32)


def matmul_nt(left, right):
    return lax.dot_general(left, right, (((1,), (1,)), ((), ())), preferred_element_type=jnp.float32)


def one_hot(matches):
    return jnp.where(matches, 1.0, 0.0).astype(jnp.bfloat16)


def place_kernel(shift, owners, ids_ref, home_ref, rank_ref, slot_ref, count_ref):
    samples, feats = ids_ref.shape
    high, low = home_ref.shape
    home = home_ref[...]
    pieces = jnp.concatenate(
        [(home & 255).astype(jnp.float32).T, (home >> 8).astype(jnp.float32).T], axis=0
    ).astype(jnp.bfloat16)
    high_at = lax.broadcasted_iota(jnp.int32, (high, feats), 0)
    low_at = lax.broadcasted_iota(jnp.int32, (low, feats), 0)
    lane = lax.broadcasted_iota(jnp.int32, (1, feats), 1)
    count_lane = lax.broadcasted_iota(jnp.int32, (8, 128), 1)

    @pl.loop(0, samples // 8)
    def _(group):
        first = pl.multiple_of(group * 8, 8)
        ids = ids_ref[pl.ds(first, 8), :]
        ranks, slots, homes = [], [], []
        for row in range(8):
            one = ids[row : row + 1]
            found = matmul(pieces, one_hot(high_at == (one >> 7)))
            value = found[:low] + 256.0 * found[low:]
            place = jnp.sum(jnp.where(low_at == (one & 127), value, 0.0), axis=0, keepdims=True)
            place = place.astype(jnp.int32)
            owner = place >> shift
            key = (owner * feats + lane).astype(jnp.float32)
            key_down = jnp.broadcast_to(key, (128, feats)).T
            parts = []
            for at in range(0, feats, 128):
                less = key_down < key[:, at : at + 128]
                parts.append(jnp.sum(jnp.where(less, 1.0, 0.0), axis=0, keepdims=True))
            ranks.append(jnp.concatenate(parts, axis=1).astype(jnp.int32))
            slots.append(place & ((1 << shift) - 1))
            homes.append(owner)
        rank_ref[pl.ds(first, 8), :] = jnp.concatenate(ranks, axis=0)
        slot_ref[pl.ds(first, 8), :] = jnp.concatenate(slots, axis=0)
        owner_all = jnp.concatenate(homes, axis=0)
        counts = jnp.zeros((8, 128), jnp.float32)
        for owner_at in range(owners):
            number = jnp.sum(jnp.where(owner_all == owner_at, 1.0, 0.0), axis=1, keepdims=True)
            counts = jnp.where(count_lane == owner_at, number, counts)
        count_ref[pl.ds(first, 8), :] = counts.astype(jnp.int32)


def place_lookups(row_ids, row_home, owners, table_rows):
    samples, feats = row_ids.shape
    return pl.pallas_call(
        functools.partial(place_kernel, table_rows.bit_length() - 1, owners),
        out_shape=(
            jax.ShapeDtypeStruct((samples, feats), jnp.int32),
            jax.ShapeDtypeStruct((samples, feats), jnp.int32),
            jax.ShapeDtypeStruct((samples, 128), jnp.int32),
        ),
        name="place_lookups",
    )(row_ids, row_home.reshape(-1, 128))


COPY_ROWS = 48


def grads_kernel(
    sizes,
    count_ref,
    me_ref,
    x_ref,
    g_ref,
    mix_ref,
    lift_ref,
    linear_ref,
    rank_ref,
    slot_ref,
    *rest,
):
    group, steps, owners, outers, per_owner, scaling = sizes
    far = owners // 2
    keep_refs, send_refs = rest[:far], rest[far : 2 * far]
    dense_ref = rest[2 * far]
    (
        mix_down,
        lift_down,
        stacked,
        mix_sum,
        lift_sum,
        linear_sum,
        sorted_a,
        sorted_b,
        row_a,
        row_b,
        staged,
        filled,
    ) = rest[2 * far + 1 :]
    width, feats = x_ref.shape[1:]
    rank = mix_ref.shape[1]
    step = pl.program_id(0)

    @pl.when(step == 0)
    def _():
        mix_down[...] = mix_ref[...].astype(jnp.float32).T.astype(jnp.bfloat16)
        lift_down[...] = lift_ref[...].astype(jnp.float32).T.astype(jnp.bfloat16)
        stacked[:feats] = linear_ref[...]
        stacked[feats:] = mix_down[...]
        mix_sum[...] = jnp.zeros_like(mix_sum)
        lift_sum[...] = jnp.zeros_like(lift_sum)
        linear_sum[...] = jnp.zeros_like(linear_sum)
        for owner in range(owners):
            filled[owner] = 0

    @pl.when(step < steps)
    def _():
        total_q, total_lift = None, None
        row_at = lax.broadcasted_iota(jnp.int32, (feats, feats), 0)
        extra_at = lax.broadcasted_iota(jnp.int32, (feats - width, feats), 0)
        for k in range(group):
            sample = step * group + k
            x_down = x_ref[k]
            g_down = g_ref[k]
            d_prod = matmul(lift_down[...], g_down).astype(jnp.bfloat16)
            both = matmul_nt(x_down, jnp.concatenate([mix_down[...], d_prod], axis=0))
            comp = both[:, :rank].astype(jnp.bfloat16)
            d_comp = (both[:, rank:] * scaling).astype(jnp.bfloat16)
            x_flat = x_down.T
            wide = matmul(x_flat, jnp.concatenate([comp, d_comp, g_down], axis=1))
            prod = (wide[:, :rank] * scaling).astype(jnp.bfloat16)
            part_lift = matmul(g_down, prod)
            d_in = g_down.astype(jnp.float32)
            d_in = d_in + matmul(jnp.concatenate([g_down, d_comp], axis=1), stacked[...])
            d_in = d_in + scaling * matmul(comp, d_prod)
            slot = slot_ref[pl.ds(sample, 1), :]
            extra = jnp.where(extra_at == 0, slot >> 4, jnp.where(extra_at == 1, slot & 15, 0))
            rows_down = jnp.concatenate(
                [d_in.astype(jnp.bfloat16), extra.astype(jnp.float32).astype(jnp.bfloat16)], axis=0
            )
            move = one_hot(row_at == rank_ref[pl.ds(sample, 1), :])
            ordered = matmul_nt(move, rows_down)
            sorted_a[k, :feats] = ordered[:, :128]
            sorted_b[k, :feats] = ordered[:, 128:]
            total_q = wide[:, rank:] if total_q is None else total_q + wide[:, rank:]
            total_lift = part_lift if total_lift is None else total_lift + part_lift
        mix_sum[...] += total_q[:, :rank]
        linear_sum[...] += total_q[:, rank:]
        lift_sum[...] += total_lift
        for k in range(group):
            sample = step * group + k
            begin = 0
            for owner in range(owners):
                number = count_ref[sample, owner]
                at = filled[owner]
                row_a[owner, pl.ds(at, COPY_ROWS), :] = sorted_a[k, pl.ds(begin, COPY_ROWS), :]
                row_b[owner, pl.ds(at, COPY_ROWS), :] = sorted_b[k, pl.ds(begin, COPY_ROWS), :]

                @pl.when(number > COPY_ROWS)
                def _(begin=begin, at=at, number=number, owner=owner, k=k):
                    def more(turn, carry):
                        off = turn * COPY_ROWS
                        row_a[owner, pl.ds(at + off, COPY_ROWS), :] = sorted_a[
                            k, pl.ds(begin + off, COPY_ROWS), :
                        ]
                        row_b[owner, pl.ds(at + off, COPY_ROWS), :] = sorted_b[
                            k, pl.ds(begin + off, COPY_ROWS), :
                        ]
                        return carry

                    lax.fori_loop(1, (number + COPY_ROWS - 1) // COPY_ROWS, more, 0)

                filled[owner] = at + number
                begin = begin + number

    @pl.when(step == steps - 1)
    def _():
        dense_ref[:feats] = mix_sum[...]
        linear = linear_sum[...].T
        for at in range(feats // 128):
            dense_ref[feats * (1 + at) : feats * (2 + at)] = linear[:, 128 * at : 128 * (at + 1)]
        dense_ref[feats * (1 + feats // 128) :] = lift_sum[...]

    @pl.when(step >= steps)
    def _():
        place = owners - 1 - (step - steps)
        owner = place ^ me_ref[1]
        piece = keep_refs[0].shape[3]
        first = row_a[owner, pl.ds(0, per_owner), :]
        second = row_b[owner, pl.ds(0, per_owner), :]
        rows_down = jnp.concatenate([first.T, second.T[: width - 128]], axis=0).astype(jnp.bfloat16)
        at = width - 128
        slots = second[:, at : at + 1] * 16.0 + second[:, at + 1 : at + 2]
        slots = slots.astype(jnp.int32)
        lanes = lax.broadcasted_iota(jnp.int32, (per_owner, piece), 1)
        for outer in range(outers):
            base = (outer ^ me_ref[0]) * piece
            hot = one_hot(lanes == slots - base)
            staged[outer] = matmul(rows_down, hot).astype(jnp.bfloat16)
        for index in range(far):

            @pl.when(place // 2 == index)
            def _(index=index):
                for outer in range(outers):
                    refs = send_refs if outer % 2 else keep_refs
                    refs[index][0, outer // 2] = staged[outer]


def local_grads(counts, me, x_down, g_down, mix, lift_down, linear, ranks, slots, owners, outers, table_rows):
    samples, width, feats = x_down.shape
    rank = mix.shape[1]
    group = 4
    steps = samples // group
    per_owner = samples * feats // owners
    piece = table_rows // outers
    far = owners // 2
    sizes = (group, steps, owners, outers, per_owner, 1.0 / math.sqrt(width))
    part = (2, outers // 2, width, piece)

    def whole(shape):
        return pl.BlockSpec(shape, lambda i, *_: (0,) * len(shape))

    def part_spec(index):
        start = steps + 2 * (far - 1 - index)
        return pl.BlockSpec(
            (1,) + part[1:], lambda i, *_: (jnp.clip(start + 1 - i, 0, 1), 0, 0, 0)
        )

    sample_spec = pl.BlockSpec(
        (group, width, feats), lambda i, *_: (jnp.minimum(i, steps - 1), 0, 0)
    )
    dense_rows = feats * (1 + feats // 128) + width
    parts = [jax.ShapeDtypeStruct(part, jnp.bfloat16)] * (2 * far)
    room = per_owner + 64
    outs = pl.pallas_call(
        functools.partial(grads_kernel, sizes),
        out_shape=parts + [jax.ShapeDtypeStruct((dense_rows, 128), jnp.float32)],
        grid_spec=pltpu.PrefetchScalarGridSpec(
            num_scalar_prefetch=2,
            grid=(steps + owners,),
            in_specs=[
                sample_spec,
                sample_spec,
                whole((feats, rank)),
                whole((width, rank)),
                whole((feats, feats)),
                whole((samples, feats)),
                whole((samples, feats)),
            ],
            out_specs=[part_spec(index) for index in range(far)] * 2
            + [whole((dense_rows, 128))],
            scratch_shapes=[
                pltpu.VMEM((rank, feats), jnp.bfloat16),
                pltpu.VMEM((rank, width), jnp.bfloat16),
                pltpu.VMEM((feats + rank, feats), jnp.bfloat16),
                pltpu.VMEM((feats, rank), jnp.float32),
                pltpu.VMEM((width, rank), jnp.float32),
                pltpu.VMEM((feats, feats), jnp.float32),
                pltpu.VMEM((group, feats + 64, 128), jnp.float32),
                pltpu.VMEM((group, feats + 64, 128), jnp.float32),
                pltpu.VMEM((owners, room, 128), jnp.float32),
                pltpu.VMEM((owners, room, 128), jnp.float32),
                pltpu.VMEM((outers, width, piece), jnp.bfloat16),
                pltpu.SMEM((owners,), jnp.int32),
            ],
        ),
        compiler_params=pltpu.CompilerParams(vmem_limit_bytes=48 * 2**20),
        name="local_grads",
    )(counts, me, x_down, g_down, mix, lift_down, linear, ranks, slots)
    return outs[:far], outs[far : 2 * far], outs[2 * far]


def adagrad_kernel(me_ref, *refs):
    pieces, (table_ref, accum_ref, new_table_ref, new_accum_ref) = refs[:-4], refs[-4:]
    for index, piece in enumerate(pieces):

        @pl.when(pl.program_id(0) == index)
        def _(piece=piece):
            grad = piece[...].astype(jnp.float32)
            mean = jnp.sum(grad * grad, axis=0, keepdims=True) / grad.shape[0]
            updated = accum_ref[...] + mean
            new_accum_ref[...] = updated
            new_table_ref[...] = table_ref[...] - LEARN_RATE * grad / jnp.sqrt(updated)


def update_table(me, pieces, table_down, accum):
    width, table_rows = table_down.shape
    piece = table_rows // len(pieces)

    def moved(rows):
        return pl.BlockSpec((rows, piece), lambda i, me: (0, i ^ me[0]))

    return pl.pallas_call(
        adagrad_kernel,
        out_shape=(
            jax.ShapeDtypeStruct((width, table_rows), jnp.float32),
            jax.ShapeDtypeStruct((1, table_rows), jnp.float32),
        ),
        grid_spec=pltpu.PrefetchScalarGridSpec(
            num_scalar_prefetch=1,
            grid=(len(pieces),),
            in_specs=[pl.BlockSpec((width, piece), lambda i, me: (0, 0))] * len(pieces)
            + [moved(width), moved(1)],
            out_specs=[moved(width), moved(1)],
        ),
        name="update_table",
    )(me, *pieces, table_down, accum)


def swap(values, axis, bit):
    size = lax.axis_size(axis)
    return lax.ppermute(values, axis, [(i, i ^ bit) for i in range(size)])


def add_half(first, second):
    return (first.astype(jnp.float32) + second.astype(jnp.float32)).astype(jnp.bfloat16)


def tree_sum(values):
    while len(values) > 1:
        values = [values[i] + values[i + 1] for i in range(0, len(values), 2)]
    return values[0]


def sum_dense(dense, owners):
    outer, inner = lax.axis_index("outer"), lax.axis_index("inner")
    cuts = (("outer", 1, outer & 1), ("outer", 2, outer >> 1), ("inner", 1, inner & 1))
    for axis, bit, side in cuts:
        halves = dense.reshape(2, dense.shape[0] // 2, dense.shape[1])
        mine = lax.dynamic_index_in_dim(halves, side, 0, keepdims=False)
        other = lax.dynamic_index_in_dim(halves, 1 - side, 0, keepdims=False)
        dense = mine + swap(other, axis, bit)
    dense = tree_sum([dense] + [swap(dense, "inner", 2 * far) for far in range(1, owners // 2)])
    for axis, bit, side in reversed(cuts):
        other = swap(dense, axis, bit)
        dense = jnp.where(
            side == 0,
            jnp.concatenate([dense, other], axis=0),
            jnp.concatenate([other, dense], axis=0),
        )
    return dense


def sum_table(keep, send, owners):
    far_count = owners // 2
    mine = {}
    for far in reversed(range(far_count)):
        other = swap(send[far], "outer", 1)
        held = keep[far]
        if far % 2:
            part = add_half(held[1], other[1])
            rest = add_half(held[0], other[0])
            rest = (rest, swap(part, "inner", 1))
            part = add_half(rest[0][1], rest[1][1])
            rest = add_half(rest[0][0], rest[1][0])
            mine[far] = (rest, swap(part, "outer", 2))
        else:
            part = add_half(held[:, 1], other[:, 1])
            rest = add_half(held[:, 0], other[:, 0])
            rest = (rest, swap(part, "outer", 2))
            part = add_half(rest[0][1], rest[1][1])
            rest = add_half(rest[0][0], rest[1][0])
            mine[far] = (rest, swap(part, "inner", 1))
    terms = []
    for far in range(far_count):
        if far:
            terms.append(swap(add_half(*mine[far]), "inner", 2 * far).astype(jnp.float32))
        else:
            terms.append(mine[0][0].astype(jnp.float32) + mine[0][1].astype(jnp.float32))
    total = tree_sum(terms).astype(jnp.bfloat16)
    across = swap(total, "outer", 2)
    return [total, swap(total, "outer", 1), across, swap(across, "outer", 1)]


def dense_table(
    layer_input,
    out_grad,
    mix_weight,
    lift_weight,
    linear_weight,
    row_ids,
    row_home,
    table,
    row_accum,
):
    owners, outers = lax.axis_size("inner"), lax.axis_size("outer")
    sample_count = layer_input.shape[0]
    table_rows = table.shape[0]
    me = jnp.stack([lax.axis_index("outer"), lax.axis_index("inner")]).astype(jnp.int32)
    ranks, slots, counts = place_lookups(row_ids, row_home, owners, table_rows)
    keep, send, dense = local_grads(
        counts,
        me,
        jnp.swapaxes(layer_input, 1, 2),
        jnp.swapaxes(out_grad, 1, 2),
        mix_weight,
        lift_weight.T,
        linear_weight,
        ranks,
        slots,
        owners,
        outers,
        table_rows,
    )
    pieces = sum_table(keep, send, owners)
    dense = sum_dense(dense, owners) * (1.0 / (sample_count * outers * owners))
    new_table, new_accum = update_table(me, pieces, table.T, row_accum.reshape(1, -1))
    feats, width = layer_input.shape[1:]
    linear = [dense[feats * (1 + i) : feats * (2 + i)] for i in range(feats // 128)]
    return (
        new_table.T,
        new_accum.reshape(-1),
        dense[:feats],
        dense[feats * (1 + feats // 128) :].T,
        jnp.concatenate(linear, axis=1),
    )


def power_of_two(number):
    return number & (number - 1) == 0


def on_device(*arrays):
    owners, outers = lax.axis_size("inner"), lax.axis_size("outer")
    layer_input, mix_weight, row_home, table = (arrays[i] for i in (0, 2, 6, 7))
    samples, feats, width = layer_input.shape
    dense_fits = (
        outers == 4
        and owners % 4 == 0
        and power_of_two(owners)
        and row_home.shape[0] <= 2 * samples * feats
        and row_home.shape[0] <= 2**15
        and power_of_two(table.shape[0])
        and 512 <= table.shape[0] <= 4096
        and samples % 16 == 0
        and feats == 256
        and mix_weight.shape[1] == 128
        and 128 < width <= feats - 16
        and width % 16 == 0
    )
    return dense_table(*arrays) if dense_fits else routed_rows(*arrays)


def solution(mesh):
    placed = (
        P(("outer", "inner"), None, None),
        P(("outer", "inner"), None, None),
        P(),
        P(),
        P(),
        P(("outer", "inner"), None),
        P(),
        P("inner", None),
        P("inner"),
    )
    return jax.shard_map(
        on_device,
        mesh=mesh,
        in_specs=placed,
        out_specs=(P("inner", None), P("inner"), P(), P(), P()),
        check_vma=False,
    )
```

```python
import functools
import math

import jax
import jax.numpy as jnp
from jax import lax
from jax.experimental import pallas as pl
from jax.experimental.pallas import tpu as pltpu
from jax.sharding import PartitionSpec as P

LEARN_RATE = 0.5


def interaction_grads(inputs, cotangent, mix_weight, lift_weight, linear_weight, scaling):
    compressed = jnp.einsum(
        "bfd,fk->bdk", inputs, mix_weight, preferred_element_type=jnp.float32
    ).astype(jnp.bfloat16)
    products = (
        jnp.einsum("bfd,bdk->bfk", inputs, compressed, preferred_element_type=jnp.float32) * scaling
    ).astype(jnp.bfloat16)
    d_products = jnp.einsum(
        "bfd,kd->bfk", cotangent, lift_weight, preferred_element_type=jnp.float32
    ).astype(jnp.bfloat16)
    d_compressed = (
        jnp.einsum("bfd,bfk->bdk", inputs, d_products, preferred_element_type=jnp.float32) * scaling
    ).astype(jnp.bfloat16)
    d_inputs = cotangent.astype(jnp.float32)
    d_inputs = d_inputs + jnp.einsum(
        "fg,bfd->bgd", linear_weight, cotangent, preferred_element_type=jnp.float32
    )
    d_inputs = d_inputs + scaling * jnp.einsum(
        "bfk,bdk->bfd", d_products, compressed, preferred_element_type=jnp.float32
    )
    d_inputs = d_inputs + jnp.einsum(
        "fk,bdk->bfd", mix_weight, d_compressed, preferred_element_type=jnp.float32
    )
    g_mix = jnp.einsum("bfd,bdk->fk", inputs, d_compressed, preferred_element_type=jnp.float32)
    g_lift = jnp.einsum("bfk,bfd->kd", products, cotangent, preferred_element_type=jnp.float32)
    g_linear = jnp.einsum("bfd,bgd->fg", cotangent, inputs, preferred_element_type=jnp.float32)
    rows_out = d_inputs.astype(jnp.bfloat16).reshape(-1, d_inputs.shape[2])
    return (rows_out, (g_mix, g_lift, g_linear))


def adagrad(weights, history, gradient):
    updated = history + jnp.mean(gradient * gradient, axis=1)
    return (weights - LEARN_RATE * gradient / jnp.sqrt(updated)[:, None], updated)


def owner_ranks(owner_of, owners):
    lookups = owner_of.shape[0]
    width = math.gcd(lookups, 128)
    groups = lookups // width
    hot = (owner_of[:, None] == jnp.arange(owners, dtype=jnp.int32)[None, :]).astype(jnp.bfloat16)
    hot = hot.reshape(groups, width, owners)
    lower = (jnp.arange(width)[:, None] > jnp.arange(width)[None, :]).astype(jnp.bfloat16)
    within = jnp.einsum("ij,gjo->gio", lower, hot, preferred_element_type=jnp.float32)
    totals = jnp.sum(hot.astype(jnp.float32), axis=1)
    before = jnp.cumsum(totals, axis=0) - totals
    counted = jnp.sum(hot.astype(jnp.float32) * (within + before[:, None, :]), axis=2)
    return counted.reshape(-1).astype(jnp.int32)


def add_rows(collected, slots, values):
    count = values.shape[0]
    table_rows = collected.shape[0]
    width = math.gcd(count, 2048)
    columns = jnp.arange(table_rows, dtype=jnp.int32)
    for block_index in range(count // width):
        start = block_index * width
        hot = (slots[start : start + width, None] == columns[None, :]).astype(jnp.bfloat16)
        collected = collected + jnp.einsum(
            "lr,ld->rd", hot, values[start : start + width], preferred_element_type=jnp.float32
        )
    return collected


def routed_rows(
    layer_input,
    out_grad,
    mix_weight,
    lift_weight,
    linear_weight,
    row_ids,
    row_home,
    table,
    row_accum,
):
    owners = lax.axis_size("inner")
    sample_count, feature_count, embed_width = layer_input.shape
    table_rows = table.shape[0]
    half_samples = sample_count // 2
    lookups = sample_count * feature_count
    per_owner = lookups // (2 * owners)
    scaling = 1.0 / math.sqrt(embed_width)
    placed = jnp.take(row_home, row_ids.reshape(-1), axis=0)
    owner_of = placed // table_rows
    target = owner_of * (2 * per_owner) + owner_ranks(owner_of, owners)
    ordering = jnp.zeros((lookups,), jnp.int32).at[target].set(jnp.arange(lookups, dtype=jnp.int32))
    ordering = ordering.reshape(owners, 2, per_owner)
    local_rows = (
        jnp.zeros((lookups,), jnp.int32)
        .at[target]
        .set(placed % table_rows)
        .reshape(owners, 2 * per_owner)
    )
    arrived_rows = lax.all_to_all(
        local_rows, "inner", split_axis=0, concat_axis=0, tiled=True
    ).reshape(owners, 2, per_owner)
    collected = jnp.zeros((table_rows, embed_width), jnp.float32)
    totals = None
    for half_index in range(2):
        first_sample = half_index * half_samples
        rows_out, partial_value = interaction_grads(
            layer_input[first_sample : first_sample + half_samples],
            out_grad[first_sample : first_sample + half_samples],
            mix_weight,
            lift_weight,
            linear_weight,
            scaling,
        )
        picked = ordering[:, half_index, :] - half_index * half_samples * feature_count
        outgoing = jnp.take(rows_out, picked.reshape(-1), axis=0).reshape(
            owners, per_owner, embed_width
        )
        incoming = lax.all_to_all(outgoing, "inner", split_axis=0, concat_axis=0, tiled=True)
        collected = add_rows(
            collected, arrived_rows[:, half_index, :].reshape(-1), incoming.reshape(-1, embed_width)
        )
        if totals is None:
            totals = partial_value
        else:
            totals = tuple((earlier + later for earlier, later in zip(totals, partial_value)))
    batch_total = sample_count * lax.axis_size("outer") * owners
    summed = lax.psum((totals[0], totals[1], totals[2]), ("outer", "inner"))
    mix_grad = summed[0] / batch_total
    lift_grad = summed[1] / batch_total
    linear_grad = summed[2] / batch_total
    complete = lax.psum(collected, "outer")
    new_table, new_accum = adagrad(table, row_accum, complete)
    return (new_table, new_accum, mix_grad, lift_grad, linear_grad)


def matmul(left, right):
    return jnp.dot(left, right, preferred_element_type=jnp.float32)


def matmul_nt(left, right):
    return lax.dot_general(left, right, (((1,), (1,)), ((), ())), preferred_element_type=jnp.float32)


def one_hot(matches):
    return jnp.where(matches, 1.0, 0.0).astype(jnp.bfloat16)


def place_kernel(shift, owners, ids_ref, home_ref, rank_ref, slot_ref, count_ref):
    samples, feats = ids_ref.shape
    high, low = home_ref.shape
    home = home_ref[...]
    pieces = jnp.concatenate(
        [(home & 255).astype(jnp.float32).T, (home >> 8).astype(jnp.float32).T], axis=0
    ).astype(jnp.bfloat16)
    high_at = lax.broadcasted_iota(jnp.int32, (high, feats), 0)
    low_at = lax.broadcasted_iota(jnp.int32, (low, feats), 0)
    lane = lax.broadcasted_iota(jnp.int32, (1, feats), 1)
    count_lane = lax.broadcasted_iota(jnp.int32, (8, 128), 1)

    @pl.loop(0, samples // 8)
    def _(group):
        first = pl.multiple_of(group * 8, 8)
        ids = ids_ref[pl.ds(first, 8), :]
        ranks, slots, homes = [], [], []
        for row in range(8):
            one = ids[row : row + 1]
            found = matmul(pieces, one_hot(high_at == (one >> 7)))
            value = found[:low] + 256.0 * found[low:]
            place = jnp.sum(jnp.where(low_at == (one & 127), value, 0.0), axis=0, keepdims=True)
            place = place.astype(jnp.int32)
            owner = place >> shift
            key = (owner * feats + lane).astype(jnp.float32)
            key_down = jnp.broadcast_to(key, (128, feats)).T
            parts = []
            for at in range(0, feats, 128):
                less = key_down < key[:, at : at + 128]
                parts.append(jnp.sum(jnp.where(less, 1.0, 0.0), axis=0, keepdims=True))
            ranks.append(jnp.concatenate(parts, axis=1).astype(jnp.int32))
            slots.append(place & ((1 << shift) - 1))
            homes.append(owner)
        rank_ref[pl.ds(first, 8), :] = jnp.concatenate(ranks, axis=0)
        slot_ref[pl.ds(first, 8), :] = jnp.concatenate(slots, axis=0)
        owner_all = jnp.concatenate(homes, axis=0)
        counts = jnp.zeros((8, 128), jnp.float32)
        for owner_at in range(owners):
            number = jnp.sum(jnp.where(owner_all == owner_at, 1.0, 0.0), axis=1, keepdims=True)
            counts = jnp.where(count_lane == owner_at, number, counts)
        count_ref[pl.ds(first, 8), :] = counts.astype(jnp.int32)


def place_lookups(row_ids, row_home, owners, table_rows):
    samples, feats = row_ids.shape
    return pl.pallas_call(
        functools.partial(place_kernel, table_rows.bit_length() - 1, owners),
        out_shape=(
            jax.ShapeDtypeStruct((samples, feats), jnp.int32),
            jax.ShapeDtypeStruct((samples, feats), jnp.int32),
            jax.ShapeDtypeStruct((samples, 128), jnp.int32),
        ),
        name="place_lookups",
    )(row_ids, row_home.reshape(-1, 128))


COPY_ROWS = 48


def grads_kernel(
    sizes,
    count_ref,
    x_ref,
    g_ref,
    mix_ref,
    lift_ref,
    linear_ref,
    rank_ref,
    slot_ref,
    rows_ref,
    dense_ref,
    mix_down,
    lift_down,
    stacked,
    mix_sum,
    lift_sum,
    linear_sum,
    sorted_a,
    sorted_b,
    row_a,
    row_b,
    filled,
):
    group, steps, owners, per_owner, scaling = sizes
    width, feats = x_ref.shape[1:]
    rank = mix_ref.shape[1]
    step = pl.program_id(0)

    @pl.when(step == 0)
    def _():
        mix_down[...] = mix_ref[...].astype(jnp.float32).T.astype(jnp.bfloat16)
        lift_down[...] = lift_ref[...].astype(jnp.float32).T.astype(jnp.bfloat16)
        stacked[:feats] = linear_ref[...]
        stacked[feats:] = mix_down[...]
        mix_sum[...] = jnp.zeros_like(mix_sum)
        lift_sum[...] = jnp.zeros_like(lift_sum)
        linear_sum[...] = jnp.zeros_like(linear_sum)
        for owner in range(owners):
            filled[owner] = 0

    total_q, total_lift = None, None
    row_at = lax.broadcasted_iota(jnp.int32, (feats, feats), 0)
    extra_at = lax.broadcasted_iota(jnp.int32, (feats - width, feats), 0)
    for k in range(group):
        sample = step * group + k
        x_down = x_ref[k]
        g_down = g_ref[k]
        d_prod = matmul(lift_down[...], g_down).astype(jnp.bfloat16)
        both = matmul_nt(x_down, jnp.concatenate([mix_down[...], d_prod], axis=0))
        comp = both[:, :rank].astype(jnp.bfloat16)
        d_comp = (both[:, rank:] * scaling).astype(jnp.bfloat16)
        x_flat = x_down.T
        wide = matmul(x_flat, jnp.concatenate([comp, d_comp, g_down], axis=1))
        prod = (wide[:, :rank] * scaling).astype(jnp.bfloat16)
        part_lift = matmul(g_down, prod)
        d_in = g_down.astype(jnp.float32)
        d_in = d_in + matmul(jnp.concatenate([g_down, d_comp], axis=1), stacked[...])
        d_in = d_in + scaling * matmul(comp, d_prod)
        slot = slot_ref[pl.ds(sample, 1), :]
        extra = jnp.where(extra_at == 0, slot >> 4, jnp.where(extra_at == 1, slot & 15, 0))
        rows_down = jnp.concatenate(
            [d_in.astype(jnp.bfloat16), extra.astype(jnp.float32).astype(jnp.bfloat16)], axis=0
        )
        move = one_hot(row_at == rank_ref[pl.ds(sample, 1), :])
        ordered = matmul_nt(move, rows_down)
        sorted_a[k, :feats] = ordered[:, :128]
        sorted_b[k, :feats] = ordered[:, 128:]
        total_q = wide[:, rank:] if total_q is None else total_q + wide[:, rank:]
        total_lift = part_lift if total_lift is None else total_lift + part_lift
    mix_sum[...] += total_q[:, :rank]
    linear_sum[...] += total_q[:, rank:]
    lift_sum[...] += total_lift
    for k in range(group):
        sample = step * group + k
        begin = 0
        for owner in range(owners):
            number = count_ref[sample, owner]
            at = filled[owner]
            row_a[owner, pl.ds(at, COPY_ROWS), :] = sorted_a[k, pl.ds(begin, COPY_ROWS), :]
            row_b[owner, pl.ds(at, COPY_ROWS), :] = sorted_b[k, pl.ds(begin, COPY_ROWS), :]

            @pl.when(number > COPY_ROWS)
            def _(begin=begin, at=at, number=number, owner=owner, k=k):
                def more(turn, carry):
                    off = turn * COPY_ROWS
                    row_a[owner, pl.ds(at + off, COPY_ROWS), :] = sorted_a[
                        k, pl.ds(begin + off, COPY_ROWS), :
                    ]
                    row_b[owner, pl.ds(at + off, COPY_ROWS), :] = sorted_b[
                        k, pl.ds(begin + off, COPY_ROWS), :
                    ]
                    return carry

                lax.fori_loop(1, (number + COPY_ROWS - 1) // COPY_ROWS, more, 0)

            filled[owner] = at + number
            begin = begin + number

    @pl.when(step == steps - 1)
    def _():
        dense_ref[:feats] = mix_sum[...]
        linear = linear_sum[...].T
        for at in range(feats // 128):
            dense_ref[feats * (1 + at) : feats * (2 + at)] = linear[:, 128 * at : 128 * (at + 1)]
        dense_ref[feats * (1 + feats // 128) :] = lift_sum[...]
        for owner in range(owners):
            rows_ref[owner, :, :128] = row_a[owner, :per_owner, :].astype(jnp.bfloat16)
            rows_ref[owner, :, 128:] = row_b[owner, :per_owner, :].astype(jnp.bfloat16)


def local_grads(counts, x_down, g_down, mix, lift_down, linear, ranks, slots, owners):
    samples, width, feats = x_down.shape
    rank = mix.shape[1]
    group = 4
    steps = samples // group
    per_owner = samples * feats // owners
    sizes = (group, steps, owners, per_owner, 1.0 / math.sqrt(width))

    def whole(shape):
        return pl.BlockSpec(shape, lambda i, *_: (0,) * len(shape))

    sample_spec = pl.BlockSpec((group, width, feats), lambda i, *_: (i, 0, 0))
    dense_rows = feats * (1 + feats // 128) + width
    room = per_owner + 64
    return pl.pallas_call(
        functools.partial(grads_kernel, sizes),
        out_shape=(
            jax.ShapeDtypeStruct((owners, per_owner, 256), jnp.bfloat16),
            jax.ShapeDtypeStruct((dense_rows, 128), jnp.float32),
        ),
        grid_spec=pltpu.PrefetchScalarGridSpec(
            num_scalar_prefetch=1,
            grid=(steps,),
            in_specs=[
                sample_spec,
                sample_spec,
                whole((feats, rank)),
                whole((width, rank)),
                whole((feats, feats)),
                whole((samples, feats)),
                whole((samples, feats)),
            ],
            out_specs=(whole((owners, per_owner, 256)), whole((dense_rows, 128))),
            scratch_shapes=[
                pltpu.VMEM((rank, feats), jnp.bfloat16),
                pltpu.VMEM((rank, width), jnp.bfloat16),
                pltpu.VMEM((feats + rank, feats), jnp.bfloat16),
                pltpu.VMEM((feats, rank), jnp.float32),
                pltpu.VMEM((width, rank), jnp.float32),
                pltpu.VMEM((feats, feats), jnp.float32),
                pltpu.VMEM((group, feats + 64, 128), jnp.float32),
                pltpu.VMEM((group, feats + 64, 128), jnp.float32),
                pltpu.VMEM((owners, room, 128), jnp.float32),
                pltpu.VMEM((owners, room, 128), jnp.float32),
                pltpu.SMEM((owners,), jnp.int32),
            ],
        ),
        compiler_params=pltpu.CompilerParams(vmem_limit_bytes=60 * 2**20),
        cost_estimate=pl.CostEstimate(
            flops=2 * samples * feats * feats * 2048, bytes_accessed=12 * 2**20, transcendentals=0
        ),
        name="local_grads",
    )(counts, x_down, g_down, mix, lift_down, linear, ranks, slots)


def build_kernel(at, me_ref, rows_ref, keep_ref, send_ref):
    outers = 2 * keep_ref.shape[1]
    piece = keep_ref.shape[2] * 2 // 3
    half = piece // 2
    rows = rows_ref[0]
    per_owner = rows.shape[0]
    lane = lax.broadcasted_iota(jnp.int32, (8, 128), 1)
    pick = jnp.where(lane == at, 16.0, jnp.where(lane == at + 1, 1.0, 0.0)).astype(jnp.bfloat16)
    slots = matmul_nt(pick, rows[:, 128:])[:1].astype(jnp.int32)
    down = lax.broadcasted_iota(jnp.int32, (piece, per_owner), 0)
    left = lax.broadcasted_iota(jnp.int32, (half, 128), 1) < at
    for outer in range(outers):
        base = (outer ^ me_ref[0]) * piece
        total = matmul(one_hot(down == slots - base), rows)
        ref = send_ref if outer % 2 else keep_ref
        ref[0, outer // 2, :piece] = total[:, :128].astype(jnp.bfloat16)
        upper, lower = total[:half, 128:], total[half:, 128:]
        joined = jnp.where(left, upper, pltpu.roll(lower, at, 1))
        ref[0, outer // 2, piece:] = joined.astype(jnp.bfloat16)


def build_part(me, rows, far, table_rows, width, outers):
    owners, per_owner, lanes = rows.shape
    piece = table_rows // outers
    part = (2, outers // 2, piece * 3 // 2, 128)
    spec = pl.BlockSpec((1,) + part[1:], lambda i, me: (i, 0, 0, 0))
    return pl.pallas_call(
        functools.partial(build_kernel, width - 128),
        out_shape=(jax.ShapeDtypeStruct(part, jnp.bfloat16),) * 2,
        grid_spec=pltpu.PrefetchScalarGridSpec(
            num_scalar_prefetch=1,
            grid=(2,),
            in_specs=[
                pl.BlockSpec((1, per_owner, lanes), lambda i, me: ((2 * far + i) ^ me[1], 0, 0))
            ],
            out_specs=(spec, spec),
        ),
        compiler_params=pltpu.CompilerParams(vmem_limit_bytes=32 * 2**20),
        cost_estimate=pl.CostEstimate(
            flops=4 * table_rows * per_owner * lanes, bytes_accessed=3 * 2**20, transcendentals=0
        ),
        name="build_part",
    )(me, rows)


def adagrad_kernel(me_ref, *refs):
    pieces, (table_ref, accum_ref, new_table_ref, new_accum_ref) = refs[:-4], refs[-4:]
    width, piece = table_ref.shape
    half, at = piece // 2, width - 128
    for index, packed in enumerate(pieces):

        @pl.when(pl.program_id(0) == index)
        def _(packed=packed):
            first = packed[:piece].astype(jnp.float32).T
            second = packed[piece:].astype(jnp.float32).T
            second = jnp.concatenate([second[:at], second[at:]], axis=1)
            grad = jnp.concatenate([first, second], axis=0)
            mean = jnp.sum(grad * grad, axis=0, keepdims=True) * (1.0 / width)
            updated = accum_ref[...] + mean
            new_accum_ref[...] = updated
            new_table_ref[...] = table_ref[...] - grad * (LEARN_RATE / jnp.sqrt(updated))


def update_table(me, pieces, table_down, accum):
    width, table_rows = table_down.shape
    piece = table_rows // len(pieces)

    def moved(rows):
        return pl.BlockSpec((rows, piece), lambda i, me: (0, i ^ me[0]))

    return pl.pallas_call(
        adagrad_kernel,
        out_shape=(
            jax.ShapeDtypeStruct((width, table_rows), jnp.float32),
            jax.ShapeDtypeStruct((1, table_rows), jnp.float32),
        ),
        grid_spec=pltpu.PrefetchScalarGridSpec(
            num_scalar_prefetch=1,
            grid=(len(pieces),),
            in_specs=[pl.BlockSpec(pieces[0].shape, lambda i, me: (0, 0))] * len(pieces)
            + [moved(width), moved(1)],
            out_specs=[moved(width), moved(1)],
        ),
        name="update_table",
    )(me, *pieces, table_down, accum)


def swap(values, axis, bit):
    size = lax.axis_size(axis)
    return lax.ppermute(values, axis, [(i, i ^ bit) for i in range(size)])


def add_half(first, second):
    return (first.astype(jnp.float32) + second.astype(jnp.float32)).astype(jnp.bfloat16)


def tree_sum(values):
    while len(values) > 1:
        values = [values[i] + values[i + 1] for i in range(0, len(values), 2)]
    return values[0]


def sum_dense(dense, owners):
    outer, inner = lax.axis_index("outer"), lax.axis_index("inner")
    cuts = (("outer", 1, outer & 1), ("outer", 2, outer >> 1), ("inner", 1, inner & 1))
    for axis, bit, side in cuts:
        halves = dense.reshape(2, dense.shape[0] // 2, dense.shape[1])
        mine = lax.dynamic_index_in_dim(halves, side, 0, keepdims=False)
        other = lax.dynamic_index_in_dim(halves, 1 - side, 0, keepdims=False)
        dense = mine + swap(other, axis, bit)
    dense = tree_sum([dense] + [swap(dense, "inner", 2 * far) for far in range(1, owners // 2)])
    for axis, bit, side in reversed(cuts):
        other = swap(dense, axis, bit)
        dense = jnp.where(
            side == 0,
            jnp.concatenate([dense, other], axis=0),
            jnp.concatenate([other, dense], axis=0),
        )
    return dense


def sum_table(keep, send, owners):
    far_count = owners // 2
    mine = {}
    for far in reversed(range(far_count)):
        other = swap(send[far], "outer", 1)
        held = keep[far]
        if far % 2:
            part = add_half(held[1], other[1])
            rest = add_half(held[0], other[0])
            rest = (rest, swap(part, "inner", 1))
            part = add_half(rest[0][1], rest[1][1])
            rest = add_half(rest[0][0], rest[1][0])
            mine[far] = (rest, swap(part, "outer", 2))
        else:
            part = add_half(held[:, 1], other[:, 1])
            rest = add_half(held[:, 0], other[:, 0])
            rest = (rest, swap(part, "outer", 2))
            part = add_half(rest[0][1], rest[1][1])
            rest = add_half(rest[0][0], rest[1][0])
            mine[far] = (rest, swap(part, "inner", 1))
    terms = []
    for far in range(far_count):
        if far:
            terms.append(swap(add_half(*mine[far]), "inner", 2 * far).astype(jnp.float32))
        else:
            terms.append(mine[0][0].astype(jnp.float32) + mine[0][1].astype(jnp.float32))
    total = tree_sum(terms).astype(jnp.bfloat16)
    across = swap(total, "outer", 2)
    return [total, swap(total, "outer", 1), across, swap(across, "outer", 1)]


def dense_table(
    layer_input,
    out_grad,
    mix_weight,
    lift_weight,
    linear_weight,
    row_ids,
    row_home,
    table,
    row_accum,
):
    owners, outers = lax.axis_size("inner"), lax.axis_size("outer")
    sample_count = layer_input.shape[0]
    table_rows = table.shape[0]
    me = jnp.stack([lax.axis_index("outer"), lax.axis_index("inner")]).astype(jnp.int32)
    ranks, slots, counts = place_lookups(row_ids, row_home, owners, table_rows)
    rows, dense = local_grads(
        counts,
        jnp.swapaxes(layer_input, 1, 2),
        jnp.swapaxes(out_grad, 1, 2),
        mix_weight,
        lift_weight.T,
        linear_weight,
        ranks,
        slots,
        owners,
    )
    width = layer_input.shape[2]
    keep, send = {}, {}
    for far in reversed(range(owners // 2)):
        keep[far], send[far] = build_part(me, rows, far, table_rows, width, outers)
    pieces = sum_table(keep, send, owners)
    dense = sum_dense(dense, owners) * (1.0 / (sample_count * outers * owners))
    new_table, new_accum = update_table(me, pieces, table.T, row_accum.reshape(1, -1))
    feats, width = layer_input.shape[1:]
    linear = [dense[feats * (1 + i) : feats * (2 + i)] for i in range(feats // 128)]
    return (
        new_table.T,
        new_accum.reshape(-1),
        dense[:feats],
        dense[feats * (1 + feats // 128) :].T,
        jnp.concatenate(linear, axis=1),
    )


def power_of_two(number):
    return number & (number - 1) == 0


def on_device(*arrays):
    owners, outers = lax.axis_size("inner"), lax.axis_size("outer")
    layer_input, mix_weight, row_home, table = (arrays[i] for i in (0, 2, 6, 7))
    samples, feats, width = layer_input.shape
    dense_fits = (
        outers == 4
        and owners % 4 == 0
        and power_of_two(owners)
        and row_home.shape[0] <= 2 * samples * feats
        and row_home.shape[0] <= 2**15
        and power_of_two(table.shape[0])
        and 512 <= table.shape[0] <= 4096
        and samples % 16 == 0
        and feats == 256
        and mix_weight.shape[1] == 128
        and 2 * (width - 128) == 128
    )
    return dense_table(*arrays) if dense_fits else routed_rows(*arrays)


def solution(mesh):
    placed = (
        P(("outer", "inner"), None, None),
        P(("outer", "inner"), None, None),
        P(),
        P(),
        P(),
        P(("outer", "inner"), None),
        P(),
        P("inner", None),
        P("inner"),
    )
    return jax.shard_map(
        on_device,
        mesh=mesh,
        in_specs=placed,
        out_specs=(P("inner", None), P("inner"), P(), P(), P()),
        check_vma=False,
    )
```

```python
import functools
import math

import jax
import jax.numpy as jnp
from jax import lax
from jax.experimental import pallas as pl
from jax.experimental.pallas import tpu as pltpu
from jax.sharding import PartitionSpec as P

LEARN_RATE = 0.5


def interaction_grads(inputs, cotangent, mix_weight, lift_weight, linear_weight, scaling):
    compressed = jnp.einsum(
        "bfd,fk->bdk", inputs, mix_weight, preferred_element_type=jnp.float32
    ).astype(jnp.bfloat16)
    products = (
        jnp.einsum("bfd,bdk->bfk", inputs, compressed, preferred_element_type=jnp.float32) * scaling
    ).astype(jnp.bfloat16)
    d_products = jnp.einsum(
        "bfd,kd->bfk", cotangent, lift_weight, preferred_element_type=jnp.float32
    ).astype(jnp.bfloat16)
    d_compressed = (
        jnp.einsum("bfd,bfk->bdk", inputs, d_products, preferred_element_type=jnp.float32) * scaling
    ).astype(jnp.bfloat16)
    d_inputs = cotangent.astype(jnp.float32)
    d_inputs = d_inputs + jnp.einsum(
        "fg,bfd->bgd", linear_weight, cotangent, preferred_element_type=jnp.float32
    )
    d_inputs = d_inputs + scaling * jnp.einsum(
        "bfk,bdk->bfd", d_products, compressed, preferred_element_type=jnp.float32
    )
    d_inputs = d_inputs + jnp.einsum(
        "fk,bdk->bfd", mix_weight, d_compressed, preferred_element_type=jnp.float32
    )
    g_mix = jnp.einsum("bfd,bdk->fk", inputs, d_compressed, preferred_element_type=jnp.float32)
    g_lift = jnp.einsum("bfk,bfd->kd", products, cotangent, preferred_element_type=jnp.float32)
    g_linear = jnp.einsum("bfd,bgd->fg", cotangent, inputs, preferred_element_type=jnp.float32)
    rows_out = d_inputs.astype(jnp.bfloat16).reshape(-1, d_inputs.shape[2])
    return (rows_out, (g_mix, g_lift, g_linear))


def adagrad(weights, history, gradient):
    updated = history + jnp.mean(gradient * gradient, axis=1)
    return (weights - LEARN_RATE * gradient / jnp.sqrt(updated)[:, None], updated)


def owner_ranks(owner_of, owners):
    lookups = owner_of.shape[0]
    width = math.gcd(lookups, 128)
    groups = lookups // width
    hot = (owner_of[:, None] == jnp.arange(owners, dtype=jnp.int32)[None, :]).astype(jnp.bfloat16)
    hot = hot.reshape(groups, width, owners)
    lower = (jnp.arange(width)[:, None] > jnp.arange(width)[None, :]).astype(jnp.bfloat16)
    within = jnp.einsum("ij,gjo->gio", lower, hot, preferred_element_type=jnp.float32)
    totals = jnp.sum(hot.astype(jnp.float32), axis=1)
    before = jnp.cumsum(totals, axis=0) - totals
    counted = jnp.sum(hot.astype(jnp.float32) * (within + before[:, None, :]), axis=2)
    return counted.reshape(-1).astype(jnp.int32)


def add_rows(collected, slots, values):
    count = values.shape[0]
    table_rows = collected.shape[0]
    width = math.gcd(count, 2048)
    columns = jnp.arange(table_rows, dtype=jnp.int32)
    for block_index in range(count // width):
        start = block_index * width
        hot = (slots[start : start + width, None] == columns[None, :]).astype(jnp.bfloat16)
        collected = collected + jnp.einsum(
            "lr,ld->rd", hot, values[start : start + width], preferred_element_type=jnp.float32
        )
    return collected


def routed_rows(
    layer_input,
    out_grad,
    mix_weight,
    lift_weight,
    linear_weight,
    row_ids,
    row_home,
    table,
    row_accum,
):
    owners = lax.axis_size("inner")
    sample_count, feature_count, embed_width = layer_input.shape
    table_rows = table.shape[0]
    half_samples = sample_count // 2
    lookups = sample_count * feature_count
    per_owner = lookups // (2 * owners)
    scaling = 1.0 / math.sqrt(embed_width)
    placed = jnp.take(row_home, row_ids.reshape(-1), axis=0)
    owner_of = placed // table_rows
    target = owner_of * (2 * per_owner) + owner_ranks(owner_of, owners)
    ordering = jnp.zeros((lookups,), jnp.int32).at[target].set(jnp.arange(lookups, dtype=jnp.int32))
    ordering = ordering.reshape(owners, 2, per_owner)
    local_rows = (
        jnp.zeros((lookups,), jnp.int32)
        .at[target]
        .set(placed % table_rows)
        .reshape(owners, 2 * per_owner)
    )
    arrived_rows = lax.all_to_all(
        local_rows, "inner", split_axis=0, concat_axis=0, tiled=True
    ).reshape(owners, 2, per_owner)
    collected = jnp.zeros((table_rows, embed_width), jnp.float32)
    totals = None
    for half_index in range(2):
        first_sample = half_index * half_samples
        rows_out, partial_value = interaction_grads(
            layer_input[first_sample : first_sample + half_samples],
            out_grad[first_sample : first_sample + half_samples],
            mix_weight,
            lift_weight,
            linear_weight,
            scaling,
        )
        picked = ordering[:, half_index, :] - half_index * half_samples * feature_count
        outgoing = jnp.take(rows_out, picked.reshape(-1), axis=0).reshape(
            owners, per_owner, embed_width
        )
        incoming = lax.all_to_all(outgoing, "inner", split_axis=0, concat_axis=0, tiled=True)
        collected = add_rows(
            collected, arrived_rows[:, half_index, :].reshape(-1), incoming.reshape(-1, embed_width)
        )
        if totals is None:
            totals = partial_value
        else:
            totals = tuple((earlier + later for earlier, later in zip(totals, partial_value)))
    batch_total = sample_count * lax.axis_size("outer") * owners
    summed = lax.psum((totals[0], totals[1], totals[2]), ("outer", "inner"))
    mix_grad = summed[0] / batch_total
    lift_grad = summed[1] / batch_total
    linear_grad = summed[2] / batch_total
    complete = lax.psum(collected, "outer")
    new_table, new_accum = adagrad(table, row_accum, complete)
    return (new_table, new_accum, mix_grad, lift_grad, linear_grad)


def matmul(left, right):
    return jnp.dot(left, right, preferred_element_type=jnp.float32)


def matmul_nt(left, right):
    return lax.dot_general(left, right, (((1,), (1,)), ((), ())), preferred_element_type=jnp.float32)


def one_hot(matches):
    return jnp.where(matches, 1.0, 0.0).astype(jnp.bfloat16)


def place_kernel(shift, owners, ids_ref, home_ref, rank_ref, slot_ref, count_ref):
    samples, feats = ids_ref.shape
    high, low = home_ref.shape
    home = home_ref[...]
    pieces = jnp.concatenate(
        [(home & 255).astype(jnp.float32).T, (home >> 8).astype(jnp.float32).T], axis=0
    ).astype(jnp.bfloat16)
    high_at = lax.broadcasted_iota(jnp.int32, (high, feats), 0)
    low_at = lax.broadcasted_iota(jnp.int32, (low, feats), 0)
    lane = lax.broadcasted_iota(jnp.int32, (1, feats), 1)
    count_lane = lax.broadcasted_iota(jnp.int32, (8, 128), 1)

    @pl.loop(0, samples // 8)
    def _(group):
        first = pl.multiple_of(group * 8, 8)
        ids = ids_ref[pl.ds(first, 8), :]
        ranks, slots, homes = [], [], []
        for row in range(8):
            one = ids[row : row + 1]
            found = matmul(pieces, one_hot(high_at == (one >> 7)))
            value = found[:low] + 256.0 * found[low:]
            place = jnp.sum(jnp.where(low_at == (one & 127), value, 0.0), axis=0, keepdims=True)
            place = place.astype(jnp.int32)
            owner = place >> shift
            key = (owner * feats + lane).astype(jnp.float32)
            key_down = jnp.broadcast_to(key, (128, feats)).T
            parts = []
            for at in range(0, feats, 128):
                less = key_down < key[:, at : at + 128]
                parts.append(jnp.sum(jnp.where(less, 1.0, 0.0), axis=0, keepdims=True))
            ranks.append(jnp.concatenate(parts, axis=1).astype(jnp.int32))
            slots.append(place & ((1 << shift) - 1))
            homes.append(owner)
        rank_ref[pl.ds(first, 8), :] = jnp.concatenate(ranks, axis=0)
        slot_ref[pl.ds(first, 8), :] = jnp.concatenate(slots, axis=0)
        owner_all = jnp.concatenate(homes, axis=0)
        counts = jnp.zeros((8, 128), jnp.float32)
        for owner_at in range(owners):
            number = jnp.sum(jnp.where(owner_all == owner_at, 1.0, 0.0), axis=1, keepdims=True)
            counts = jnp.where(count_lane == owner_at, number, counts)
        most = jnp.max(counts, axis=1, keepdims=True)
        counts = jnp.where(count_lane == owners, most, counts)
        count_ref[pl.ds(first, 8), :] = counts.astype(jnp.int32)


def place_lookups(row_ids, row_home, owners, table_rows):
    samples, feats = row_ids.shape
    return pl.pallas_call(
        functools.partial(place_kernel, table_rows.bit_length() - 1, owners),
        out_shape=(
            jax.ShapeDtypeStruct((samples, feats), jnp.int32),
            jax.ShapeDtypeStruct((samples, feats), jnp.int32),
            jax.ShapeDtypeStruct((samples, 128), jnp.int32),
        ),
        name="place_lookups",
    )(row_ids, row_home.reshape(-1, 128))


COPY_ROWS = 56


def sum_list(values):
    total = values[0]
    for value in values[1:]:
        total = total + value
    return total


def grads_kernel(
    sizes,
    count_ref,
    x_ref,
    g_ref,
    mix_ref,
    lift_ref,
    linear_ref,
    rank_ref,
    slot_ref,
    rows_ref,
    dense_ref,
    mix_down,
    lift_down,
    mix_sum,
    lift_sum,
    linear_sum,
    sorted_a,
    sorted_b,
    row_a,
    row_b,
    filled,
):
    group, steps, owners, per_owner, scaling = sizes
    width, feats = x_ref.shape[1:]
    rank = mix_ref.shape[1]
    step = pl.program_id(0)

    @pl.when(step == 0)
    def _():
        mix_down[...] = mix_ref[...].astype(jnp.float32).T.astype(jnp.bfloat16)
        lift_down[...] = lift_ref[...].astype(jnp.float32).T.astype(jnp.bfloat16)
        mix_sum[...] = jnp.zeros_like(mix_sum)
        lift_sum[...] = jnp.zeros_like(lift_sum)
        linear_sum[...] = jnp.zeros_like(linear_sum)
        for owner in range(owners):
            filled[owner] = 0

    row_at = lax.broadcasted_iota(jnp.int32, (feats, feats), 0)
    extra_at = lax.broadcasted_iota(jnp.int32, (feats - width, feats), 0)
    every = range(group)
    d_prods = [matmul(lift_down[...], g_ref[k]).astype(jnp.bfloat16) for k in every]
    boths = [
        matmul_nt(x_ref[k], jnp.concatenate([mix_down[...], d_prods[k]], axis=0)) for k in every
    ]
    comps = [both[:, :rank].astype(jnp.bfloat16) for both in boths]
    d_comps = [(both[:, rank:] * scaling).astype(jnp.bfloat16) for both in boths]
    x_flats = [x_ref[k].T for k in every]
    pairs = [
        matmul(x_flats[k], jnp.concatenate([comps[k], d_comps[k]], axis=1)) for k in every
    ]
    prods = [(pair[:, :rank] * scaling).astype(jnp.bfloat16) for pair in pairs]
    mix_sum[...] += sum_list([pair[:, rank:] for pair in pairs])
    g_all = g_ref[...].reshape(group * width, feats)
    d_all = g_all.astype(jnp.float32) + matmul(g_all, linear_ref[...])
    d_all = d_all + matmul(jnp.concatenate(d_comps, axis=0), mix_down[...])
    d_ins = [
        d_all[k * width : (k + 1) * width] + scaling * matmul(comps[k], d_prods[k]) for k in every
    ]
    moves, rows_downs = [], []
    for k in every:
        slot = slot_ref[pl.ds(step * group + k, 1), :]
        extra = jnp.where(extra_at == 0, slot >> 4, jnp.where(extra_at == 1, slot & 15, 0))
        rows_downs.append(
            jnp.concatenate(
                [d_ins[k].astype(jnp.bfloat16), extra.astype(jnp.float32).astype(jnp.bfloat16)],
                axis=0,
            )
        )
        moves.append(one_hot(row_at == rank_ref[pl.ds(step * group + k, 1), :]))
    for k in every:
        ordered = matmul_nt(moves[k], rows_downs[k])
        sorted_a[k, :feats] = ordered[:, :128]
        sorted_b[k, :feats] = ordered[:, 128:]
    linear_sum[...] += sum_list([matmul(x_flats[k], g_ref[k]) for k in every])
    lift_sum[...] += sum_list([matmul(g_ref[k], prods[k]) for k in every])

    starts = [filled[owner] for owner in range(owners)]
    ends = list(starts)
    for k in every:
        begin = 0
        for owner in range(owners):
            number = count_ref[step * group + k, owner]
            at = ends[owner]
            row_a[owner, pl.ds(at, COPY_ROWS), :] = sorted_a[k, pl.ds(begin, COPY_ROWS), :]
            row_b[owner, pl.ds(at, COPY_ROWS), :] = sorted_b[k, pl.ds(begin, COPY_ROWS), :]
            ends[owner] = at + number
            begin = begin + number
    most = count_ref[step * group, owners]
    for k in range(1, group):
        most = jnp.maximum(most, count_ref[step * group + k, owners])

    @pl.when(most > COPY_ROWS)
    def _():
        again = list(starts)
        for k in every:
            begin = 0
            for owner in range(owners):
                number = count_ref[step * group + k, owner]

                def copy(turn, carry, begin=begin, at=again[owner], owner=owner, k=k):
                    off = turn * COPY_ROWS
                    source, target = pl.ds(begin + off, COPY_ROWS), pl.ds(at + off, COPY_ROWS)
                    row_a[owner, target, :] = sorted_a[k, source, :]
                    row_b[owner, target, :] = sorted_b[k, source, :]
                    return carry

                lax.fori_loop(0, (number + COPY_ROWS - 1) // COPY_ROWS, copy, 0)
                again[owner] = again[owner] + number
                begin = begin + number

    for owner in range(owners):
        filled[owner] = ends[owner]

    @pl.when(step == steps - 1)
    def _():
        dense_ref[:feats] = mix_sum[...]
        linear = linear_sum[...].T
        for at in range(feats // 128):
            dense_ref[feats * (1 + at) : feats * (2 + at)] = linear[:, 128 * at : 128 * (at + 1)]
        dense_ref[feats * (1 + feats // 128) :] = lift_sum[...]
        for owner in range(owners):
            rows_ref[owner, :, :128] = row_a[owner, :per_owner, :].astype(jnp.bfloat16)
            rows_ref[owner, :, 128:] = row_b[owner, :per_owner, :].astype(jnp.bfloat16)


def local_grads(counts, x_down, g_down, mix, lift_down, linear, ranks, slots, owners):
    samples, width, feats = x_down.shape
    rank = mix.shape[1]
    group = 4
    steps = samples // group
    per_owner = samples * feats // owners
    sizes = (group, steps, owners, per_owner, 1.0 / math.sqrt(width))

    def whole(shape):
        return pl.BlockSpec(shape, lambda i, *_: (0,) * len(shape))

    sample_spec = pl.BlockSpec((group, width, feats), lambda i, *_: (i, 0, 0))
    dense_rows = feats * (1 + feats // 128) + width
    room = per_owner + 64
    return pl.pallas_call(
        functools.partial(grads_kernel, sizes),
        out_shape=(
            jax.ShapeDtypeStruct((owners, per_owner, 256), jnp.bfloat16),
            jax.ShapeDtypeStruct((dense_rows, 128), jnp.float32),
        ),
        grid_spec=pltpu.PrefetchScalarGridSpec(
            num_scalar_prefetch=1,
            grid=(steps,),
            in_specs=[
                sample_spec,
                sample_spec,
                whole((feats, rank)),
                whole((width, rank)),
                whole((feats, feats)),
                whole((samples, feats)),
                whole((samples, feats)),
            ],
            out_specs=(whole((owners, per_owner, 256)), whole((dense_rows, 128))),
            scratch_shapes=[
                pltpu.VMEM((rank, feats), jnp.bfloat16),
                pltpu.VMEM((rank, width), jnp.bfloat16),
                pltpu.VMEM((feats, rank), jnp.float32),
                pltpu.VMEM((width, rank), jnp.float32),
                pltpu.VMEM((feats, feats), jnp.float32),
                pltpu.VMEM((group, feats + 64, 128), jnp.float32),
                pltpu.VMEM((group, feats + 64, 128), jnp.float32),
                pltpu.VMEM((owners, room, 128), jnp.float32),
                pltpu.VMEM((owners, room, 128), jnp.float32),
                pltpu.SMEM((owners,), jnp.int32),
            ],
        ),
        compiler_params=pltpu.CompilerParams(vmem_limit_bytes=60 * 2**20),
        cost_estimate=pl.CostEstimate(
            flops=2 * samples * feats * feats * 2048, bytes_accessed=12 * 2**20, transcendentals=0
        ),
        name="local_grads",
    )(counts, x_down, g_down, mix, lift_down, linear, ranks, slots)


def build_kernel(at, me_ref, rows_ref, keep_ref, send_ref):
    outers = 2 * keep_ref.shape[1]
    piece = keep_ref.shape[2] * 2 // 3
    half = piece // 2
    rows = rows_ref[0]
    per_owner = rows.shape[0]
    lane = lax.broadcasted_iota(jnp.int32, (8, 128), 1)
    pick = jnp.where(lane == at, 16.0, jnp.where(lane == at + 1, 1.0, 0.0)).astype(jnp.bfloat16)
    slots = matmul_nt(pick, rows[:, 128:]).astype(jnp.int32)
    left = lax.broadcasted_iota(jnp.int32, (half, 128), 1) < at
    down = lax.broadcasted_iota(jnp.int32, (128, 128), 0).astype(jnp.float32).astype(jnp.bfloat16)
    one, zero = jnp.ones((128, 128), jnp.bfloat16), jnp.zeros((128, 128), jnp.bfloat16)
    for outer in range(outers):
        base = (outer ^ me_ref[0]) * piece
        blocks = []
        for block in range(piece // 128):
            local = slots - (base + block * 128)
            local = jnp.where((local >= 0) & (local < 128), local, 128)
            local = local.astype(jnp.float32).astype(jnp.bfloat16)[:1]
            parts = []
            for lanes in range(0, per_owner, 128):
                same = down == local[:, lanes : lanes + 128]
                parts.append(jnp.where(same, one, zero))
            blocks.append(jnp.concatenate(parts, axis=1))
        total = matmul(jnp.concatenate(blocks, axis=0), rows)
        ref = send_ref if outer % 2 else keep_ref
        ref[0, outer // 2, :piece] = total[:, :128].astype(jnp.bfloat16)
        upper, lower = total[:half, 128:], total[half:, 128:]
        joined = jnp.where(left, upper, pltpu.roll(lower, at, 1))
        ref[0, outer // 2, piece:] = joined.astype(jnp.bfloat16)


def build_part(me, rows, far, table_rows, width, outers):
    owners, per_owner, lanes = rows.shape
    piece = table_rows // outers
    part = (2, outers // 2, piece * 3 // 2, 128)
    spec = pl.BlockSpec((1,) + part[1:], lambda i, me: (i, 0, 0, 0))
    return pl.pallas_call(
        functools.partial(build_kernel, width - 128),
        out_shape=(jax.ShapeDtypeStruct(part, jnp.bfloat16),) * 2,
        grid_spec=pltpu.PrefetchScalarGridSpec(
            num_scalar_prefetch=1,
            grid=(2,),
            in_specs=[
                pl.BlockSpec((1, per_owner, lanes), lambda i, me: ((2 * far + i) ^ me[1], 0, 0))
            ],
            out_specs=(spec, spec),
        ),
        compiler_params=pltpu.CompilerParams(vmem_limit_bytes=60 * 2**20),
        cost_estimate=pl.CostEstimate(
            flops=4 * table_rows * per_owner * lanes, bytes_accessed=3 * 2**20, transcendentals=0
        ),
        name="build_part",
    )(me, rows)


def adagrad_kernel(me_ref, *refs):
    pieces, (table_ref, accum_ref, new_table_ref, new_accum_ref) = refs[:-4], refs[-4:]
    width, piece = table_ref.shape
    half, at = piece // 2, width - 128
    for index, packed in enumerate(pieces):

        @pl.when(pl.program_id(0) == index)
        def _(packed=packed):
            first = packed[:piece].astype(jnp.float32).T
            second = packed[piece:].astype(jnp.float32).T
            second = jnp.concatenate([second[:at], second[at:]], axis=1)
            grad = jnp.concatenate([first, second], axis=0)
            mean = jnp.sum(grad * grad, axis=0, keepdims=True) * (1.0 / width)
            updated = accum_ref[...] + mean
            new_accum_ref[...] = updated
            new_table_ref[...] = table_ref[...] - grad * (LEARN_RATE / jnp.sqrt(updated))


def update_table(me, pieces, table_down, accum):
    width, table_rows = table_down.shape
    piece = table_rows // len(pieces)

    def moved(rows):
        return pl.BlockSpec((rows, piece), lambda i, me: (0, i ^ me[0]))

    return pl.pallas_call(
        adagrad_kernel,
        out_shape=(
            jax.ShapeDtypeStruct((width, table_rows), jnp.float32),
            jax.ShapeDtypeStruct((1, table_rows), jnp.float32),
        ),
        grid_spec=pltpu.PrefetchScalarGridSpec(
            num_scalar_prefetch=1,
            grid=(len(pieces),),
            in_specs=[pl.BlockSpec(pieces[0].shape, lambda i, me: (0, 0))] * len(pieces)
            + [moved(width), moved(1)],
            out_specs=[moved(width), moved(1)],
        ),
        name="update_table",
    )(me, *pieces, table_down, accum)


def swap(values, axis, bit):
    size = lax.axis_size(axis)
    return lax.ppermute(values, axis, [(i, i ^ bit) for i in range(size)])


def add_half(first, second):
    return (first.astype(jnp.float32) + second.astype(jnp.float32)).astype(jnp.bfloat16)


def tree_sum(values):
    while len(values) > 1:
        values = [values[i] + values[i + 1] for i in range(0, len(values), 2)]
    return values[0]


def after(value, *ready):
    return lax.optimization_barrier((value,) + ready)[0]


def halves(dense, side):
    cut = dense.reshape(2, dense.shape[0] // 2, dense.shape[1])
    mine = lax.dynamic_index_in_dim(cut, side, 0, keepdims=False)
    return mine, lax.dynamic_index_in_dim(cut, 1 - side, 0, keepdims=False)


def both_halves(dense, other, side):
    return jnp.where(
        side == 0,
        jnp.concatenate([dense, other], axis=0),
        jnp.concatenate([other, dense], axis=0),
    )


def sum_all(me, rows, dense, table_rows, width):
    owners, outers = lax.axis_size("inner"), lax.axis_size("outer")
    outer, inner = lax.axis_index("outer"), lax.axis_index("inner")
    cuts = (("outer", 1, outer & 1), ("outer", 2, outer >> 1), ("inner", 1, inner & 1))
    far_count = owners // 2
    mine, other = halves(dense, cuts[0][2])
    dense = mine + swap(other, "outer", 1)
    kept, parts, sent = {}, {}, {}
    ready = []
    for far in reversed(range(far_count)):
        source = after(rows, ready[-2]) if len(ready) > 1 else rows
        held, send = build_part(me, source, far, table_rows, width, outers)
        came = swap(send, "outer", 1)
        if far % 2:
            parts[far] = add_half(held[1], came[1])
            kept[far] = add_half(held[0], came[0])
            sent[far] = swap(parts[far], "inner", 1)
        else:
            parts[far] = add_half(held[:, 1], came[:, 1])
            kept[far] = add_half(held[:, 0], came[:, 0])
            sent[far] = swap(parts[far], "outer", 2)
        ready.append(parts[far])
    for stage, (axis, bit, side) in enumerate(cuts[1:]):
        mine, other = halves(after(dense, ready[2 * stage]), side)
        dense = mine + swap(other, axis, bit)
    dense = after(dense, ready[-1])
    far_dense = [swap(dense, "inner", 2 * far) for far in range(1, far_count)]
    terms, second = {}, {}
    for far in reversed(range(far_count)):
        part = add_half(kept[far][1], sent[far][1])
        rest = add_half(kept[far][0], sent[far][0])
        second[far] = (rest, swap(part, *(("outer", 2) if far % 2 else ("inner", 1))))
    for far in reversed(range(1, far_count)):
        terms[far] = swap(add_half(*second[far]), "inner", 2 * far).astype(jnp.float32)
    terms[0] = second[0][0].astype(jnp.float32) + second[0][1].astype(jnp.float32)
    dense = tree_sum([dense] + far_dense)
    total = tree_sum([terms[far] for far in range(far_count)]).astype(jnp.bfloat16)
    dense = after(dense, terms[0])
    for axis, bit, side in reversed(cuts):
        dense = both_halves(dense, swap(dense, axis, bit), side)
    across = swap(total, "outer", 2)
    return [total, swap(total, "outer", 1), across, swap(across, "outer", 1)], dense


def dense_table(
    layer_input,
    out_grad,
    mix_weight,
    lift_weight,
    linear_weight,
    row_ids,
    row_home,
    table,
    row_accum,
):
    owners, outers = lax.axis_size("inner"), lax.axis_size("outer")
    sample_count = layer_input.shape[0]
    table_rows = table.shape[0]
    me = jnp.stack([lax.axis_index("outer"), lax.axis_index("inner")]).astype(jnp.int32)
    ranks, slots, counts = place_lookups(row_ids, row_home, owners, table_rows)
    rows, dense = local_grads(
        counts,
        jnp.swapaxes(layer_input, 1, 2),
        jnp.swapaxes(out_grad, 1, 2),
        mix_weight,
        lift_weight.T,
        linear_weight,
        ranks,
        slots,
        owners,
    )
    width = layer_input.shape[2]
    pieces, dense = sum_all(me, rows, dense, table_rows, width)
    dense = dense * (1.0 / (sample_count * outers * owners))
    new_table, new_accum = update_table(me, pieces, table.T, row_accum.reshape(1, -1))
    feats, width = layer_input.shape[1:]
    linear = [dense[feats * (1 + i) : feats * (2 + i)] for i in range(feats // 128)]
    return (
        new_table.T,
        new_accum.reshape(-1),
        dense[:feats],
        dense[feats * (1 + feats // 128) :].T,
        jnp.concatenate(linear, axis=1),
    )


def power_of_two(number):
    return number & (number - 1) == 0


def on_device(*arrays):
    owners, outers = lax.axis_size("inner"), lax.axis_size("outer")
    layer_input, mix_weight, row_home, table = (arrays[i] for i in (0, 2, 6, 7))
    samples, feats, width = layer_input.shape
    dense_fits = (
        outers == 4
        and owners % 4 == 0
        and power_of_two(owners)
        and row_home.shape[0] <= 2 * samples * feats
        and row_home.shape[0] <= 2**15
        and power_of_two(table.shape[0])
        and 512 <= table.shape[0] <= 4096
        and samples % 16 == 0
        and feats == 256
        and mix_weight.shape[1] == 128
        and 2 * (width - 128) == 128
    )
    return dense_table(*arrays) if dense_fits else routed_rows(*arrays)


def solution(mesh):
    placed = (
        P(("outer", "inner"), None, None),
        P(("outer", "inner"), None, None),
        P(),
        P(),
        P(),
        P(("outer", "inner"), None),
        P(),
        P("inner", None),
        P("inner"),
    )
    return jax.shard_map(
        on_device,
        mesh=mesh,
        in_specs=placed,
        out_specs=(P("inner", None), P("inner"), P(), P(), P()),
        check_vma=False,
    )
```

```python
import functools
import math

import jax
import jax.numpy as jnp
from jax import lax
from jax.experimental import pallas as pl
from jax.experimental.pallas import tpu as pltpu
from jax.sharding import PartitionSpec as P

LEARN_RATE = 0.5


def interaction_grads(inputs, cotangent, mix_weight, lift_weight, linear_weight, scaling):
    compressed = jnp.einsum(
        "bfd,fk->bdk", inputs, mix_weight, preferred_element_type=jnp.float32
    ).astype(jnp.bfloat16)
    products = (
        jnp.einsum("bfd,bdk->bfk", inputs, compressed, preferred_element_type=jnp.float32) * scaling
    ).astype(jnp.bfloat16)
    d_products = jnp.einsum(
        "bfd,kd->bfk", cotangent, lift_weight, preferred_element_type=jnp.float32
    ).astype(jnp.bfloat16)
    d_compressed = (
        jnp.einsum("bfd,bfk->bdk", inputs, d_products, preferred_element_type=jnp.float32) * scaling
    ).astype(jnp.bfloat16)
    d_inputs = cotangent.astype(jnp.float32)
    d_inputs = d_inputs + jnp.einsum(
        "fg,bfd->bgd", linear_weight, cotangent, preferred_element_type=jnp.float32
    )
    d_inputs = d_inputs + scaling * jnp.einsum(
        "bfk,bdk->bfd", d_products, compressed, preferred_element_type=jnp.float32
    )
    d_inputs = d_inputs + jnp.einsum(
        "fk,bdk->bfd", mix_weight, d_compressed, preferred_element_type=jnp.float32
    )
    g_mix = jnp.einsum("bfd,bdk->fk", inputs, d_compressed, preferred_element_type=jnp.float32)
    g_lift = jnp.einsum("bfk,bfd->kd", products, cotangent, preferred_element_type=jnp.float32)
    g_linear = jnp.einsum("bfd,bgd->fg", cotangent, inputs, preferred_element_type=jnp.float32)
    rows_out = d_inputs.astype(jnp.bfloat16).reshape(-1, d_inputs.shape[2])
    return (rows_out, (g_mix, g_lift, g_linear))


def adagrad(weights, history, gradient):
    updated = history + jnp.mean(gradient * gradient, axis=1)
    return (weights - LEARN_RATE * gradient / jnp.sqrt(updated)[:, None], updated)


def owner_ranks(owner_of, owners):
    lookups = owner_of.shape[0]
    width = math.gcd(lookups, 128)
    groups = lookups // width
    hot = (owner_of[:, None] == jnp.arange(owners, dtype=jnp.int32)[None, :]).astype(jnp.bfloat16)
    hot = hot.reshape(groups, width, owners)
    lower = (jnp.arange(width)[:, None] > jnp.arange(width)[None, :]).astype(jnp.bfloat16)
    within = jnp.einsum("ij,gjo->gio", lower, hot, preferred_element_type=jnp.float32)
    totals = jnp.sum(hot.astype(jnp.float32), axis=1)
    before = jnp.cumsum(totals, axis=0) - totals
    counted = jnp.sum(hot.astype(jnp.float32) * (within + before[:, None, :]), axis=2)
    return counted.reshape(-1).astype(jnp.int32)


def add_rows(collected, slots, values):
    count = values.shape[0]
    table_rows = collected.shape[0]
    width = math.gcd(count, 2048)
    columns = jnp.arange(table_rows, dtype=jnp.int32)
    for block_index in range(count // width):
        start = block_index * width
        hot = (slots[start : start + width, None] == columns[None, :]).astype(jnp.bfloat16)
        collected = collected + jnp.einsum(
            "lr,ld->rd", hot, values[start : start + width], preferred_element_type=jnp.float32
        )
    return collected


def routed_rows(
    layer_input,
    out_grad,
    mix_weight,
    lift_weight,
    linear_weight,
    row_ids,
    row_home,
    table,
    row_accum,
):
    owners = lax.axis_size("inner")
    sample_count, feature_count, embed_width = layer_input.shape
    table_rows = table.shape[0]
    half_samples = sample_count // 2
    lookups = sample_count * feature_count
    per_owner = lookups // (2 * owners)
    scaling = 1.0 / math.sqrt(embed_width)
    placed = jnp.take(row_home, row_ids.reshape(-1), axis=0)
    owner_of = placed // table_rows
    target = owner_of * (2 * per_owner) + owner_ranks(owner_of, owners)
    ordering = jnp.zeros((lookups,), jnp.int32).at[target].set(jnp.arange(lookups, dtype=jnp.int32))
    ordering = ordering.reshape(owners, 2, per_owner)
    local_rows = (
        jnp.zeros((lookups,), jnp.int32)
        .at[target]
        .set(placed % table_rows)
        .reshape(owners, 2 * per_owner)
    )
    arrived_rows = lax.all_to_all(
        local_rows, "inner", split_axis=0, concat_axis=0, tiled=True
    ).reshape(owners, 2, per_owner)
    collected = jnp.zeros((table_rows, embed_width), jnp.float32)
    totals = None
    for half_index in range(2):
        first_sample = half_index * half_samples
        rows_out, partial_value = interaction_grads(
            layer_input[first_sample : first_sample + half_samples],
            out_grad[first_sample : first_sample + half_samples],
            mix_weight,
            lift_weight,
            linear_weight,
            scaling,
        )
        picked = ordering[:, half_index, :] - half_index * half_samples * feature_count
        outgoing = jnp.take(rows_out, picked.reshape(-1), axis=0).reshape(
            owners, per_owner, embed_width
        )
        incoming = lax.all_to_all(outgoing, "inner", split_axis=0, concat_axis=0, tiled=True)
        collected = add_rows(
            collected, arrived_rows[:, half_index, :].reshape(-1), incoming.reshape(-1, embed_width)
        )
        if totals is None:
            totals = partial_value
        else:
            totals = tuple((earlier + later for earlier, later in zip(totals, partial_value)))
    batch_total = sample_count * lax.axis_size("outer") * owners
    summed = lax.psum((totals[0], totals[1], totals[2]), ("outer", "inner"))
    mix_grad = summed[0] / batch_total
    lift_grad = summed[1] / batch_total
    linear_grad = summed[2] / batch_total
    complete = lax.psum(collected, "outer")
    new_table, new_accum = adagrad(table, row_accum, complete)
    return (new_table, new_accum, mix_grad, lift_grad, linear_grad)


def matmul(left, right):
    return jnp.dot(left, right, preferred_element_type=jnp.float32)


def matmul_nt(left, right):
    return lax.dot_general(left, right, (((1,), (1,)), ((), ())), preferred_element_type=jnp.float32)


def one_hot(matches):
    return jnp.where(matches, 1.0, 0.0).astype(jnp.bfloat16)


def place_kernel(shift, owners, ids_ref, home_ref, rank_ref, slot_ref, count_ref):
    samples, feats = ids_ref.shape
    high, low = home_ref.shape
    home = home_ref[...]
    pieces = jnp.concatenate(
        [(home & 255).astype(jnp.float32).T, (home >> 8).astype(jnp.float32).T], axis=0
    ).astype(jnp.bfloat16)
    high_at = lax.broadcasted_iota(jnp.int32, (high, feats), 0)
    low_at = lax.broadcasted_iota(jnp.int32, (low, feats), 0)
    lane = lax.broadcasted_iota(jnp.int32, (1, feats), 1)
    count_lane = lax.broadcasted_iota(jnp.int32, (8, 128), 1)

    @pl.loop(0, samples // 8)
    def _(group):
        first = pl.multiple_of(group * 8, 8)
        ids = ids_ref[pl.ds(first, 8), :]
        ranks, slots, homes = [], [], []
        for row in range(8):
            one = ids[row : row + 1]
            found = matmul(pieces, one_hot(high_at == (one >> 7)))
            value = found[:low] + 256.0 * found[low:]
            place = jnp.sum(jnp.where(low_at == (one & 127), value, 0.0), axis=0, keepdims=True)
            place = place.astype(jnp.int32)
            owner = place >> shift
            key = (owner * feats + lane).astype(jnp.float32)
            key_down = jnp.broadcast_to(key, (128, feats)).T
            parts = []
            for at in range(0, feats, 128):
                less = key_down < key[:, at : at + 128]
                parts.append(jnp.sum(jnp.where(less, 1.0, 0.0), axis=0, keepdims=True))
            ranks.append(jnp.concatenate(parts, axis=1).astype(jnp.int32))
            slots.append(place & ((1 << shift) - 1))
            homes.append(owner)
        rank_ref[pl.ds(first, 8), :] = jnp.concatenate(ranks, axis=0)
        slot_ref[pl.ds(first, 8), :] = jnp.concatenate(slots, axis=0)
        owner_all = jnp.concatenate(homes, axis=0)
        counts = jnp.zeros((8, 128), jnp.float32)
        for owner_at in range(owners):
            number = jnp.sum(jnp.where(owner_all == owner_at, 1.0, 0.0), axis=1, keepdims=True)
            counts = jnp.where(count_lane == owner_at, number, counts)
        most = jnp.max(counts, axis=1, keepdims=True)
        counts = jnp.where(count_lane == owners, most, counts)
        count_ref[pl.ds(first, 8), :] = counts.astype(jnp.int32)


def place_lookups(row_ids, row_home, owners, table_rows):
    samples, feats = row_ids.shape
    return pl.pallas_call(
        functools.partial(place_kernel, table_rows.bit_length() - 1, owners),
        out_shape=(
            jax.ShapeDtypeStruct((samples, feats), jnp.int32),
            jax.ShapeDtypeStruct((samples, feats), jnp.int32),
            jax.ShapeDtypeStruct((samples, 128), jnp.int32),
        ),
        name="place_lookups",
    )(row_ids, row_home.reshape(-1, 128))


COPY_ROWS = 56
SCRATCH = 10


def sum_list(values):
    total = values[0]
    for value in values[1:]:
        total = total + value
    return total


def grads_kernel(
    sizes,
    count_ref,
    me_ref,
    x_ref,
    g_ref,
    mix_ref,
    lift_ref,
    linear_ref,
    rank_ref,
    slot_ref,
    *rest,
):
    group, steps, owners, per_owner, scaling = sizes
    far_count = (len(rest) - SCRATCH - 2) // 2
    keep_refs, send_refs = rest[:far_count], rest[far_count : 2 * far_count]
    rows_ref, dense_ref = rest[2 * far_count : 2 * far_count + 2]
    scratch = rest[2 * far_count + 2 :]
    step = pl.program_id(0)

    @pl.when(step < steps)
    def _():
        gather_rows(
            sizes,
            count_ref,
            me_ref,
            x_ref,
            g_ref,
            mix_ref,
            lift_ref,
            linear_ref,
            rank_ref,
            slot_ref,
            rows_ref,
            dense_ref,
            *scratch,
        )

    @pl.when(step >= steps)
    def _():
        place = owners - 1 - (step - steps)
        row_a, row_b = scratch[-3], scratch[-2]
        owner = place ^ me_ref[1]
        rows = jnp.concatenate(
            [row_a[owner, pl.ds(0, per_owner), :], row_b[owner, pl.ds(0, per_owner), :]], axis=1
        ).astype(jnp.bfloat16)
        build_rows(x_ref.shape[1] - 128, me_ref, rows, place, far_count, keep_refs, send_refs)


def gather_rows(
    sizes,
    count_ref,
    me_ref,
    x_ref,
    g_ref,
    mix_ref,
    lift_ref,
    linear_ref,
    rank_ref,
    slot_ref,
    rows_ref,
    dense_ref,
    mix_down,
    lift_down,
    mix_sum,
    lift_sum,
    linear_sum,
    sorted_a,
    sorted_b,
    row_a,
    row_b,
    filled,
):
    group, steps, owners, per_owner, scaling = sizes
    width, feats = x_ref.shape[1:]
    rank = mix_ref.shape[1]
    step = pl.program_id(0)

    @pl.when(step == 0)
    def _():
        mix_down[...] = mix_ref[...].astype(jnp.float32).T.astype(jnp.bfloat16)
        lift_down[...] = lift_ref[...].astype(jnp.float32).T.astype(jnp.bfloat16)
        mix_sum[...] = jnp.zeros_like(mix_sum)
        lift_sum[...] = jnp.zeros_like(lift_sum)
        linear_sum[...] = jnp.zeros_like(linear_sum)
        for owner in range(owners):
            filled[owner] = 0

    row_at = lax.broadcasted_iota(jnp.int32, (feats, feats), 0)
    extra_at = lax.broadcasted_iota(jnp.int32, (feats - width, feats), 0)
    every = range(group)
    d_prods = [matmul(lift_down[...], g_ref[k]).astype(jnp.bfloat16) for k in every]
    boths = [
        matmul_nt(x_ref[k], jnp.concatenate([mix_down[...], d_prods[k]], axis=0)) for k in every
    ]
    comps = [both[:, :rank].astype(jnp.bfloat16) for both in boths]
    d_comps = [(both[:, rank:] * scaling).astype(jnp.bfloat16) for both in boths]
    x_flats = [x_ref[k].T for k in every]
    pairs = [
        matmul(x_flats[k], jnp.concatenate([comps[k], d_comps[k]], axis=1)) for k in every
    ]
    prods = [(pair[:, :rank] * scaling).astype(jnp.bfloat16) for pair in pairs]
    mix_sum[...] += sum_list([pair[:, rank:] for pair in pairs])
    g_all = g_ref[...].reshape(group * width, feats)
    d_all = g_all.astype(jnp.float32) + matmul(g_all, linear_ref[...])
    d_all = d_all + matmul(jnp.concatenate(d_comps, axis=0), mix_down[...])
    d_ins = [
        d_all[k * width : (k + 1) * width] + scaling * matmul(comps[k], d_prods[k]) for k in every
    ]
    moves, rows_downs = [], []
    for k in every:
        slot = slot_ref[pl.ds(step * group + k, 1), :]
        extra = jnp.where(extra_at == 0, slot >> 4, jnp.where(extra_at == 1, slot & 15, 0))
        rows_downs.append(
            jnp.concatenate(
                [d_ins[k].astype(jnp.bfloat16), extra.astype(jnp.float32).astype(jnp.bfloat16)],
                axis=0,
            )
        )
        moves.append(one_hot(row_at == rank_ref[pl.ds(step * group + k, 1), :]))
    for k in every:
        ordered = matmul_nt(moves[k], rows_downs[k])
        sorted_a[k, :feats] = ordered[:, :128]
        sorted_b[k, :feats] = ordered[:, 128:]
    linear_sum[...] += sum_list([matmul(x_flats[k], g_ref[k]) for k in every])
    lift_sum[...] += sum_list([matmul(g_ref[k], prods[k]) for k in every])

    starts = [filled[owner] for owner in range(owners)]
    ends = list(starts)
    for k in every:
        begin = 0
        for owner in range(owners):
            number = count_ref[step * group + k, owner]
            at = ends[owner]
            row_a[owner, pl.ds(at, COPY_ROWS), :] = sorted_a[k, pl.ds(begin, COPY_ROWS), :]
            row_b[owner, pl.ds(at, COPY_ROWS), :] = sorted_b[k, pl.ds(begin, COPY_ROWS), :]
            ends[owner] = at + number
            begin = begin + number
    most = count_ref[step * group, owners]
    for k in range(1, group):
        most = jnp.maximum(most, count_ref[step * group + k, owners])

    @pl.when(most > COPY_ROWS)
    def _():
        again = list(starts)
        for k in every:
            begin = 0
            for owner in range(owners):
                number = count_ref[step * group + k, owner]

                def copy(turn, carry, begin=begin, at=again[owner], owner=owner, k=k):
                    off = turn * COPY_ROWS
                    source, target = pl.ds(begin + off, COPY_ROWS), pl.ds(at + off, COPY_ROWS)
                    row_a[owner, target, :] = sorted_a[k, source, :]
                    row_b[owner, target, :] = sorted_b[k, source, :]
                    return carry

                lax.fori_loop(0, (number + COPY_ROWS - 1) // COPY_ROWS, copy, 0)
                again[owner] = again[owner] + number
                begin = begin + number

    for owner in range(owners):
        filled[owner] = ends[owner]

    @pl.when(step == steps - 1)
    def _():
        dense_ref[:feats] = mix_sum[...]
        linear = linear_sum[...].T
        for at in range(feats // 128):
            dense_ref[feats * (1 + at) : feats * (2 + at)] = linear[:, 128 * at : 128 * (at + 1)]
        dense_ref[feats * (1 + feats // 128) :] = lift_sum[...]
        for place in range(rows_ref.shape[0]):
            owner = place ^ me_ref[1]
            rows_ref[place, :, :128] = row_a[owner, pl.ds(0, per_owner), :].astype(jnp.bfloat16)
            rows_ref[place, :, 128:] = row_b[owner, pl.ds(0, per_owner), :].astype(jnp.bfloat16)


def build_rows(at, me_ref, rows, place, first, keep_refs, send_refs):
    shape = keep_refs[0].shape
    outers = 2 * shape[1]
    piece = shape[2] * 2 // 3
    half = piece // 2
    per_owner = rows.shape[0]
    lane = lax.broadcasted_iota(jnp.int32, (8, 128), 1)
    pick = jnp.where(lane == at, 16.0, jnp.where(lane == at + 1, 1.0, 0.0)).astype(jnp.bfloat16)
    slots = matmul_nt(pick, rows[:, 128:])[:1].astype(jnp.int32)
    down = lax.broadcasted_iota(jnp.int32, (piece, per_owner), 0)
    left = lax.broadcasted_iota(jnp.int32, (half, 128), 1) < at
    firsts, seconds = [], []
    for outer in range(outers):
        base = (outer ^ me_ref[0]) * piece
        total = matmul(one_hot(down == slots - base), rows)
        upper, lower = total[:half, 128:], total[half:, 128:]
        joined = jnp.where(left, upper, pltpu.roll(lower, at, 1))
        firsts.append(total[:, :128].astype(jnp.bfloat16))
        seconds.append(joined.astype(jnp.bfloat16))
    for index in range(len(keep_refs)):

        @pl.when(place // 2 == first + index)
        def _(index=index):
            for outer in range(outers):
                ref = (send_refs if outer % 2 else keep_refs)[index]
                ref[0, outer // 2, :piece] = firsts[outer]
                ref[0, outer // 2, piece:] = seconds[outer]


def part_specs(start, first, count, part):
    def spec(index):
        begin = start + 2 * (count - 1 - index)
        return pl.BlockSpec(
            (1,) + part[1:], lambda i, *_: (jnp.clip(begin + 1 - i, 0, 1), 0, 0, 0)
        )

    return [spec(index) for index in range(count)] * 2


def local_grads(counts, me, x_down, g_down, mix, lift_down, linear, ranks, slots, owners, part):
    samples, width, feats = x_down.shape
    rank = mix.shape[1]
    group = 4
    steps = samples // group
    per_owner = samples * feats // owners
    far_count = owners // 4
    sizes = (group, steps, owners, per_owner, 1.0 / math.sqrt(width))

    def whole(shape):
        return pl.BlockSpec(shape, lambda i, *_: (0,) * len(shape))

    sample_spec = pl.BlockSpec(
        (group, width, feats), lambda i, *_: (jnp.minimum(i, steps - 1), 0, 0)
    )
    dense_rows = feats * (1 + feats // 128) + width
    room = per_owner + 64
    rows_shape = (owners // 2, per_owner, 256)
    scratch = [
        pltpu.VMEM((rank, feats), jnp.bfloat16),
        pltpu.VMEM((rank, width), jnp.bfloat16),
        pltpu.VMEM((feats, rank), jnp.float32),
        pltpu.VMEM((width, rank), jnp.float32),
        pltpu.VMEM((feats, feats), jnp.float32),
        pltpu.VMEM((group, feats + 64, 128), jnp.float32),
        pltpu.VMEM((group, feats + 64, 128), jnp.float32),
        pltpu.VMEM((owners, room, 128), jnp.float32),
        pltpu.VMEM((owners, room, 128), jnp.float32),
        pltpu.SMEM((owners,), jnp.int32),
    ]
    outs = pl.pallas_call(
        functools.partial(grads_kernel, sizes),
        out_shape=[jax.ShapeDtypeStruct(part, jnp.bfloat16)] * (2 * far_count)
        + [
            jax.ShapeDtypeStruct(rows_shape, jnp.bfloat16),
            jax.ShapeDtypeStruct((dense_rows, 128), jnp.float32),
        ],
        grid_spec=pltpu.PrefetchScalarGridSpec(
            num_scalar_prefetch=2,
            grid=(steps + owners // 2,),
            in_specs=[
                sample_spec,
                sample_spec,
                whole((feats, rank)),
                whole((width, rank)),
                whole((feats, feats)),
                whole((samples, feats)),
                whole((samples, feats)),
            ],
            out_specs=part_specs(steps, owners // 2 - far_count, far_count, part)
            + [whole(rows_shape), whole((dense_rows, 128))],
            scratch_shapes=scratch,
        ),
        compiler_params=pltpu.CompilerParams(vmem_limit_bytes=60 * 2**20),
        cost_estimate=pl.CostEstimate(
            flops=2 * samples * feats * feats * 3072, bytes_accessed=12 * 2**20, transcendentals=0
        ),
        name="local_grads",
    )(counts, me, x_down, g_down, mix, lift_down, linear, ranks, slots)
    keep, send = outs[:far_count], outs[far_count : 2 * far_count]
    return keep, send, outs[2 * far_count], outs[2 * far_count + 1]


def build_kernel(at, me_ref, rows_ref, *refs):
    half = len(refs) // 2
    place = 2 * half - 1 - pl.program_id(0)
    build_rows(at, me_ref, rows_ref[0], place, 0, refs[:half], refs[half:])


def build_parts(me, rows, part, width):
    places, per_owner, lanes = rows.shape
    far_count = places // 2
    outs = pl.pallas_call(
        functools.partial(build_kernel, width - 128),
        out_shape=[jax.ShapeDtypeStruct(part, jnp.bfloat16)] * places,
        grid_spec=pltpu.PrefetchScalarGridSpec(
            num_scalar_prefetch=1,
            grid=(places,),
            in_specs=[pl.BlockSpec((1, per_owner, lanes), lambda i, me: (places - 1 - i, 0, 0))],
            out_specs=part_specs(0, 0, far_count, part),
        ),
        compiler_params=pltpu.CompilerParams(vmem_limit_bytes=60 * 2**20),
        cost_estimate=pl.CostEstimate(
            flops=2 * part[2] * part[1] * part[0] * places * per_owner * lanes,
            bytes_accessed=6 * 2**20,
            transcendentals=0,
        ),
        name="build_parts",
    )(me, rows)
    return outs[:far_count], outs[far_count:]


def adagrad_kernel(me_ref, *refs):
    pieces, (table_ref, accum_ref, new_table_ref, new_accum_ref) = refs[:-4], refs[-4:]
    width, piece = table_ref.shape
    half, at = piece // 2, width - 128
    for index, packed in enumerate(pieces):

        @pl.when(pl.program_id(0) == index)
        def _(packed=packed):
            first = packed[:piece].astype(jnp.float32).T
            second = packed[piece:].astype(jnp.float32).T
            second = jnp.concatenate([second[:at], second[at:]], axis=1)
            grad = jnp.concatenate([first, second], axis=0)
            mean = jnp.sum(grad * grad, axis=0, keepdims=True) * (1.0 / width)
            updated = accum_ref[...] + mean
            new_accum_ref[...] = updated
            new_table_ref[...] = table_ref[...] - grad * (LEARN_RATE / jnp.sqrt(updated))


def update_table(me, pieces, table_down, accum):
    width, table_rows = table_down.shape
    piece = table_rows // len(pieces)

    def moved(rows):
        return pl.BlockSpec((rows, piece), lambda i, me: (0, i ^ me[0]))

    return pl.pallas_call(
        adagrad_kernel,
        out_shape=(
            jax.ShapeDtypeStruct((width, table_rows), jnp.float32),
            jax.ShapeDtypeStruct((1, table_rows), jnp.float32),
        ),
        grid_spec=pltpu.PrefetchScalarGridSpec(
            num_scalar_prefetch=1,
            grid=(len(pieces),),
            in_specs=[pl.BlockSpec(pieces[0].shape, lambda i, me: (0, 0))] * len(pieces)
            + [moved(width), moved(1)],
            out_specs=[moved(width), moved(1)],
        ),
        name="update_table",
    )(me, *pieces, table_down, accum)


def swap(values, axis, bit):
    size = lax.axis_size(axis)
    return lax.ppermute(values, axis, [(i, i ^ bit) for i in range(size)])


def add_half(first, second):
    return (first.astype(jnp.float32) + second.astype(jnp.float32)).astype(jnp.bfloat16)


def tree_sum(values):
    while len(values) > 1:
        values = [values[i] + values[i + 1] for i in range(0, len(values), 2)]
    return values[0]


def after(value, *ready):
    return lax.optimization_barrier((value,) + ready)[0]


def halves(dense, side):
    cut = dense.reshape(2, dense.shape[0] // 2, dense.shape[1])
    mine = lax.dynamic_index_in_dim(cut, side, 0, keepdims=False)
    return mine, lax.dynamic_index_in_dim(cut, 1 - side, 0, keepdims=False)


def both_halves(dense, other, side):
    return jnp.where(
        side == 0,
        jnp.concatenate([dense, other], axis=0),
        jnp.concatenate([other, dense], axis=0),
    )


def sum_all(me, keep, send, rows, dense, part, width):
    owners = lax.axis_size("inner")
    outer, inner = lax.axis_index("outer"), lax.axis_index("inner")
    cuts = (("outer", 1, outer & 1), ("outer", 2, outer >> 1), ("inner", 1, inner & 1))
    far_count = owners // 2
    first = far_count - len(keep)
    keep = dict(enumerate(keep, first))
    came = {}
    for far in reversed(range(first, far_count)):
        came[far] = swap(send[far - first], "outer", 1)
    mine, other = halves(dense, cuts[0][2])
    other = swap(other, "outer", 1)
    low_keep, low_send = build_parts(me, rows, part, width)
    dense = mine + after(other, low_send[0])
    mine, other = halves(dense, cuts[1][2])
    other = swap(other, "outer", 2)
    keep.update(enumerate(low_keep))
    for far in reversed(range(first)):
        came[far] = swap(low_send[far], "outer", 1)
    parts, kept, sent = {}, {}, {}
    for far in reversed(range(far_count)):
        held = keep[far]
        if far % 2:
            parts[far] = add_half(held[1], came[far][1])
            kept[far] = add_half(held[0], came[far][0])
            sent[far] = swap(parts[far], "inner", 1)
        else:
            parts[far] = add_half(held[:, 1], came[far][:, 1])
            kept[far] = add_half(held[:, 0], came[far][:, 0])
            sent[far] = swap(parts[far], "outer", 2)
        if far == first:
            dense = mine + after(other, parts[far])
            mine, other = halves(dense, cuts[2][2])
            other = swap(other, "inner", 1)
    dense = mine + after(other, parts[0])
    far_dense = [swap(dense, "inner", 2 * far) for far in range(1, far_count)]
    terms, second = {}, {}
    for far in reversed(range(far_count)):
        came_next = after(sent[far], *(parts[index] for index in range(first)))
        part_next = add_half(kept[far][1], came_next[1])
        rest = add_half(kept[far][0], came_next[0])
        second[far] = (rest, swap(part_next, *(("outer", 2) if far % 2 else ("inner", 1))))
        if far == first:
            far_dense = list(after(tuple(far_dense), part_next))
            dense = tree_sum([dense] + far_dense)
            other = swap(dense, "inner", 1)
    for far in reversed(range(1, far_count)):
        last = add_half(*second[far])
        terms[far] = swap(last, "inner", 2 * far).astype(jnp.float32)
        if far == first:
            dense = both_halves(dense, after(other, last), cuts[2][2])
            other = swap(dense, "outer", 2)
    terms[0] = second[0][0].astype(jnp.float32) + second[0][1].astype(jnp.float32)
    total = tree_sum([terms[far] for far in range(far_count)]).astype(jnp.bfloat16)
    dense = both_halves(dense, after(other, total), cuts[1][2])
    across = swap(total, "outer", 2)
    pieces = [total, swap(total, "outer", 1), across, swap(across, "outer", 1)]
    return pieces, both_halves(dense, swap(dense, "outer", 1), cuts[0][2])


def dense_table(
    layer_input,
    out_grad,
    mix_weight,
    lift_weight,
    linear_weight,
    row_ids,
    row_home,
    table,
    row_accum,
):
    owners, outers = lax.axis_size("inner"), lax.axis_size("outer")
    sample_count = layer_input.shape[0]
    table_rows = table.shape[0]
    me = jnp.stack([lax.axis_index("outer"), lax.axis_index("inner")]).astype(jnp.int32)
    ranks, slots, counts = place_lookups(row_ids, row_home, owners, table_rows)
    width = layer_input.shape[2]
    part = (2, outers // 2, table_rows // outers * 3 // 2, 128)
    keep, send, rows, dense = local_grads(
        counts,
        me,
        jnp.swapaxes(layer_input, 1, 2),
        jnp.swapaxes(out_grad, 1, 2),
        mix_weight,
        lift_weight.T,
        linear_weight,
        ranks,
        slots,
        owners,
        part,
    )
    pieces, dense = sum_all(me, keep, send, rows, dense, part, width)
    dense = dense * (1.0 / (sample_count * outers * owners))
    new_table, new_accum = update_table(me, pieces, table.T, row_accum.reshape(1, -1))
    feats = layer_input.shape[1]
    linear = [dense[feats * (1 + i) : feats * (2 + i)] for i in range(feats // 128)]
    return (
        new_table.T,
        new_accum.reshape(-1),
        dense[:feats],
        dense[feats * (1 + feats // 128) :].T,
        jnp.concatenate(linear, axis=1),
    )


def power_of_two(number):
    return number & (number - 1) == 0


def on_device(*arrays):
    owners, outers = lax.axis_size("inner"), lax.axis_size("outer")
    layer_input, mix_weight, row_home, table = (arrays[i] for i in (0, 2, 6, 7))
    samples, feats, width = layer_input.shape
    dense_fits = (
        outers == 4
        and owners % 4 == 0
        and power_of_two(owners)
        and row_home.shape[0] <= 2 * samples * feats
        and row_home.shape[0] <= 2**15
        and power_of_two(table.shape[0])
        and 512 <= table.shape[0] <= 4096
        and samples % 16 == 0
        and feats == 256
        and mix_weight.shape[1] == 128
        and 2 * (width - 128) == 128
    )
    return dense_table(*arrays) if dense_fits else routed_rows(*arrays)


def solution(mesh):
    placed = (
        P(("outer", "inner"), None, None),
        P(("outer", "inner"), None, None),
        P(),
        P(),
        P(),
        P(("outer", "inner"), None),
        P(),
        P("inner", None),
        P("inner"),
    )
    return jax.shard_map(
        on_device,
        mesh=mesh,
        in_specs=placed,
        out_specs=(P("inner", None), P("inner"), P(), P(), P()),
        check_vma=False,
    )
```

```python
import functools
import math

import jax
import jax.numpy as jnp
from jax import lax
from jax.experimental import pallas as pl
from jax.experimental.pallas import tpu as pltpu
from jax.sharding import PartitionSpec as P

LEARN_RATE = 0.5


def interaction_grads(inputs, cotangent, mix_weight, lift_weight, linear_weight, scaling):
    compressed = jnp.einsum(
        "bfd,fk->bdk", inputs, mix_weight, preferred_element_type=jnp.float32
    ).astype(jnp.bfloat16)
    products = (
        jnp.einsum("bfd,bdk->bfk", inputs, compressed, preferred_element_type=jnp.float32) * scaling
    ).astype(jnp.bfloat16)
    d_products = jnp.einsum(
        "bfd,kd->bfk", cotangent, lift_weight, preferred_element_type=jnp.float32
    ).astype(jnp.bfloat16)
    d_compressed = (
        jnp.einsum("bfd,bfk->bdk", inputs, d_products, preferred_element_type=jnp.float32) * scaling
    ).astype(jnp.bfloat16)
    d_inputs = cotangent.astype(jnp.float32)
    d_inputs = d_inputs + jnp.einsum(
        "fg,bfd->bgd", linear_weight, cotangent, preferred_element_type=jnp.float32
    )
    d_inputs = d_inputs + scaling * jnp.einsum(
        "bfk,bdk->bfd", d_products, compressed, preferred_element_type=jnp.float32
    )
    d_inputs = d_inputs + jnp.einsum(
        "fk,bdk->bfd", mix_weight, d_compressed, preferred_element_type=jnp.float32
    )
    g_mix = jnp.einsum("bfd,bdk->fk", inputs, d_compressed, preferred_element_type=jnp.float32)
    g_lift = jnp.einsum("bfk,bfd->kd", products, cotangent, preferred_element_type=jnp.float32)
    g_linear = jnp.einsum("bfd,bgd->fg", cotangent, inputs, preferred_element_type=jnp.float32)
    rows_out = d_inputs.astype(jnp.bfloat16).reshape(-1, d_inputs.shape[2])
    return (rows_out, (g_mix, g_lift, g_linear))


def adagrad(weights, history, gradient):
    updated = history + jnp.mean(gradient * gradient, axis=1)
    return (weights - LEARN_RATE * gradient / jnp.sqrt(updated)[:, None], updated)


def owner_ranks(owner_of, owners):
    lookups = owner_of.shape[0]
    width = math.gcd(lookups, 128)
    groups = lookups // width
    hot = (owner_of[:, None] == jnp.arange(owners, dtype=jnp.int32)[None, :]).astype(jnp.bfloat16)
    hot = hot.reshape(groups, width, owners)
    lower = (jnp.arange(width)[:, None] > jnp.arange(width)[None, :]).astype(jnp.bfloat16)
    within = jnp.einsum("ij,gjo->gio", lower, hot, preferred_element_type=jnp.float32)
    totals = jnp.sum(hot.astype(jnp.float32), axis=1)
    before = jnp.cumsum(totals, axis=0) - totals
    counted = jnp.sum(hot.astype(jnp.float32) * (within + before[:, None, :]), axis=2)
    return counted.reshape(-1).astype(jnp.int32)


def add_rows(collected, slots, values):
    count = values.shape[0]
    table_rows = collected.shape[0]
    width = math.gcd(count, 2048)
    columns = jnp.arange(table_rows, dtype=jnp.int32)
    for block_index in range(count // width):
        start = block_index * width
        hot = (slots[start : start + width, None] == columns[None, :]).astype(jnp.bfloat16)
        collected = collected + jnp.einsum(
            "lr,ld->rd", hot, values[start : start + width], preferred_element_type=jnp.float32
        )
    return collected


def routed_rows(
    layer_input,
    out_grad,
    mix_weight,
    lift_weight,
    linear_weight,
    row_ids,
    row_home,
    table,
    row_accum,
):
    owners = lax.axis_size("inner")
    sample_count, feature_count, embed_width = layer_input.shape
    table_rows = table.shape[0]
    half_samples = sample_count // 2
    lookups = sample_count * feature_count
    per_owner = lookups // (2 * owners)
    scaling = 1.0 / math.sqrt(embed_width)
    placed = jnp.take(row_home, row_ids.reshape(-1), axis=0)
    owner_of = placed // table_rows
    target = owner_of * (2 * per_owner) + owner_ranks(owner_of, owners)
    ordering = jnp.zeros((lookups,), jnp.int32).at[target].set(jnp.arange(lookups, dtype=jnp.int32))
    ordering = ordering.reshape(owners, 2, per_owner)
    local_rows = (
        jnp.zeros((lookups,), jnp.int32)
        .at[target]
        .set(placed % table_rows)
        .reshape(owners, 2 * per_owner)
    )
    arrived_rows = lax.all_to_all(
        local_rows, "inner", split_axis=0, concat_axis=0, tiled=True
    ).reshape(owners, 2, per_owner)
    collected = jnp.zeros((table_rows, embed_width), jnp.float32)
    totals = None
    for half_index in range(2):
        first_sample = half_index * half_samples
        rows_out, partial_value = interaction_grads(
            layer_input[first_sample : first_sample + half_samples],
            out_grad[first_sample : first_sample + half_samples],
            mix_weight,
            lift_weight,
            linear_weight,
            scaling,
        )
        picked = ordering[:, half_index, :] - half_index * half_samples * feature_count
        outgoing = jnp.take(rows_out, picked.reshape(-1), axis=0).reshape(
            owners, per_owner, embed_width
        )
        incoming = lax.all_to_all(outgoing, "inner", split_axis=0, concat_axis=0, tiled=True)
        collected = add_rows(
            collected, arrived_rows[:, half_index, :].reshape(-1), incoming.reshape(-1, embed_width)
        )
        if totals is None:
            totals = partial_value
        else:
            totals = tuple((earlier + later for earlier, later in zip(totals, partial_value)))
    batch_total = sample_count * lax.axis_size("outer") * owners
    summed = lax.psum((totals[0], totals[1], totals[2]), ("outer", "inner"))
    mix_grad = summed[0] / batch_total
    lift_grad = summed[1] / batch_total
    linear_grad = summed[2] / batch_total
    complete = lax.psum(collected, "outer")
    new_table, new_accum = adagrad(table, row_accum, complete)
    return (new_table, new_accum, mix_grad, lift_grad, linear_grad)


def matmul(left, right):
    return jnp.dot(left, right, preferred_element_type=jnp.float32)


def matmul_nt(left, right):
    return lax.dot_general(left, right, (((1,), (1,)), ((), ())), preferred_element_type=jnp.float32)


def one_hot(matches):
    return jnp.where(matches, 1.0, 0.0).astype(jnp.bfloat16)


def place_kernel(shift, owners, ids_ref, home_ref, rank_ref, slot_ref, count_ref):
    samples, feats = ids_ref.shape
    high, low = home_ref.shape
    half = low // 2
    home = home_ref[...]
    pieces = []
    for part in (home & 255, home >> 8):
        down = part.astype(jnp.float32).T
        pieces.append(jnp.concatenate([down[:half], down[half:]], axis=1))
    pieces = jnp.concatenate(pieces, axis=0).astype(jnp.bfloat16)
    high_at = lax.broadcasted_iota(jnp.int32, (2 * high, feats), 0)
    low_at = lax.broadcasted_iota(jnp.int32, (half, feats), 0)
    lane = lax.broadcasted_iota(jnp.int32, (1, feats), 1)
    count_lane = lax.broadcasted_iota(jnp.int32, (8, 128), 1)

    @pl.loop(0, samples // 8)
    def _(group):
        first = pl.multiple_of(group * 8, 8)
        ids = ids_ref[pl.ds(first, 8), :]
        every = range(8)
        ones = [ids[row : row + 1] for row in every]
        hots = [one_hot(high_at == ((one >> 6) & 1) * high + (one >> 7)) for one in ones]
        founds = [matmul(pieces, hot) for hot in hots]
        places = []
        for row in every:
            value = founds[row][:half] + 256.0 * founds[row][half:]
            value = jnp.where(low_at == (ones[row] & (half - 1)), value, 0.0)
            places.append(jnp.sum(value, axis=0, keepdims=True))
        place = jnp.concatenate(places, axis=0).astype(jnp.int32)
        owner_all = place >> shift
        slot_ref[pl.ds(first, 8), :] = place & ((1 << shift) - 1)
        keys = (owner_all * feats + lane).astype(jnp.float32)
        downs = [jnp.broadcast_to(keys[row : row + 1], (128, feats)).T for row in every]
        ranks = []
        for row in every:
            parts = []
            for at in range(0, feats, 128):
                less = downs[row] < keys[row : row + 1, at : at + 128]
                parts.append(jnp.sum(jnp.where(less, 1.0, 0.0), axis=0, keepdims=True))
            ranks.append(jnp.concatenate(parts, axis=1))
        rank_ref[pl.ds(first, 8), :] = jnp.concatenate(ranks, axis=0).astype(jnp.int32)
        counts = jnp.zeros((8, 128), jnp.float32)
        for owner_at in range(owners):
            number = jnp.sum(jnp.where(owner_all == owner_at, 1.0, 0.0), axis=1, keepdims=True)
            counts = jnp.where(count_lane == owner_at, number, counts)
        most = jnp.max(counts, axis=1, keepdims=True)
        counts = jnp.where(count_lane == owners, most, counts)
        count_ref[pl.ds(first, 8), :] = counts.astype(jnp.int32)


def place_lookups(row_ids, row_home, owners, table_rows):
    samples, feats = row_ids.shape
    return pl.pallas_call(
        functools.partial(place_kernel, table_rows.bit_length() - 1, owners),
        out_shape=(
            jax.ShapeDtypeStruct((samples, feats), jnp.int32),
            jax.ShapeDtypeStruct((samples, feats), jnp.int32),
            jax.ShapeDtypeStruct((samples, 128), jnp.int32),
        ),
        name="place_lookups",
    )(row_ids, row_home.reshape(-1, 128))


COPY_ROWS = 56
SCRATCH = 10


def sum_list(values):
    total = values[0]
    for value in values[1:]:
        total = total + value
    return total


def grads_kernel(
    sizes,
    count_ref,
    me_ref,
    x_ref,
    g_ref,
    mix_ref,
    lift_ref,
    linear_ref,
    rank_ref,
    slot_ref,
    *rest,
):
    group, steps, owners, per_owner, scaling = sizes
    far_count = (len(rest) - SCRATCH - 2) // 2
    keep_refs, send_refs = rest[:far_count], rest[far_count : 2 * far_count]
    rows_ref, dense_ref = rest[2 * far_count : 2 * far_count + 2]
    scratch = rest[2 * far_count + 2 :]
    step = pl.program_id(0)

    @pl.when(step < steps)
    def _():
        gather_rows(
            sizes,
            count_ref,
            me_ref,
            x_ref,
            g_ref,
            mix_ref,
            lift_ref,
            linear_ref,
            rank_ref,
            slot_ref,
            rows_ref,
            dense_ref,
            *scratch,
        )

    @pl.when(step >= steps)
    def _():
        place = owners - 1 - (step - steps)
        row_a, row_b = scratch[-3], scratch[-2]
        owner = place ^ me_ref[1]
        first_rows = row_a[owner, pl.ds(0, per_owner), :]
        second_rows = row_b[owner, pl.ds(0, per_owner), :]
        at = x_ref.shape[1] - 128
        build_rows(at, me_ref, first_rows, second_rows, place, far_count, keep_refs, send_refs)


def join_rows(count_ref, filled, sorted_a, sorted_b, row_a, row_b, step, group, owners):
    begun = (step >= 0).astype(jnp.int32)
    now = (step + 2) % 2
    first = jnp.maximum(step, 0) * group
    every = range(group)
    numbers = [[count_ref[first + k, owner] * begun for owner in range(owners)] for k in every]
    starts = [filled[owner] for owner in range(owners)]
    ends = list(starts)
    for k in every:
        begin = 0
        for owner in range(owners):
            source, target = pl.ds(begin, COPY_ROWS), pl.ds(ends[owner], COPY_ROWS)
            row_a[owner, target, :] = sorted_a[now, k, source, :]
            row_b[owner, target, :] = sorted_b[now, k, source, :]
            ends[owner] = ends[owner] + numbers[k][owner]
            begin = begin + numbers[k][owner]
    most = count_ref[first, owners] * begun
    for k in range(1, group):
        most = jnp.maximum(most, count_ref[first + k, owners] * begun)

    @pl.when(most > COPY_ROWS)
    def _():
        again = list(starts)
        for k in every:
            begin = 0
            for owner in range(owners):

                def copy(turn, carry, begin=begin, at=again[owner], owner=owner, k=k):
                    off = turn * COPY_ROWS
                    source, target = pl.ds(begin + off, COPY_ROWS), pl.ds(at + off, COPY_ROWS)
                    row_a[owner, target, :] = sorted_a[now, k, source, :]
                    row_b[owner, target, :] = sorted_b[now, k, source, :]
                    return carry

                turns = (numbers[k][owner] + COPY_ROWS - 1) // COPY_ROWS
                lax.fori_loop(0, turns, copy, 0)
                again[owner] = again[owner] + numbers[k][owner]
                begin = begin + numbers[k][owner]

    for owner in range(owners):
        filled[owner] = ends[owner]


def gather_rows(
    sizes,
    count_ref,
    me_ref,
    x_ref,
    g_ref,
    mix_ref,
    lift_ref,
    linear_ref,
    rank_ref,
    slot_ref,
    rows_ref,
    dense_ref,
    mix_down,
    lift_down,
    mix_sum,
    lift_sum,
    linear_sum,
    sorted_a,
    sorted_b,
    row_a,
    row_b,
    filled,
):
    group, steps, owners, per_owner, scaling = sizes
    width, feats = x_ref.shape[1:]
    rank = mix_ref.shape[1]
    step = pl.program_id(0)

    @pl.when(step == 0)
    def _():
        mix_down[...] = mix_ref[...].astype(jnp.float32).T.astype(jnp.bfloat16)
        lift_down[...] = lift_ref[...].astype(jnp.float32).T.astype(jnp.bfloat16)
        mix_sum[...] = jnp.zeros_like(mix_sum)
        lift_sum[...] = jnp.zeros_like(lift_sum)
        linear_sum[...] = jnp.zeros_like(linear_sum)
        for owner in range(owners):
            filled[owner] = 0

    now = step % 2
    join_rows(count_ref, filled, sorted_a, sorted_b, row_a, row_b, step - 1, group, owners)
    row_at = lax.broadcasted_iota(jnp.int32, (feats, feats), 0)
    extra_at = lax.broadcasted_iota(jnp.int32, (feats - width, feats), 0)
    every = range(group)
    d_prods = [matmul(lift_down[...], g_ref[k]).astype(jnp.bfloat16) for k in every]
    boths = [
        matmul_nt(x_ref[k], jnp.concatenate([mix_down[...], d_prods[k]], axis=0)) for k in every
    ]
    comps = [both[:, :rank].astype(jnp.bfloat16) for both in boths]
    d_comps = [(both[:, rank:] * scaling).astype(jnp.bfloat16) for both in boths]
    x_flat = x_ref[...].reshape(group * width, feats).T
    x_flats = [x_flat[:, k * width : (k + 1) * width] for k in every]
    pairs = [
        matmul(x_flats[k], jnp.concatenate([comps[k], d_comps[k]], axis=1)) for k in every
    ]
    prods = [(pair[:, :rank] * scaling).astype(jnp.bfloat16) for pair in pairs]
    mix_sum[...] += sum_list([pair[:, rank:] for pair in pairs])
    g_all = g_ref[...].reshape(group * width, feats)
    d_all = g_all.astype(jnp.float32) + matmul(g_all, linear_ref[...])
    d_all = d_all + matmul(jnp.concatenate(d_comps, axis=0), mix_down[...])
    d_ins = [
        d_all[k * width : (k + 1) * width] + scaling * matmul(comps[k], d_prods[k]) for k in every
    ]
    moves, rows_downs = [], []
    for k in every:
        slot = slot_ref[pl.ds(step * group + k, 1), :]
        extra = jnp.where(extra_at == 0, slot >> 4, jnp.where(extra_at == 1, slot & 15, 0))
        rows_downs.append(
            jnp.concatenate(
                [d_ins[k].astype(jnp.bfloat16), extra.astype(jnp.float32).astype(jnp.bfloat16)],
                axis=0,
            )
        )
        moves.append(one_hot(row_at == rank_ref[pl.ds(step * group + k, 1), :]))
    for k in every:
        ordered = matmul_nt(moves[k], rows_downs[k])
        sorted_a[now, k, :feats] = ordered[:, :128]
        sorted_b[now, k, :feats] = ordered[:, 128:]
    linear_sum[...] += matmul(x_flat, g_all)
    lift_sum[...] += sum_list([matmul(g_ref[k], prods[k]) for k in every])

    @pl.when(step == steps - 1)
    def _():
        join_rows(count_ref, filled, sorted_a, sorted_b, row_a, row_b, step, group, owners)
        dense_ref[:feats] = mix_sum[...]
        linear = linear_sum[...].T
        for at in range(feats // 128):
            dense_ref[feats * (1 + at) : feats * (2 + at)] = linear[:, 128 * at : 128 * (at + 1)]
        dense_ref[feats * (1 + feats // 128) :] = lift_sum[...]
        for place in range(rows_ref.shape[0]):
            owner = place ^ me_ref[1]
            rows_ref[place, :, :128] = row_a[owner, pl.ds(0, per_owner), :].astype(jnp.bfloat16)
            rows_ref[place, :, 128:] = row_b[owner, pl.ds(0, per_owner), :].astype(jnp.bfloat16)


def build_rows(at, me_ref, first_rows, second_rows, place, first, keep_refs, send_refs):
    outers, piece = 2 * keep_refs[0].shape[1], keep_refs[0].shape[3]
    per_owner = first_rows.shape[0]
    rows_down = jnp.concatenate([first_rows.T, second_rows.T[:at]], axis=0).astype(jnp.bfloat16)
    slots = second_rows[:, at : at + 1] * 16.0 + second_rows[:, at + 1 : at + 2]
    slots = slots.astype(jnp.int32)
    lanes = lax.broadcasted_iota(jnp.int32, (per_owner, piece), 1)
    totals = []
    for outer in range(outers):
        base = (outer ^ me_ref[0]) * piece
        totals.append(matmul(rows_down, one_hot(lanes == slots - base)).astype(jnp.bfloat16))
    for index in range(len(keep_refs)):

        @pl.when(place // 2 == first + index)
        def _(index=index):
            for outer in range(outers):
                ref = (send_refs if outer % 2 else keep_refs)[index]
                ref[0, outer // 2] = totals[outer]


def part_specs(start, first, count, part):
    def spec(index):
        begin = start + 2 * (count - 1 - index)
        return pl.BlockSpec(
            (1,) + part[1:], lambda i, *_: (jnp.clip(begin + 1 - i, 0, 1), 0, 0, 0)
        )

    return [spec(index) for index in range(count)] * 2


def local_grads(counts, me, x_down, g_down, mix, lift_down, linear, ranks, slots, owners, part):
    samples, width, feats = x_down.shape
    rank = mix.shape[1]
    group = 4
    steps = samples // group
    per_owner = samples * feats // owners
    far_count = owners // 4
    sizes = (group, steps, owners, per_owner, 1.0 / math.sqrt(width))

    def whole(shape):
        return pl.BlockSpec(shape, lambda i, *_: (0,) * len(shape))

    sample_spec = pl.BlockSpec(
        (group, width, feats), lambda i, *_: (jnp.minimum(i, steps - 1), 0, 0)
    )
    dense_rows = feats * (1 + feats // 128) + width
    room = per_owner + 64
    rows_shape = (owners // 2, per_owner, 256)
    scratch = [
        pltpu.VMEM((rank, feats), jnp.bfloat16),
        pltpu.VMEM((rank, width), jnp.bfloat16),
        pltpu.VMEM((feats, rank), jnp.float32),
        pltpu.VMEM((width, rank), jnp.float32),
        pltpu.VMEM((feats, feats), jnp.float32),
        pltpu.VMEM((2, group, feats + 64, 128), jnp.float32),
        pltpu.VMEM((2, group, feats + 64, 128), jnp.float32),
        pltpu.VMEM((owners, room, 128), jnp.float32),
        pltpu.VMEM((owners, room, 128), jnp.float32),
        pltpu.SMEM((owners,), jnp.int32),
    ]
    outs = pl.pallas_call(
        functools.partial(grads_kernel, sizes),
        out_shape=[jax.ShapeDtypeStruct(part, jnp.bfloat16)] * (2 * far_count)
        + [
            jax.ShapeDtypeStruct(rows_shape, jnp.bfloat16),
            jax.ShapeDtypeStruct((dense_rows, 128), jnp.float32),
        ],
        grid_spec=pltpu.PrefetchScalarGridSpec(
            num_scalar_prefetch=2,
            grid=(steps + owners // 2,),
            in_specs=[
                sample_spec,
                sample_spec,
                whole((feats, rank)),
                whole((width, rank)),
                whole((feats, feats)),
                whole((samples, feats)),
                whole((samples, feats)),
            ],
            out_specs=part_specs(steps, owners // 2 - far_count, far_count, part)
            + [whole(rows_shape), whole((dense_rows, 128))],
            scratch_shapes=scratch,
        ),
        compiler_params=pltpu.CompilerParams(vmem_limit_bytes=60 * 2**20),
        cost_estimate=pl.CostEstimate(
            flops=2 * samples * feats * feats * 3072, bytes_accessed=12 * 2**20, transcendentals=0
        ),
        name="local_grads",
    )(counts, me, x_down, g_down, mix, lift_down, linear, ranks, slots)
    keep, send = outs[:far_count], outs[far_count : 2 * far_count]
    return keep, send, outs[2 * far_count], outs[2 * far_count + 1]


def build_kernel(at, me_ref, rows_ref, *refs):
    half = len(refs) // 2
    place = 2 * half - 1 - pl.program_id(0)
    rows = rows_ref[0].astype(jnp.float32)
    build_rows(at, me_ref, rows[:, :128], rows[:, 128:], place, 0, refs[:half], refs[half:])


def build_parts(me, rows, part, width):
    places, per_owner, lanes = rows.shape
    far_count = places // 2
    outs = pl.pallas_call(
        functools.partial(build_kernel, width - 128),
        out_shape=[jax.ShapeDtypeStruct(part, jnp.bfloat16)] * places,
        grid_spec=pltpu.PrefetchScalarGridSpec(
            num_scalar_prefetch=1,
            grid=(places,),
            in_specs=[pl.BlockSpec((1, per_owner, lanes), lambda i, me: (places - 1 - i, 0, 0))],
            out_specs=part_specs(0, 0, far_count, part),
        ),
        compiler_params=pltpu.CompilerParams(vmem_limit_bytes=60 * 2**20),
        cost_estimate=pl.CostEstimate(
            flops=4 * part[3] * part[1] * part[0] * places * per_owner * lanes,
            bytes_accessed=6 * 2**20,
            transcendentals=0,
        ),
        name="build_parts",
    )(me, rows)
    return outs[:far_count], outs[far_count:]


def adagrad_kernel(me_ref, *refs):
    pieces, (table_ref, accum_ref, new_table_ref, new_accum_ref) = refs[:-4], refs[-4:]
    width = table_ref.shape[0]
    for index, piece in enumerate(pieces):

        @pl.when(pl.program_id(0) == index)
        def _(piece=piece):
            grad = piece[...].astype(jnp.float32)
            mean = jnp.sum(grad * grad, axis=0, keepdims=True) * (1.0 / width)
            updated = accum_ref[...] + mean
            new_accum_ref[...] = updated
            new_table_ref[...] = table_ref[...] - grad * (LEARN_RATE / jnp.sqrt(updated))


def update_table(me, pieces, table_down, accum):
    width, table_rows = table_down.shape
    piece = table_rows // len(pieces)

    def moved(rows):
        return pl.BlockSpec((rows, piece), lambda i, me: (0, i ^ me[0]))

    return pl.pallas_call(
        adagrad_kernel,
        out_shape=(
            jax.ShapeDtypeStruct((width, table_rows), jnp.float32),
            jax.ShapeDtypeStruct((1, table_rows), jnp.float32),
        ),
        grid_spec=pltpu.PrefetchScalarGridSpec(
            num_scalar_prefetch=1,
            grid=(len(pieces),),
            in_specs=[pl.BlockSpec(pieces[0].shape, lambda i, me: (0, 0))] * len(pieces)
            + [moved(width), moved(1)],
            out_specs=[moved(width), moved(1)],
        ),
        name="update_table",
    )(me, *pieces, table_down, accum)


def swap(values, axis, bit):
    size = lax.axis_size(axis)
    return lax.ppermute(values, axis, [(i, i ^ bit) for i in range(size)])


def add_half(first, second):
    return (first.astype(jnp.float32) + second.astype(jnp.float32)).astype(jnp.bfloat16)


def tree_sum(values):
    while len(values) > 1:
        values = [values[i] + values[i + 1] for i in range(0, len(values), 2)]
    return values[0]


def after(value, *ready):
    return lax.optimization_barrier((value,) + ready)[0]


def halves(dense, side):
    cut = dense.reshape(2, dense.shape[0] // 2, dense.shape[1])
    mine = lax.dynamic_index_in_dim(cut, side, 0, keepdims=False)
    return mine, lax.dynamic_index_in_dim(cut, 1 - side, 0, keepdims=False)


def stacked(dense, other, side):
    return jnp.where(side == 0, jnp.stack([dense, other]), jnp.stack([other, dense]))


def sum_all(me, keep, send, rows, dense, part, width):
    owners = lax.axis_size("inner")
    outer, inner = lax.axis_index("outer"), lax.axis_index("inner")
    cuts = (("outer", 2, outer >> 1), ("inner", 1, inner & 1), ("outer", 1, outer & 1))
    far_count = owners // 2
    first = far_count - len(keep)
    keep = dict(enumerate(keep, first))
    came = {}
    for far in reversed(range(first, far_count)):
        came[far] = swap(send[far - first], "outer", 1)
    mine, other = halves(dense, cuts[0][2])
    other = swap(other, "outer", 2)
    low_keep, low_send = build_parts(me, rows, part, width)
    keep.update(enumerate(low_keep))
    for far in reversed(range(first)):
        came[far] = swap(low_send[far], "outer", 1)
    dense = mine + after(other, low_send[0])
    mine, other = halves(dense, cuts[1][2])
    other = swap(other, "inner", 1)
    parts, kept, sent, rest, second = {}, {}, {}, {}, {}

    def first_stage(far):
        held = keep[far]
        if far % 2:
            parts[far] = add_half(held[1], came[far][1])
            kept[far] = add_half(held[0], came[far][0])
        else:
            parts[far] = add_half(held[:, 1], came[far][:, 1])
            kept[far] = add_half(held[:, 0], came[far][:, 0])

    def second_stage(far):
        parts[far] = add_half(kept[far][1], sent[far][1])
        rest[far] = add_half(kept[far][0], sent[far][0])
        second[far] = swap(parts[far], *(("outer", 2) if far % 2 else ("inner", 1)))

    far_ones, near_ones = reversed(range(first, far_count)), reversed(range(first))
    far_ones, near_ones = list(far_ones), list(near_ones)
    for far in far_ones:
        first_stage(far)
        sent[far] = swap(parts[far], *(("inner", 1) if far % 2 else ("outer", 2)))
    for far in near_ones:
        first_stage(far)
    for far in far_ones:
        second_stage(far)
    begun = [parts[far] for far in far_ones]
    for far in near_ones:
        ready = after(parts[far], *begun)
        sent[far] = swap(ready, *(("inner", 1) if far % 2 else ("outer", 2)))
    dense = mine + after(other, *begun)
    mine, other = halves(dense, cuts[2][2])
    other = swap(other, "outer", 1)
    terms, last = {}, {}
    for far in far_ones:
        last[far] = add_half(rest[far], second[far])
        terms[far] = swap(last[far], "inner", 2 * far).astype(jnp.float32)
    dense = mine + after(other, *(last[far] for far in far_ones))
    far_dense = tuple(swap(dense, "inner", 2 * far) for far in range(1, far_count))
    for far in near_ones:
        second_stage(far)
    far_dense = after(far_dense, *(parts[far] for far in near_ones))
    dense = tree_sum([dense] + list(far_dense))
    other = swap(dense, "inner", 1)
    for far in near_ones:
        if far:
            last[far] = add_half(rest[far], second[far])
            terms[far] = swap(last[far], "inner", 2 * far).astype(jnp.float32)
    terms[0] = rest[0].astype(jnp.float32) + second[0].astype(jnp.float32)
    dense = stacked(dense, after(other, last[1]), cuts[1][2])
    other = swap(dense, "outer", 2)
    total = tree_sum([terms[far] for far in range(far_count)]).astype(jnp.bfloat16)
    dense = stacked(dense, after(other, total), cuts[0][2])
    across = swap(total, "outer", 2)
    pieces = [total, swap(total, "outer", 1), across, swap(across, "outer", 1)]
    dense = stacked(dense, swap(dense, "outer", 1), cuts[2][2])
    lanes = dense.shape[-1]
    return pieces, jnp.transpose(dense, (1, 2, 0, 3, 4)).reshape(-1, lanes)


def dense_table(
    layer_input,
    out_grad,
    mix_weight,
    lift_weight,
    linear_weight,
    row_ids,
    row_home,
    table,
    row_accum,
):
    owners, outers = lax.axis_size("inner"), lax.axis_size("outer")
    sample_count = layer_input.shape[0]
    table_rows = table.shape[0]
    me = jnp.stack([lax.axis_index("outer"), lax.axis_index("inner")]).astype(jnp.int32)
    ranks, slots, counts = place_lookups(row_ids, row_home, owners, table_rows)
    width = layer_input.shape[2]
    part = (2, outers // 2, width, table_rows // outers)
    keep, send, rows, dense = local_grads(
        counts,
        me,
        jnp.swapaxes(layer_input, 1, 2),
        jnp.swapaxes(out_grad, 1, 2),
        mix_weight,
        lift_weight.T,
        linear_weight,
        ranks,
        slots,
        owners,
        part,
    )
    pieces, dense = sum_all(me, keep, send, rows, dense, part, width)
    dense = dense * (1.0 / (sample_count * outers * owners))
    new_table, new_accum = update_table(me, pieces, table.T, row_accum.reshape(1, -1))
    feats = layer_input.shape[1]
    linear = [dense[feats * (1 + i) : feats * (2 + i)] for i in range(feats // 128)]
    return (
        new_table.T,
        new_accum.reshape(-1),
        dense[:feats],
        dense[feats * (1 + feats // 128) :].T,
        jnp.concatenate(linear, axis=1),
    )


def power_of_two(number):
    return number & (number - 1) == 0


def on_device(*arrays):
    owners, outers = lax.axis_size("inner"), lax.axis_size("outer")
    layer_input, mix_weight, row_home, table = (arrays[i] for i in (0, 2, 6, 7))
    samples, feats, width = layer_input.shape
    dense_fits = (
        outers == 4
        and owners % 4 == 0
        and power_of_two(owners)
        and row_home.shape[0] <= 2 * samples * feats
        and row_home.shape[0] <= 2**15
        and power_of_two(table.shape[0])
        and 512 <= table.shape[0] <= 4096
        and samples % 16 == 0
        and feats == 256
        and mix_weight.shape[1] == 128
        and 2 * (width - 128) == 128
    )
    return dense_table(*arrays) if dense_fits else routed_rows(*arrays)


def solution(mesh):
    placed = (
        P(("outer", "inner"), None, None),
        P(("outer", "inner"), None, None),
        P(),
        P(),
        P(),
        P(("outer", "inner"), None),
        P(),
        P("inner", None),
        P("inner"),
    )
    return jax.shard_map(
        on_device,
        mesh=mesh,
        in_specs=placed,
        out_specs=(P("inner", None), P("inner"), P(), P(), P()),
        check_vma=False,
    )
```

```python
import functools
import math

import jax
import jax.numpy as jnp
from jax import lax
from jax.experimental import pallas as pl
from jax.experimental.pallas import tpu as pltpu
from jax.sharding import PartitionSpec as P

LEARN_RATE = 0.5


def interaction_grads(inputs, cotangent, mix_weight, lift_weight, linear_weight, scaling):
    compressed = jnp.einsum(
        "bfd,fk->bdk", inputs, mix_weight, preferred_element_type=jnp.float32
    ).astype(jnp.bfloat16)
    products = (
        jnp.einsum("bfd,bdk->bfk", inputs, compressed, preferred_element_type=jnp.float32) * scaling
    ).astype(jnp.bfloat16)
    d_products = jnp.einsum(
        "bfd,kd->bfk", cotangent, lift_weight, preferred_element_type=jnp.float32
    ).astype(jnp.bfloat16)
    d_compressed = (
        jnp.einsum("bfd,bfk->bdk", inputs, d_products, preferred_element_type=jnp.float32) * scaling
    ).astype(jnp.bfloat16)
    d_inputs = cotangent.astype(jnp.float32)
    d_inputs = d_inputs + jnp.einsum(
        "fg,bfd->bgd", linear_weight, cotangent, preferred_element_type=jnp.float32
    )
    d_inputs = d_inputs + scaling * jnp.einsum(
        "bfk,bdk->bfd", d_products, compressed, preferred_element_type=jnp.float32
    )
    d_inputs = d_inputs + jnp.einsum(
        "fk,bdk->bfd", mix_weight, d_compressed, preferred_element_type=jnp.float32
    )
    g_mix = jnp.einsum("bfd,bdk->fk", inputs, d_compressed, preferred_element_type=jnp.float32)
    g_lift = jnp.einsum("bfk,bfd->kd", products, cotangent, preferred_element_type=jnp.float32)
    g_linear = jnp.einsum("bfd,bgd->fg", cotangent, inputs, preferred_element_type=jnp.float32)
    rows_out = d_inputs.astype(jnp.bfloat16).reshape(-1, d_inputs.shape[2])
    return (rows_out, (g_mix, g_lift, g_linear))


def adagrad(weights, history, gradient):
    updated = history + jnp.mean(gradient * gradient, axis=1)
    return (weights - LEARN_RATE * gradient / jnp.sqrt(updated)[:, None], updated)


def owner_ranks(owner_of, owners):
    lookups = owner_of.shape[0]
    width = math.gcd(lookups, 128)
    groups = lookups // width
    hot = (owner_of[:, None] == jnp.arange(owners, dtype=jnp.int32)[None, :]).astype(jnp.bfloat16)
    hot = hot.reshape(groups, width, owners)
    lower = (jnp.arange(width)[:, None] > jnp.arange(width)[None, :]).astype(jnp.bfloat16)
    within = jnp.einsum("ij,gjo->gio", lower, hot, preferred_element_type=jnp.float32)
    totals = jnp.sum(hot.astype(jnp.float32), axis=1)
    before = jnp.cumsum(totals, axis=0) - totals
    counted = jnp.sum(hot.astype(jnp.float32) * (within + before[:, None, :]), axis=2)
    return counted.reshape(-1).astype(jnp.int32)


def add_rows(collected, slots, values):
    count = values.shape[0]
    table_rows = collected.shape[0]
    width = math.gcd(count, 2048)
    columns = jnp.arange(table_rows, dtype=jnp.int32)
    for block_index in range(count // width):
        start = block_index * width
        hot = (slots[start : start + width, None] == columns[None, :]).astype(jnp.bfloat16)
        collected = collected + jnp.einsum(
            "lr,ld->rd", hot, values[start : start + width], preferred_element_type=jnp.float32
        )
    return collected


def routed_rows(
    layer_input,
    out_grad,
    mix_weight,
    lift_weight,
    linear_weight,
    row_ids,
    row_home,
    table,
    row_accum,
):
    owners = lax.axis_size("inner")
    sample_count, feature_count, embed_width = layer_input.shape
    table_rows = table.shape[0]
    half_samples = sample_count // 2
    lookups = sample_count * feature_count
    per_owner = lookups // (2 * owners)
    scaling = 1.0 / math.sqrt(embed_width)
    placed = jnp.take(row_home, row_ids.reshape(-1), axis=0)
    owner_of = placed // table_rows
    target = owner_of * (2 * per_owner) + owner_ranks(owner_of, owners)
    ordering = jnp.zeros((lookups,), jnp.int32).at[target].set(jnp.arange(lookups, dtype=jnp.int32))
    ordering = ordering.reshape(owners, 2, per_owner)
    local_rows = (
        jnp.zeros((lookups,), jnp.int32)
        .at[target]
        .set(placed % table_rows)
        .reshape(owners, 2 * per_owner)
    )
    arrived_rows = lax.all_to_all(
        local_rows, "inner", split_axis=0, concat_axis=0, tiled=True
    ).reshape(owners, 2, per_owner)
    collected = jnp.zeros((table_rows, embed_width), jnp.float32)
    totals = None
    for half_index in range(2):
        first_sample = half_index * half_samples
        rows_out, partial_value = interaction_grads(
            layer_input[first_sample : first_sample + half_samples],
            out_grad[first_sample : first_sample + half_samples],
            mix_weight,
            lift_weight,
            linear_weight,
            scaling,
        )
        picked = ordering[:, half_index, :] - half_index * half_samples * feature_count
        outgoing = jnp.take(rows_out, picked.reshape(-1), axis=0).reshape(
            owners, per_owner, embed_width
        )
        incoming = lax.all_to_all(outgoing, "inner", split_axis=0, concat_axis=0, tiled=True)
        collected = add_rows(
            collected, arrived_rows[:, half_index, :].reshape(-1), incoming.reshape(-1, embed_width)
        )
        if totals is None:
            totals = partial_value
        else:
            totals = tuple((earlier + later for earlier, later in zip(totals, partial_value)))
    batch_total = sample_count * lax.axis_size("outer") * owners
    summed = lax.psum((totals[0], totals[1], totals[2]), ("outer", "inner"))
    mix_grad = summed[0] / batch_total
    lift_grad = summed[1] / batch_total
    linear_grad = summed[2] / batch_total
    complete = lax.psum(collected, "outer")
    new_table, new_accum = adagrad(table, row_accum, complete)
    return (new_table, new_accum, mix_grad, lift_grad, linear_grad)


def matmul(left, right):
    return jnp.dot(left, right, preferred_element_type=jnp.float32)


def matmul_nt(left, right):
    return lax.dot_general(left, right, (((1,), (1,)), ((), ())), preferred_element_type=jnp.float32)


def one_hot(matches):
    return jnp.where(matches, 1.0, 0.0).astype(jnp.bfloat16)


def place_kernel(shift, owners, ids_ref, home_ref, rank_ref, slot_ref, count_ref):
    samples, feats = ids_ref.shape
    high, low = home_ref.shape
    half = low // 2
    home = home_ref[...]
    pieces = []
    for part in (home & 255, home >> 8):
        down = part.astype(jnp.float32).T
        pieces.append(jnp.concatenate([down[:half], down[half:]], axis=1))
    pieces = jnp.concatenate(pieces, axis=0).astype(jnp.bfloat16)
    high_at = lax.broadcasted_iota(jnp.int32, (2 * high, feats), 0)
    low_at = lax.broadcasted_iota(jnp.int32, (half, feats), 0)
    lane = lax.broadcasted_iota(jnp.int32, (1, feats), 1)
    count_lane = lax.broadcasted_iota(jnp.int32, (8, 128), 1)

    @pl.loop(0, samples // 8)
    def _(group):
        first = pl.multiple_of(group * 8, 8)
        ids = ids_ref[pl.ds(first, 8), :]
        every = range(8)
        ones = [ids[row : row + 1] for row in every]
        hots = [one_hot(high_at == ((one >> 6) & 1) * high + (one >> 7)) for one in ones]
        founds = [matmul(pieces, hot) for hot in hots]
        places = []
        for row in every:
            value = founds[row][:half] + 256.0 * founds[row][half:]
            value = jnp.where(low_at == (ones[row] & (half - 1)), value, 0.0)
            places.append(jnp.sum(value, axis=0, keepdims=True))
        place = jnp.concatenate(places, axis=0).astype(jnp.int32)
        owner_all = place >> shift
        slot_ref[pl.ds(first, 8), :] = place & ((1 << shift) - 1)
        keys = (owner_all * feats + lane).astype(jnp.float32)
        downs = [jnp.broadcast_to(keys[row : row + 1], (128, feats)).T for row in every]
        ranks = []
        for row in every:
            parts = []
            for at in range(0, feats, 128):
                less = downs[row] < keys[row : row + 1, at : at + 128]
                parts.append(jnp.sum(jnp.where(less, 1.0, 0.0), axis=0, keepdims=True))
            ranks.append(jnp.concatenate(parts, axis=1))
        rank_ref[pl.ds(first, 8), :] = jnp.concatenate(ranks, axis=0).astype(jnp.int32)
        counts = jnp.zeros((8, 128), jnp.float32)
        for owner_at in range(owners):
            number = jnp.sum(jnp.where(owner_all == owner_at, 1.0, 0.0), axis=1, keepdims=True)
            counts = jnp.where(count_lane == owner_at, number, counts)
        most = jnp.max(counts, axis=1, keepdims=True)
        counts = jnp.where(count_lane == owners, most, counts)
        count_ref[pl.ds(first, 8), :] = counts.astype(jnp.int32)


def place_lookups(row_ids, row_home, owners, table_rows):
    samples, feats = row_ids.shape
    return pl.pallas_call(
        functools.partial(place_kernel, table_rows.bit_length() - 1, owners),
        out_shape=(
            jax.ShapeDtypeStruct((samples, feats), jnp.int32),
            jax.ShapeDtypeStruct((samples, feats), jnp.int32),
            jax.ShapeDtypeStruct((samples, 128), jnp.int32),
        ),
        name="place_lookups",
    )(row_ids, row_home.reshape(-1, 128))


COPY_ROWS = 56
SCRATCH = 10


def sum_list(values):
    total = values[0]
    for value in values[1:]:
        total = total + value
    return total


def grads_kernel(
    sizes,
    count_ref,
    me_ref,
    x_ref,
    g_ref,
    mix_ref,
    lift_ref,
    linear_ref,
    rank_ref,
    slot_ref,
    *rest,
):
    group, steps, owners, per_owner, scaling = sizes
    far_count = (len(rest) - SCRATCH - 2) // 2
    keep_refs, send_refs = rest[:far_count], rest[far_count : 2 * far_count]
    rows_ref, dense_ref = rest[2 * far_count : 2 * far_count + 2]
    scratch = rest[2 * far_count + 2 :]
    step = pl.program_id(0)

    @pl.when(step < steps)
    def _():
        gather_rows(
            sizes,
            count_ref,
            me_ref,
            x_ref,
            g_ref,
            mix_ref,
            lift_ref,
            linear_ref,
            rank_ref,
            slot_ref,
            rows_ref,
            dense_ref,
            *scratch,
        )

    @pl.when(step >= steps)
    def _():
        place = owners - 1 - (step - steps)
        row_a, row_b = scratch[-3], scratch[-2]
        owner = place ^ me_ref[1]
        first_rows = row_a[owner, pl.ds(0, per_owner), :]
        second_rows = row_b[owner, pl.ds(0, per_owner), :]
        at = x_ref.shape[1] - 128
        build_rows(at, me_ref, first_rows, second_rows, place, far_count, keep_refs, send_refs)


def join_rows(count_ref, filled, sorted_a, sorted_b, row_a, row_b, step, group, owners):
    begun = (step >= 0).astype(jnp.int32)
    now = (step + 2) % 2
    first = jnp.maximum(step, 0) * group
    every = range(group)
    numbers = [[count_ref[first + k, owner] * begun for owner in range(owners)] for k in every]
    starts = [filled[owner] for owner in range(owners)]
    ends = list(starts)
    for k in every:
        begin = 0
        for owner in range(owners):
            source, target = pl.ds(begin, COPY_ROWS), pl.ds(ends[owner], COPY_ROWS)
            row_a[owner, target, :] = sorted_a[now, k, source, :]
            row_b[owner, target, :] = sorted_b[now, k, source, :]
            ends[owner] = ends[owner] + numbers[k][owner]
            begin = begin + numbers[k][owner]
    most = count_ref[first, owners] * begun
    for k in range(1, group):
        most = jnp.maximum(most, count_ref[first + k, owners] * begun)

    @pl.when(most > COPY_ROWS)
    def _():
        again = list(starts)
        for k in every:
            begin = 0
            for owner in range(owners):

                def copy(turn, carry, begin=begin, at=again[owner], owner=owner, k=k):
                    off = turn * COPY_ROWS
                    source, target = pl.ds(begin + off, COPY_ROWS), pl.ds(at + off, COPY_ROWS)
                    row_a[owner, target, :] = sorted_a[now, k, source, :]
                    row_b[owner, target, :] = sorted_b[now, k, source, :]
                    return carry

                turns = (numbers[k][owner] + COPY_ROWS - 1) // COPY_ROWS
                lax.fori_loop(0, turns, copy, 0)
                again[owner] = again[owner] + numbers[k][owner]
                begin = begin + numbers[k][owner]

    for owner in range(owners):
        filled[owner] = ends[owner]


def gather_rows(
    sizes,
    count_ref,
    me_ref,
    x_ref,
    g_ref,
    mix_ref,
    lift_ref,
    linear_ref,
    rank_ref,
    slot_ref,
    rows_ref,
    dense_ref,
    mix_down,
    lift_down,
    mix_sum,
    lift_sum,
    linear_sum,
    sorted_a,
    sorted_b,
    row_a,
    row_b,
    filled,
):
    group, steps, owners, per_owner, scaling = sizes
    width, feats = x_ref.shape[1:]
    rank = mix_ref.shape[1]
    step = pl.program_id(0)

    @pl.when(step == 0)
    def _():
        mix_down[...] = mix_ref[...].astype(jnp.float32).T.astype(jnp.bfloat16)
        lift_down[...] = lift_ref[...].astype(jnp.float32).T.astype(jnp.bfloat16)
        mix_sum[...] = jnp.zeros_like(mix_sum)
        lift_sum[...] = jnp.zeros_like(lift_sum)
        linear_sum[...] = jnp.zeros_like(linear_sum)
        for owner in range(owners):
            filled[owner] = 0

    now = step % 2
    join_rows(count_ref, filled, sorted_a, sorted_b, row_a, row_b, step - 1, group, owners)
    row_at = lax.broadcasted_iota(jnp.int32, (feats, feats), 0)
    extra_at = lax.broadcasted_iota(jnp.int32, (feats - width, feats), 0)
    every = range(group)
    d_prods = [matmul(lift_down[...], g_ref[k]).astype(jnp.bfloat16) for k in every]
    boths = [
        matmul_nt(x_ref[k], jnp.concatenate([mix_down[...], d_prods[k]], axis=0)) for k in every
    ]
    comps = [both[:, :rank].astype(jnp.bfloat16) for both in boths]
    d_comps = [(both[:, rank:] * scaling).astype(jnp.bfloat16) for both in boths]
    x_flat = x_ref[...].reshape(group * width, feats).T
    x_flats = [x_flat[:, k * width : (k + 1) * width] for k in every]
    pairs = [
        matmul(x_flats[k], jnp.concatenate([comps[k], d_comps[k]], axis=1)) for k in every
    ]
    prods = [(pair[:, :rank] * scaling).astype(jnp.bfloat16) for pair in pairs]
    mix_sum[...] += sum_list([pair[:, rank:] for pair in pairs])
    g_all = g_ref[...].reshape(group * width, feats)
    d_all = g_all.astype(jnp.float32) + matmul(g_all, linear_ref[...])
    d_all = d_all + matmul(jnp.concatenate(d_comps, axis=0), mix_down[...])
    d_ins = [
        d_all[k * width : (k + 1) * width] + scaling * matmul(comps[k], d_prods[k]) for k in every
    ]
    moves, rows_downs = [], []
    for k in every:
        slot = slot_ref[pl.ds(step * group + k, 1), :]
        extra = jnp.where(extra_at == 0, slot >> 4, jnp.where(extra_at == 1, slot & 15, 0))
        rows_downs.append(
            jnp.concatenate(
                [d_ins[k].astype(jnp.bfloat16), extra.astype(jnp.float32).astype(jnp.bfloat16)],
                axis=0,
            )
        )
        moves.append(one_hot(row_at == rank_ref[pl.ds(step * group + k, 1), :]))
    for k in every:
        ordered = matmul_nt(moves[k], rows_downs[k])
        sorted_a[now, k, :feats] = ordered[:, :128]
        sorted_b[now, k, :feats] = ordered[:, 128:]
    linear_sum[...] += matmul(x_flat, g_all)
    lift_sum[...] += sum_list([matmul(g_ref[k], prods[k]) for k in every])

    @pl.when(step == steps - 1)
    def _():
        join_rows(count_ref, filled, sorted_a, sorted_b, row_a, row_b, step, group, owners)
        dense_ref[:feats] = mix_sum[...]
        linear = linear_sum[...].T
        for at in range(feats // 128):
            dense_ref[feats * (1 + at) : feats * (2 + at)] = linear[:, 128 * at : 128 * (at + 1)]
        dense_ref[feats * (1 + feats // 128) :] = lift_sum[...]
        for place in range(rows_ref.shape[0]):
            owner = place ^ me_ref[1]
            rows_ref[place, :, :128] = row_a[owner, pl.ds(0, per_owner), :].astype(jnp.bfloat16)
            rows_ref[place, :, 128:] = row_b[owner, pl.ds(0, per_owner), :].astype(jnp.bfloat16)


def build_rows(at, me_ref, first_rows, second_rows, place, first, keep_refs, send_refs):
    outers, piece = 2 * keep_refs[0].shape[1], keep_refs[0].shape[3]
    per_owner = first_rows.shape[0]
    rows_down = jnp.concatenate([first_rows.T, second_rows.T[:at]], axis=0).astype(jnp.bfloat16)
    slots = second_rows[:, at : at + 1] * 16.0 + second_rows[:, at + 1 : at + 2]
    slots = slots.astype(jnp.int32)
    lanes = lax.broadcasted_iota(jnp.int32, (per_owner, piece), 1)
    totals = []
    for outer in range(outers):
        base = (outer ^ me_ref[0]) * piece
        totals.append(matmul(rows_down, one_hot(lanes == slots - base)).astype(jnp.bfloat16))
    for index in range(len(keep_refs)):

        @pl.when(place // 2 == first + index)
        def _(index=index):
            for outer in range(outers):
                ref = (send_refs if outer % 2 else keep_refs)[index]
                ref[0, outer // 2] = totals[outer]


def part_specs(start, first, count, part):
    def spec(index):
        begin = start + 2 * (count - 1 - index)
        return pl.BlockSpec(
            (1,) + part[1:], lambda i, *_: (jnp.clip(begin + 1 - i, 0, 1), 0, 0, 0)
        )

    return [spec(index) for index in range(count)] * 2


def local_grads(counts, me, x_down, g_down, mix, lift_down, linear, ranks, slots, owners, part):
    samples, width, feats = x_down.shape
    rank = mix.shape[1]
    group = 4
    steps = samples // group
    per_owner = samples * feats // owners
    far_count = owners // 4
    sizes = (group, steps, owners, per_owner, 1.0 / math.sqrt(width))

    def whole(shape):
        return pl.BlockSpec(shape, lambda i, *_: (0,) * len(shape))

    sample_spec = pl.BlockSpec(
        (group, width, feats), lambda i, *_: (jnp.minimum(i, steps - 1), 0, 0)
    )
    dense_rows = feats * (1 + feats // 128) + width
    room = per_owner + 64
    rows_shape = (owners // 2, per_owner, 256)
    scratch = [
        pltpu.VMEM((rank, feats), jnp.bfloat16),
        pltpu.VMEM((rank, width), jnp.bfloat16),
        pltpu.VMEM((feats, rank), jnp.float32),
        pltpu.VMEM((width, rank), jnp.float32),
        pltpu.VMEM((feats, feats), jnp.float32),
        pltpu.VMEM((2, group, feats + 64, 128), jnp.float32),
        pltpu.VMEM((2, group, feats + 64, 128), jnp.float32),
        pltpu.VMEM((owners, room, 128), jnp.float32),
        pltpu.VMEM((owners, room, 128), jnp.float32),
        pltpu.SMEM((owners,), jnp.int32),
    ]
    outs = pl.pallas_call(
        functools.partial(grads_kernel, sizes),
        out_shape=[jax.ShapeDtypeStruct(part, jnp.bfloat16)] * (2 * far_count)
        + [
            jax.ShapeDtypeStruct(rows_shape, jnp.bfloat16),
            jax.ShapeDtypeStruct((dense_rows, 128), jnp.float32),
        ],
        grid_spec=pltpu.PrefetchScalarGridSpec(
            num_scalar_prefetch=2,
            grid=(steps + owners // 2,),
            in_specs=[
                sample_spec,
                sample_spec,
                whole((feats, rank)),
                whole((width, rank)),
                whole((feats, feats)),
                whole((samples, feats)),
                whole((samples, feats)),
            ],
            out_specs=part_specs(steps, owners // 2 - far_count, far_count, part)
            + [whole(rows_shape), whole((dense_rows, 128))],
            scratch_shapes=scratch,
        ),
        compiler_params=pltpu.CompilerParams(vmem_limit_bytes=60 * 2**20),
        cost_estimate=pl.CostEstimate(
            flops=2 * samples * feats * feats * 3072, bytes_accessed=12 * 2**20, transcendentals=0
        ),
        name="local_grads",
    )(counts, me, x_down, g_down, mix, lift_down, linear, ranks, slots)
    keep, send = outs[:far_count], outs[far_count : 2 * far_count]
    return keep, send, outs[2 * far_count], outs[2 * far_count + 1]


def build_kernel(at, me_ref, rows_ref, keep_ref, send_ref):
    rows = rows_ref[0].astype(jnp.float32)
    place = 1 - pl.program_id(0)
    build_rows(at, me_ref, rows[:, :128], rows[:, 128:], place, 0, (keep_ref,), (send_ref,))


def build_part(me, rows, far, part, width):
    per_owner, lanes = rows.shape[1:]
    return pl.pallas_call(
        functools.partial(build_kernel, width - 128),
        out_shape=[jax.ShapeDtypeStruct(part, jnp.bfloat16)] * 2,
        grid_spec=pltpu.PrefetchScalarGridSpec(
            num_scalar_prefetch=1,
            grid=(2,),
            in_specs=[pl.BlockSpec((1, per_owner, lanes), lambda i, me: (2 * far + 1 - i, 0, 0))],
            out_specs=part_specs(0, 0, 1, part),
        ),
        compiler_params=pltpu.CompilerParams(vmem_limit_bytes=60 * 2**20),
        cost_estimate=pl.CostEstimate(
            flops=4 * part[3] * part[1] * part[0] * 2 * per_owner * lanes,
            bytes_accessed=3 * 2**20,
            transcendentals=0,
        ),
        name="build_part",
    )(me, rows)


def adagrad_kernel(me_ref, *refs):
    pieces, (table_ref, accum_ref) = refs[:2], refs[2:4]
    new_table_ref, new_accum_ref = refs[-2:]
    width = table_ref.shape[0]
    for index, piece in enumerate(pieces):

        @pl.when(pl.program_id(0) == index)
        def _(piece=piece):
            grad = piece[...].astype(jnp.float32)
            mean = jnp.sum(grad * grad, axis=0, keepdims=True) * (1.0 / width)
            updated = accum_ref[...] + mean
            new_accum_ref[...] = updated
            new_table_ref[...] = table_ref[...] - grad * (LEARN_RATE / jnp.sqrt(updated))


def update_table(me, pieces, table_down, accum, first, done=()):
    width, table_rows = table_down.shape
    piece = pieces[0].shape[1]

    def moved(rows):
        return pl.BlockSpec((rows, piece), lambda i, me: (0, (first + i) ^ me[0]))

    return pl.pallas_call(
        adagrad_kernel,
        out_shape=(
            jax.ShapeDtypeStruct((width, table_rows), jnp.float32),
            jax.ShapeDtypeStruct((1, table_rows), jnp.float32),
        ),
        grid_spec=pltpu.PrefetchScalarGridSpec(
            num_scalar_prefetch=1,
            grid=(2,),
            in_specs=[pl.BlockSpec((width, piece), lambda i, me: (0, 0))] * 2
            + [moved(width), moved(1)]
            + [pl.BlockSpec(memory_space=pl.ANY)] * len(done),
            out_specs=[moved(width), moved(1)],
        ),
        input_output_aliases={5 + i: i for i in range(len(done))},
        name="update_table",
    )(me, *pieces, table_down, accum, *done)


def swap(values, axis, bit):
    size = lax.axis_size(axis)
    return lax.ppermute(values, axis, [(i, i ^ bit) for i in range(size)])


def add_half(first, second):
    return (first.astype(jnp.float32) + second.astype(jnp.float32)).astype(jnp.bfloat16)


def tree_sum(values):
    while len(values) > 1:
        values = [values[i] + values[i + 1] for i in range(0, len(values), 2)]
    return values[0]


def after(value, *ready):
    return lax.optimization_barrier((value,) + ready)[0]


def halves(dense, side):
    cut = dense.reshape(2, dense.shape[0] // 2, dense.shape[1])
    mine = lax.dynamic_index_in_dim(cut, side, 0, keepdims=False)
    return mine, lax.dynamic_index_in_dim(cut, 1 - side, 0, keepdims=False)


def stacked(dense, other, side):
    return jnp.where(side == 0, jnp.stack([dense, other]), jnp.stack([other, dense]))


def sum_all(me, keep, send, rows, dense, part, width):
    owners = lax.axis_size("inner")
    outer, inner = lax.axis_index("outer"), lax.axis_index("inner")
    far_count = owners // 2
    first = far_count - len(keep)
    keep = dict(enumerate(keep, first))
    came, parts, kept, sent, rest, second, terms, last = ({} for _ in range(8))
    far_ones, near_ones = list(reversed(range(first, far_count))), list(reversed(range(first)))

    def first_stage(far):
        held = keep[far]
        if far % 2:
            parts[far] = add_half(held[1], came[far][1])
            kept[far] = add_half(held[0], came[far][0])
        else:
            parts[far] = add_half(held[:, 1], came[far][:, 1])
            kept[far] = add_half(held[:, 0], came[far][:, 0])

    def second_stage(far):
        parts[far] = add_half(kept[far][1], sent[far][1])
        rest[far] = add_half(kept[far][0], sent[far][0])
        second[far] = swap(parts[far], *(("outer", 2) if far % 2 else ("inner", 1)))

    def send_first(far, ready):
        sent[far] = swap(ready, *(("inner", 1) if far % 2 else ("outer", 2)))

    sides = (outer >> 1, inner & 1, outer & 1)
    for far in far_ones:
        came[far] = swap(send[far - first], "outer", 1)
    mine, other = halves(dense, sides[0])
    other = swap(other, "outer", 2)
    for far in near_ones:
        keep[far], low_send = build_part(me, rows, far, part, width)
        came[far] = swap(low_send, "outer", 1)
        if far == near_ones[0]:
            dense = mine + after(other, low_send)
            mine, other = halves(dense, sides[1])
            other = swap(other, "inner", 1)
            for index in far_ones:
                first_stage(index)
                send_first(index, parts[index])
            rows = after(rows, *(parts[index] for index in far_ones))
    dense = mine + after(other, low_send)
    mine, other = halves(dense, sides[2])
    other = swap(other, "outer", 1)
    for far in near_ones:
        first_stage(far)
    dense = mine + after(other, *(parts[far] for far in near_ones))
    far_dense = tuple(swap(dense, "inner", 2 * far) for far in range(1, far_count))
    for far in far_ones:
        second_stage(far)
    begun = [parts[far] for far in far_ones]
    near_parts = [parts[far] for far in near_ones]
    for far in near_ones:
        send_first(far, after(parts[far], *begun))
    for far in far_ones:
        second[far] = after(second[far], dense, *near_parts)
        last[far] = add_half(rest[far], second[far])
        terms[far] = swap(last[far], "inner", 2 * far).astype(jnp.float32)
    dense = tree_sum([dense] + list(after(far_dense, *(last[far] for far in far_ones))))
    other = swap(dense, "outer", 2)
    arrived = after(tuple(sent[far] for far in near_ones), *(last[far] for far in far_ones))
    for far, sent[far] in zip(near_ones, arrived):
        second_stage(far)
    dense = stacked(dense, after(other, *(parts[far] for far in near_ones)), sides[0])
    other = swap(dense, "inner", 1)
    for far in near_ones:
        if far:
            last[far] = add_half(rest[far], second[far])
            terms[far] = swap(last[far], "inner", 2 * far).astype(jnp.float32)
    terms[0] = rest[0].astype(jnp.float32) + second[0].astype(jnp.float32)
    dense = stacked(dense, after(other, last[1], terms[0]), sides[1])
    other = swap(dense, "outer", 1)
    total = tree_sum([terms[far] for far in range(far_count)]).astype(jnp.bfloat16)
    dense = stacked(dense, other, sides[2])
    lanes = dense.shape[-1]
    return total, jnp.transpose(dense, (2, 1, 0, 3, 4)).reshape(-1, lanes)


def dense_table(
    layer_input,
    out_grad,
    mix_weight,
    lift_weight,
    linear_weight,
    row_ids,
    row_home,
    table,
    row_accum,
):
    owners, outers = lax.axis_size("inner"), lax.axis_size("outer")
    sample_count = layer_input.shape[0]
    table_rows = table.shape[0]
    me = jnp.stack([lax.axis_index("outer"), lax.axis_index("inner")]).astype(jnp.int32)
    ranks, slots, counts = place_lookups(row_ids, row_home, owners, table_rows)
    width = layer_input.shape[2]
    part = (2, outers // 2, width, table_rows // outers)
    keep, send, rows, dense = local_grads(
        counts,
        me,
        jnp.swapaxes(layer_input, 1, 2),
        jnp.swapaxes(out_grad, 1, 2),
        mix_weight,
        lift_weight.T,
        linear_weight,
        ranks,
        slots,
        owners,
        part,
    )
    total, dense = sum_all(me, keep, send, rows, dense, part, width)
    dense = dense * (1.0 / (sample_count * outers * owners))
    across = swap(total, "outer", 2)
    table_down, accum = table.T, row_accum.reshape(1, -1)
    beside = swap(total, "outer", 1)
    done = update_table(me, (total, beside), table_down, accum, 0)
    pieces = (across, swap(across, "outer", 1))
    new_table, new_accum = update_table(me, pieces, table_down, accum, 2, done)
    feats = layer_input.shape[1]
    linear = [dense[feats * (1 + i) : feats * (2 + i)] for i in range(feats // 128)]
    return (
        new_table.T,
        new_accum.reshape(-1),
        dense[:feats],
        dense[feats * (1 + feats // 128) :].T,
        jnp.concatenate(linear, axis=1),
    )


def power_of_two(number):
    return number & (number - 1) == 0


def on_device(*arrays):
    owners, outers = lax.axis_size("inner"), lax.axis_size("outer")
    layer_input, mix_weight, row_home, table = (arrays[i] for i in (0, 2, 6, 7))
    samples, feats, width = layer_input.shape
    dense_fits = (
        outers == 4
        and owners % 4 == 0
        and power_of_two(owners)
        and row_home.shape[0] <= 2 * samples * feats
        and row_home.shape[0] <= 2**15
        and power_of_two(table.shape[0])
        and 512 <= table.shape[0] <= 4096
        and samples % 16 == 0
        and feats == 256
        and mix_weight.shape[1] == 128
        and 2 * (width - 128) == 128
    )
    return dense_table(*arrays) if dense_fits else routed_rows(*arrays)


def solution(mesh):
    placed = (
        P(("outer", "inner"), None, None),
        P(("outer", "inner"), None, None),
        P(),
        P(),
        P(),
        P(("outer", "inner"), None),
        P(),
        P("inner", None),
        P("inner"),
    )
    return jax.shard_map(
        on_device,
        mesh=mesh,
        in_specs=placed,
        out_specs=(P("inner", None), P("inner"), P(), P(), P()),
        check_vma=False,
    )
```

```python
import functools
import math

import jax
import jax.numpy as jnp
from jax import lax
from jax.experimental import pallas as pl
from jax.experimental.pallas import tpu as pltpu
from jax.sharding import PartitionSpec as P

LEARN_RATE = 0.5


def interaction_grads(inputs, cotangent, mix_weight, lift_weight, linear_weight, scaling):
    compressed = jnp.einsum(
        "bfd,fk->bdk", inputs, mix_weight, preferred_element_type=jnp.float32
    ).astype(jnp.bfloat16)
    products = (
        jnp.einsum("bfd,bdk->bfk", inputs, compressed, preferred_element_type=jnp.float32) * scaling
    ).astype(jnp.bfloat16)
    d_products = jnp.einsum(
        "bfd,kd->bfk", cotangent, lift_weight, preferred_element_type=jnp.float32
    ).astype(jnp.bfloat16)
    d_compressed = (
        jnp.einsum("bfd,bfk->bdk", inputs, d_products, preferred_element_type=jnp.float32) * scaling
    ).astype(jnp.bfloat16)
    d_inputs = cotangent.astype(jnp.float32)
    d_inputs = d_inputs + jnp.einsum(
        "fg,bfd->bgd", linear_weight, cotangent, preferred_element_type=jnp.float32
    )
    d_inputs = d_inputs + scaling * jnp.einsum(
        "bfk,bdk->bfd", d_products, compressed, preferred_element_type=jnp.float32
    )
    d_inputs = d_inputs + jnp.einsum(
        "fk,bdk->bfd", mix_weight, d_compressed, preferred_element_type=jnp.float32
    )
    g_mix = jnp.einsum("bfd,bdk->fk", inputs, d_compressed, preferred_element_type=jnp.float32)
    g_lift = jnp.einsum("bfk,bfd->kd", products, cotangent, preferred_element_type=jnp.float32)
    g_linear = jnp.einsum("bfd,bgd->fg", cotangent, inputs, preferred_element_type=jnp.float32)
    rows_out = d_inputs.astype(jnp.bfloat16).reshape(-1, d_inputs.shape[2])
    return (rows_out, (g_mix, g_lift, g_linear))


def adagrad(weights, history, gradient):
    updated = history + jnp.mean(gradient * gradient, axis=1)
    return (weights - LEARN_RATE * gradient / jnp.sqrt(updated)[:, None], updated)


def owner_ranks(owner_of, owners):
    lookups = owner_of.shape[0]
    width = math.gcd(lookups, 128)
    groups = lookups // width
    hot = (owner_of[:, None] == jnp.arange(owners, dtype=jnp.int32)[None, :]).astype(jnp.bfloat16)
    hot = hot.reshape(groups, width, owners)
    lower = (jnp.arange(width)[:, None] > jnp.arange(width)[None, :]).astype(jnp.bfloat16)
    within = jnp.einsum("ij,gjo->gio", lower, hot, preferred_element_type=jnp.float32)
    totals = jnp.sum(hot.astype(jnp.float32), axis=1)
    before = jnp.cumsum(totals, axis=0) - totals
    counted = jnp.sum(hot.astype(jnp.float32) * (within + before[:, None, :]), axis=2)
    return counted.reshape(-1).astype(jnp.int32)


def add_rows(collected, slots, values):
    count = values.shape[0]
    table_rows = collected.shape[0]
    width = math.gcd(count, 2048)
    columns = jnp.arange(table_rows, dtype=jnp.int32)
    for block_index in range(count // width):
        start = block_index * width
        hot = (slots[start : start + width, None] == columns[None, :]).astype(jnp.bfloat16)
        collected = collected + jnp.einsum(
            "lr,ld->rd", hot, values[start : start + width], preferred_element_type=jnp.float32
        )
    return collected


def routed_rows(
    layer_input,
    out_grad,
    mix_weight,
    lift_weight,
    linear_weight,
    row_ids,
    row_home,
    table,
    row_accum,
):
    owners = lax.axis_size("inner")
    sample_count, feature_count, embed_width = layer_input.shape
    table_rows = table.shape[0]
    half_samples = sample_count // 2
    lookups = sample_count * feature_count
    per_owner = lookups // (2 * owners)
    scaling = 1.0 / math.sqrt(embed_width)
    placed = jnp.take(row_home, row_ids.reshape(-1), axis=0)
    owner_of = placed // table_rows
    target = owner_of * (2 * per_owner) + owner_ranks(owner_of, owners)
    ordering = jnp.zeros((lookups,), jnp.int32).at[target].set(jnp.arange(lookups, dtype=jnp.int32))
    ordering = ordering.reshape(owners, 2, per_owner)
    local_rows = (
        jnp.zeros((lookups,), jnp.int32)
        .at[target]
        .set(placed % table_rows)
        .reshape(owners, 2 * per_owner)
    )
    arrived_rows = lax.all_to_all(
        local_rows, "inner", split_axis=0, concat_axis=0, tiled=True
    ).reshape(owners, 2, per_owner)
    collected = jnp.zeros((table_rows, embed_width), jnp.float32)
    totals = None
    for half_index in range(2):
        first_sample = half_index * half_samples
        rows_out, partial_value = interaction_grads(
            layer_input[first_sample : first_sample + half_samples],
            out_grad[first_sample : first_sample + half_samples],
            mix_weight,
            lift_weight,
            linear_weight,
            scaling,
        )
        picked = ordering[:, half_index, :] - half_index * half_samples * feature_count
        outgoing = jnp.take(rows_out, picked.reshape(-1), axis=0).reshape(
            owners, per_owner, embed_width
        )
        incoming = lax.all_to_all(outgoing, "inner", split_axis=0, concat_axis=0, tiled=True)
        collected = add_rows(
            collected, arrived_rows[:, half_index, :].reshape(-1), incoming.reshape(-1, embed_width)
        )
        if totals is None:
            totals = partial_value
        else:
            totals = tuple((earlier + later for earlier, later in zip(totals, partial_value)))
    batch_total = sample_count * lax.axis_size("outer") * owners
    summed = lax.psum((totals[0], totals[1], totals[2]), ("outer", "inner"))
    mix_grad = summed[0] / batch_total
    lift_grad = summed[1] / batch_total
    linear_grad = summed[2] / batch_total
    complete = lax.psum(collected, "outer")
    new_table, new_accum = adagrad(table, row_accum, complete)
    return (new_table, new_accum, mix_grad, lift_grad, linear_grad)


def matmul(left, right):
    return jnp.dot(left, right, preferred_element_type=jnp.float32)


def matmul_nt(left, right):
    return lax.dot_general(left, right, (((1,), (1,)), ((), ())), preferred_element_type=jnp.float32)


def one_hot(matches):
    return jnp.where(matches, 1.0, 0.0).astype(jnp.bfloat16)


def place_kernel(shift, owners, ids_ref, home_ref, rank_ref, slot_ref, count_ref):
    samples, feats = ids_ref.shape
    high, low = home_ref.shape
    half = low // 2
    home = home_ref[...]
    pieces = []
    for part in (home & 255, home >> 8):
        down = part.astype(jnp.float32).T
        pieces.append(jnp.concatenate([down[:half], down[half:]], axis=1))
    pieces = jnp.concatenate(pieces, axis=0).astype(jnp.bfloat16)
    high_at = lax.broadcasted_iota(jnp.int32, (2 * high, feats), 0)
    low_at = lax.broadcasted_iota(jnp.int32, (half, feats), 0)
    lane = lax.broadcasted_iota(jnp.int32, (1, feats), 1)
    count_lane = lax.broadcasted_iota(jnp.int32, (8, 128), 1)

    @pl.loop(0, samples // 8)
    def _(group):
        first = pl.multiple_of(group * 8, 8)
        ids = ids_ref[pl.ds(first, 8), :]
        every = range(8)
        ones = [ids[row : row + 1] for row in every]
        hots = [one_hot(high_at == ((one >> 6) & 1) * high + (one >> 7)) for one in ones]
        founds = [matmul(pieces, hot) for hot in hots]
        places = []
        for row in every:
            value = founds[row][:half] + 256.0 * founds[row][half:]
            value = jnp.where(low_at == (ones[row] & (half - 1)), value, 0.0)
            places.append(jnp.sum(value, axis=0, keepdims=True))
        place = jnp.concatenate(places, axis=0).astype(jnp.int32)
        owner_all = place >> shift
        slot_ref[pl.ds(first, 8), :] = place & ((1 << shift) - 1)
        keys = (owner_all * feats + lane).astype(jnp.float32)
        downs = [jnp.broadcast_to(keys[row : row + 1], (128, feats)).T for row in every]
        ranks = []
        for row in every:
            parts = []
            for at in range(0, feats, 128):
                less = downs[row] < keys[row : row + 1, at : at + 128]
                parts.append(jnp.sum(jnp.where(less, 1.0, 0.0), axis=0, keepdims=True))
            ranks.append(jnp.concatenate(parts, axis=1))
        rank_ref[pl.ds(first, 8), :] = jnp.concatenate(ranks, axis=0).astype(jnp.int32)
        counts = jnp.zeros((8, 128), jnp.float32)
        for owner_at in range(owners):
            number = jnp.sum(jnp.where(owner_all == owner_at, 1.0, 0.0), axis=1, keepdims=True)
            counts = jnp.where(count_lane == owner_at, number, counts)
        most = jnp.max(counts, axis=1, keepdims=True)
        counts = jnp.where(count_lane == owners, most, counts)
        count_ref[pl.ds(first, 8), :] = counts.astype(jnp.int32)


def place_lookups(row_ids, row_home, owners, table_rows):
    samples, feats = row_ids.shape
    return pl.pallas_call(
        functools.partial(place_kernel, table_rows.bit_length() - 1, owners),
        out_shape=(
            jax.ShapeDtypeStruct((samples, feats), jnp.int32),
            jax.ShapeDtypeStruct((samples, feats), jnp.int32),
            jax.ShapeDtypeStruct((samples, 128), jnp.int32),
        ),
        name="place_lookups",
    )(row_ids, row_home.reshape(-1, 128))


COPY_ROWS = 56
SCRATCH = 11


def sum_list(values):
    total = values[0]
    for value in values[1:]:
        total = total + value
    return total


def grads_kernel(
    sizes,
    count_ref,
    me_ref,
    x_ref,
    g_ref,
    mix_ref,
    lift_ref,
    linear_ref,
    rank_ref,
    slot_ref,
    *rest,
):
    group, steps, owners, per_owner, scaling = sizes
    far_count = owners // 4
    keep_refs, send_refs = rest[:far_count], rest[far_count : 2 * far_count]
    rows_ref = rest[2 * far_count]
    dense_refs, scratch = rest[2 * far_count + 1 : -SCRATCH], rest[-SCRATCH:]
    step = pl.program_id(0)

    @pl.when(step < steps)
    def _():
        gather_rows(
            sizes,
            count_ref,
            me_ref,
            x_ref,
            g_ref,
            mix_ref,
            lift_ref,
            linear_ref,
            rank_ref,
            slot_ref,
            rows_ref,
            dense_refs,
            *scratch,
        )

    @pl.when(step >= steps)
    def _():
        place = owners - 1 - (step - steps)
        row_a, row_b = scratch[-4], scratch[-3]
        owner = place ^ me_ref[1]
        first_rows = row_a[owner, pl.ds(0, per_owner), :]
        second_rows = row_b[owner, pl.ds(0, per_owner), :]
        at = x_ref.shape[1] - 128
        build_rows(at, me_ref, first_rows, second_rows, place, far_count, keep_refs, send_refs)


def join_rows(count_ref, filled, sorted_a, sorted_b, row_a, row_b, step, group, owners):
    begun = (step >= 0).astype(jnp.int32)
    now = (step + 2) % 2
    first = jnp.maximum(step, 0) * group
    every = range(group)
    numbers = [[count_ref[first + k, owner] * begun for owner in range(owners)] for k in every]
    starts = [filled[owner] for owner in range(owners)]
    ends = list(starts)
    for k in every:
        begin = 0
        for owner in range(owners):
            source, target = pl.ds(begin, COPY_ROWS), pl.ds(ends[owner], COPY_ROWS)
            row_a[owner, target, :] = sorted_a[now, k, source, :]
            row_b[owner, target, :] = sorted_b[now, k, source, :]
            ends[owner] = ends[owner] + numbers[k][owner]
            begin = begin + numbers[k][owner]
    most = count_ref[first, owners] * begun
    for k in range(1, group):
        most = jnp.maximum(most, count_ref[first + k, owners] * begun)

    @pl.when(most > COPY_ROWS)
    def _():
        again = list(starts)
        for k in every:
            begin = 0
            for owner in range(owners):

                def copy(turn, carry, begin=begin, at=again[owner], owner=owner, k=k):
                    off = turn * COPY_ROWS
                    source, target = pl.ds(begin + off, COPY_ROWS), pl.ds(at + off, COPY_ROWS)
                    row_a[owner, target, :] = sorted_a[now, k, source, :]
                    row_b[owner, target, :] = sorted_b[now, k, source, :]
                    return carry

                turns = (numbers[k][owner] + COPY_ROWS - 1) // COPY_ROWS
                lax.fori_loop(0, turns, copy, 0)
                again[owner] = again[owner] + numbers[k][owner]
                begin = begin + numbers[k][owner]

    for owner in range(owners):
        filled[owner] = ends[owner]


def gather_rows(
    sizes,
    count_ref,
    me_ref,
    x_ref,
    g_ref,
    mix_ref,
    lift_ref,
    linear_ref,
    rank_ref,
    slot_ref,
    rows_ref,
    dense_refs,
    mix_down,
    lift_down,
    mix_sum,
    lift_sum,
    linear_sum,
    sorted_a,
    sorted_b,
    row_a,
    row_b,
    dense_ref,
    filled,
):
    group, steps, owners, per_owner, scaling = sizes
    width, feats = x_ref.shape[1:]
    rank = mix_ref.shape[1]
    step = pl.program_id(0)

    @pl.when(step == 0)
    def _():
        mix_down[...] = mix_ref[...].astype(jnp.float32).T.astype(jnp.bfloat16)
        lift_down[...] = lift_ref[...].astype(jnp.float32).T.astype(jnp.bfloat16)
        mix_sum[...] = jnp.zeros_like(mix_sum)
        lift_sum[...] = jnp.zeros_like(lift_sum)
        linear_sum[...] = jnp.zeros_like(linear_sum)
        for owner in range(owners):
            filled[owner] = 0

    now = step % 2
    join_rows(count_ref, filled, sorted_a, sorted_b, row_a, row_b, step - 1, group, owners)
    row_at = lax.broadcasted_iota(jnp.int32, (feats, feats), 0)
    extra_at = lax.broadcasted_iota(jnp.int32, (feats - width, feats), 0)
    every = range(group)
    d_prods = [matmul(lift_down[...], g_ref[k]).astype(jnp.bfloat16) for k in every]
    boths = [
        matmul_nt(x_ref[k], jnp.concatenate([mix_down[...], d_prods[k]], axis=0)) for k in every
    ]
    comps = [both[:, :rank].astype(jnp.bfloat16) for both in boths]
    d_comps = [(both[:, rank:] * scaling).astype(jnp.bfloat16) for both in boths]
    x_flat = x_ref[...].reshape(group * width, feats).T
    x_flats = [x_flat[:, k * width : (k + 1) * width] for k in every]
    pairs = [
        matmul(x_flats[k], jnp.concatenate([comps[k], d_comps[k]], axis=1)) for k in every
    ]
    prods = [(pair[:, :rank] * scaling).astype(jnp.bfloat16) for pair in pairs]
    mix_sum[...] += sum_list([pair[:, rank:] for pair in pairs])
    g_all = g_ref[...].reshape(group * width, feats)
    d_all = g_all.astype(jnp.float32) + matmul(g_all, linear_ref[...])
    d_all = d_all + matmul(jnp.concatenate(d_comps, axis=0), mix_down[...])
    d_ins = [
        d_all[k * width : (k + 1) * width] + scaling * matmul(comps[k], d_prods[k]) for k in every
    ]
    moves, rows_downs = [], []
    for k in every:
        slot = slot_ref[pl.ds(step * group + k, 1), :]
        extra = jnp.where(extra_at == 0, slot >> 4, jnp.where(extra_at == 1, slot & 15, 0))
        rows_downs.append(
            jnp.concatenate(
                [d_ins[k].astype(jnp.bfloat16), extra.astype(jnp.float32).astype(jnp.bfloat16)],
                axis=0,
            )
        )
        moves.append(one_hot(row_at == rank_ref[pl.ds(step * group + k, 1), :]))
    for k in every:
        ordered = matmul_nt(moves[k], rows_downs[k])
        sorted_a[now, k, :feats] = ordered[:, :128]
        sorted_b[now, k, :feats] = ordered[:, 128:]
    linear_sum[...] += matmul(x_flat, g_all)
    lift_sum[...] += sum_list([matmul(g_ref[k], prods[k]) for k in every])

    @pl.when(step == steps - 1)
    def _():
        join_rows(count_ref, filled, sorted_a, sorted_b, row_a, row_b, step, group, owners)
        dense_ref[:feats] = mix_sum[...]
        linear = linear_sum[...].T
        for at in range(feats // 128):
            dense_ref[feats * (1 + at) : feats * (2 + at)] = linear[:, 128 * at : 128 * (at + 1)]
        dense_ref[feats * (1 + feats // 128) :] = lift_sum[...]
        piece = dense_refs[0].shape[0]
        for index, ref in enumerate(dense_refs):
            first = pl.multiple_of((index ^ me_ref[0]) * piece, piece)
            ref[...] = dense_ref[pl.ds(first, piece), :]
        for place in range(rows_ref.shape[0]):
            owner = place ^ me_ref[1]
            rows_ref[place, :, :128] = row_a[owner, pl.ds(0, per_owner), :].astype(jnp.bfloat16)
            rows_ref[place, :, 128:] = row_b[owner, pl.ds(0, per_owner), :].astype(jnp.bfloat16)


def build_rows(at, me_ref, first_rows, second_rows, place, first, keep_refs, send_refs):
    outers, piece = 2 * keep_refs[0].shape[1], keep_refs[0].shape[3]
    per_owner = first_rows.shape[0]
    rows_down = jnp.concatenate([first_rows.T, second_rows.T[:at]], axis=0).astype(jnp.bfloat16)
    slots = second_rows[:, at : at + 1] * 16.0 + second_rows[:, at + 1 : at + 2]
    slots = slots.astype(jnp.int32)
    lanes = lax.broadcasted_iota(jnp.int32, (per_owner, piece), 1)
    totals = []
    for outer in range(outers):
        base = (outer ^ me_ref[0]) * piece
        totals.append(matmul(rows_down, one_hot(lanes == slots - base)).astype(jnp.bfloat16))
    for index in range(len(keep_refs)):

        @pl.when(place // 2 == first + index)
        def _(index=index):
            for outer in range(outers):
                ref = (send_refs if outer % 2 else keep_refs)[index]
                ref[0, outer // 2] = totals[outer]


def part_specs(start, first, count, part):
    def spec(index):
        begin = start + 2 * (count - 1 - index)
        return pl.BlockSpec(
            (1,) + part[1:], lambda i, *_: (jnp.clip(begin + 1 - i, 0, 1), 0, 0, 0)
        )

    return [spec(index) for index in range(count)] * 2


def local_grads(counts, me, x_down, g_down, mix, lift_down, linear, ranks, slots, owners, part):
    samples, width, feats = x_down.shape
    rank = mix.shape[1]
    group = 8
    steps = samples // group
    per_owner = samples * feats // owners
    far_count = owners // 4
    sizes = (group, steps, owners, per_owner, 1.0 / math.sqrt(width))

    def whole(shape):
        return pl.BlockSpec(shape, lambda i, *_: (0,) * len(shape))

    sample_spec = pl.BlockSpec(
        (group, width, feats), lambda i, *_: (jnp.minimum(i, steps - 1), 0, 0)
    )
    dense_rows = feats * (1 + feats // 128) + width
    outers = 2 * part[1]
    dense_piece = (dense_rows // outers, 128)
    room = per_owner + 64
    rows_shape = (owners // 2, per_owner, 256)
    scratch = [
        pltpu.VMEM((rank, feats), jnp.bfloat16),
        pltpu.VMEM((rank, width), jnp.bfloat16),
        pltpu.VMEM((feats, rank), jnp.float32),
        pltpu.VMEM((width, rank), jnp.float32),
        pltpu.VMEM((feats, feats), jnp.float32),
        pltpu.VMEM((2, group, feats + 64, 128), jnp.float32),
        pltpu.VMEM((2, group, feats + 64, 128), jnp.float32),
        pltpu.VMEM((owners, room, 128), jnp.float32),
        pltpu.VMEM((owners, room, 128), jnp.float32),
        pltpu.VMEM((dense_rows, 128), jnp.float32),
        pltpu.SMEM((owners,), jnp.int32),
    ]
    outs = pl.pallas_call(
        functools.partial(grads_kernel, sizes),
        out_shape=[jax.ShapeDtypeStruct(part, jnp.bfloat16)] * (2 * far_count)
        + [
            jax.ShapeDtypeStruct(rows_shape, jnp.bfloat16),
        ]
        + [jax.ShapeDtypeStruct(dense_piece, jnp.float32)] * outers,
        grid_spec=pltpu.PrefetchScalarGridSpec(
            num_scalar_prefetch=2,
            grid=(steps + owners // 2,),
            in_specs=[
                sample_spec,
                sample_spec,
                whole((feats, rank)),
                whole((width, rank)),
                whole((feats, feats)),
                whole((samples, feats)),
                whole((samples, feats)),
            ],
            out_specs=part_specs(steps, owners // 2 - far_count, far_count, part)
            + [whole(rows_shape)]
            + [whole(dense_piece)] * outers,
            scratch_shapes=scratch,
        ),
        compiler_params=pltpu.CompilerParams(vmem_limit_bytes=60 * 2**20),
        cost_estimate=pl.CostEstimate(
            flops=2 * samples * feats * feats * 3072, bytes_accessed=12 * 2**20, transcendentals=0
        ),
        name="local_grads",
    )(counts, me, x_down, g_down, mix, lift_down, linear, ranks, slots)
    keep, send = outs[:far_count], outs[far_count : 2 * far_count]
    return keep, send, outs[2 * far_count], outs[2 * far_count + 1 :]


def build_kernel(at, me_ref, rows_ref, keep_ref, send_ref):
    rows = rows_ref[0].astype(jnp.float32)
    place = 1 - pl.program_id(0)
    build_rows(at, me_ref, rows[:, :128], rows[:, 128:], place, 0, (keep_ref,), (send_ref,))


def build_part(me, rows, far, part, width):
    per_owner, lanes = rows.shape[1:]
    return pl.pallas_call(
        functools.partial(build_kernel, width - 128),
        out_shape=[jax.ShapeDtypeStruct(part, jnp.bfloat16)] * 2,
        grid_spec=pltpu.PrefetchScalarGridSpec(
            num_scalar_prefetch=1,
            grid=(2,),
            in_specs=[pl.BlockSpec((1, per_owner, lanes), lambda i, me: (2 * far + 1 - i, 0, 0))],
            out_specs=part_specs(0, 0, 1, part),
        ),
        compiler_params=pltpu.CompilerParams(vmem_limit_bytes=60 * 2**20),
        cost_estimate=pl.CostEstimate(
            flops=4 * part[3] * part[1] * part[0] * 2 * per_owner * lanes,
            bytes_accessed=3 * 2**20,
            transcendentals=0,
        ),
        name="build_part",
    )(me, rows)


def adagrad_kernel(me_ref, *refs):
    pieces, (table_ref, accum_ref) = refs[:2], refs[2:4]
    new_table_ref, new_accum_ref = refs[-2:]
    width = table_ref.shape[0]
    for index, piece in enumerate(pieces):

        @pl.when(pl.program_id(0) == index)
        def _(piece=piece):
            grad = piece[...].astype(jnp.float32)
            mean = jnp.sum(grad * grad, axis=0, keepdims=True) * (1.0 / width)
            updated = accum_ref[...] + mean
            new_accum_ref[...] = updated
            new_table_ref[...] = table_ref[...] - grad * (LEARN_RATE / jnp.sqrt(updated))


def update_table(me, pieces, table_down, accum, first, done=()):
    width, table_rows = table_down.shape
    piece = pieces[0].shape[1]

    def moved(rows):
        return pl.BlockSpec((rows, piece), lambda i, me: (0, (first + i) ^ me[0]))

    return pl.pallas_call(
        adagrad_kernel,
        out_shape=(
            jax.ShapeDtypeStruct((width, table_rows), jnp.float32),
            jax.ShapeDtypeStruct((1, table_rows), jnp.float32),
        ),
        grid_spec=pltpu.PrefetchScalarGridSpec(
            num_scalar_prefetch=1,
            grid=(2,),
            in_specs=[pl.BlockSpec((width, piece), lambda i, me: (0, 0))] * 2
            + [moved(width), moved(1)]
            + [pl.BlockSpec(memory_space=pl.ANY)] * len(done),
            out_specs=[moved(width), moved(1)],
        ),
        input_output_aliases={5 + i: i for i in range(len(done))},
        compiler_params=pltpu.CompilerParams(vmem_limit_bytes=60 * 2**20),
        name="update_table",
    )(me, *pieces, table_down, accum, *done)


def swap(values, axis, bit):
    size = lax.axis_size(axis)
    return lax.ppermute(values, axis, [(i, i ^ bit) for i in range(size)])


def add_half(first, second):
    return (first.astype(jnp.float32) + second.astype(jnp.float32)).astype(jnp.bfloat16)


def tree_sum(values):
    while len(values) > 1:
        values = [values[i] + values[i + 1] for i in range(0, len(values), 2)]
    return values[0]


def after(value, *ready):
    return lax.optimization_barrier((value,) + ready)[0]


def halves(dense, side):
    cut = dense.reshape(2, dense.shape[0] // 2, dense.shape[1])
    mine = lax.dynamic_index_in_dim(cut, side, 0, keepdims=False)
    return mine, lax.dynamic_index_in_dim(cut, 1 - side, 0, keepdims=False)


def stacked(dense, other, side):
    return jnp.where(side == 0, jnp.stack([dense, other]), jnp.stack([other, dense]))


def sum_all(me, keep, send, rows, dense, part, width):
    owners = lax.axis_size("inner")
    outer, inner = lax.axis_index("outer"), lax.axis_index("inner")
    far_count = owners // 2
    first = far_count - len(keep)
    keep = dict(enumerate(keep, first))
    came, parts, kept, sent, rest, second, terms, last = ({} for _ in range(8))
    far_ones, near_ones = list(reversed(range(first, far_count))), list(reversed(range(first)))

    def first_stage(far):
        held = keep[far]
        if far % 2:
            parts[far] = add_half(held[1], came[far][1])
            kept[far] = add_half(held[0], came[far][0])
        else:
            parts[far] = add_half(held[:, 1], came[far][:, 1])
            kept[far] = add_half(held[:, 0], came[far][:, 0])

    def second_stage(far):
        parts[far] = add_half(kept[far][1], sent[far][1])
        rest[far] = add_half(kept[far][0], sent[far][0])
        second[far] = swap(parts[far], *(("outer", 2) if far % 2 else ("inner", 1)))

    def send_first(far, ready):
        sent[far] = swap(ready, *(("inner", 1) if far % 2 else ("outer", 2)))

    sides = (outer & 1, outer >> 1, inner & 1)
    for far in far_ones:
        came[far] = swap(send[far - first], "outer", 1)
    others = tuple(swap(dense[bits], "outer", bits) for bits in range(1, len(dense)))
    for far in near_ones:
        keep[far], low_send = build_part(me, rows, far, part, width)
        came[far] = swap(low_send, "outer", 1)
        if far == near_ones[0]:
            dense = sum_list((dense[0],) + after(others, low_send))
            mine, other = halves(dense, sides[2])
            other = swap(other, "inner", 1)
            for index in far_ones:
                first_stage(index)
                send_first(index, parts[index])
            rows = after(rows, *(parts[index] for index in far_ones))
    dense = mine + after(other, low_send)
    other = swap(dense, "inner", 2)
    for far in near_ones:
        first_stage(far)
    for far in far_ones:
        second_stage(far)
    begun = [parts[far] for far in far_ones]
    near_parts = [parts[far] for far in near_ones]
    for far in near_ones:
        send_first(far, after(parts[far], *begun))
    dense = dense + after(other, *begun)
    others = tuple(swap(dense, "inner", bits) for bits in range(4, owners, 4))
    for far in far_ones:
        second[far] = after(second[far], dense, *near_parts)
        last[far] = add_half(rest[far], second[far])
        terms[far] = swap(last[far], "inner", 2 * far)
    far_last = [last[far] for far in far_ones]
    dense = tree_sum([dense] + list(after(others, *far_last)))
    other = swap(dense, "inner", 1)
    arrived = after(tuple(sent[far] for far in near_ones), dense, *far_last)
    for far, sent[far] in zip(near_ones, arrived):
        second_stage(far)
    dense = stacked(dense, after(other, *(parts[far] for far in near_ones)), sides[2])
    other = swap(dense, "outer", 2)
    for far in near_ones:
        second[far] = after(second[far], dense)
        if far:
            last[far] = add_half(rest[far], second[far])
            terms[far] = swap(last[far], "inner", 2 * far)
    dense = stacked(dense, after(other, last[1]), sides[1])
    mine, came_last = after((rest[0], second[0]), dense, last[1])
    terms = after(tuple(terms[far] for far in range(1, far_count)), dense, last[1])
    terms = [mine.astype(jnp.float32) + came_last.astype(jnp.float32)] + [
        term.astype(jnp.float32) for term in terms
    ]
    total = tree_sum(terms).astype(jnp.bfloat16)
    across = swap(total, "outer", 2)
    dense = stacked(dense, swap(dense, "outer", 1), sides[0])
    lanes = dense.shape[-1]
    return total, across, jnp.transpose(dense, (1, 0, 2, 3, 4)).reshape(-1, lanes)


def dense_table(
    layer_input,
    out_grad,
    mix_weight,
    lift_weight,
    linear_weight,
    row_ids,
    row_home,
    table,
    row_accum,
):
    owners, outers = lax.axis_size("inner"), lax.axis_size("outer")
    sample_count = layer_input.shape[0]
    table_rows = table.shape[0]
    me = jnp.stack([lax.axis_index("outer"), lax.axis_index("inner")]).astype(jnp.int32)
    ranks, slots, counts = place_lookups(row_ids, row_home, owners, table_rows)
    width = layer_input.shape[2]
    part = (2, outers // 2, width, table_rows // outers)
    keep, send, rows, dense = local_grads(
        counts,
        me,
        jnp.swapaxes(layer_input, 1, 2),
        jnp.swapaxes(out_grad, 1, 2),
        mix_weight,
        lift_weight.T,
        linear_weight,
        ranks,
        slots,
        owners,
        part,
    )
    total, across, dense = sum_all(me, keep, send, rows, dense, part, width)
    dense = dense * (1.0 / (sample_count * outers * owners))
    feats = layer_input.shape[1]
    linear = [dense[feats * (1 + i) : feats * (2 + i)] for i in range(feats // 128)]
    weights = (
        dense[:feats],
        dense[feats * (1 + feats // 128) :].T,
        jnp.concatenate(linear, axis=1),
    )
    table_down, accum = table.T, row_accum.reshape(1, -1)
    beside = swap(total, "outer", 1)
    done = update_table(me, (total, beside), table_down, accum, 0)
    across = after(across, done[1], *weights)
    pieces = (across, swap(across, "outer", 1))
    new_table, new_accum = update_table(me, pieces, table_down, accum, 2, done)
    return (new_table.T, new_accum.reshape(-1)) + weights


def power_of_two(number):
    return number & (number - 1) == 0


def on_device(*arrays):
    owners, outers = lax.axis_size("inner"), lax.axis_size("outer")
    layer_input, mix_weight, row_home, table = (arrays[i] for i in (0, 2, 6, 7))
    samples, feats, width = layer_input.shape
    dense_fits = (
        outers == 4
        and owners % 4 == 0
        and power_of_two(owners)
        and row_home.shape[0] <= 2 * samples * feats
        and row_home.shape[0] <= 2**15
        and power_of_two(table.shape[0])
        and 512 <= table.shape[0] <= 4096
        and samples % 16 == 0
        and (feats * (1 + feats // 128) + width) % 64 == 0
        and feats == 256
        and mix_weight.shape[1] == 128
        and 2 * (width - 128) == 128
    )
    return dense_table(*arrays) if dense_fits else routed_rows(*arrays)


def solution(mesh):
    placed = (
        P(("outer", "inner"), None, None),
        P(("outer", "inner"), None, None),
        P(),
        P(),
        P(),
        P(("outer", "inner"), None),
        P(),
        P("inner", None),
        P("inner"),
    )
    return jax.shard_map(
        on_device,
        mesh=mesh,
        in_specs=placed,
        out_specs=(P("inner", None), P("inner"), P(), P(), P()),
        check_vma=False,
    )
```

```python
import functools
import math

import jax
import jax.numpy as jnp
from jax import lax
from jax.experimental import pallas as pl
from jax.experimental.pallas import tpu as pltpu
from jax.sharding import PartitionSpec as P

LEARN_RATE = 0.5


def interaction_grads(inputs, cotangent, mix_weight, lift_weight, linear_weight, scaling):
    compressed = jnp.einsum(
        "bfd,fk->bdk", inputs, mix_weight, preferred_element_type=jnp.float32
    ).astype(jnp.bfloat16)
    products = (
        jnp.einsum("bfd,bdk->bfk", inputs, compressed, preferred_element_type=jnp.float32) * scaling
    ).astype(jnp.bfloat16)
    d_products = jnp.einsum(
        "bfd,kd->bfk", cotangent, lift_weight, preferred_element_type=jnp.float32
    ).astype(jnp.bfloat16)
    d_compressed = (
        jnp.einsum("bfd,bfk->bdk", inputs, d_products, preferred_element_type=jnp.float32) * scaling
    ).astype(jnp.bfloat16)
    d_inputs = cotangent.astype(jnp.float32)
    d_inputs = d_inputs + jnp.einsum(
        "fg,bfd->bgd", linear_weight, cotangent, preferred_element_type=jnp.float32
    )
    d_inputs = d_inputs + scaling * jnp.einsum(
        "bfk,bdk->bfd", d_products, compressed, preferred_element_type=jnp.float32
    )
    d_inputs = d_inputs + jnp.einsum(
        "fk,bdk->bfd", mix_weight, d_compressed, preferred_element_type=jnp.float32
    )
    g_mix = jnp.einsum("bfd,bdk->fk", inputs, d_compressed, preferred_element_type=jnp.float32)
    g_lift = jnp.einsum("bfk,bfd->kd", products, cotangent, preferred_element_type=jnp.float32)
    g_linear = jnp.einsum("bfd,bgd->fg", cotangent, inputs, preferred_element_type=jnp.float32)
    rows_out = d_inputs.astype(jnp.bfloat16).reshape(-1, d_inputs.shape[2])
    return (rows_out, (g_mix, g_lift, g_linear))


def adagrad(weights, history, gradient):
    updated = history + jnp.mean(gradient * gradient, axis=1)
    return (weights - LEARN_RATE * gradient / jnp.sqrt(updated)[:, None], updated)


def owner_ranks(owner_of, owners):
    lookups = owner_of.shape[0]
    width = math.gcd(lookups, 128)
    groups = lookups // width
    hot = (owner_of[:, None] == jnp.arange(owners, dtype=jnp.int32)[None, :]).astype(jnp.bfloat16)
    hot = hot.reshape(groups, width, owners)
    lower = (jnp.arange(width)[:, None] > jnp.arange(width)[None, :]).astype(jnp.bfloat16)
    within = jnp.einsum("ij,gjo->gio", lower, hot, preferred_element_type=jnp.float32)
    totals = jnp.sum(hot.astype(jnp.float32), axis=1)
    before = jnp.cumsum(totals, axis=0) - totals
    counted = jnp.sum(hot.astype(jnp.float32) * (within + before[:, None, :]), axis=2)
    return counted.reshape(-1).astype(jnp.int32)


def add_rows(collected, slots, values):
    count = values.shape[0]
    table_rows = collected.shape[0]
    width = math.gcd(count, 2048)
    columns = jnp.arange(table_rows, dtype=jnp.int32)
    for block_index in range(count // width):
        start = block_index * width
        hot = (slots[start : start + width, None] == columns[None, :]).astype(jnp.bfloat16)
        collected = collected + jnp.einsum(
            "lr,ld->rd", hot, values[start : start + width], preferred_element_type=jnp.float32
        )
    return collected


def routed_rows(
    layer_input,
    out_grad,
    mix_weight,
    lift_weight,
    linear_weight,
    row_ids,
    row_home,
    table,
    row_accum,
):
    owners = lax.axis_size("inner")
    sample_count, feature_count, embed_width = layer_input.shape
    table_rows = table.shape[0]
    half_samples = sample_count // 2
    lookups = sample_count * feature_count
    per_owner = lookups // (2 * owners)
    scaling = 1.0 / math.sqrt(embed_width)
    placed = jnp.take(row_home, row_ids.reshape(-1), axis=0)
    owner_of = placed // table_rows
    target = owner_of * (2 * per_owner) + owner_ranks(owner_of, owners)
    ordering = jnp.zeros((lookups,), jnp.int32).at[target].set(jnp.arange(lookups, dtype=jnp.int32))
    ordering = ordering.reshape(owners, 2, per_owner)
    local_rows = (
        jnp.zeros((lookups,), jnp.int32)
        .at[target]
        .set(placed % table_rows)
        .reshape(owners, 2 * per_owner)
    )
    arrived_rows = lax.all_to_all(
        local_rows, "inner", split_axis=0, concat_axis=0, tiled=True
    ).reshape(owners, 2, per_owner)
    collected = jnp.zeros((table_rows, embed_width), jnp.float32)
    totals = None
    for half_index in range(2):
        first_sample = half_index * half_samples
        rows_out, partial_value = interaction_grads(
            layer_input[first_sample : first_sample + half_samples],
            out_grad[first_sample : first_sample + half_samples],
            mix_weight,
            lift_weight,
            linear_weight,
            scaling,
        )
        picked = ordering[:, half_index, :] - half_index * half_samples * feature_count
        outgoing = jnp.take(rows_out, picked.reshape(-1), axis=0).reshape(
            owners, per_owner, embed_width
        )
        incoming = lax.all_to_all(outgoing, "inner", split_axis=0, concat_axis=0, tiled=True)
        collected = add_rows(
            collected, arrived_rows[:, half_index, :].reshape(-1), incoming.reshape(-1, embed_width)
        )
        if totals is None:
            totals = partial_value
        else:
            totals = tuple((earlier + later for earlier, later in zip(totals, partial_value)))
    batch_total = sample_count * lax.axis_size("outer") * owners
    summed = lax.psum((totals[0], totals[1], totals[2]), ("outer", "inner"))
    mix_grad = summed[0] / batch_total
    lift_grad = summed[1] / batch_total
    linear_grad = summed[2] / batch_total
    complete = lax.psum(collected, "outer")
    new_table, new_accum = adagrad(table, row_accum, complete)
    return (new_table, new_accum, mix_grad, lift_grad, linear_grad)


def matmul(left, right):
    return jnp.dot(left, right, preferred_element_type=jnp.float32)


def matmul_nt(left, right):
    return lax.dot_general(left, right, (((1,), (1,)), ((), ())), preferred_element_type=jnp.float32)


def one_hot(matches):
    return jnp.where(matches, 1.0, 0.0).astype(jnp.bfloat16)


def place_kernel(shift, owners, ids_ref, home_ref, rank_ref, slot_ref, count_ref):
    samples, feats = ids_ref.shape
    high, low = home_ref.shape
    half = low // 2
    home = home_ref[...]
    pieces = []
    for part in (home & 255, home >> 8):
        down = part.astype(jnp.float32).T
        pieces.append(jnp.concatenate([down[:half], down[half:]], axis=1))
    pieces = jnp.concatenate(pieces, axis=0).astype(jnp.bfloat16)
    high_at = lax.broadcasted_iota(jnp.int32, (2 * high, feats), 0)
    low_at = lax.broadcasted_iota(jnp.int32, (half, feats), 0)
    lane = lax.broadcasted_iota(jnp.int32, (1, feats), 1)
    count_lane = lax.broadcasted_iota(jnp.int32, (8, 128), 1)

    @pl.loop(0, samples // 8)
    def _(group):
        first = pl.multiple_of(group * 8, 8)
        ids = ids_ref[pl.ds(first, 8), :]
        every = range(8)
        ones = [ids[row : row + 1] for row in every]
        hots = [one_hot(high_at == ((one >> 6) & 1) * high + (one >> 7)) for one in ones]
        founds = [matmul(pieces, hot) for hot in hots]
        places = []
        for row in every:
            value = founds[row][:half] + 256.0 * founds[row][half:]
            value = jnp.where(low_at == (ones[row] & (half - 1)), value, 0.0)
            places.append(jnp.sum(value, axis=0, keepdims=True))
        place = jnp.concatenate(places, axis=0).astype(jnp.int32)
        owner_all = place >> shift
        slot_ref[pl.ds(first, 8), :] = place & ((1 << shift) - 1)
        keys = (owner_all * feats + lane).astype(jnp.float32)
        downs = [jnp.broadcast_to(keys[row : row + 1], (128, feats)).T for row in every]
        ranks = []
        for row in every:
            parts = []
            for at in range(0, feats, 128):
                less = downs[row] < keys[row : row + 1, at : at + 128]
                parts.append(jnp.sum(jnp.where(less, 1.0, 0.0), axis=0, keepdims=True))
            ranks.append(jnp.concatenate(parts, axis=1))
        rank_ref[pl.ds(first, 8), :] = jnp.concatenate(ranks, axis=0).astype(jnp.int32)
        counts = jnp.zeros((8, 128), jnp.float32)
        for owner_at in range(owners):
            number = jnp.sum(jnp.where(owner_all == owner_at, 1.0, 0.0), axis=1, keepdims=True)
            counts = jnp.where(count_lane == owner_at, number, counts)
        most = jnp.max(counts, axis=1, keepdims=True)
        counts = jnp.where(count_lane == owners, most, counts)
        count_ref[pl.ds(first, 8), :] = counts.astype(jnp.int32)


COPY_ROWS = 56
SCRATCH = 16


def sum_list(values):
    total = values[0]
    for value in values[1:]:
        total = total + value
    return total


def positions():
    return lax.axis_index("outer"), lax.axis_index("inner")


def grads_kernel(
    sizes,
    x_ref,
    g_ref,
    mix_ref,
    lift_ref,
    linear_ref,
    ids_ref,
    home_ref,
    *rest,
):
    group, steps, owners, per_owner, scaling, shift = sizes
    far_count = owners // 4
    keep_refs, send_refs = rest[:far_count], rest[far_count : 2 * far_count]
    rows_ref = rest[2 * far_count]
    dense_refs, scratch = rest[2 * far_count + 1 : -SCRATCH], rest[-SCRATCH:]
    rank_ref, slot_ref, found_ref, count_ref, copied = scratch[:5]
    step = pl.program_id(0)
    outer, inner = positions()

    @pl.when(step == 0)
    def _():
        place_kernel(shift, owners, ids_ref, home_ref, rank_ref, slot_ref, found_ref)
        copy = pltpu.make_async_copy(found_ref, count_ref, copied)
        copy.start()
        copy.wait()

    @pl.when((step > 0) & (step <= steps))
    def _():
        gather_rows(
            step - 1,
            outer,
            inner,
            sizes,
            count_ref,
            x_ref,
            g_ref,
            mix_ref,
            lift_ref,
            linear_ref,
            rank_ref,
            slot_ref,
            rows_ref,
            dense_refs,
            *scratch[5:],
        )

    @pl.when(step > steps)
    def _():
        place = owners - 1 - (step - steps - 1)
        row_a, row_b = scratch[-4], scratch[-3]
        owner = place ^ inner
        first_rows = row_a[owner, pl.ds(0, per_owner), :]
        second_rows = row_b[owner, pl.ds(0, per_owner), :]
        at = x_ref.shape[1] - 128
        build_rows(at, outer, first_rows, second_rows, place, far_count, keep_refs, send_refs)


def join_rows(count_ref, filled, sorted_a, sorted_b, row_a, row_b, step, group, owners):
    begun = (step >= 0).astype(jnp.int32)
    now = (step + 2) % 2
    first = jnp.maximum(step, 0) * group
    every = range(group)
    numbers = [[count_ref[first + k, owner] * begun for owner in range(owners)] for k in every]
    starts = [filled[owner] for owner in range(owners)]
    ends = list(starts)
    for k in every:
        begin = 0
        for owner in range(owners):
            source, target = pl.ds(begin, COPY_ROWS), pl.ds(ends[owner], COPY_ROWS)
            row_a[owner, target, :] = sorted_a[now, k, source, :]
            row_b[owner, target, :] = sorted_b[now, k, source, :]
            ends[owner] = ends[owner] + numbers[k][owner]
            begin = begin + numbers[k][owner]
    most = count_ref[first, owners] * begun
    for k in range(1, group):
        most = jnp.maximum(most, count_ref[first + k, owners] * begun)

    @pl.when(most > COPY_ROWS)
    def _():
        again = list(starts)
        for k in every:
            begin = 0
            for owner in range(owners):

                def copy(turn, carry, begin=begin, at=again[owner], owner=owner, k=k):
                    off = turn * COPY_ROWS
                    source, target = pl.ds(begin + off, COPY_ROWS), pl.ds(at + off, COPY_ROWS)
                    row_a[owner, target, :] = sorted_a[now, k, source, :]
                    row_b[owner, target, :] = sorted_b[now, k, source, :]
                    return carry

                turns = (numbers[k][owner] + COPY_ROWS - 1) // COPY_ROWS
                lax.fori_loop(0, turns, copy, 0)
                again[owner] = again[owner] + numbers[k][owner]
                begin = begin + numbers[k][owner]

    for owner in range(owners):
        filled[owner] = ends[owner]


def gather_rows(
    step,
    outer,
    inner,
    sizes,
    count_ref,
    x_ref,
    g_ref,
    mix_ref,
    lift_ref,
    linear_ref,
    rank_ref,
    slot_ref,
    rows_ref,
    dense_refs,
    mix_down,
    lift_down,
    mix_sum,
    lift_sum,
    linear_sum,
    sorted_a,
    sorted_b,
    row_a,
    row_b,
    dense_ref,
    filled,
):
    group, steps, owners, per_owner, scaling, _ = sizes
    width, feats = x_ref.shape[1:]
    rank = mix_ref.shape[1]

    @pl.when(step == 0)
    def _():
        mix_down[...] = mix_ref[...].astype(jnp.float32).T.astype(jnp.bfloat16)
        lift_down[...] = lift_ref[...].astype(jnp.float32).T.astype(jnp.bfloat16)
        mix_sum[...] = jnp.zeros_like(mix_sum)
        lift_sum[...] = jnp.zeros_like(lift_sum)
        linear_sum[...] = jnp.zeros_like(linear_sum)
        for owner in range(owners):
            filled[owner] = 0

    now = step % 2
    join_rows(count_ref, filled, sorted_a, sorted_b, row_a, row_b, step - 1, group, owners)
    row_at = lax.broadcasted_iota(jnp.int32, (feats, feats), 0)
    extra_at = lax.broadcasted_iota(jnp.int32, (feats - width, feats), 0)
    every = range(group)
    d_prods = [matmul(lift_down[...], g_ref[k]).astype(jnp.bfloat16) for k in every]
    boths = [
        matmul_nt(x_ref[k], jnp.concatenate([mix_down[...], d_prods[k]], axis=0)) for k in every
    ]
    comps = [both[:, :rank].astype(jnp.bfloat16) for both in boths]
    d_comps = [(both[:, rank:] * scaling).astype(jnp.bfloat16) for both in boths]
    x_flat = x_ref[...].reshape(group * width, feats).T
    x_flats = [x_flat[:, k * width : (k + 1) * width] for k in every]
    pairs = [
        matmul(x_flats[k], jnp.concatenate([comps[k], d_comps[k]], axis=1)) for k in every
    ]
    prods = [(pair[:, :rank] * scaling).astype(jnp.bfloat16) for pair in pairs]
    mix_sum[...] += sum_list([pair[:, rank:] for pair in pairs])
    g_all = g_ref[...].reshape(group * width, feats)
    d_all = g_all.astype(jnp.float32) + matmul(g_all, linear_ref[...])
    d_all = d_all + matmul(jnp.concatenate(d_comps, axis=0), mix_down[...])
    d_ins = [
        d_all[k * width : (k + 1) * width] + scaling * matmul(comps[k], d_prods[k]) for k in every
    ]
    moves, rows_downs = [], []
    for k in every:
        slot = slot_ref[pl.ds(step * group + k, 1), :]
        extra = jnp.where(extra_at == 0, slot >> 4, jnp.where(extra_at == 1, slot & 15, 0))
        rows_downs.append(
            jnp.concatenate(
                [d_ins[k].astype(jnp.bfloat16), extra.astype(jnp.float32).astype(jnp.bfloat16)],
                axis=0,
            )
        )
        moves.append(one_hot(row_at == rank_ref[pl.ds(step * group + k, 1), :]))
    for k in every:
        ordered = matmul_nt(moves[k], rows_downs[k])
        sorted_a[now, k, :feats] = ordered[:, :128]
        sorted_b[now, k, :feats] = ordered[:, 128:]
    linear_sum[...] += matmul(x_flat, g_all)
    lift_sum[...] += sum_list([matmul(g_ref[k], prods[k]) for k in every])

    @pl.when(step == steps - 1)
    def _():
        join_rows(count_ref, filled, sorted_a, sorted_b, row_a, row_b, step, group, owners)
        dense_ref[:feats] = mix_sum[...]
        linear = linear_sum[...].T
        for at in range(feats // 128):
            dense_ref[feats * (1 + at) : feats * (2 + at)] = linear[:, 128 * at : 128 * (at + 1)]
        dense_ref[feats * (1 + feats // 128) :] = lift_sum[...]
        piece = dense_refs[0].shape[0]
        for index, ref in enumerate(dense_refs):
            first = pl.multiple_of((index ^ outer) * piece, piece)
            ref[...] = dense_ref[pl.ds(first, piece), :]
        for place in range(rows_ref.shape[0]):
            owner = place ^ inner
            rows_ref[place, :, :128] = row_a[owner, pl.ds(0, per_owner), :].astype(jnp.bfloat16)
            rows_ref[place, :, 128:] = row_b[owner, pl.ds(0, per_owner), :].astype(jnp.bfloat16)


def build_rows(at, my_outer, first_rows, second_rows, place, first, keep_refs, send_refs):
    outers, piece = 2 * keep_refs[0].shape[1], keep_refs[0].shape[3]
    per_owner = first_rows.shape[0]
    rows_down = jnp.concatenate([first_rows.T, second_rows.T[:at]], axis=0).astype(jnp.bfloat16)
    slots = second_rows[:, at : at + 1] * 16.0 + second_rows[:, at + 1 : at + 2]
    slots = slots.astype(jnp.int32)
    lanes = lax.broadcasted_iota(jnp.int32, (per_owner, piece), 1)
    totals = []
    for outer in range(outers):
        base = (outer ^ my_outer) * piece
        totals.append(matmul(rows_down, one_hot(lanes == slots - base)).astype(jnp.bfloat16))
    for index in range(len(keep_refs)):

        @pl.when(place // 2 == first + index)
        def _(index=index):
            for outer in range(outers):
                ref = (send_refs if outer % 2 else keep_refs)[index]
                ref[0, outer // 2] = totals[outer]


def part_specs(start, first, count, part):
    def spec(index):
        begin = start + 2 * (count - 1 - index)
        return pl.BlockSpec(
            (1,) + part[1:], lambda i, *_: (jnp.clip(begin + 1 - i, 0, 1), 0, 0, 0)
        )

    return [spec(index) for index in range(count)] * 2


def local_grads(x_down, g_down, mix, lift_down, linear, ids, home, owners, part):
    samples, width, feats = x_down.shape
    rank = mix.shape[1]
    group = 8
    steps = samples // group
    per_owner = samples * feats // owners
    far_count = owners // 4
    shift = (part[1] * 2 * part[3]).bit_length() - 1
    sizes = (group, steps, owners, per_owner, 1.0 / math.sqrt(width), shift)

    def whole(shape):
        return pl.BlockSpec(shape, lambda i, *_: (0,) * len(shape))

    sample_spec = pl.BlockSpec(
        (group, width, feats), lambda i: (jnp.clip(i - 1, 0, steps - 1), 0, 0)
    )
    dense_rows = feats * (1 + feats // 128) + width
    outers = 2 * part[1]
    dense_piece = (dense_rows // outers, 128)
    room = per_owner + 64
    rows_shape = (owners // 2, per_owner, 256)
    scratch = [
        pltpu.VMEM((samples, feats), jnp.int32),
        pltpu.VMEM((samples, feats), jnp.int32),
        pltpu.VMEM((samples, 128), jnp.int32),
        pltpu.SMEM((samples, 128), jnp.int32),
        pltpu.SemaphoreType.DMA,
        pltpu.VMEM((rank, feats), jnp.bfloat16),
        pltpu.VMEM((rank, width), jnp.bfloat16),
        pltpu.VMEM((feats, rank), jnp.float32),
        pltpu.VMEM((width, rank), jnp.float32),
        pltpu.VMEM((feats, feats), jnp.float32),
        pltpu.VMEM((2, group, feats + 64, 128), jnp.float32),
        pltpu.VMEM((2, group, feats + 64, 128), jnp.float32),
        pltpu.VMEM((owners, room, 128), jnp.float32),
        pltpu.VMEM((owners, room, 128), jnp.float32),
        pltpu.VMEM((dense_rows, 128), jnp.float32),
        pltpu.SMEM((owners,), jnp.int32),
    ]
    outs = pl.pallas_call(
        functools.partial(grads_kernel, sizes),
        out_shape=[jax.ShapeDtypeStruct(part, jnp.bfloat16)] * (2 * far_count)
        + [
            jax.ShapeDtypeStruct(rows_shape, jnp.bfloat16),
        ]
        + [jax.ShapeDtypeStruct(dense_piece, jnp.float32)] * outers,
        grid=(1 + steps + owners // 2,),
        in_specs=[
            sample_spec,
            sample_spec,
            whole((feats, rank)),
            whole((width, rank)),
            whole((feats, feats)),
            whole((samples, feats)),
            whole(home.shape),
        ],
        out_specs=part_specs(1 + steps, owners // 2 - far_count, far_count, part)
        + [whole(rows_shape)]
        + [whole(dense_piece)] * outers,
        scratch_shapes=scratch,
        compiler_params=pltpu.CompilerParams(vmem_limit_bytes=60 * 2**20),
        cost_estimate=pl.CostEstimate(
            flops=2 * samples * feats * feats * 3072, bytes_accessed=12 * 2**20, transcendentals=0
        ),
        name="local_grads",
    )(x_down, g_down, mix, lift_down, linear, ids, home)
    keep, send = outs[:far_count], outs[far_count : 2 * far_count]
    return keep, send, outs[2 * far_count], outs[2 * far_count + 1 :]


def build_kernel(at, rows_ref, *refs):
    half = len(refs) // 2
    rows = rows_ref[0].astype(jnp.float32)
    place = 2 * half - 1 - pl.program_id(0)
    keep_refs, send_refs = refs[:half], refs[half:]
    outer, _ = positions()
    build_rows(at, outer, rows[:, :128], rows[:, 128:], place, 0, keep_refs, send_refs)


def build_parts(rows, part, width):
    places, per_owner, lanes = rows.shape
    far_count = places // 2
    outs = pl.pallas_call(
        functools.partial(build_kernel, width - 128),
        out_shape=[jax.ShapeDtypeStruct(part, jnp.bfloat16)] * places,
        grid=(places,),
        in_specs=[pl.BlockSpec((1, per_owner, lanes), lambda i: (places - 1 - i, 0, 0))],
        out_specs=part_specs(0, 0, far_count, part),
        compiler_params=pltpu.CompilerParams(vmem_limit_bytes=60 * 2**20),
        cost_estimate=pl.CostEstimate(
            flops=4 * part[3] * part[1] * part[0] * places * per_owner * lanes,
            bytes_accessed=6 * 2**20,
            transcendentals=0,
        ),
        name="build_parts",
    )(rows)
    return outs[:far_count], outs[far_count:]


def adagrad_kernel(me_ref, *refs):
    pieces, (table_ref, accum_ref) = refs[:2], refs[2:4]
    new_table_ref, new_accum_ref = refs[-2:]
    width = table_ref.shape[0]
    for index, piece in enumerate(pieces):

        @pl.when(pl.program_id(0) == index)
        def _(piece=piece):
            grad = piece[...].astype(jnp.float32)
            mean = jnp.sum(grad * grad, axis=0, keepdims=True) * (1.0 / width)
            updated = accum_ref[...] + mean
            new_accum_ref[...] = updated
            new_table_ref[...] = table_ref[...] - grad * (LEARN_RATE / jnp.sqrt(updated))


def update_table(me, pieces, table_down, accum, first, done=()):
    width, table_rows = table_down.shape
    piece = pieces[0].shape[1]

    def moved(rows):
        return pl.BlockSpec((rows, piece), lambda i, me: (0, (first + i) ^ me[0]))

    return pl.pallas_call(
        adagrad_kernel,
        out_shape=(
            jax.ShapeDtypeStruct((width, table_rows), jnp.float32),
            jax.ShapeDtypeStruct((1, table_rows), jnp.float32),
        ),
        grid_spec=pltpu.PrefetchScalarGridSpec(
            num_scalar_prefetch=1,
            grid=(2,),
            in_specs=[pl.BlockSpec((width, piece), lambda i, me: (0, 0))] * 2
            + [moved(width), moved(1)]
            + [pl.BlockSpec(memory_space=pl.ANY)] * len(done),
            out_specs=[moved(width), moved(1)],
        ),
        input_output_aliases={5 + i: i for i in range(len(done))},
        compiler_params=pltpu.CompilerParams(vmem_limit_bytes=60 * 2**20),
        name="update_table",
    )(me, *pieces, table_down, accum, *done)


def swap(values, axis, bit):
    size = lax.axis_size(axis)
    return lax.ppermute(values, axis, [(i, i ^ bit) for i in range(size)])


def add_half(first, second):
    return (first.astype(jnp.float32) + second.astype(jnp.float32)).astype(jnp.bfloat16)


def tree_sum(values):
    while len(values) > 1:
        values = [values[i] + values[i + 1] for i in range(0, len(values), 2)]
    return values[0]


def after(value, *ready):
    return lax.optimization_barrier((value,) + ready)[0]


def halves(dense, side):
    cut = dense.reshape(2, dense.shape[0] // 2, dense.shape[1])
    mine = lax.dynamic_index_in_dim(cut, side, 0, keepdims=False)
    return mine, lax.dynamic_index_in_dim(cut, 1 - side, 0, keepdims=False)


def stacked(dense, other, side):
    return jnp.where(side == 0, jnp.stack([dense, other]), jnp.stack([other, dense]))


def sum_all(me, keep, send, rows, dense, part, width):
    owners = lax.axis_size("inner")
    outer, inner = lax.axis_index("outer"), lax.axis_index("inner")
    far_count = owners // 2
    first = far_count - len(keep)
    keep = dict(enumerate(keep, first))
    came, parts, kept, sent, rest, second, terms, last = ({} for _ in range(8))
    far_ones, near_ones = list(reversed(range(first, far_count))), list(reversed(range(first)))

    def first_stage(far):
        held = keep[far]
        if far % 2:
            parts[far] = add_half(held[1], came[far][1])
            kept[far] = add_half(held[0], came[far][0])
        else:
            parts[far] = add_half(held[:, 1], came[far][:, 1])
            kept[far] = add_half(held[:, 0], came[far][:, 0])

    def second_stage(far):
        parts[far] = add_half(kept[far][1], sent[far][1])
        rest[far] = add_half(kept[far][0], sent[far][0])
        second[far] = swap(parts[far], *(("outer", 2) if far % 2 else ("inner", 1)))

    def send_first(far, ready):
        sent[far] = swap(ready, *(("inner", 1) if far % 2 else ("outer", 2)))

    sides = (outer & 1, outer >> 1, inner & 1)
    for far in far_ones:
        came[far] = swap(send[far - first], "outer", 1)
    others = tuple(swap(dense[bits], "outer", bits) for bits in range(1, len(dense)))
    for far in far_ones:
        first_stage(far)
        send_first(far, parts[far])
    rows = after(rows, *(parts[far] for far in far_ones))
    low_keep, low_send = build_parts(rows, part, width)
    for far in near_ones:
        keep[far] = low_keep[far]
        came[far] = swap(low_send[far], "outer", 1)
    dense = sum_list((dense[0],) + after(others, low_send[0]))
    mine, other = halves(dense, sides[2])
    other = swap(other, "inner", 1)
    for far in far_ones:
        second_stage(far)
    begun = [parts[far] for far in far_ones]
    for far in near_ones:
        first_stage(far)
    near_parts = [parts[far] for far in near_ones]
    for far in near_ones:
        send_first(far, parts[far])
    dense = mine + after(other, *near_parts)
    other = swap(dense, "inner", 2)
    for far in far_ones:
        second[far] = after(second[far], dense, me, *near_parts)
        last[far] = add_half(rest[far], second[far])
        terms[far] = swap(last[far], "inner", 2 * far)
    far_last = [last[far] for far in far_ones]
    dense = dense + after(other, *far_last)
    others = tuple(swap(dense, "inner", bits) for bits in range(4, owners, 4))
    arrived = after(tuple(sent[far] for far in near_ones), dense, *far_last)
    for far, sent[far] in zip(near_ones, arrived):
        second_stage(far)
    dense = tree_sum([dense] + list(after(others, *(parts[far] for far in near_ones))))
    other = swap(dense, "inner", 1)
    for far in near_ones:
        second[far] = after(second[far], dense)
        if far:
            last[far] = add_half(rest[far], second[far])
            terms[far] = swap(last[far], "inner", 2 * far)
    dense = stacked(dense, after(other, last[1]), sides[2])
    other = swap(dense, "outer", 2)
    mine, came_last = after((rest[0], second[0]), dense, last[1])
    terms = after(tuple(terms[far] for far in range(1, far_count)), dense, last[1])
    terms = [mine.astype(jnp.float32) + came_last.astype(jnp.float32)] + [
        term.astype(jnp.float32) for term in terms
    ]
    total = tree_sum(terms).astype(jnp.bfloat16)
    across = swap(total, "outer", 2)
    beside = swap(total, "outer", 1)
    dense = stacked(dense, after(other, beside), sides[1])
    dense = stacked(dense, swap(dense, "outer", 1), sides[0])
    lanes = dense.shape[-1]
    return total, beside, across, jnp.transpose(dense, (1, 0, 2, 3, 4)).reshape(-1, lanes)


def dense_table(
    layer_input,
    out_grad,
    mix_weight,
    lift_weight,
    linear_weight,
    row_ids,
    row_home,
    table,
    row_accum,
):
    owners, outers = lax.axis_size("inner"), lax.axis_size("outer")
    sample_count = layer_input.shape[0]
    table_rows = table.shape[0]
    me = jnp.stack([lax.axis_index("outer"), lax.axis_index("inner")]).astype(jnp.int32)
    width = layer_input.shape[2]
    part = (2, outers // 2, width, table_rows // outers)
    keep, send, rows, dense = local_grads(
        jnp.swapaxes(layer_input, 1, 2),
        jnp.swapaxes(out_grad, 1, 2),
        mix_weight,
        lift_weight.T,
        linear_weight,
        row_ids,
        row_home.reshape(-1, 128),
        owners,
        part,
    )
    total, beside, across, dense = sum_all(me, keep, send, rows, dense, part, width)
    dense = dense * (1.0 / (sample_count * outers * owners))
    feats = layer_input.shape[1]
    linear = [dense[feats * (1 + i) : feats * (2 + i)] for i in range(feats // 128)]
    weights = (
        dense[:feats],
        dense[feats * (1 + feats // 128) :].T,
        jnp.concatenate(linear, axis=1),
    )
    table_down, accum = table.T, row_accum.reshape(1, -1)
    done = update_table(me, (total, beside), table_down, accum, 0)
    across = after(across, done[1], *weights)
    pieces = (across, swap(across, "outer", 1))
    new_table, new_accum = update_table(me, pieces, table_down, accum, 2, done)
    return (new_table.T, new_accum.reshape(-1)) + weights


def power_of_two(number):
    return number & (number - 1) == 0


def on_device(*arrays):
    owners, outers = lax.axis_size("inner"), lax.axis_size("outer")
    layer_input, mix_weight, row_home, table = (arrays[i] for i in (0, 2, 6, 7))
    samples, feats, width = layer_input.shape
    dense_fits = (
        outers == 4
        and owners % 4 == 0
        and power_of_two(owners)
        and row_home.shape[0] <= 2 * samples * feats
        and row_home.shape[0] <= 2**15
        and power_of_two(table.shape[0])
        and 512 <= table.shape[0] <= 4096
        and samples % 16 == 0
        and (feats * (1 + feats // 128) + width) % 64 == 0
        and feats == 256
        and mix_weight.shape[1] == 128
        and 2 * (width - 128) == 128
    )
    return dense_table(*arrays) if dense_fits else routed_rows(*arrays)


def solution(mesh):
    placed = (
        P(("outer", "inner"), None, None),
        P(("outer", "inner"), None, None),
        P(),
        P(),
        P(),
        P(("outer", "inner"), None),
        P(),
        P("inner", None),
        P("inner"),
    )
    return jax.shard_map(
        on_device,
        mesh=mesh,
        in_specs=placed,
        out_specs=(P("inner", None), P("inner"), P(), P(), P()),
        check_vma=False,
    )
```

```python
import functools
import math

import jax
import jax.numpy as jnp
from jax import lax
from jax.experimental import pallas as pl
from jax.experimental.pallas import tpu as pltpu
from jax.sharding import PartitionSpec as P

LEARN_RATE = 0.5


def interaction_grads(inputs, cotangent, mix_weight, lift_weight, linear_weight, scaling):
    compressed = jnp.einsum(
        "bfd,fk->bdk", inputs, mix_weight, preferred_element_type=jnp.float32
    ).astype(jnp.bfloat16)
    products = (
        jnp.einsum("bfd,bdk->bfk", inputs, compressed, preferred_element_type=jnp.float32) * scaling
    ).astype(jnp.bfloat16)
    d_products = jnp.einsum(
        "bfd,kd->bfk", cotangent, lift_weight, preferred_element_type=jnp.float32
    ).astype(jnp.bfloat16)
    d_compressed = (
        jnp.einsum("bfd,bfk->bdk", inputs, d_products, preferred_element_type=jnp.float32) * scaling
    ).astype(jnp.bfloat16)
    d_inputs = cotangent.astype(jnp.float32)
    d_inputs = d_inputs + jnp.einsum(
        "fg,bfd->bgd", linear_weight, cotangent, preferred_element_type=jnp.float32
    )
    d_inputs = d_inputs + scaling * jnp.einsum(
        "bfk,bdk->bfd", d_products, compressed, preferred_element_type=jnp.float32
    )
    d_inputs = d_inputs + jnp.einsum(
        "fk,bdk->bfd", mix_weight, d_compressed, preferred_element_type=jnp.float32
    )
    g_mix = jnp.einsum("bfd,bdk->fk", inputs, d_compressed, preferred_element_type=jnp.float32)
    g_lift = jnp.einsum("bfk,bfd->kd", products, cotangent, preferred_element_type=jnp.float32)
    g_linear = jnp.einsum("bfd,bgd->fg", cotangent, inputs, preferred_element_type=jnp.float32)
    rows_out = d_inputs.astype(jnp.bfloat16).reshape(-1, d_inputs.shape[2])
    return (rows_out, (g_mix, g_lift, g_linear))


def adagrad(weights, history, gradient):
    updated = history + jnp.mean(gradient * gradient, axis=1)
    return (weights - LEARN_RATE * gradient / jnp.sqrt(updated)[:, None], updated)


def owner_ranks(owner_of, owners):
    lookups = owner_of.shape[0]
    width = math.gcd(lookups, 128)
    groups = lookups // width
    hot = (owner_of[:, None] == jnp.arange(owners, dtype=jnp.int32)[None, :]).astype(jnp.bfloat16)
    hot = hot.reshape(groups, width, owners)
    lower = (jnp.arange(width)[:, None] > jnp.arange(width)[None, :]).astype(jnp.bfloat16)
    within = jnp.einsum("ij,gjo->gio", lower, hot, preferred_element_type=jnp.float32)
    totals = jnp.sum(hot.astype(jnp.float32), axis=1)
    before = jnp.cumsum(totals, axis=0) - totals
    counted = jnp.sum(hot.astype(jnp.float32) * (within + before[:, None, :]), axis=2)
    return counted.reshape(-1).astype(jnp.int32)


def add_rows(collected, slots, values):
    count = values.shape[0]
    table_rows = collected.shape[0]
    width = math.gcd(count, 2048)
    columns = jnp.arange(table_rows, dtype=jnp.int32)
    for block_index in range(count // width):
        start = block_index * width
        hot = (slots[start : start + width, None] == columns[None, :]).astype(jnp.bfloat16)
        collected = collected + jnp.einsum(
            "lr,ld->rd", hot, values[start : start + width], preferred_element_type=jnp.float32
        )
    return collected


def routed_rows(
    layer_input,
    out_grad,
    mix_weight,
    lift_weight,
    linear_weight,
    row_ids,
    row_home,
    table,
    row_accum,
):
    owners = lax.axis_size("inner")
    sample_count, feature_count, embed_width = layer_input.shape
    table_rows = table.shape[0]
    half_samples = sample_count // 2
    lookups = sample_count * feature_count
    per_owner = lookups // (2 * owners)
    scaling = 1.0 / math.sqrt(embed_width)
    placed = jnp.take(row_home, row_ids.reshape(-1), axis=0)
    owner_of = placed // table_rows
    target = owner_of * (2 * per_owner) + owner_ranks(owner_of, owners)
    ordering = jnp.zeros((lookups,), jnp.int32).at[target].set(jnp.arange(lookups, dtype=jnp.int32))
    ordering = ordering.reshape(owners, 2, per_owner)
    local_rows = (
        jnp.zeros((lookups,), jnp.int32)
        .at[target]
        .set(placed % table_rows)
        .reshape(owners, 2 * per_owner)
    )
    arrived_rows = lax.all_to_all(
        local_rows, "inner", split_axis=0, concat_axis=0, tiled=True
    ).reshape(owners, 2, per_owner)
    collected = jnp.zeros((table_rows, embed_width), jnp.float32)
    totals = None
    for half_index in range(2):
        first_sample = half_index * half_samples
        rows_out, partial_value = interaction_grads(
            layer_input[first_sample : first_sample + half_samples],
            out_grad[first_sample : first_sample + half_samples],
            mix_weight,
            lift_weight,
            linear_weight,
            scaling,
        )
        picked = ordering[:, half_index, :] - half_index * half_samples * feature_count
        outgoing = jnp.take(rows_out, picked.reshape(-1), axis=0).reshape(
            owners, per_owner, embed_width
        )
        incoming = lax.all_to_all(outgoing, "inner", split_axis=0, concat_axis=0, tiled=True)
        collected = add_rows(
            collected, arrived_rows[:, half_index, :].reshape(-1), incoming.reshape(-1, embed_width)
        )
        if totals is None:
            totals = partial_value
        else:
            totals = tuple((earlier + later for earlier, later in zip(totals, partial_value)))
    batch_total = sample_count * lax.axis_size("outer") * owners
    summed = lax.psum((totals[0], totals[1], totals[2]), ("outer", "inner"))
    mix_grad = summed[0] / batch_total
    lift_grad = summed[1] / batch_total
    linear_grad = summed[2] / batch_total
    complete = lax.psum(collected, "outer")
    new_table, new_accum = adagrad(table, row_accum, complete)
    return (new_table, new_accum, mix_grad, lift_grad, linear_grad)


def matmul(left, right):
    return jnp.dot(left, right, preferred_element_type=jnp.float32)


def matmul_nt(left, right):
    return lax.dot_general(left, right, (((1,), (1,)), ((), ())), preferred_element_type=jnp.float32)


def one_hot(matches):
    return jnp.where(matches, 1.0, 0.0).astype(jnp.bfloat16)


def place_kernel(shift, owners, ids_ref, home_ref, rank_ref, slot_ref, count_ref):
    samples, feats = ids_ref.shape
    high, low = home_ref.shape
    half = low // 2
    home = home_ref[...]
    pieces = []
    for part in (home & 255, home >> 8):
        down = part.astype(jnp.float32).T
        pieces.append(jnp.concatenate([down[:half], down[half:]], axis=1))
    pieces = jnp.concatenate(pieces, axis=0).astype(jnp.bfloat16)
    high_at = lax.broadcasted_iota(jnp.int32, (2 * high, feats), 0)
    low_at = lax.broadcasted_iota(jnp.int32, (half, feats), 0)
    lane = lax.broadcasted_iota(jnp.int32, (1, feats), 1)
    count_lane = lax.broadcasted_iota(jnp.int32, (8, 128), 1)

    @pl.loop(0, samples // 8)
    def _(group):
        first = pl.multiple_of(group * 8, 8)
        ids = ids_ref[pl.ds(first, 8), :]
        every = range(8)
        ones = [ids[row : row + 1] for row in every]
        hots = [one_hot(high_at == ((one >> 6) & 1) * high + (one >> 7)) for one in ones]
        founds = [matmul(pieces, hot) for hot in hots]
        places = []
        for row in every:
            value = founds[row][:half] + 256.0 * founds[row][half:]
            value = jnp.where(low_at == (ones[row] & (half - 1)), value, 0.0)
            places.append(jnp.sum(value, axis=0, keepdims=True))
        place = jnp.concatenate(places, axis=0).astype(jnp.int32)
        owner_all = place >> shift
        slot_ref[pl.ds(first, 8), :] = place & ((1 << shift) - 1)
        keys = (owner_all * feats + lane).astype(jnp.float32)
        downs = [jnp.broadcast_to(keys[row : row + 1], (128, feats)).T for row in every]
        ranks = []
        for row in every:
            parts = []
            for at in range(0, feats, 128):
                less = downs[row] < keys[row : row + 1, at : at + 128]
                parts.append(jnp.sum(jnp.where(less, 1.0, 0.0), axis=0, keepdims=True))
            ranks.append(jnp.concatenate(parts, axis=1))
        rank_ref[pl.ds(first, 8), :] = jnp.concatenate(ranks, axis=0).astype(jnp.int32)
        counts = jnp.zeros((8, 128), jnp.float32)
        for owner_at in range(owners):
            number = jnp.sum(jnp.where(owner_all == owner_at, 1.0, 0.0), axis=1, keepdims=True)
            counts = jnp.where(count_lane == owner_at, number, counts)
        most = jnp.max(counts, axis=1, keepdims=True)
        counts = jnp.where(count_lane == owners, most, counts)
        count_ref[pl.ds(first, 8), :] = counts.astype(jnp.int32)


COPY_ROWS = 56
SCRATCH = 16


def sum_list(values):
    total = values[0]
    for value in values[1:]:
        total = total + value
    return total


def positions():
    return lax.axis_index("outer"), lax.axis_index("inner")


def grads_kernel(
    sizes,
    x_ref,
    g_ref,
    mix_ref,
    lift_ref,
    linear_ref,
    ids_ref,
    home_ref,
    *rest,
):
    group, steps, owners, per_owner, scaling, shift = sizes
    far_count = owners // 4
    keep_refs, send_refs = rest[:far_count], rest[far_count : 2 * far_count]
    rows_ref = rest[2 * far_count]
    dense_refs, scratch = rest[2 * far_count + 1 : -SCRATCH], rest[-SCRATCH:]
    rank_ref, slot_ref, found_ref, count_ref, copied = scratch[:5]
    step = pl.program_id(0)
    outer, inner = positions()

    @pl.when(step == 0)
    def _():
        place_kernel(shift, owners, ids_ref, home_ref, rank_ref, slot_ref, found_ref)
        copy = pltpu.make_async_copy(found_ref, count_ref, copied)
        copy.start()
        copy.wait()

    @pl.when((step > 0) & (step <= steps))
    def _():
        gather_rows(
            step - 1,
            outer,
            sizes,
            count_ref,
            x_ref,
            g_ref,
            mix_ref,
            lift_ref,
            linear_ref,
            rank_ref,
            slot_ref,
            dense_refs,
            *scratch[5:],
        )

    @pl.when(step > steps)
    def _():
        place = owners - 1 - (step - steps - 1)
        row_a, row_b = scratch[-4], scratch[-3]
        near = (step - steps - 1) ^ inner
        rows_ref[0, :, :128] = row_a[near, pl.ds(0, per_owner), :].astype(jnp.bfloat16)
        rows_ref[0, :, 128:] = row_b[near, pl.ds(0, per_owner), :].astype(jnp.bfloat16)
        owner = place ^ inner
        first_rows = row_a[owner, pl.ds(0, per_owner), :]
        second_rows = row_b[owner, pl.ds(0, per_owner), :]
        at = x_ref.shape[1] - 128
        build_rows(at, outer, first_rows, second_rows, place, far_count, keep_refs, send_refs)


def join_rows(count_ref, filled, sorted_a, sorted_b, row_a, row_b, step, group, owners):
    begun = (step >= 0).astype(jnp.int32)
    now = (step + 2) % 2
    first = jnp.maximum(step, 0) * group
    every = range(group)
    numbers = [[count_ref[first + k, owner] * begun for owner in range(owners)] for k in every]
    starts = [filled[owner] for owner in range(owners)]
    ends = list(starts)
    for k in every:
        begin = 0
        for owner in range(owners):
            source, target = pl.ds(begin, COPY_ROWS), pl.ds(ends[owner], COPY_ROWS)
            row_a[owner, target, :] = sorted_a[now, k, source, :]
            row_b[owner, target, :] = sorted_b[now, k, source, :]
            ends[owner] = ends[owner] + numbers[k][owner]
            begin = begin + numbers[k][owner]
    most = count_ref[first, owners] * begun
    for k in range(1, group):
        most = jnp.maximum(most, count_ref[first + k, owners] * begun)

    @pl.when(most > COPY_ROWS)
    def _():
        again = list(starts)
        for k in every:
            begin = 0
            for owner in range(owners):

                def copy(turn, carry, begin=begin, at=again[owner], owner=owner, k=k):
                    off = turn * COPY_ROWS
                    source, target = pl.ds(begin + off, COPY_ROWS), pl.ds(at + off, COPY_ROWS)
                    row_a[owner, target, :] = sorted_a[now, k, source, :]
                    row_b[owner, target, :] = sorted_b[now, k, source, :]
                    return carry

                turns = (numbers[k][owner] + COPY_ROWS - 1) // COPY_ROWS
                lax.fori_loop(0, turns, copy, 0)
                again[owner] = again[owner] + numbers[k][owner]
                begin = begin + numbers[k][owner]

    for owner in range(owners):
        filled[owner] = ends[owner]


def gather_rows(
    step,
    outer,
    sizes,
    count_ref,
    x_ref,
    g_ref,
    mix_ref,
    lift_ref,
    linear_ref,
    rank_ref,
    slot_ref,
    dense_refs,
    mix_down,
    lift_down,
    mix_sum,
    lift_sum,
    linear_sum,
    sorted_a,
    sorted_b,
    row_a,
    row_b,
    dense_ref,
    filled,
):
    group, steps, owners, _, scaling, _ = sizes
    width, feats = x_ref.shape[1:]
    rank = mix_ref.shape[1]

    @pl.when(step == 0)
    def _():
        mix_down[...] = mix_ref[...].astype(jnp.float32).T.astype(jnp.bfloat16)
        lift_down[...] = lift_ref[...].astype(jnp.float32).T.astype(jnp.bfloat16)
        mix_sum[...] = jnp.zeros_like(mix_sum)
        lift_sum[...] = jnp.zeros_like(lift_sum)
        linear_sum[...] = jnp.zeros_like(linear_sum)
        for owner in range(owners):
            filled[owner] = 0

    now = step % 2
    join_rows(count_ref, filled, sorted_a, sorted_b, row_a, row_b, step - 1, group, owners)
    row_at = lax.broadcasted_iota(jnp.int32, (feats, feats), 0)
    extra_at = lax.broadcasted_iota(jnp.int32, (feats - width, feats), 0)
    every = range(group)
    d_prods = [matmul(lift_down[...], g_ref[k]).astype(jnp.bfloat16) for k in every]
    boths = [
        matmul_nt(x_ref[k], jnp.concatenate([mix_down[...], d_prods[k]], axis=0)) for k in every
    ]
    comps = [both[:, :rank].astype(jnp.bfloat16) for both in boths]
    d_comps = [(both[:, rank:] * scaling).astype(jnp.bfloat16) for both in boths]
    x_flat = x_ref[...].reshape(group * width, feats).T
    x_flats = [x_flat[:, k * width : (k + 1) * width] for k in every]
    pairs = [
        matmul(x_flats[k], jnp.concatenate([comps[k], d_comps[k]], axis=1)) for k in every
    ]
    prods = [(pair[:, :rank] * scaling).astype(jnp.bfloat16) for pair in pairs]
    mix_sum[...] += sum_list([pair[:, rank:] for pair in pairs])
    g_all = g_ref[...].reshape(group * width, feats)
    d_all = g_all.astype(jnp.float32) + matmul(g_all, linear_ref[...])
    d_all = d_all + matmul(jnp.concatenate(d_comps, axis=0), mix_down[...])
    d_ins = [
        d_all[k * width : (k + 1) * width] + scaling * matmul(comps[k], d_prods[k]) for k in every
    ]
    moves, rows_downs = [], []
    for k in every:
        slot = slot_ref[pl.ds(step * group + k, 1), :]
        extra = jnp.where(extra_at == 0, slot >> 4, jnp.where(extra_at == 1, slot & 15, 0))
        rows_downs.append(
            jnp.concatenate(
                [d_ins[k].astype(jnp.bfloat16), extra.astype(jnp.float32).astype(jnp.bfloat16)],
                axis=0,
            )
        )
        moves.append(one_hot(row_at == rank_ref[pl.ds(step * group + k, 1), :]))
    for k in every:
        ordered = matmul_nt(moves[k], rows_downs[k])
        sorted_a[now, k, :feats] = ordered[:, :128]
        sorted_b[now, k, :feats] = ordered[:, 128:]
    linear_sum[...] += matmul(x_flat, g_all)
    lift_sum[...] += sum_list([matmul(g_ref[k], prods[k]) for k in every])

    @pl.when(step == steps - 1)
    def _():
        join_rows(count_ref, filled, sorted_a, sorted_b, row_a, row_b, step, group, owners)
        dense_ref[:feats] = mix_sum[...]
        linear = linear_sum[...].T
        for at in range(feats // 128):
            dense_ref[feats * (1 + at) : feats * (2 + at)] = linear[:, 128 * at : 128 * (at + 1)]
        dense_ref[feats * (1 + feats // 128) :] = lift_sum[...]
        piece = dense_refs[0].shape[0]
        for index, ref in enumerate(dense_refs):
            first = pl.multiple_of((index ^ outer) * piece, piece)
            ref[...] = dense_ref[pl.ds(first, piece), :]


def build_rows(at, my_outer, first_rows, second_rows, place, first, keep_refs, send_refs):
    outers, piece = 2 * keep_refs[0].shape[1], keep_refs[0].shape[3]
    per_owner = first_rows.shape[0]
    rows_down = jnp.concatenate([first_rows.T, second_rows.T[:at]], axis=0).astype(jnp.bfloat16)
    slots = second_rows[:, at : at + 1] * 16.0 + second_rows[:, at + 1 : at + 2]
    slots = slots.astype(jnp.int32)
    lanes = lax.broadcasted_iota(jnp.int32, (per_owner, piece), 1)
    totals = []
    for outer in range(outers):
        base = (outer ^ my_outer) * piece
        totals.append(matmul(rows_down, one_hot(lanes == slots - base)).astype(jnp.bfloat16))
    for index in range(len(keep_refs)):

        @pl.when(place // 2 == first + index)
        def _(index=index):
            for outer in range(outers):
                ref = (send_refs if outer % 2 else keep_refs)[index]
                ref[0, outer // 2] = totals[outer]


def part_specs(start, first, count, part):
    def spec(index):
        begin = start + 2 * (count - 1 - index)
        return pl.BlockSpec(
            (1,) + part[1:], lambda i, *_: (jnp.clip(begin + 1 - i, 0, 1), 0, 0, 0)
        )

    return [spec(index) for index in range(count)] * 2


def local_grads(x_down, g_down, mix, lift_down, linear, ids, home, owners, part):
    samples, width, feats = x_down.shape
    rank = mix.shape[1]
    group = 8
    steps = samples // group
    per_owner = samples * feats // owners
    far_count = owners // 4
    shift = (part[1] * 2 * part[3]).bit_length() - 1
    sizes = (group, steps, owners, per_owner, 1.0 / math.sqrt(width), shift)

    def whole(shape):
        return pl.BlockSpec(shape, lambda i, *_: (0,) * len(shape))

    sample_spec = pl.BlockSpec(
        (group, width, feats), lambda i: (jnp.clip(i - 1, 0, steps - 1), 0, 0)
    )
    dense_rows = feats * (1 + feats // 128) + width
    outers = 2 * part[1]
    dense_piece = (dense_rows // outers, 128)
    room = per_owner + 64
    rows_shape = (owners // 2, per_owner, 256)
    scratch = [
        pltpu.VMEM((samples, feats), jnp.int32),
        pltpu.VMEM((samples, feats), jnp.int32),
        pltpu.VMEM((samples, 128), jnp.int32),
        pltpu.SMEM((samples, 128), jnp.int32),
        pltpu.SemaphoreType.DMA,
        pltpu.VMEM((rank, feats), jnp.bfloat16),
        pltpu.VMEM((rank, width), jnp.bfloat16),
        pltpu.VMEM((feats, rank), jnp.float32),
        pltpu.VMEM((width, rank), jnp.float32),
        pltpu.VMEM((feats, feats), jnp.float32),
        pltpu.VMEM((2, group, feats + 64, 128), jnp.float32),
        pltpu.VMEM((2, group, feats + 64, 128), jnp.float32),
        pltpu.VMEM((owners, room, 128), jnp.float32),
        pltpu.VMEM((owners, room, 128), jnp.float32),
        pltpu.VMEM((dense_rows, 128), jnp.float32),
        pltpu.SMEM((owners,), jnp.int32),
    ]
    outs = pl.pallas_call(
        functools.partial(grads_kernel, sizes),
        out_shape=[jax.ShapeDtypeStruct(part, jnp.bfloat16)] * (2 * far_count)
        + [
            jax.ShapeDtypeStruct(rows_shape, jnp.bfloat16),
        ]
        + [jax.ShapeDtypeStruct(dense_piece, jnp.float32)] * outers,
        grid=(1 + steps + owners // 2,),
        in_specs=[
            sample_spec,
            sample_spec,
            whole((feats, rank)),
            whole((width, rank)),
            whole((feats, feats)),
            whole((samples, feats)),
            whole(home.shape),
        ],
        out_specs=part_specs(1 + steps, owners // 2 - far_count, far_count, part)
        + [
            pl.BlockSpec(
                (1,) + rows_shape[1:],
                lambda i: (jnp.clip(i - 1 - steps, 0, owners // 2 - 1), 0, 0),
            )
        ]
        + [whole(dense_piece)] * outers,
        scratch_shapes=scratch,
        compiler_params=pltpu.CompilerParams(vmem_limit_bytes=60 * 2**20),
        cost_estimate=pl.CostEstimate(
            flops=2 * samples * feats * feats * 3072, bytes_accessed=12 * 2**20, transcendentals=0
        ),
        name="local_grads",
    )(x_down, g_down, mix, lift_down, linear, ids, home)
    keep, send = outs[:far_count], outs[far_count : 2 * far_count]
    return keep, send, outs[2 * far_count], outs[2 * far_count + 1 :]


def build_kernel(at, rows_ref, *refs):
    half = len(refs) // 2
    rows = rows_ref[0].astype(jnp.float32)
    place = 2 * half - 1 - pl.program_id(0)
    keep_refs, send_refs = refs[:half], refs[half:]
    outer, _ = positions()
    build_rows(at, outer, rows[:, :128], rows[:, 128:], place, 0, keep_refs, send_refs)


def build_parts(rows, part, width):
    places, per_owner, lanes = rows.shape
    far_count = places // 2
    outs = pl.pallas_call(
        functools.partial(build_kernel, width - 128),
        out_shape=[jax.ShapeDtypeStruct(part, jnp.bfloat16)] * places,
        grid=(places,),
        in_specs=[pl.BlockSpec((1, per_owner, lanes), lambda i: (places - 1 - i, 0, 0))],
        out_specs=part_specs(0, 0, far_count, part),
        compiler_params=pltpu.CompilerParams(vmem_limit_bytes=60 * 2**20),
        cost_estimate=pl.CostEstimate(
            flops=4 * part[3] * part[1] * part[0] * places * per_owner * lanes,
            bytes_accessed=6 * 2**20,
            transcendentals=0,
        ),
        name="build_parts",
    )(rows)
    return outs[:far_count], outs[far_count:]


def adagrad_kernel(me_ref, *refs):
    pieces, (table_ref, accum_ref) = refs[:2], refs[2:4]
    new_table_ref, new_accum_ref = refs[-2:]
    width = table_ref.shape[0]
    for index, piece in enumerate(pieces):

        @pl.when(pl.program_id(0) == index)
        def _(piece=piece):
            grad = piece[...].astype(jnp.float32)
            mean = jnp.sum(grad * grad, axis=0, keepdims=True) * (1.0 / width)
            updated = accum_ref[...] + mean
            new_accum_ref[...] = updated
            new_table_ref[...] = table_ref[...] - grad * (LEARN_RATE / jnp.sqrt(updated))


def update_table(me, pieces, table_down, accum, first, done=()):
    width, table_rows = table_down.shape
    piece = pieces[0].shape[1]

    def moved(rows):
        return pl.BlockSpec((rows, piece), lambda i, me: (0, (first + i) ^ me[0]))

    return pl.pallas_call(
        adagrad_kernel,
        out_shape=(
            jax.ShapeDtypeStruct((width, table_rows), jnp.float32),
            jax.ShapeDtypeStruct((1, table_rows), jnp.float32),
        ),
        grid_spec=pltpu.PrefetchScalarGridSpec(
            num_scalar_prefetch=1,
            grid=(2,),
            in_specs=[pl.BlockSpec(memory_space=pltpu.VMEM)] * 2
            + [moved(width), moved(1)]
            + [pl.BlockSpec(memory_space=pl.ANY)] * len(done),
            out_specs=[moved(width), moved(1)],
        ),
        input_output_aliases={5 + i: i for i in range(len(done))},
        compiler_params=pltpu.CompilerParams(vmem_limit_bytes=16 * 2**20),
        name="update_table",
    )(me, *pieces, table_down, accum, *done)


def swap(values, axis, bit):
    size = lax.axis_size(axis)
    return lax.ppermute(values, axis, [(i, i ^ bit) for i in range(size)])


def add_half(first, second):
    return (first.astype(jnp.float32) + second.astype(jnp.float32)).astype(jnp.bfloat16)


def tree_sum(values):
    while len(values) > 1:
        values = [values[i] + values[i + 1] for i in range(0, len(values), 2)]
    return values[0]


def after(value, *ready):
    return lax.optimization_barrier((value,) + ready)[0]


def halves(dense, side):
    cut = dense.reshape(2, dense.shape[0] // 2, dense.shape[1])
    mine = lax.dynamic_index_in_dim(cut, side, 0, keepdims=False)
    return mine, lax.dynamic_index_in_dim(cut, 1 - side, 0, keepdims=False)


def stacked(dense, other, side):
    return jnp.where(side == 0, jnp.stack([dense, other]), jnp.stack([other, dense]))


def sum_all(me, keep, send, rows, dense, part, width):
    owners = lax.axis_size("inner")
    outer, inner = lax.axis_index("outer"), lax.axis_index("inner")
    far_count = owners // 2
    first = far_count - len(keep)
    keep = dict(enumerate(keep, first))
    came, parts, kept, sent, rest, second, terms, last = ({} for _ in range(8))
    far_ones, near_ones = list(reversed(range(first, far_count))), list(reversed(range(first)))

    def first_stage(far):
        held = keep[far]
        if far % 2:
            parts[far] = add_half(held[1], came[far][1])
            kept[far] = add_half(held[0], came[far][0])
        else:
            parts[far] = add_half(held[:, 1], came[far][:, 1])
            kept[far] = add_half(held[:, 0], came[far][:, 0])

    def second_stage(far):
        parts[far] = add_half(kept[far][1], sent[far][1])
        rest[far] = add_half(kept[far][0], sent[far][0])
        second[far] = swap(parts[far], *(("outer", 2) if far % 2 else ("inner", 1)))

    def send_first(far, ready):
        sent[far] = swap(ready, *(("inner", 1) if far % 2 else ("outer", 2)))

    sides = (outer & 1, outer >> 1, inner & 1)
    for far in far_ones:
        came[far] = swap(send[far - first], "outer", 1)
    others = tuple(swap(dense[bits], "outer", bits) for bits in range(1, len(dense)))
    for far in far_ones:
        first_stage(far)
        send_first(far, parts[far])
    rows = after(rows, *(parts[far] for far in far_ones))
    low_keep, low_send = build_parts(rows, part, width)
    for far in near_ones:
        keep[far] = low_keep[far]
        came[far] = swap(low_send[far], "outer", 1)
    dense = sum_list((dense[0],) + after(others, low_send[0]))
    mine, other = halves(dense, sides[2])
    other = swap(other, "inner", 1)
    for far in far_ones:
        second_stage(far)
    begun = [parts[far] for far in far_ones]
    for far in near_ones:
        first_stage(far)
    near_parts = [parts[far] for far in near_ones]
    for far in near_ones:
        send_first(far, parts[far])
    dense = mine + after(other, *near_parts)
    others = tuple(swap(dense, "inner", 2 * far) for far in range(1, far_count))
    for far in far_ones:
        second[far] = after(second[far], dense, me, *near_parts)
        last[far] = add_half(rest[far], second[far])
        terms[far] = swap(last[far], "inner", 2 * far)
    far_last = [last[far] for far in far_ones]
    dense = tree_sum([dense] + list(after(others, *far_last)))
    other = swap(dense, "inner", 1)
    arrived = after(tuple(sent[far] for far in near_ones), *far_last)
    for far, sent[far] in zip(near_ones, arrived):
        second_stage(far)
    dense = stacked(dense, after(other, *(parts[far] for far in near_ones)), sides[2])
    other = swap(dense, "outer", 2)
    for far in near_ones:
        second[far] = after(second[far], dense)
        if far:
            last[far] = add_half(rest[far], second[far])
            terms[far] = swap(last[far], "inner", 2 * far)
    dense = stacked(dense, after(other, last[1]), sides[1])
    mine, came_last = after((rest[0], second[0]), dense, last[1])
    terms = after(tuple(terms[far] for far in range(1, far_count)), dense, last[1])
    terms = [mine.astype(jnp.float32) + came_last.astype(jnp.float32)] + [
        term.astype(jnp.float32) for term in terms
    ]
    total = tree_sum(terms).astype(jnp.bfloat16)
    across = swap(total, "outer", 2)
    beside = swap(total, "outer", 1)
    dense = stacked(dense, swap(dense, "outer", 1), sides[0])
    lanes = dense.shape[-1]
    return total, beside, across, jnp.transpose(dense, (1, 0, 2, 3, 4)).reshape(-1, lanes)


def dense_table(
    layer_input,
    out_grad,
    mix_weight,
    lift_weight,
    linear_weight,
    row_ids,
    row_home,
    table,
    row_accum,
):
    owners, outers = lax.axis_size("inner"), lax.axis_size("outer")
    sample_count = layer_input.shape[0]
    table_rows = table.shape[0]
    me = jnp.stack([lax.axis_index("outer"), lax.axis_index("inner")]).astype(jnp.int32)
    width = layer_input.shape[2]
    part = (2, outers // 2, width, table_rows // outers)
    keep, send, rows, dense = local_grads(
        jnp.swapaxes(layer_input, 1, 2),
        jnp.swapaxes(out_grad, 1, 2),
        mix_weight,
        lift_weight.T,
        linear_weight,
        row_ids,
        row_home.reshape(-1, 128),
        owners,
        part,
    )
    total, beside, across, dense = sum_all(me, keep, send, rows, dense, part, width)
    dense = dense * (1.0 / (sample_count * outers * owners))
    feats = layer_input.shape[1]
    linear = [dense[feats * (1 + i) : feats * (2 + i)] for i in range(feats // 128)]
    weights = (
        dense[:feats],
        dense[feats * (1 + feats // 128) :].T,
        jnp.concatenate(linear, axis=1),
    )
    table_down, accum = table.T, row_accum.reshape(1, -1)
    done = update_table(me, (total, beside), table_down, accum, 0)
    across = after(across, done[1], *weights)
    pieces = (across, swap(across, "outer", 1))
    new_table, new_accum = update_table(me, pieces, table_down, accum, 2, done)
    return (new_table.T, new_accum.reshape(-1)) + weights


def power_of_two(number):
    return number & (number - 1) == 0


def on_device(*arrays):
    owners, outers = lax.axis_size("inner"), lax.axis_size("outer")
    layer_input, mix_weight, row_home, table = (arrays[i] for i in (0, 2, 6, 7))
    samples, feats, width = layer_input.shape
    dense_fits = (
        outers == 4
        and owners % 4 == 0
        and power_of_two(owners)
        and row_home.shape[0] <= 2 * samples * feats
        and row_home.shape[0] <= 2**15
        and power_of_two(table.shape[0])
        and 512 <= table.shape[0] <= 4096
        and samples % 16 == 0
        and (feats * (1 + feats // 128) + width) % 64 == 0
        and feats == 256
        and mix_weight.shape[1] == 128
        and 2 * (width - 128) == 128
    )
    return dense_table(*arrays) if dense_fits else routed_rows(*arrays)


def solution(mesh):
    placed = (
        P(("outer", "inner"), None, None),
        P(("outer", "inner"), None, None),
        P(),
        P(),
        P(),
        P(("outer", "inner"), None),
        P(),
        P("inner", None),
        P("inner"),
    )
    return jax.shard_map(
        on_device,
        mesh=mesh,
        in_specs=placed,
        out_specs=(P("inner", None), P("inner"), P(), P(), P()),
        check_vma=False,
    )
```

```python
import functools
import math

import jax
import jax.numpy as jnp
from jax import lax
from jax.experimental import pallas as pl
from jax.experimental.pallas import tpu as pltpu
from jax.sharding import PartitionSpec as P

LEARN_RATE = 0.5


def interaction_grads(inputs, cotangent, mix_weight, lift_weight, linear_weight, scaling):
    compressed = jnp.einsum(
        "bfd,fk->bdk", inputs, mix_weight, preferred_element_type=jnp.float32
    ).astype(jnp.bfloat16)
    products = (
        jnp.einsum("bfd,bdk->bfk", inputs, compressed, preferred_element_type=jnp.float32) * scaling
    ).astype(jnp.bfloat16)
    d_products = jnp.einsum(
        "bfd,kd->bfk", cotangent, lift_weight, preferred_element_type=jnp.float32
    ).astype(jnp.bfloat16)
    d_compressed = (
        jnp.einsum("bfd,bfk->bdk", inputs, d_products, preferred_element_type=jnp.float32) * scaling
    ).astype(jnp.bfloat16)
    d_inputs = cotangent.astype(jnp.float32)
    d_inputs = d_inputs + jnp.einsum(
        "fg,bfd->bgd", linear_weight, cotangent, preferred_element_type=jnp.float32
    )
    d_inputs = d_inputs + scaling * jnp.einsum(
        "bfk,bdk->bfd", d_products, compressed, preferred_element_type=jnp.float32
    )
    d_inputs = d_inputs + jnp.einsum(
        "fk,bdk->bfd", mix_weight, d_compressed, preferred_element_type=jnp.float32
    )
    g_mix = jnp.einsum("bfd,bdk->fk", inputs, d_compressed, preferred_element_type=jnp.float32)
    g_lift = jnp.einsum("bfk,bfd->kd", products, cotangent, preferred_element_type=jnp.float32)
    g_linear = jnp.einsum("bfd,bgd->fg", cotangent, inputs, preferred_element_type=jnp.float32)
    rows_out = d_inputs.astype(jnp.bfloat16).reshape(-1, d_inputs.shape[2])
    return (rows_out, (g_mix, g_lift, g_linear))


def adagrad(weights, history, gradient):
    updated = history + jnp.mean(gradient * gradient, axis=1)
    return (weights - LEARN_RATE * gradient / jnp.sqrt(updated)[:, None], updated)


def owner_ranks(owner_of, owners):
    lookups = owner_of.shape[0]
    width = math.gcd(lookups, 128)
    groups = lookups // width
    hot = (owner_of[:, None] == jnp.arange(owners, dtype=jnp.int32)[None, :]).astype(jnp.bfloat16)
    hot = hot.reshape(groups, width, owners)
    lower = (jnp.arange(width)[:, None] > jnp.arange(width)[None, :]).astype(jnp.bfloat16)
    within = jnp.einsum("ij,gjo->gio", lower, hot, preferred_element_type=jnp.float32)
    totals = jnp.sum(hot.astype(jnp.float32), axis=1)
    before = jnp.cumsum(totals, axis=0) - totals
    counted = jnp.sum(hot.astype(jnp.float32) * (within + before[:, None, :]), axis=2)
    return counted.reshape(-1).astype(jnp.int32)


def add_rows(collected, slots, values):
    count = values.shape[0]
    table_rows = collected.shape[0]
    width = math.gcd(count, 2048)
    columns = jnp.arange(table_rows, dtype=jnp.int32)
    for block_index in range(count // width):
        start = block_index * width
        hot = (slots[start : start + width, None] == columns[None, :]).astype(jnp.bfloat16)
        collected = collected + jnp.einsum(
            "lr,ld->rd", hot, values[start : start + width], preferred_element_type=jnp.float32
        )
    return collected


def routed_rows(
    layer_input,
    out_grad,
    mix_weight,
    lift_weight,
    linear_weight,
    row_ids,
    row_home,
    table,
    row_accum,
):
    owners = lax.axis_size("inner")
    sample_count, feature_count, embed_width = layer_input.shape
    table_rows = table.shape[0]
    half_samples = sample_count // 2
    lookups = sample_count * feature_count
    per_owner = lookups // (2 * owners)
    scaling = 1.0 / math.sqrt(embed_width)
    placed = jnp.take(row_home, row_ids.reshape(-1), axis=0)
    owner_of = placed // table_rows
    target = owner_of * (2 * per_owner) + owner_ranks(owner_of, owners)
    ordering = jnp.zeros((lookups,), jnp.int32).at[target].set(jnp.arange(lookups, dtype=jnp.int32))
    ordering = ordering.reshape(owners, 2, per_owner)
    local_rows = (
        jnp.zeros((lookups,), jnp.int32)
        .at[target]
        .set(placed % table_rows)
        .reshape(owners, 2 * per_owner)
    )
    arrived_rows = lax.all_to_all(
        local_rows, "inner", split_axis=0, concat_axis=0, tiled=True
    ).reshape(owners, 2, per_owner)
    collected = jnp.zeros((table_rows, embed_width), jnp.float32)
    totals = None
    for half_index in range(2):
        first_sample = half_index * half_samples
        rows_out, partial_value = interaction_grads(
            layer_input[first_sample : first_sample + half_samples],
            out_grad[first_sample : first_sample + half_samples],
            mix_weight,
            lift_weight,
            linear_weight,
            scaling,
        )
        picked = ordering[:, half_index, :] - half_index * half_samples * feature_count
        outgoing = jnp.take(rows_out, picked.reshape(-1), axis=0).reshape(
            owners, per_owner, embed_width
        )
        incoming = lax.all_to_all(outgoing, "inner", split_axis=0, concat_axis=0, tiled=True)
        collected = add_rows(
            collected, arrived_rows[:, half_index, :].reshape(-1), incoming.reshape(-1, embed_width)
        )
        if totals is None:
            totals = partial_value
        else:
            totals = tuple((earlier + later for earlier, later in zip(totals, partial_value)))
    batch_total = sample_count * lax.axis_size("outer") * owners
    summed = lax.psum((totals[0], totals[1], totals[2]), ("outer", "inner"))
    mix_grad = summed[0] / batch_total
    lift_grad = summed[1] / batch_total
    linear_grad = summed[2] / batch_total
    complete = lax.psum(collected, "outer")
    new_table, new_accum = adagrad(table, row_accum, complete)
    return (new_table, new_accum, mix_grad, lift_grad, linear_grad)


def matmul(left, right):
    return jnp.dot(left, right, preferred_element_type=jnp.float32)


def matmul_nt(left, right):
    return lax.dot_general(left, right, (((1,), (1,)), ((), ())), preferred_element_type=jnp.float32)


def one_hot(matches):
    return jnp.where(matches, 1.0, 0.0).astype(jnp.bfloat16)


def place_kernel(shift, owners, ids_ref, home_ref, rank_ref, slot_ref, count_ref):
    samples, feats = ids_ref.shape
    high, low = home_ref.shape
    half = low // 2
    home = home_ref[...]
    pieces = []
    for part in (home & 255, home >> 8):
        down = part.astype(jnp.float32).T
        pieces.append(jnp.concatenate([down[:half], down[half:]], axis=1))
    pieces = jnp.concatenate(pieces, axis=0).astype(jnp.bfloat16)
    high_at = lax.broadcasted_iota(jnp.int32, (2 * high, feats), 0)
    low_at = lax.broadcasted_iota(jnp.int32, (half, feats), 0)
    lane = lax.broadcasted_iota(jnp.int32, (1, feats), 1)
    count_lane = lax.broadcasted_iota(jnp.int32, (8, 128), 1)

    @pl.loop(0, samples // 8)
    def _(group):
        first = pl.multiple_of(group * 8, 8)
        ids = ids_ref[pl.ds(first, 8), :]
        every = range(8)
        ones = [ids[row : row + 1] for row in every]
        hots = [one_hot(high_at == ((one >> 6) & 1) * high + (one >> 7)) for one in ones]
        founds = [matmul(pieces, hot) for hot in hots]
        places = []
        for row in every:
            value = founds[row][:half] + 256.0 * founds[row][half:]
            value = jnp.where(low_at == (ones[row] & (half - 1)), value, 0.0)
            places.append(jnp.sum(value, axis=0, keepdims=True))
        place = jnp.concatenate(places, axis=0).astype(jnp.int32)
        owner_all = place >> shift
        slot_ref[pl.ds(first, 8), :] = place & ((1 << shift) - 1)
        keys = (owner_all * feats + lane).astype(jnp.float32)
        downs = [jnp.broadcast_to(keys[row : row + 1], (128, feats)).T for row in every]
        ranks = []
        for row in every:
            parts = []
            for at in range(0, feats, 128):
                less = downs[row] < keys[row : row + 1, at : at + 128]
                parts.append(jnp.sum(jnp.where(less, 1.0, 0.0), axis=0, keepdims=True))
            ranks.append(jnp.concatenate(parts, axis=1))
        rank_ref[pl.ds(first, 8), :] = jnp.concatenate(ranks, axis=0).astype(jnp.int32)
        counts = jnp.zeros((8, 128), jnp.float32)
        for owner_at in range(owners):
            number = jnp.sum(jnp.where(owner_all == owner_at, 1.0, 0.0), axis=1, keepdims=True)
            counts = jnp.where(count_lane == owner_at, number, counts)
        most = jnp.max(counts, axis=1, keepdims=True)
        counts = jnp.where(count_lane == owners, most, counts)
        count_ref[pl.ds(first, 8), :] = counts.astype(jnp.int32)


COPY_ROWS = 56
SCRATCH = 16


def sum_list(values):
    total = values[0]
    for value in values[1:]:
        total = total + value
    return total


def positions():
    return lax.axis_index("outer"), lax.axis_index("inner")


def grads_kernel(
    sizes,
    x_ref,
    g_ref,
    mix_ref,
    lift_ref,
    linear_ref,
    ids_ref,
    home_ref,
    *rest,
):
    group, steps, owners, per_owner, scaling, shift = sizes
    far_count = owners // 4
    keep_refs, send_refs = rest[:far_count], rest[far_count : 2 * far_count]
    rows_ref = rest[2 * far_count]
    dense_refs, scratch = rest[2 * far_count + 1 : -SCRATCH], rest[-SCRATCH:]
    rank_ref, slot_ref, found_ref, count_ref, copied = scratch[:5]
    step = pl.program_id(0)
    outer, inner = positions()

    @pl.when(step == 0)
    def _():
        place_kernel(shift, owners, ids_ref, home_ref, rank_ref, slot_ref, found_ref)
        copy = pltpu.make_async_copy(found_ref, count_ref, copied)
        copy.start()
        copy.wait()

    @pl.when((step > 0) & (step <= steps))
    def _():
        gather_rows(
            step - 1,
            outer,
            sizes,
            count_ref,
            x_ref,
            g_ref,
            mix_ref,
            lift_ref,
            linear_ref,
            rank_ref,
            slot_ref,
            dense_refs,
            *scratch[5:],
        )

    @pl.when(step > steps)
    def _():
        place = owners - 1 - (step - steps - 1)
        row_a, row_b = scratch[-4], scratch[-3]
        near = (step - steps - 1) ^ inner
        rows_ref[0, :, :128] = row_a[near, pl.ds(0, per_owner), :].astype(jnp.bfloat16)
        rows_ref[0, :, 128:] = row_b[near, pl.ds(0, per_owner), :].astype(jnp.bfloat16)
        owner = place ^ inner
        first_rows = row_a[owner, pl.ds(0, per_owner), :]
        second_rows = row_b[owner, pl.ds(0, per_owner), :]
        at = x_ref.shape[1] - 128
        build_rows(at, outer, first_rows, second_rows, place, far_count, keep_refs, send_refs)


def join_rows(count_ref, filled, sorted_a, sorted_b, row_a, row_b, step, group, owners):
    begun = (step >= 0).astype(jnp.int32)
    now = (step + 2) % 2
    first = jnp.maximum(step, 0) * group
    every = range(group)
    numbers = [[count_ref[first + k, owner] * begun for owner in range(owners)] for k in every]
    starts = [filled[owner] for owner in range(owners)]
    ends = list(starts)
    for k in every:
        begin = 0
        for owner in range(owners):
            source, target = pl.ds(begin, COPY_ROWS), pl.ds(ends[owner], COPY_ROWS)
            row_a[owner, target, :] = sorted_a[now, k, source, :]
            row_b[owner, target, :] = sorted_b[now, k, source, :]
            ends[owner] = ends[owner] + numbers[k][owner]
            begin = begin + numbers[k][owner]
    most = count_ref[first, owners] * begun
    for k in range(1, group):
        most = jnp.maximum(most, count_ref[first + k, owners] * begun)

    @pl.when(most > COPY_ROWS)
    def _():
        again = list(starts)
        for k in every:
            begin = 0
            for owner in range(owners):

                def copy(turn, carry, begin=begin, at=again[owner], owner=owner, k=k):
                    off = turn * COPY_ROWS
                    source, target = pl.ds(begin + off, COPY_ROWS), pl.ds(at + off, COPY_ROWS)
                    row_a[owner, target, :] = sorted_a[now, k, source, :]
                    row_b[owner, target, :] = sorted_b[now, k, source, :]
                    return carry

                turns = (numbers[k][owner] + COPY_ROWS - 1) // COPY_ROWS
                lax.fori_loop(0, turns, copy, 0)
                again[owner] = again[owner] + numbers[k][owner]
                begin = begin + numbers[k][owner]

    for owner in range(owners):
        filled[owner] = ends[owner]


def gather_rows(
    step,
    outer,
    sizes,
    count_ref,
    x_ref,
    g_ref,
    mix_ref,
    lift_ref,
    linear_ref,
    rank_ref,
    slot_ref,
    dense_refs,
    mix_down,
    lift_down,
    mix_sum,
    lift_sum,
    linear_sum,
    sorted_a,
    sorted_b,
    row_a,
    row_b,
    dense_ref,
    filled,
):
    group, steps, owners, _, scaling, _ = sizes
    width, feats = x_ref.shape[1:]
    rank = mix_ref.shape[1]

    @pl.when(step == 0)
    def _():
        mix_down[...] = mix_ref[...].astype(jnp.float32).T.astype(jnp.bfloat16)
        lift_down[...] = lift_ref[...].astype(jnp.float32).T.astype(jnp.bfloat16)
        mix_sum[...] = jnp.zeros_like(mix_sum)
        lift_sum[...] = jnp.zeros_like(lift_sum)
        linear_sum[...] = jnp.zeros_like(linear_sum)
        for owner in range(owners):
            filled[owner] = 0

    now = step % 2
    join_rows(count_ref, filled, sorted_a, sorted_b, row_a, row_b, step - 1, group, owners)
    row_at = lax.broadcasted_iota(jnp.int32, (feats, feats), 0)
    extra_at = lax.broadcasted_iota(jnp.int32, (feats - width, feats), 0)
    every = range(group)
    d_prods = [matmul(lift_down[...], g_ref[k]).astype(jnp.bfloat16) for k in every]
    boths = [
        matmul_nt(x_ref[k], jnp.concatenate([mix_down[...], d_prods[k]], axis=0)) for k in every
    ]
    comps = [both[:, :rank].astype(jnp.bfloat16) for both in boths]
    d_comps = [(both[:, rank:] * scaling).astype(jnp.bfloat16) for both in boths]
    x_flat = x_ref[...].reshape(group * width, feats).T
    x_flats = [x_flat[:, k * width : (k + 1) * width] for k in every]
    pairs = [
        matmul(x_flats[k], jnp.concatenate([comps[k], d_comps[k]], axis=1)) for k in every
    ]
    prods = [(pair[:, :rank] * scaling).astype(jnp.bfloat16) for pair in pairs]
    mix_sum[...] += sum_list([pair[:, rank:] for pair in pairs])
    g_all = g_ref[...].reshape(group * width, feats)
    d_all = g_all.astype(jnp.float32) + matmul(g_all, linear_ref[...])
    d_all = d_all + matmul(jnp.concatenate(d_comps, axis=0), mix_down[...])
    d_ins = [
        d_all[k * width : (k + 1) * width] + scaling * matmul(comps[k], d_prods[k]) for k in every
    ]
    moves, rows_downs = [], []
    for k in every:
        slot = slot_ref[pl.ds(step * group + k, 1), :]
        extra = jnp.where(extra_at == 0, slot >> 4, jnp.where(extra_at == 1, slot & 15, 0))
        rows_downs.append(
            jnp.concatenate(
                [d_ins[k].astype(jnp.bfloat16), extra.astype(jnp.float32).astype(jnp.bfloat16)],
                axis=0,
            )
        )
        moves.append(one_hot(row_at == rank_ref[pl.ds(step * group + k, 1), :]))
    for k in every:
        ordered = matmul_nt(moves[k], rows_downs[k])
        sorted_a[now, k, :feats] = ordered[:, :128]
        sorted_b[now, k, :feats] = ordered[:, 128:]
    linear_sum[...] += matmul(x_flat, g_all)
    lift_sum[...] += sum_list([matmul(g_ref[k], prods[k]) for k in every])

    @pl.when(step == steps - 1)
    def _():
        join_rows(count_ref, filled, sorted_a, sorted_b, row_a, row_b, step, group, owners)
        dense_ref[:feats] = mix_sum[...]
        linear = linear_sum[...].T
        for at in range(feats // 128):
            dense_ref[feats * (1 + at) : feats * (2 + at)] = linear[:, 128 * at : 128 * (at + 1)]
        dense_ref[feats * (1 + feats // 128) :] = lift_sum[...]
        piece = dense_refs[0].shape[0]
        for index, ref in enumerate(dense_refs):
            first = pl.multiple_of((index ^ outer) * piece, piece)
            ref[...] = dense_ref[pl.ds(first, piece), :]


def build_rows(at, my_outer, first_rows, second_rows, place, first, keep_refs, send_refs):
    outers, piece = 2 * keep_refs[0].shape[1], keep_refs[0].shape[3]
    per_owner = first_rows.shape[0]
    rows_down = jnp.concatenate([first_rows.T, second_rows.T[:at]], axis=0).astype(jnp.bfloat16)
    slots = second_rows[:, at : at + 1] * 16.0 + second_rows[:, at + 1 : at + 2]
    slots = slots.astype(jnp.int32)
    lanes = lax.broadcasted_iota(jnp.int32, (per_owner, piece), 1)
    totals = []
    for outer in range(outers):
        base = (outer ^ my_outer) * piece
        totals.append(matmul(rows_down, one_hot(lanes == slots - base)).astype(jnp.bfloat16))
    for index in range(len(keep_refs)):

        @pl.when(place // 2 == first + index)
        def _(index=index):
            for outer in range(outers):
                ref = (send_refs if outer % 2 else keep_refs)[index]
                ref[0, outer // 2] = totals[outer]


def part_specs(start, first, count, part):
    def spec(index):
        begin = start + 2 * (count - 1 - index)
        return pl.BlockSpec(
            (1,) + part[1:], lambda i, *_: (jnp.clip(begin + 1 - i, 0, 1), 0, 0, 0)
        )

    return [spec(index) for index in range(count)] * 2


def local_grads(x_down, g_down, mix, lift_down, linear, ids, home, owners, part):
    samples, width, feats = x_down.shape
    rank = mix.shape[1]
    group = 8
    steps = samples // group
    per_owner = samples * feats // owners
    far_count = owners // 4
    shift = (part[1] * 2 * part[3]).bit_length() - 1
    sizes = (group, steps, owners, per_owner, 1.0 / math.sqrt(width), shift)

    def whole(shape):
        return pl.BlockSpec(shape, lambda i, *_: (0,) * len(shape))

    sample_spec = pl.BlockSpec(
        (group, width, feats), lambda i: (jnp.clip(i - 1, 0, steps - 1), 0, 0)
    )
    dense_rows = feats * (1 + feats // 128) + width
    outers = 2 * part[1]
    dense_piece = (dense_rows // outers, 128)
    room = per_owner + 64
    rows_shape = (owners // 2, per_owner, 256)
    scratch = [
        pltpu.VMEM((samples, feats), jnp.int32),
        pltpu.VMEM((samples, feats), jnp.int32),
        pltpu.VMEM((samples, 128), jnp.int32),
        pltpu.SMEM((samples, 128), jnp.int32),
        pltpu.SemaphoreType.DMA,
        pltpu.VMEM((rank, feats), jnp.bfloat16),
        pltpu.VMEM((rank, width), jnp.bfloat16),
        pltpu.VMEM((feats, rank), jnp.float32),
        pltpu.VMEM((width, rank), jnp.float32),
        pltpu.VMEM((feats, feats), jnp.float32),
        pltpu.VMEM((2, group, feats + 64, 128), jnp.float32),
        pltpu.VMEM((2, group, feats + 64, 128), jnp.float32),
        pltpu.VMEM((owners, room, 128), jnp.float32),
        pltpu.VMEM((owners, room, 128), jnp.float32),
        pltpu.VMEM((dense_rows, 128), jnp.float32),
        pltpu.SMEM((owners,), jnp.int32),
    ]
    outs = pl.pallas_call(
        functools.partial(grads_kernel, sizes),
        out_shape=[jax.ShapeDtypeStruct(part, jnp.bfloat16)] * (2 * far_count)
        + [
            jax.ShapeDtypeStruct(rows_shape, jnp.bfloat16),
        ]
        + [jax.ShapeDtypeStruct(dense_piece, jnp.float32)] * outers,
        grid=(1 + steps + owners // 2,),
        in_specs=[
            sample_spec,
            sample_spec,
            whole((feats, rank)),
            whole((width, rank)),
            whole((feats, feats)),
            whole((samples, feats)),
            whole(home.shape),
        ],
        out_specs=part_specs(1 + steps, owners // 2 - far_count, far_count, part)
        + [
            pl.BlockSpec(
                (1,) + rows_shape[1:],
                lambda i: (jnp.clip(i - 1 - steps, 0, owners // 2 - 1), 0, 0),
            )
        ]
        + [whole(dense_piece)] * outers,
        scratch_shapes=scratch,
        compiler_params=pltpu.CompilerParams(vmem_limit_bytes=60 * 2**20),
        cost_estimate=pl.CostEstimate(
            flops=2 * samples * feats * feats * 3072, bytes_accessed=12 * 2**20, transcendentals=0
        ),
        name="local_grads",
    )(x_down, g_down, mix, lift_down, linear, ids, home)
    keep, send = outs[:far_count], outs[far_count : 2 * far_count]
    return keep, send, outs[2 * far_count], outs[2 * far_count + 1 :]


def build_kernel(at, rows_ref, *refs):
    half = len(refs) // 2
    rows = rows_ref[0].astype(jnp.float32)
    place = 2 * half - 1 - pl.program_id(0)
    keep_refs, send_refs = refs[:half], refs[half:]
    outer, _ = positions()
    build_rows(at, outer, rows[:, :128], rows[:, 128:], place, 0, keep_refs, send_refs)


def build_parts(rows, part, width):
    places, per_owner, lanes = rows.shape
    far_count = places // 2
    outs = pl.pallas_call(
        functools.partial(build_kernel, width - 128),
        out_shape=[jax.ShapeDtypeStruct(part, jnp.bfloat16)] * places,
        grid=(places,),
        in_specs=[pl.BlockSpec((1, per_owner, lanes), lambda i: (places - 1 - i, 0, 0))],
        out_specs=part_specs(0, 0, far_count, part),
        compiler_params=pltpu.CompilerParams(vmem_limit_bytes=60 * 2**20),
        cost_estimate=pl.CostEstimate(
            flops=4 * part[3] * part[1] * part[0] * places * per_owner * lanes,
            bytes_accessed=6 * 2**20,
            transcendentals=0,
        ),
        name="build_parts",
    )(rows)
    return outs[:far_count], outs[far_count:]


def adagrad_kernel(me_ref, *refs):
    pieces, (table_ref, accum_ref) = refs[:2], refs[2:4]
    new_table_ref, new_accum_ref = refs[-2:]
    width = table_ref.shape[0]
    for index, piece in enumerate(pieces):

        @pl.when(pl.program_id(0) == index)
        def _(piece=piece):
            grad = piece[...].astype(jnp.float32)
            mean = jnp.sum(grad * grad, axis=0, keepdims=True) * (1.0 / width)
            updated = accum_ref[...] + mean
            new_accum_ref[...] = updated
            new_table_ref[...] = table_ref[...] - grad * (LEARN_RATE / jnp.sqrt(updated))


def update_table(me, pieces, table_down, accum, first, done=()):
    width, table_rows = table_down.shape
    piece = pieces[0].shape[1]

    def moved(rows):
        return pl.BlockSpec((rows, piece), lambda i, me: (0, (first + i) ^ me[0]))

    return pl.pallas_call(
        adagrad_kernel,
        out_shape=(
            jax.ShapeDtypeStruct((width, table_rows), jnp.float32),
            jax.ShapeDtypeStruct((1, table_rows), jnp.float32),
        ),
        grid_spec=pltpu.PrefetchScalarGridSpec(
            num_scalar_prefetch=1,
            grid=(2,),
            in_specs=[pl.BlockSpec(memory_space=pltpu.VMEM)] * 2
            + [moved(width), moved(1)]
            + [pl.BlockSpec(memory_space=pl.ANY)] * len(done),
            out_specs=[moved(width), moved(1)],
        ),
        input_output_aliases={5 + i: i for i in range(len(done))},
        compiler_params=pltpu.CompilerParams(vmem_limit_bytes=16 * 2**20),
        name="update_table",
    )(me, *pieces, table_down, accum, *done)


def swap(values, axis, bit):
    size = lax.axis_size(axis)
    return lax.ppermute(values, axis, [(i, i ^ bit) for i in range(size)])


def add_half(first, second):
    return (first.astype(jnp.float32) + second.astype(jnp.float32)).astype(jnp.bfloat16)


def tree_sum(values):
    while len(values) > 1:
        values = [values[i] + values[i + 1] for i in range(0, len(values), 2)]
    return values[0]


def after(value, *ready):
    return lax.optimization_barrier((value,) + ready)[0]


def halves(dense, side):
    cut = dense.reshape(2, dense.shape[0] // 2, dense.shape[1])
    mine = lax.dynamic_index_in_dim(cut, side, 0, keepdims=False)
    return mine, lax.dynamic_index_in_dim(cut, 1 - side, 0, keepdims=False)


def stacked(dense, other, side):
    return jnp.where(side == 0, jnp.stack([dense, other]), jnp.stack([other, dense]))


def sum_all(me, keep, send, rows, dense, part, width):
    owners = lax.axis_size("inner")
    outer, inner = lax.axis_index("outer"), lax.axis_index("inner")
    far_count = owners // 2
    first = far_count - len(keep)
    keep = dict(enumerate(keep, first))
    came, parts, kept, sent, rest, second, terms, last = ({} for _ in range(8))
    far_ones, near_ones = list(reversed(range(first, far_count))), list(reversed(range(first)))

    def first_stage(far):
        held = keep[far]
        if far % 2:
            parts[far] = add_half(held[1], came[far][1])
            kept[far] = add_half(held[0], came[far][0])
        else:
            parts[far] = add_half(held[:, 1], came[far][:, 1])
            kept[far] = add_half(held[:, 0], came[far][:, 0])

    def second_stage(far):
        parts[far] = add_half(kept[far][1], sent[far][1])
        rest[far] = add_half(kept[far][0], sent[far][0])
        second[far] = swap(parts[far], *(("outer", 2) if far % 2 else ("inner", 1)))

    def send_first(far, ready):
        sent[far] = swap(ready, *(("inner", 1) if far % 2 else ("outer", 2)))

    sides = (outer & 1, outer >> 1, inner & 1)
    for far in far_ones:
        came[far] = swap(send[far - first], "outer", 1)
    others = tuple(swap(dense[bits], "outer", bits) for bits in range(1, len(dense)))
    for far in far_ones:
        first_stage(far)
        send_first(far, parts[far])
    far_parts = [parts[far] for far in far_ones]
    rows = after(rows, *far_parts)
    low_keep, low_send = build_parts(rows, part, width)
    for far in near_ones:
        keep[far] = low_keep[far]
        came[far] = swap(low_send[far], "outer", 1)
    dense = sum_list((dense[0],) + after(others, low_send[0]))
    mine, other = halves(dense, sides[2])
    other = swap(other, "inner", 1)
    for far in far_ones:
        second_stage(far)
    for far in near_ones:
        first_stage(far)
    near_parts = [parts[far] for far in near_ones]
    for far in near_ones:
        send_first(far, parts[far])
    dense = mine + after(other, *near_parts)
    other = swap(dense, "inner", 2)

    def send_last(far, *ready):
        low = far & -far
        value = rest[far].astype(jnp.float32) + second[far].astype(jnp.float32)
        came_far = [terms[far + bit] for bit in (1 << at for at in range(8)) if bit < low]
        if came_far:
            for one in after(tuple(came_far), *ready):
                value = value + one.astype(jnp.float32)
        last[far] = value.astype(jnp.bfloat16)
        terms[far] = swap(last[far], "inner", 2 * low)

    for far in far_ones:
        second[far] = after(second[far], me, *near_parts)
    odd_ones = [far for far in far_ones if far % 2]
    for far in odd_ones:
        send_last(far)
    odd_last = [last[far] for far in odd_ones]
    for bit in range(1, far_count.bit_length() - 1):
        dense = dense + after(other, *odd_last)
        other = swap(dense, "inner", 2 << bit)
    arrived = after(tuple(sent[far] for far in near_ones), *odd_last)
    for far, sent[far] in zip(near_ones, arrived):
        second_stage(far)
    near_parts = [parts[far] for far in near_ones]
    dense = dense + after(other, *near_parts)
    other = swap(dense, "inner", 1)
    for far in far_ones:
        if far % 2 == 0:
            send_last(far, *near_parts)
    even_last = [last[far] for far in far_ones if far % 2 == 0]
    dense = stacked(dense, after(other, *even_last), sides[2])
    other = swap(dense, "outer", 2)
    for far in near_ones:
        second[far] = after(second[far], dense)
        if far:
            send_last(far)
    dense = stacked(dense, after(other, last[1]), sides[1])
    mine, came_last = after((rest[0], second[0]), dense, last[1])
    total = mine.astype(jnp.float32) + came_last.astype(jnp.float32)
    ends = tuple(terms[1 << bit] for bit in range(far_count.bit_length() - 1))
    for term in after(ends, dense, last[1]):
        total = total + term.astype(jnp.float32)
    total = total.astype(jnp.bfloat16)
    across = swap(total, "outer", 2)
    beside = swap(total, "outer", 1)
    dense = stacked(dense, swap(dense, "outer", 1), sides[0])
    lanes = dense.shape[-1]
    return total, beside, across, jnp.transpose(dense, (1, 0, 2, 3, 4)).reshape(-1, lanes)


def dense_table(
    layer_input,
    out_grad,
    mix_weight,
    lift_weight,
    linear_weight,
    row_ids,
    row_home,
    table,
    row_accum,
):
    owners, outers = lax.axis_size("inner"), lax.axis_size("outer")
    sample_count = layer_input.shape[0]
    table_rows = table.shape[0]
    me = jnp.stack([lax.axis_index("outer"), lax.axis_index("inner")]).astype(jnp.int32)
    width = layer_input.shape[2]
    part = (2, outers // 2, width, table_rows // outers)
    keep, send, rows, dense = local_grads(
        jnp.swapaxes(layer_input, 1, 2),
        jnp.swapaxes(out_grad, 1, 2),
        mix_weight,
        lift_weight.T,
        linear_weight,
        row_ids,
        row_home.reshape(-1, 128),
        owners,
        part,
    )
    total, beside, across, dense = sum_all(me, keep, send, rows, dense, part, width)
    dense = dense * (1.0 / (sample_count * outers * owners))
    feats = layer_input.shape[1]
    linear = [dense[feats * (1 + i) : feats * (2 + i)] for i in range(feats // 128)]
    weights = (
        dense[:feats],
        dense[feats * (1 + feats // 128) :].T,
        jnp.concatenate(linear, axis=1),
    )
    table_down, accum = table.T, row_accum.reshape(1, -1)
    done = update_table(me, (total, beside), table_down, accum, 0)
    across = after(across, done[1], *weights)
    pieces = (across, swap(across, "outer", 1))
    new_table, new_accum = update_table(me, pieces, table_down, accum, 2, done)
    return (new_table.T, new_accum.reshape(-1)) + weights


def power_of_two(number):
    return number & (number - 1) == 0


def on_device(*arrays):
    owners, outers = lax.axis_size("inner"), lax.axis_size("outer")
    layer_input, mix_weight, row_home, table = (arrays[i] for i in (0, 2, 6, 7))
    samples, feats, width = layer_input.shape
    dense_fits = (
        outers == 4
        and owners % 4 == 0
        and power_of_two(owners)
        and row_home.shape[0] <= 2 * samples * feats
        and row_home.shape[0] <= 2**15
        and power_of_two(table.shape[0])
        and 512 <= table.shape[0] <= 4096
        and samples % 16 == 0
        and (feats * (1 + feats // 128) + width) % 64 == 0
        and feats == 256
        and mix_weight.shape[1] == 128
        and 2 * (width - 128) == 128
    )
    return dense_table(*arrays) if dense_fits else routed_rows(*arrays)


def solution(mesh):
    placed = (
        P(("outer", "inner"), None, None),
        P(("outer", "inner"), None, None),
        P(),
        P(),
        P(),
        P(("outer", "inner"), None),
        P(),
        P("inner", None),
        P("inner"),
    )
    return jax.shard_map(
        on_device,
        mesh=mesh,
        in_specs=placed,
        out_specs=(P("inner", None), P("inner"), P(), P(), P()),
        check_vma=False,
    )
```

```python
import functools
import math

import jax
import jax.numpy as jnp
from jax import lax
from jax.experimental import pallas as pl
from jax.experimental.pallas import tpu as pltpu
from jax.sharding import PartitionSpec as P

LEARN_RATE = 0.5


def interaction_grads(inputs, cotangent, mix_weight, lift_weight, linear_weight, scaling):
    compressed = jnp.einsum(
        "bfd,fk->bdk", inputs, mix_weight, preferred_element_type=jnp.float32
    ).astype(jnp.bfloat16)
    products = (
        jnp.einsum("bfd,bdk->bfk", inputs, compressed, preferred_element_type=jnp.float32) * scaling
    ).astype(jnp.bfloat16)
    d_products = jnp.einsum(
        "bfd,kd->bfk", cotangent, lift_weight, preferred_element_type=jnp.float32
    ).astype(jnp.bfloat16)
    d_compressed = (
        jnp.einsum("bfd,bfk->bdk", inputs, d_products, preferred_element_type=jnp.float32) * scaling
    ).astype(jnp.bfloat16)
    d_inputs = cotangent.astype(jnp.float32)
    d_inputs = d_inputs + jnp.einsum(
        "fg,bfd->bgd", linear_weight, cotangent, preferred_element_type=jnp.float32
    )
    d_inputs = d_inputs + scaling * jnp.einsum(
        "bfk,bdk->bfd", d_products, compressed, preferred_element_type=jnp.float32
    )
    d_inputs = d_inputs + jnp.einsum(
        "fk,bdk->bfd", mix_weight, d_compressed, preferred_element_type=jnp.float32
    )
    g_mix = jnp.einsum("bfd,bdk->fk", inputs, d_compressed, preferred_element_type=jnp.float32)
    g_lift = jnp.einsum("bfk,bfd->kd", products, cotangent, preferred_element_type=jnp.float32)
    g_linear = jnp.einsum("bfd,bgd->fg", cotangent, inputs, preferred_element_type=jnp.float32)
    rows_out = d_inputs.astype(jnp.bfloat16).reshape(-1, d_inputs.shape[2])
    return (rows_out, (g_mix, g_lift, g_linear))


def adagrad(weights, history, gradient):
    updated = history + jnp.mean(gradient * gradient, axis=1)
    return (weights - LEARN_RATE * gradient / jnp.sqrt(updated)[:, None], updated)


def owner_ranks(owner_of, owners):
    lookups = owner_of.shape[0]
    width = math.gcd(lookups, 128)
    groups = lookups // width
    hot = (owner_of[:, None] == jnp.arange(owners, dtype=jnp.int32)[None, :]).astype(jnp.bfloat16)
    hot = hot.reshape(groups, width, owners)
    lower = (jnp.arange(width)[:, None] > jnp.arange(width)[None, :]).astype(jnp.bfloat16)
    within = jnp.einsum("ij,gjo->gio", lower, hot, preferred_element_type=jnp.float32)
    totals = jnp.sum(hot.astype(jnp.float32), axis=1)
    before = jnp.cumsum(totals, axis=0) - totals
    counted = jnp.sum(hot.astype(jnp.float32) * (within + before[:, None, :]), axis=2)
    return counted.reshape(-1).astype(jnp.int32)


def add_rows(collected, slots, values):
    count = values.shape[0]
    table_rows = collected.shape[0]
    width = math.gcd(count, 2048)
    columns = jnp.arange(table_rows, dtype=jnp.int32)
    for block_index in range(count // width):
        start = block_index * width
        hot = (slots[start : start + width, None] == columns[None, :]).astype(jnp.bfloat16)
        collected = collected + jnp.einsum(
            "lr,ld->rd", hot, values[start : start + width], preferred_element_type=jnp.float32
        )
    return collected


def routed_rows(
    layer_input,
    out_grad,
    mix_weight,
    lift_weight,
    linear_weight,
    row_ids,
    row_home,
    table,
    row_accum,
):
    owners = lax.axis_size("inner")
    sample_count, feature_count, embed_width = layer_input.shape
    table_rows = table.shape[0]
    half_samples = sample_count // 2
    lookups = sample_count * feature_count
    per_owner = lookups // (2 * owners)
    scaling = 1.0 / math.sqrt(embed_width)
    placed = jnp.take(row_home, row_ids.reshape(-1), axis=0)
    owner_of = placed // table_rows
    target = owner_of * (2 * per_owner) + owner_ranks(owner_of, owners)
    ordering = jnp.zeros((lookups,), jnp.int32).at[target].set(jnp.arange(lookups, dtype=jnp.int32))
    ordering = ordering.reshape(owners, 2, per_owner)
    local_rows = (
        jnp.zeros((lookups,), jnp.int32)
        .at[target]
        .set(placed % table_rows)
        .reshape(owners, 2 * per_owner)
    )
    arrived_rows = lax.all_to_all(
        local_rows, "inner", split_axis=0, concat_axis=0, tiled=True
    ).reshape(owners, 2, per_owner)
    collected = jnp.zeros((table_rows, embed_width), jnp.float32)
    totals = None
    for half_index in range(2):
        first_sample = half_index * half_samples
        rows_out, partial_value = interaction_grads(
            layer_input[first_sample : first_sample + half_samples],
            out_grad[first_sample : first_sample + half_samples],
            mix_weight,
            lift_weight,
            linear_weight,
            scaling,
        )
        picked = ordering[:, half_index, :] - half_index * half_samples * feature_count
        outgoing = jnp.take(rows_out, picked.reshape(-1), axis=0).reshape(
            owners, per_owner, embed_width
        )
        incoming = lax.all_to_all(outgoing, "inner", split_axis=0, concat_axis=0, tiled=True)
        collected = add_rows(
            collected, arrived_rows[:, half_index, :].reshape(-1), incoming.reshape(-1, embed_width)
        )
        if totals is None:
            totals = partial_value
        else:
            totals = tuple((earlier + later for earlier, later in zip(totals, partial_value)))
    batch_total = sample_count * lax.axis_size("outer") * owners
    summed = lax.psum((totals[0], totals[1], totals[2]), ("outer", "inner"))
    mix_grad = summed[0] / batch_total
    lift_grad = summed[1] / batch_total
    linear_grad = summed[2] / batch_total
    complete = lax.psum(collected, "outer")
    new_table, new_accum = adagrad(table, row_accum, complete)
    return (new_table, new_accum, mix_grad, lift_grad, linear_grad)


def matmul(left, right):
    return jnp.dot(left, right, preferred_element_type=jnp.float32)


def matmul_nt(left, right):
    return lax.dot_general(left, right, (((1,), (1,)), ((), ())), preferred_element_type=jnp.float32)


def one_hot(matches):
    return jnp.where(matches, 1.0, 0.0).astype(jnp.bfloat16)


def place_kernel(shift, owners, ids_ref, home_ref, rank_ref, slot_ref, count_ref):
    samples, feats = ids_ref.shape
    high, low = home_ref.shape
    half = low // 2
    home = home_ref[...]
    pieces = []
    for part in (home & 255, home >> 8):
        down = part.astype(jnp.float32).T
        pieces.append(jnp.concatenate([down[:half], down[half:]], axis=1))
    pieces = jnp.concatenate(pieces, axis=0).astype(jnp.bfloat16)
    high_at = lax.broadcasted_iota(jnp.int32, (2 * high, feats), 0)
    low_at = lax.broadcasted_iota(jnp.int32, (half, feats), 0)
    lane = lax.broadcasted_iota(jnp.int32, (1, feats), 1)
    count_lane = lax.broadcasted_iota(jnp.int32, (8, 128), 1)

    @pl.loop(0, samples // 8)
    def _(group):
        first = pl.multiple_of(group * 8, 8)
        ids = ids_ref[pl.ds(first, 8), :]
        every = range(8)
        ones = [ids[row : row + 1] for row in every]
        hots = [one_hot(high_at == ((one >> 6) & 1) * high + (one >> 7)) for one in ones]
        founds = [matmul(pieces, hot) for hot in hots]
        places = []
        for row in every:
            value = founds[row][:half] + 256.0 * founds[row][half:]
            value = jnp.where(low_at == (ones[row] & (half - 1)), value, 0.0)
            places.append(jnp.sum(value, axis=0, keepdims=True))
        place = jnp.concatenate(places, axis=0).astype(jnp.int32)
        owner_all = place >> shift
        slot_ref[pl.ds(first, 8), :] = place & ((1 << shift) - 1)
        keys = (owner_all * feats + lane).astype(jnp.float32)
        downs = [jnp.broadcast_to(keys[row : row + 1], (128, feats)).T for row in every]
        ranks = []
        for row in every:
            parts = []
            for at in range(0, feats, 128):
                less = downs[row] < keys[row : row + 1, at : at + 128]
                parts.append(jnp.sum(jnp.where(less, 1.0, 0.0), axis=0, keepdims=True))
            ranks.append(jnp.concatenate(parts, axis=1))
        rank_ref[pl.ds(first, 8), :] = jnp.concatenate(ranks, axis=0).astype(jnp.int32)
        counts = jnp.zeros((8, 128), jnp.float32)
        for owner_at in range(owners):
            number = jnp.sum(jnp.where(owner_all == owner_at, 1.0, 0.0), axis=1, keepdims=True)
            counts = jnp.where(count_lane == owner_at, number, counts)
        most = jnp.max(counts, axis=1, keepdims=True)
        counts = jnp.where(count_lane == owners, most, counts)
        count_ref[pl.ds(first, 8), :] = counts.astype(jnp.int32)


COPY_ROWS = 56
SCRATCH = 16


def sum_list(values):
    total = values[0]
    for value in values[1:]:
        total = total + value
    return total


def positions():
    return lax.axis_index("outer"), lax.axis_index("inner")


def grads_kernel(
    sizes,
    x_ref,
    g_ref,
    mix_ref,
    lift_ref,
    linear_ref,
    ids_ref,
    home_ref,
    *rest,
):
    group, steps, owners, per_owner, scaling, shift = sizes
    far_count = owners // 4
    keep_refs, send_refs = rest[:far_count], rest[far_count : 2 * far_count]
    rows_ref = rest[2 * far_count]
    dense_refs, scratch = rest[2 * far_count + 1 : -SCRATCH], rest[-SCRATCH:]
    rank_ref, slot_ref, found_ref, count_ref, copied = scratch[:5]
    step = pl.program_id(0)
    outer, inner = positions()

    @pl.when(step == 0)
    def _():
        place_kernel(shift, owners, ids_ref, home_ref, rank_ref, slot_ref, found_ref)
        copy = pltpu.make_async_copy(found_ref, count_ref, copied)
        copy.start()
        copy.wait()

    @pl.when((step > 0) & (step <= steps))
    def _():
        gather_rows(
            step - 1,
            outer,
            sizes,
            count_ref,
            x_ref,
            g_ref,
            mix_ref,
            lift_ref,
            linear_ref,
            rank_ref,
            slot_ref,
            dense_refs,
            *scratch[5:],
        )

    @pl.when(step > steps)
    def _():
        place = owners - 1 - (step - steps - 1)
        row_a, row_b = scratch[-4], scratch[-3]
        near = (step - steps - 1) ^ inner
        rows_ref[0, :, :128] = row_a[near, pl.ds(0, per_owner), :].astype(jnp.bfloat16)
        rows_ref[0, :, 128:] = row_b[near, pl.ds(0, per_owner), :].astype(jnp.bfloat16)
        owner = place ^ inner
        first_rows = row_a[owner, pl.ds(0, per_owner), :]
        second_rows = row_b[owner, pl.ds(0, per_owner), :]
        at = x_ref.shape[1] - 128
        build_rows(at, outer, first_rows, second_rows, place, far_count, keep_refs, send_refs)


def join_rows(count_ref, filled, sorted_a, sorted_b, row_a, row_b, step, group, owners):
    begun = (step >= 0).astype(jnp.int32)
    now = (step + 2) % 2
    first = jnp.maximum(step, 0) * group
    every = range(group)
    numbers = [[count_ref[first + k, owner] * begun for owner in range(owners)] for k in every]
    starts = [filled[owner] for owner in range(owners)]
    ends = list(starts)
    for k in every:
        begin = 0
        for owner in range(owners):
            source, target = pl.ds(begin, COPY_ROWS), pl.ds(ends[owner], COPY_ROWS)
            row_a[owner, target, :] = sorted_a[now, k, source, :]
            row_b[owner, target, :] = sorted_b[now, k, source, :]
            ends[owner] = ends[owner] + numbers[k][owner]
            begin = begin + numbers[k][owner]
    most = count_ref[first, owners] * begun
    for k in range(1, group):
        most = jnp.maximum(most, count_ref[first + k, owners] * begun)

    @pl.when(most > COPY_ROWS)
    def _():
        again = list(starts)
        for k in every:
            begin = 0
            for owner in range(owners):

                def copy(turn, carry, begin=begin, at=again[owner], owner=owner, k=k):
                    off = turn * COPY_ROWS
                    source, target = pl.ds(begin + off, COPY_ROWS), pl.ds(at + off, COPY_ROWS)
                    row_a[owner, target, :] = sorted_a[now, k, source, :]
                    row_b[owner, target, :] = sorted_b[now, k, source, :]
                    return carry

                turns = (numbers[k][owner] + COPY_ROWS - 1) // COPY_ROWS
                lax.fori_loop(0, turns, copy, 0)
                again[owner] = again[owner] + numbers[k][owner]
                begin = begin + numbers[k][owner]

    for owner in range(owners):
        filled[owner] = ends[owner]


def gather_rows(
    step,
    outer,
    sizes,
    count_ref,
    x_ref,
    g_ref,
    mix_ref,
    lift_ref,
    linear_ref,
    rank_ref,
    slot_ref,
    dense_refs,
    mix_down,
    lift_down,
    mix_sum,
    lift_sum,
    linear_sum,
    sorted_a,
    sorted_b,
    row_a,
    row_b,
    dense_ref,
    filled,
):
    group, steps, owners, _, scaling, _ = sizes
    width, feats = x_ref.shape[1:]
    rank = mix_ref.shape[1]

    @pl.when(step == 0)
    def _():
        mix_down[...] = mix_ref[...].astype(jnp.float32).T.astype(jnp.bfloat16)
        lift_down[...] = lift_ref[...].astype(jnp.float32).T.astype(jnp.bfloat16)
        mix_sum[...] = jnp.zeros_like(mix_sum)
        lift_sum[...] = jnp.zeros_like(lift_sum)
        linear_sum[...] = jnp.zeros_like(linear_sum)
        for owner in range(owners):
            filled[owner] = 0

    now = step % 2
    join_rows(count_ref, filled, sorted_a, sorted_b, row_a, row_b, step - 1, group, owners)
    row_at = lax.broadcasted_iota(jnp.int32, (feats, feats), 0)
    extra_at = lax.broadcasted_iota(jnp.int32, (feats - width, feats), 0)
    every = range(group)
    d_prods = [matmul(lift_down[...], g_ref[k]).astype(jnp.bfloat16) for k in every]
    boths = [
        matmul_nt(x_ref[k], jnp.concatenate([mix_down[...], d_prods[k]], axis=0)) for k in every
    ]
    comps = [both[:, :rank].astype(jnp.bfloat16) for both in boths]
    scaled = [(both * scaling).astype(jnp.bfloat16) for both in boths]
    d_comps = [both[:, rank:] for both in scaled]
    x_flat = x_ref[...].reshape(group * width, feats).T
    x_flats = [x_flat[:, k * width : (k + 1) * width] for k in every]
    pairs = [
        matmul(x_flats[k], jnp.concatenate([comps[k], d_comps[k]], axis=1)) for k in every
    ]
    prods = [(pair[:, :rank] * scaling).astype(jnp.bfloat16) for pair in pairs]
    mix_sum[...] += sum_list([pair[:, rank:] for pair in pairs])
    g_all = g_ref[...].reshape(group * width, feats)
    d_all = g_all.astype(jnp.float32) + matmul(g_all, linear_ref[...])
    d_ins = [
        d_all[k * width : (k + 1) * width]
        + matmul(scaled[k], jnp.concatenate([d_prods[k], mix_down[...]], axis=0))
        for k in every
    ]
    moves, rows_downs = [], []
    for k in every:
        slot = slot_ref[pl.ds(step * group + k, 1), :]
        extra = jnp.where(extra_at == 0, slot >> 4, jnp.where(extra_at == 1, slot & 15, 0))
        rows_downs.append(
            jnp.concatenate(
                [d_ins[k].astype(jnp.bfloat16), extra.astype(jnp.float32).astype(jnp.bfloat16)],
                axis=0,
            )
        )
        moves.append(one_hot(row_at == rank_ref[pl.ds(step * group + k, 1), :]))
    for k in every:
        ordered = matmul_nt(moves[k], rows_downs[k])
        sorted_a[now, k, :feats] = ordered[:, :128]
        sorted_b[now, k, :feats] = ordered[:, 128:]
    linear_sum[...] += matmul(x_flat, g_all)
    lift_sum[...] += sum_list([matmul(g_ref[k], prods[k]) for k in every])

    @pl.when(step == steps - 1)
    def _():
        join_rows(count_ref, filled, sorted_a, sorted_b, row_a, row_b, step, group, owners)
        dense_ref[:feats] = mix_sum[...]
        linear = linear_sum[...].T
        for at in range(feats // 128):
            dense_ref[feats * (1 + at) : feats * (2 + at)] = linear[:, 128 * at : 128 * (at + 1)]
        dense_ref[feats * (1 + feats // 128) :] = lift_sum[...]
        piece = dense_refs[0].shape[0]
        for index, ref in enumerate(dense_refs):
            first = pl.multiple_of((index ^ outer) * piece, piece)
            ref[...] = dense_ref[pl.ds(first, piece), :]


def build_rows(at, my_outer, first_rows, second_rows, place, first, keep_refs, send_refs):
    outers, piece = 2 * keep_refs[0].shape[1], keep_refs[0].shape[3]
    per_owner = first_rows.shape[0]
    rows_down = jnp.concatenate([first_rows.T, second_rows.T[:at]], axis=0).astype(jnp.bfloat16)
    slots = second_rows[:, at : at + 1] * 16.0 + second_rows[:, at + 1 : at + 2]
    slots = slots.astype(jnp.int32)
    lanes = lax.broadcasted_iota(jnp.int32, (per_owner, piece), 1)
    totals = []
    for outer in range(outers):
        base = (outer ^ my_outer) * piece
        totals.append(matmul(rows_down, one_hot(lanes == slots - base)).astype(jnp.bfloat16))
    for index in range(len(keep_refs)):

        @pl.when(place // 2 == first + index)
        def _(index=index):
            for outer in range(outers):
                ref = (send_refs if outer % 2 else keep_refs)[index]
                ref[0, outer // 2] = totals[outer]


def part_specs(start, first, count, part):
    def spec(index):
        begin = start + 2 * (count - 1 - index)
        return pl.BlockSpec(
            (1,) + part[1:], lambda i, *_: (jnp.clip(begin + 1 - i, 0, 1), 0, 0, 0)
        )

    return [spec(index) for index in range(count)] * 2


def local_grads(x_down, g_down, mix, lift_down, linear, ids, home, owners, part):
    samples, width, feats = x_down.shape
    rank = mix.shape[1]
    group = 8
    steps = samples // group
    per_owner = samples * feats // owners
    far_count = owners // 4
    shift = (part[1] * 2 * part[3]).bit_length() - 1
    sizes = (group, steps, owners, per_owner, 1.0 / math.sqrt(width), shift)

    def whole(shape):
        return pl.BlockSpec(shape, lambda i, *_: (0,) * len(shape))

    sample_spec = pl.BlockSpec(
        (group, width, feats), lambda i: (jnp.clip(i - 1, 0, steps - 1), 0, 0)
    )
    dense_rows = feats * (1 + feats // 128) + width
    outers = 2 * part[1]
    dense_piece = (dense_rows // outers, 128)
    room = per_owner + 64
    rows_shape = (owners // 2, per_owner, 256)
    scratch = [
        pltpu.VMEM((samples, feats), jnp.int32),
        pltpu.VMEM((samples, feats), jnp.int32),
        pltpu.VMEM((samples, 128), jnp.int32),
        pltpu.SMEM((samples, 128), jnp.int32),
        pltpu.SemaphoreType.DMA,
        pltpu.VMEM((rank, feats), jnp.bfloat16),
        pltpu.VMEM((rank, width), jnp.bfloat16),
        pltpu.VMEM((feats, rank), jnp.float32),
        pltpu.VMEM((width, rank), jnp.float32),
        pltpu.VMEM((feats, feats), jnp.float32),
        pltpu.VMEM((2, group, feats + 64, 128), jnp.float32),
        pltpu.VMEM((2, group, feats + 64, 128), jnp.float32),
        pltpu.VMEM((owners, room, 128), jnp.float32),
        pltpu.VMEM((owners, room, 128), jnp.float32),
        pltpu.VMEM((dense_rows, 128), jnp.float32),
        pltpu.SMEM((owners,), jnp.int32),
    ]
    outs = pl.pallas_call(
        functools.partial(grads_kernel, sizes),
        out_shape=[jax.ShapeDtypeStruct(part, jnp.bfloat16)] * (2 * far_count)
        + [
            jax.ShapeDtypeStruct(rows_shape, jnp.bfloat16),
        ]
        + [jax.ShapeDtypeStruct(dense_piece, jnp.float32)] * outers,
        grid=(1 + steps + owners // 2,),
        in_specs=[
            sample_spec,
            sample_spec,
            whole((feats, rank)),
            whole((width, rank)),
            whole((feats, feats)),
            whole((samples, feats)),
            whole(home.shape),
        ],
        out_specs=part_specs(1 + steps, owners // 2 - far_count, far_count, part)
        + [
            pl.BlockSpec(
                (1,) + rows_shape[1:],
                lambda i: (jnp.clip(i - 1 - steps, 0, owners // 2 - 1), 0, 0),
            )
        ]
        + [whole(dense_piece)] * outers,
        scratch_shapes=scratch,
        compiler_params=pltpu.CompilerParams(vmem_limit_bytes=60 * 2**20),
        cost_estimate=pl.CostEstimate(
            flops=2 * samples * feats * feats * 3072, bytes_accessed=12 * 2**20, transcendentals=0
        ),
        name="local_grads",
    )(x_down, g_down, mix, lift_down, linear, ids, home)
    keep, send = outs[:far_count], outs[far_count : 2 * far_count]
    return keep, send, outs[2 * far_count], outs[2 * far_count + 1 :]


def build_kernel(at, rows_ref, *refs):
    half = len(refs) // 2
    rows = rows_ref[0].astype(jnp.float32)
    place = 2 * half - 1 - pl.program_id(0)
    keep_refs, send_refs = refs[:half], refs[half:]
    outer, _ = positions()
    build_rows(at, outer, rows[:, :128], rows[:, 128:], place, 0, keep_refs, send_refs)


def build_parts(rows, part, width):
    places, per_owner, lanes = rows.shape
    far_count = places // 2
    outs = pl.pallas_call(
        functools.partial(build_kernel, width - 128),
        out_shape=[jax.ShapeDtypeStruct(part, jnp.bfloat16)] * places,
        grid=(places,),
        in_specs=[pl.BlockSpec((1, per_owner, lanes), lambda i: (places - 1 - i, 0, 0))],
        out_specs=part_specs(0, 0, far_count, part),
        compiler_params=pltpu.CompilerParams(vmem_limit_bytes=60 * 2**20),
        cost_estimate=pl.CostEstimate(
            flops=4 * part[3] * part[1] * part[0] * places * per_owner * lanes,
            bytes_accessed=6 * 2**20,
            transcendentals=0,
        ),
        name="build_parts",
    )(rows)
    return outs[:far_count], outs[far_count:]


def adagrad_kernel(me_ref, *refs):
    pieces, (table_ref, accum_ref) = refs[:2], refs[2:4]
    new_table_ref, new_accum_ref = refs[-2:]
    width = table_ref.shape[0]
    for index, piece in enumerate(pieces):

        @pl.when(pl.program_id(0) == index)
        def _(piece=piece):
            grad = piece[...].astype(jnp.float32)
            mean = jnp.sum(grad * grad, axis=0, keepdims=True) * (1.0 / width)
            updated = accum_ref[...] + mean
            new_accum_ref[...] = updated
            new_table_ref[...] = table_ref[...] - grad * (LEARN_RATE / jnp.sqrt(updated))


def update_table(me, pieces, table_down, accum, first, done=()):
    width, table_rows = table_down.shape
    piece = pieces[0].shape[1]

    def moved(rows):
        return pl.BlockSpec((rows, piece), lambda i, me: (0, (first + i) ^ me[0]))

    return pl.pallas_call(
        adagrad_kernel,
        out_shape=(
            jax.ShapeDtypeStruct((width, table_rows), jnp.float32),
            jax.ShapeDtypeStruct((1, table_rows), jnp.float32),
        ),
        grid_spec=pltpu.PrefetchScalarGridSpec(
            num_scalar_prefetch=1,
            grid=(2,),
            in_specs=[pl.BlockSpec(memory_space=pltpu.VMEM)] * 2
            + [moved(width), moved(1)]
            + [pl.BlockSpec(memory_space=pl.ANY)] * len(done),
            out_specs=[moved(width), moved(1)],
        ),
        input_output_aliases={5 + i: i for i in range(len(done))},
        compiler_params=pltpu.CompilerParams(vmem_limit_bytes=16 * 2**20),
        name="update_table",
    )(me, *pieces, table_down, accum, *done)


def swap(values, axis, bit):
    size = lax.axis_size(axis)
    return lax.ppermute(values, axis, [(i, i ^ bit) for i in range(size)])


def add_half(first, second):
    return (first.astype(jnp.float32) + second.astype(jnp.float32)).astype(jnp.bfloat16)


def tree_sum(values):
    while len(values) > 1:
        values = [values[i] + values[i + 1] for i in range(0, len(values), 2)]
    return values[0]


def after(value, *ready):
    return lax.optimization_barrier((value,) + ready)[0]


def halves(dense, side):
    cut = dense.reshape(2, dense.shape[0] // 2, dense.shape[1])
    mine = lax.dynamic_index_in_dim(cut, side, 0, keepdims=False)
    return mine, lax.dynamic_index_in_dim(cut, 1 - side, 0, keepdims=False)


def stacked(dense, other, side):
    return jnp.where(side == 0, jnp.stack([dense, other]), jnp.stack([other, dense]))


def sum_all(me, keep, send, rows, dense, part, width):
    owners = lax.axis_size("inner")
    outer, inner = lax.axis_index("outer"), lax.axis_index("inner")
    far_count = owners // 2
    first = far_count - len(keep)
    keep = dict(enumerate(keep, first))
    came, parts, kept, sent, rest, second, terms, last = ({} for _ in range(8))
    far_ones, near_ones = list(reversed(range(first, far_count))), list(reversed(range(first)))

    def first_stage(far):
        held = keep[far]
        if far % 2:
            parts[far] = add_half(held[1], came[far][1])
            kept[far] = add_half(held[0], came[far][0])
        else:
            parts[far] = add_half(held[:, 1], came[far][:, 1])
            kept[far] = add_half(held[:, 0], came[far][:, 0])

    def second_stage(far):
        parts[far] = add_half(kept[far][1], sent[far][1])
        rest[far] = add_half(kept[far][0], sent[far][0])
        second[far] = swap(parts[far], *(("outer", 2) if far % 2 else ("inner", 1)))

    def send_first(far, ready):
        sent[far] = swap(ready, *(("inner", 1) if far % 2 else ("outer", 2)))

    sides = (outer & 1, outer >> 1, inner & 1)
    for far in far_ones:
        came[far] = swap(send[far - first], "outer", 1)
    others = tuple(swap(dense[bits], "outer", bits) for bits in range(1, len(dense)))
    for far in far_ones:
        first_stage(far)
        send_first(far, parts[far])
    far_parts = [parts[far] for far in far_ones]
    rows = after(rows, *far_parts)
    low_keep, low_send = build_parts(rows, part, width)
    for far in near_ones:
        keep[far] = low_keep[far]
        came[far] = swap(low_send[far], "outer", 1)
    dense = sum_list((dense[0],) + after(others, low_send[0]))
    mine, other = halves(dense, sides[2])
    other = swap(other, "inner", 1)
    for far in far_ones:
        second_stage(far)
    for far in near_ones:
        first_stage(far)
    near_parts = [parts[far] for far in near_ones]
    for far in near_ones:
        send_first(far, parts[far])
    dense = mine + after(other, *near_parts)
    other = swap(dense, "inner", 2)

    def send_last(far, *ready):
        low = far & -far
        value = rest[far].astype(jnp.float32) + second[far].astype(jnp.float32)
        came_far = [terms[far + bit] for bit in (1 << at for at in range(8)) if bit < low]
        if came_far:
            for one in after(tuple(came_far), *ready):
                value = value + one.astype(jnp.float32)
        last[far] = value.astype(jnp.bfloat16)
        terms[far] = swap(last[far], "inner", 2 * low)

    for far in far_ones:
        second[far] = after(second[far], me, dense, *near_parts)
    odd_ones = [far for far in far_ones if far % 2]
    for far in odd_ones:
        send_last(far)
    odd_last = [last[far] for far in odd_ones]
    for bit in range(1, far_count.bit_length() - 1):
        dense = dense + after(other, *odd_last)
        other = swap(dense, "inner", 2 << bit)
    arrived = after(tuple(sent[far] for far in near_ones), *odd_last)
    for far, sent[far] in zip(near_ones, arrived):
        second_stage(far)
    near_parts = [parts[far] for far in near_ones]
    dense = dense + after(other, *near_parts)
    other = swap(dense, "inner", 1)
    for far in far_ones:
        if far % 2 == 0:
            send_last(far, *near_parts)
    even_last = [last[far] for far in far_ones if far % 2 == 0]
    dense = stacked(dense, after(other, *even_last), sides[2])
    other = swap(dense, "outer", 2)
    for far in near_ones:
        second[far] = after(second[far], dense)
        if far:
            send_last(far)
    dense = stacked(dense, after(other, last[1]), sides[1])
    mine, came_last = after((rest[0], second[0]), dense, last[1])
    total = mine.astype(jnp.float32) + came_last.astype(jnp.float32)
    ends = tuple(terms[1 << bit] for bit in range(far_count.bit_length() - 1))
    for term in after(ends, dense, last[1]):
        total = total + term.astype(jnp.float32)
    total = total.astype(jnp.bfloat16)
    across = swap(total, "outer", 2)
    beside = swap(total, "outer", 1)
    dense = stacked(dense, swap(dense, "outer", 1), sides[0])
    lanes = dense.shape[-1]
    return total, beside, across, jnp.transpose(dense, (1, 0, 2, 3, 4)).reshape(-1, lanes)


def dense_table(
    layer_input,
    out_grad,
    mix_weight,
    lift_weight,
    linear_weight,
    row_ids,
    row_home,
    table,
    row_accum,
):
    owners, outers = lax.axis_size("inner"), lax.axis_size("outer")
    sample_count = layer_input.shape[0]
    table_rows = table.shape[0]
    me = jnp.stack([lax.axis_index("outer"), lax.axis_index("inner")]).astype(jnp.int32)
    width = layer_input.shape[2]
    part = (2, outers // 2, width, table_rows // outers)
    keep, send, rows, dense = local_grads(
        jnp.swapaxes(layer_input, 1, 2),
        jnp.swapaxes(out_grad, 1, 2),
        mix_weight,
        lift_weight.T,
        linear_weight,
        row_ids,
        row_home.reshape(-1, 128),
        owners,
        part,
    )
    total, beside, across, dense = sum_all(me, keep, send, rows, dense, part, width)
    dense = dense * (1.0 / (sample_count * outers * owners))
    feats = layer_input.shape[1]
    linear = [dense[feats * (1 + i) : feats * (2 + i)] for i in range(feats // 128)]
    weights = (
        dense[:feats],
        dense[feats * (1 + feats // 128) :].T,
        jnp.concatenate(linear, axis=1),
    )
    table_down, accum = table.T, row_accum.reshape(1, -1)
    done = update_table(me, (total, beside), table_down, accum, 0)
    across = after(across, done[1], *weights)
    pieces = (across, swap(across, "outer", 1))
    new_table, new_accum = update_table(me, pieces, table_down, accum, 2, done)
    return (new_table.T, new_accum.reshape(-1)) + weights


def power_of_two(number):
    return number & (number - 1) == 0


def on_device(*arrays):
    owners, outers = lax.axis_size("inner"), lax.axis_size("outer")
    layer_input, mix_weight, row_home, table = (arrays[i] for i in (0, 2, 6, 7))
    samples, feats, width = layer_input.shape
    dense_fits = (
        outers == 4
        and owners % 4 == 0
        and power_of_two(owners)
        and row_home.shape[0] <= 2 * samples * feats
        and row_home.shape[0] <= 2**15
        and power_of_two(table.shape[0])
        and 512 <= table.shape[0] <= 4096
        and samples % 16 == 0
        and (feats * (1 + feats // 128) + width) % 64 == 0
        and feats == 256
        and mix_weight.shape[1] == 128
        and 2 * (width - 128) == 128
    )
    return dense_table(*arrays) if dense_fits else routed_rows(*arrays)


def solution(mesh):
    placed = (
        P(("outer", "inner"), None, None),
        P(("outer", "inner"), None, None),
        P(),
        P(),
        P(),
        P(("outer", "inner"), None),
        P(),
        P("inner", None),
        P("inner"),
    )
    return jax.shard_map(
        on_device,
        mesh=mesh,
        in_specs=placed,
        out_specs=(P("inner", None), P("inner"), P(), P(), P()),
        check_vma=False,
    )
```

```python
import functools
import math

import jax
import jax.numpy as jnp
from jax import lax
from jax.experimental import pallas as pl
from jax.experimental.pallas import tpu as pltpu
from jax.sharding import PartitionSpec as P

LEARN_RATE = 0.5


def interaction_grads(inputs, cotangent, mix_weight, lift_weight, linear_weight, scaling):
    compressed = jnp.einsum(
        "bfd,fk->bdk", inputs, mix_weight, preferred_element_type=jnp.float32
    ).astype(jnp.bfloat16)
    products = (
        jnp.einsum("bfd,bdk->bfk", inputs, compressed, preferred_element_type=jnp.float32) * scaling
    ).astype(jnp.bfloat16)
    d_products = jnp.einsum(
        "bfd,kd->bfk", cotangent, lift_weight, preferred_element_type=jnp.float32
    ).astype(jnp.bfloat16)
    d_compressed = (
        jnp.einsum("bfd,bfk->bdk", inputs, d_products, preferred_element_type=jnp.float32) * scaling
    ).astype(jnp.bfloat16)
    d_inputs = cotangent.astype(jnp.float32)
    d_inputs = d_inputs + jnp.einsum(
        "fg,bfd->bgd", linear_weight, cotangent, preferred_element_type=jnp.float32
    )
    d_inputs = d_inputs + scaling * jnp.einsum(
        "bfk,bdk->bfd", d_products, compressed, preferred_element_type=jnp.float32
    )
    d_inputs = d_inputs + jnp.einsum(
        "fk,bdk->bfd", mix_weight, d_compressed, preferred_element_type=jnp.float32
    )
    g_mix = jnp.einsum("bfd,bdk->fk", inputs, d_compressed, preferred_element_type=jnp.float32)
    g_lift = jnp.einsum("bfk,bfd->kd", products, cotangent, preferred_element_type=jnp.float32)
    g_linear = jnp.einsum("bfd,bgd->fg", cotangent, inputs, preferred_element_type=jnp.float32)
    rows_out = d_inputs.astype(jnp.bfloat16).reshape(-1, d_inputs.shape[2])
    return (rows_out, (g_mix, g_lift, g_linear))


def adagrad(weights, history, gradient):
    updated = history + jnp.mean(gradient * gradient, axis=1)
    return (weights - LEARN_RATE * gradient / jnp.sqrt(updated)[:, None], updated)


def owner_ranks(owner_of, owners):
    lookups = owner_of.shape[0]
    width = math.gcd(lookups, 128)
    groups = lookups // width
    hot = (owner_of[:, None] == jnp.arange(owners, dtype=jnp.int32)[None, :]).astype(jnp.bfloat16)
    hot = hot.reshape(groups, width, owners)
    lower = (jnp.arange(width)[:, None] > jnp.arange(width)[None, :]).astype(jnp.bfloat16)
    within = jnp.einsum("ij,gjo->gio", lower, hot, preferred_element_type=jnp.float32)
    totals = jnp.sum(hot.astype(jnp.float32), axis=1)
    before = jnp.cumsum(totals, axis=0) - totals
    counted = jnp.sum(hot.astype(jnp.float32) * (within + before[:, None, :]), axis=2)
    return counted.reshape(-1).astype(jnp.int32)


def add_rows(collected, slots, values):
    count = values.shape[0]
    table_rows = collected.shape[0]
    width = math.gcd(count, 2048)
    columns = jnp.arange(table_rows, dtype=jnp.int32)
    for block_index in range(count // width):
        start = block_index * width
        hot = (slots[start : start + width, None] == columns[None, :]).astype(jnp.bfloat16)
        collected = collected + jnp.einsum(
            "lr,ld->rd", hot, values[start : start + width], preferred_element_type=jnp.float32
        )
    return collected


def routed_rows(
    layer_input,
    out_grad,
    mix_weight,
    lift_weight,
    linear_weight,
    row_ids,
    row_home,
    table,
    row_accum,
):
    owners = lax.axis_size("inner")
    sample_count, feature_count, embed_width = layer_input.shape
    table_rows = table.shape[0]
    half_samples = sample_count // 2
    lookups = sample_count * feature_count
    per_owner = lookups // (2 * owners)
    scaling = 1.0 / math.sqrt(embed_width)
    placed = jnp.take(row_home, row_ids.reshape(-1), axis=0)
    owner_of = placed // table_rows
    target = owner_of * (2 * per_owner) + owner_ranks(owner_of, owners)
    ordering = jnp.zeros((lookups,), jnp.int32).at[target].set(jnp.arange(lookups, dtype=jnp.int32))
    ordering = ordering.reshape(owners, 2, per_owner)
    local_rows = (
        jnp.zeros((lookups,), jnp.int32)
        .at[target]
        .set(placed % table_rows)
        .reshape(owners, 2 * per_owner)
    )
    arrived_rows = lax.all_to_all(
        local_rows, "inner", split_axis=0, concat_axis=0, tiled=True
    ).reshape(owners, 2, per_owner)
    collected = jnp.zeros((table_rows, embed_width), jnp.float32)
    totals = None
    for half_index in range(2):
        first_sample = half_index * half_samples
        rows_out, partial_value = interaction_grads(
            layer_input[first_sample : first_sample + half_samples],
            out_grad[first_sample : first_sample + half_samples],
            mix_weight,
            lift_weight,
            linear_weight,
            scaling,
        )
        picked = ordering[:, half_index, :] - half_index * half_samples * feature_count
        outgoing = jnp.take(rows_out, picked.reshape(-1), axis=0).reshape(
            owners, per_owner, embed_width
        )
        incoming = lax.all_to_all(outgoing, "inner", split_axis=0, concat_axis=0, tiled=True)
        collected = add_rows(
            collected, arrived_rows[:, half_index, :].reshape(-1), incoming.reshape(-1, embed_width)
        )
        if totals is None:
            totals = partial_value
        else:
            totals = tuple((earlier + later for earlier, later in zip(totals, partial_value)))
    batch_total = sample_count * lax.axis_size("outer") * owners
    summed = lax.psum((totals[0], totals[1], totals[2]), ("outer", "inner"))
    mix_grad = summed[0] / batch_total
    lift_grad = summed[1] / batch_total
    linear_grad = summed[2] / batch_total
    complete = lax.psum(collected, "outer")
    new_table, new_accum = adagrad(table, row_accum, complete)
    return (new_table, new_accum, mix_grad, lift_grad, linear_grad)


def matmul(left, right):
    return jnp.dot(left, right, preferred_element_type=jnp.float32)


def matmul_nt(left, right):
    return lax.dot_general(left, right, (((1,), (1,)), ((), ())), preferred_element_type=jnp.float32)


def one_hot(matches):
    return jnp.where(matches, 1.0, 0.0).astype(jnp.bfloat16)


def place_kernel(shift, owners, ids_ref, home_ref, rank_ref, slot_ref, count_ref):
    samples, feats = ids_ref.shape
    high, low = home_ref.shape
    half = low // 2
    home = home_ref[...]
    pieces = []
    for part in (home & 255, home >> 8):
        down = part.astype(jnp.float32).T
        pieces.append(jnp.concatenate([down[:half], down[half:]], axis=1))
    pieces = jnp.concatenate(pieces, axis=0).astype(jnp.bfloat16)
    high_at = lax.broadcasted_iota(jnp.int32, (2 * high, feats), 0)
    low_at = lax.broadcasted_iota(jnp.int32, (half, feats), 0)
    lane = lax.broadcasted_iota(jnp.int32, (1, feats), 1)
    count_lane = lax.broadcasted_iota(jnp.int32, (8, 128), 1)

    @pl.loop(0, samples // 8)
    def _(group):
        first = pl.multiple_of(group * 8, 8)
        ids = ids_ref[pl.ds(first, 8), :]
        every = range(8)
        ones = [ids[row : row + 1] for row in every]
        hots = [one_hot(high_at == ((one >> 6) & 1) * high + (one >> 7)) for one in ones]
        founds = [matmul(pieces, hot) for hot in hots]
        places = []
        for row in every:
            value = founds[row][:half] + 256.0 * founds[row][half:]
            value = jnp.where(low_at == (ones[row] & (half - 1)), value, 0.0)
            places.append(jnp.sum(value, axis=0, keepdims=True))
        place = jnp.concatenate(places, axis=0).astype(jnp.int32)
        owner_all = place >> shift
        slot_ref[pl.ds(first, 8), :] = place & ((1 << shift) - 1)
        keys = (owner_all * feats + lane).astype(jnp.float32)
        downs = [jnp.broadcast_to(keys[row : row + 1], (128, feats)).T for row in every]
        ranks = []
        for row in every:
            parts = []
            for at in range(0, feats, 128):
                less = downs[row] < keys[row : row + 1, at : at + 128]
                parts.append(jnp.sum(jnp.where(less, 1.0, 0.0), axis=0, keepdims=True))
            ranks.append(jnp.concatenate(parts, axis=1))
        rank_ref[pl.ds(first, 8), :] = jnp.concatenate(ranks, axis=0).astype(jnp.int32)
        counts = jnp.zeros((8, 128), jnp.float32)
        for owner_at in range(owners):
            number = jnp.sum(jnp.where(owner_all == owner_at, 1.0, 0.0), axis=1, keepdims=True)
            counts = jnp.where(count_lane == owner_at, number, counts)
        most = jnp.max(counts, axis=1, keepdims=True)
        counts = jnp.where(count_lane == owners, most, counts)
        count_ref[pl.ds(first, 8), :] = counts.astype(jnp.int32)


COPY_ROWS = 56
SCRATCH = 16


def sum_list(values):
    total = values[0]
    for value in values[1:]:
        total = total + value
    return total


def positions():
    return lax.axis_index("outer"), lax.axis_index("inner")


def grads_kernel(
    sizes,
    x_ref,
    g_ref,
    mix_ref,
    lift_ref,
    linear_ref,
    ids_ref,
    home_ref,
    *rest,
):
    group, steps, owners, per_owner, scaling, shift = sizes
    far_count = owners // 4
    keep_refs, send_refs = rest[:far_count], rest[far_count : 2 * far_count]
    rows_ref = rest[2 * far_count]
    dense_refs, scratch = rest[2 * far_count + 1 : -SCRATCH], rest[-SCRATCH:]
    rank_ref, slot_ref, found_ref, count_ref, copied = scratch[:5]
    step = pl.program_id(0)
    outer, inner = positions()

    @pl.when(step == 0)
    def _():
        place_kernel(shift, owners, ids_ref, home_ref, rank_ref, slot_ref, found_ref)
        copy = pltpu.make_async_copy(found_ref, count_ref, copied)
        copy.start()
        copy.wait()

    @pl.when((step > 0) & (step <= steps))
    def _():
        gather_rows(
            step - 1,
            outer,
            sizes,
            count_ref,
            x_ref,
            g_ref,
            mix_ref,
            lift_ref,
            linear_ref,
            rank_ref,
            slot_ref,
            dense_refs,
            *scratch[5:],
        )

    @pl.when(step > steps)
    def _():
        place = owners - 1 - (step - steps - 1)
        row_a, row_b = scratch[-4], scratch[-3]
        near = (step - steps - 1) ^ inner
        rows_ref[0, :, :128] = row_a[near, pl.ds(0, per_owner), :].astype(jnp.bfloat16)
        rows_ref[0, :, 128:] = row_b[near, pl.ds(0, per_owner), :].astype(jnp.bfloat16)
        owner = place ^ inner
        first_rows = row_a[owner, pl.ds(0, per_owner), :]
        second_rows = row_b[owner, pl.ds(0, per_owner), :]
        at = x_ref.shape[1] - 128
        build_rows(at, outer, first_rows, second_rows, place, far_count, keep_refs, send_refs)


def join_rows(count_ref, filled, sorted_a, sorted_b, row_a, row_b, step, group, owners):
    begun = (step >= 0).astype(jnp.int32)
    now = (step + 2) % 2
    first = jnp.maximum(step, 0) * group
    every = range(group)
    numbers = [[count_ref[first + k, owner] * begun for owner in range(owners)] for k in every]
    starts = [filled[owner] for owner in range(owners)]
    ends = list(starts)
    for k in every:
        begin = 0
        for owner in range(owners):
            source, target = pl.ds(begin, COPY_ROWS), pl.ds(ends[owner], COPY_ROWS)
            row_a[owner, target, :] = sorted_a[now, k, source, :]
            row_b[owner, target, :] = sorted_b[now, k, source, :]
            ends[owner] = ends[owner] + numbers[k][owner]
            begin = begin + numbers[k][owner]
    most = count_ref[first, owners] * begun
    for k in range(1, group):
        most = jnp.maximum(most, count_ref[first + k, owners] * begun)

    @pl.when(most > COPY_ROWS)
    def _():
        again = list(starts)
        for k in every:
            begin = 0
            for owner in range(owners):

                def copy(turn, carry, begin=begin, at=again[owner], owner=owner, k=k):
                    off = turn * COPY_ROWS
                    source, target = pl.ds(begin + off, COPY_ROWS), pl.ds(at + off, COPY_ROWS)
                    row_a[owner, target, :] = sorted_a[now, k, source, :]
                    row_b[owner, target, :] = sorted_b[now, k, source, :]
                    return carry

                turns = (numbers[k][owner] + COPY_ROWS - 1) // COPY_ROWS
                lax.fori_loop(0, turns, copy, 0)
                again[owner] = again[owner] + numbers[k][owner]
                begin = begin + numbers[k][owner]

    for owner in range(owners):
        filled[owner] = ends[owner]


def gather_rows(
    step,
    outer,
    sizes,
    count_ref,
    x_ref,
    g_ref,
    mix_ref,
    lift_ref,
    linear_ref,
    rank_ref,
    slot_ref,
    dense_refs,
    mix_down,
    lift_down,
    mix_sum,
    lift_sum,
    linear_sum,
    sorted_a,
    sorted_b,
    row_a,
    row_b,
    dense_ref,
    filled,
):
    group, steps, owners, _, scaling, _ = sizes
    width, feats = x_ref.shape[1:]
    rank = mix_ref.shape[1]

    @pl.when(step == 0)
    def _():
        mix_down[...] = mix_ref[...].astype(jnp.float32).T.astype(jnp.bfloat16)
        lift_down[...] = lift_ref[...].astype(jnp.float32).T.astype(jnp.bfloat16)
        mix_sum[...] = jnp.zeros_like(mix_sum)
        lift_sum[...] = jnp.zeros_like(lift_sum)
        linear_sum[...] = jnp.zeros_like(linear_sum)
        for owner in range(owners):
            filled[owner] = 0

    now = step % 2
    join_rows(count_ref, filled, sorted_a, sorted_b, row_a, row_b, step - 1, group, owners)
    row_at = lax.broadcasted_iota(jnp.int32, (feats, feats), 0)
    extra_at = lax.broadcasted_iota(jnp.int32, (feats - width, feats), 0)
    every = range(group)
    d_prods = [matmul(lift_down[...], g_ref[k]).astype(jnp.bfloat16) for k in every]
    boths = [
        matmul_nt(x_ref[k], jnp.concatenate([mix_down[...], d_prods[k]], axis=0)) for k in every
    ]
    comps = [both[:, :rank].astype(jnp.bfloat16) for both in boths]
    d_comps = [(both[:, rank:] * scaling).astype(jnp.bfloat16) for both in boths]
    x_flat = x_ref[...].reshape(group * width, feats).T
    x_flats = [x_flat[:, k * width : (k + 1) * width] for k in every]
    pairs = [
        matmul(x_flats[k], jnp.concatenate([comps[k], d_comps[k]], axis=1)) for k in every
    ]
    prods = [(pair[:, :rank] * scaling).astype(jnp.bfloat16) for pair in pairs]
    mix_sum[...] += sum_list([pair[:, rank:] for pair in pairs])
    g_all = g_ref[...].reshape(group * width, feats)
    d_all = g_all.astype(jnp.float32) + matmul(g_all, linear_ref[...])
    d_all = d_all + matmul(jnp.concatenate(d_comps, axis=0), mix_down[...])
    d_ins = [
        d_all[k * width : (k + 1) * width] + scaling * matmul(comps[k], d_prods[k]) for k in every
    ]
    moves, rows_downs = [], []
    for k in every:
        slot = slot_ref[pl.ds(step * group + k, 1), :]
        extra = jnp.where(extra_at == 0, slot >> 4, jnp.where(extra_at == 1, slot & 15, 0))
        rows_downs.append(
            jnp.concatenate(
                [d_ins[k].astype(jnp.bfloat16), extra.astype(jnp.float32).astype(jnp.bfloat16)],
                axis=0,
            )
        )
        moves.append(one_hot(row_at == rank_ref[pl.ds(step * group + k, 1), :]))
    for k in every:
        ordered = matmul_nt(moves[k], rows_downs[k])
        sorted_a[now, k, :feats] = ordered[:, :128]
        sorted_b[now, k, :feats] = ordered[:, 128:]
    linear_sum[...] += matmul(x_flat, g_all)
    lift_sum[...] += sum_list([matmul(g_ref[k], prods[k]) for k in every])

    @pl.when(step == steps - 1)
    def _():
        join_rows(count_ref, filled, sorted_a, sorted_b, row_a, row_b, step, group, owners)
        dense_ref[:feats] = mix_sum[...]
        linear = linear_sum[...].T
        for at in range(feats // 128):
            dense_ref[feats * (1 + at) : feats * (2 + at)] = linear[:, 128 * at : 128 * (at + 1)]
        dense_ref[feats * (1 + feats // 128) :] = lift_sum[...]
        piece = dense_refs[0].shape[0]
        for index, ref in enumerate(dense_refs):
            first = pl.multiple_of((index ^ outer) * piece, piece)
            ref[...] = dense_ref[pl.ds(first, piece), :]


def build_rows(at, my_outer, first_rows, second_rows, place, first, keep_refs, send_refs):
    outers, piece = 2 * keep_refs[0].shape[1], keep_refs[0].shape[3]
    per_owner = first_rows.shape[0]
    rows_down = jnp.concatenate([first_rows.T, second_rows.T[:at]], axis=0).astype(jnp.bfloat16)
    slots = second_rows[:, at : at + 1] * 16.0 + second_rows[:, at + 1 : at + 2]
    slots = slots.astype(jnp.int32)
    lanes = lax.broadcasted_iota(jnp.int32, (per_owner, piece), 1)
    totals = []
    for outer in range(outers):
        base = (outer ^ my_outer) * piece
        totals.append(matmul(rows_down, one_hot(lanes == slots - base)).astype(jnp.bfloat16))
    for index in range(len(keep_refs)):

        @pl.when(place // 2 == first + index)
        def _(index=index):
            for outer in range(outers):
                ref = (send_refs if outer % 2 else keep_refs)[index]
                ref[0, outer // 2] = totals[outer]


def part_specs(start, first, count, part):
    def spec(index):
        begin = start + 2 * (count - 1 - index)
        return pl.BlockSpec(
            (1,) + part[1:], lambda i, *_: (jnp.clip(begin + 1 - i, 0, 1), 0, 0, 0)
        )

    return [spec(index) for index in range(count)] * 2


def local_grads(x_down, g_down, mix, lift_down, linear, ids, home, owners, part):
    samples, width, feats = x_down.shape
    rank = mix.shape[1]
    group = 8
    steps = samples // group
    per_owner = samples * feats // owners
    far_count = owners // 4
    shift = (part[1] * 2 * part[3]).bit_length() - 1
    sizes = (group, steps, owners, per_owner, 1.0 / math.sqrt(width), shift)

    def whole(shape):
        return pl.BlockSpec(shape, lambda i, *_: (0,) * len(shape))

    sample_spec = pl.BlockSpec(
        (group, width, feats), lambda i: (jnp.clip(i - 1, 0, steps - 1), 0, 0)
    )
    dense_rows = feats * (1 + feats // 128) + width
    outers = 2 * part[1]
    dense_piece = (dense_rows // outers, 128)
    room = per_owner + 64
    rows_shape = (owners // 2, per_owner, 256)
    scratch = [
        pltpu.VMEM((samples, feats), jnp.int32),
        pltpu.VMEM((samples, feats), jnp.int32),
        pltpu.VMEM((samples, 128), jnp.int32),
        pltpu.SMEM((samples, 128), jnp.int32),
        pltpu.SemaphoreType.DMA,
        pltpu.VMEM((rank, feats), jnp.bfloat16),
        pltpu.VMEM((rank, width), jnp.bfloat16),
        pltpu.VMEM((feats, rank), jnp.float32),
        pltpu.VMEM((width, rank), jnp.float32),
        pltpu.VMEM((feats, feats), jnp.float32),
        pltpu.VMEM((2, group, feats + 64, 128), jnp.float32),
        pltpu.VMEM((2, group, feats + 64, 128), jnp.float32),
        pltpu.VMEM((owners, room, 128), jnp.float32),
        pltpu.VMEM((owners, room, 128), jnp.float32),
        pltpu.VMEM((dense_rows, 128), jnp.float32),
        pltpu.SMEM((owners,), jnp.int32),
    ]
    outs = pl.pallas_call(
        functools.partial(grads_kernel, sizes),
        out_shape=[jax.ShapeDtypeStruct(part, jnp.bfloat16)] * (2 * far_count)
        + [
            jax.ShapeDtypeStruct(rows_shape, jnp.bfloat16),
        ]
        + [jax.ShapeDtypeStruct(dense_piece, jnp.float32)] * outers,
        grid=(1 + steps + owners // 2,),
        in_specs=[
            sample_spec,
            sample_spec,
            whole((feats, rank)),
            whole((width, rank)),
            whole((feats, feats)),
            whole((samples, feats)),
            whole(home.shape),
        ],
        out_specs=part_specs(1 + steps, owners // 2 - far_count, far_count, part)
        + [
            pl.BlockSpec(
                (1,) + rows_shape[1:],
                lambda i: (jnp.clip(i - 1 - steps, 0, owners // 2 - 1), 0, 0),
            )
        ]
        + [whole(dense_piece)] * outers,
        scratch_shapes=scratch,
        compiler_params=pltpu.CompilerParams(vmem_limit_bytes=60 * 2**20),
        cost_estimate=pl.CostEstimate(
            flops=2 * samples * feats * feats * 3072, bytes_accessed=12 * 2**20, transcendentals=0
        ),
        name="local_grads",
    )(x_down, g_down, mix, lift_down, linear, ids, home)
    keep, send = outs[:far_count], outs[far_count : 2 * far_count]
    return keep, send, outs[2 * far_count], outs[2 * far_count + 1 :]


def build_kernel(at, rows_ref, *refs):
    half = len(refs) // 2
    rows = rows_ref[0].astype(jnp.float32)
    place = 2 * half - 1 - pl.program_id(0)
    keep_refs, send_refs = refs[:half], refs[half:]
    outer, _ = positions()
    build_rows(at, outer, rows[:, :128], rows[:, 128:], place, 0, keep_refs, send_refs)


def build_parts(rows, part, width):
    places, per_owner, lanes = rows.shape
    far_count = places // 2
    outs = pl.pallas_call(
        functools.partial(build_kernel, width - 128),
        out_shape=[jax.ShapeDtypeStruct(part, jnp.bfloat16)] * places,
        grid=(places,),
        in_specs=[pl.BlockSpec((1, per_owner, lanes), lambda i: (places - 1 - i, 0, 0))],
        out_specs=part_specs(0, 0, far_count, part),
        compiler_params=pltpu.CompilerParams(vmem_limit_bytes=60 * 2**20),
        cost_estimate=pl.CostEstimate(
            flops=4 * part[3] * part[1] * part[0] * places * per_owner * lanes,
            bytes_accessed=6 * 2**20,
            transcendentals=0,
        ),
        name="build_parts",
    )(rows)
    return outs[:far_count], outs[far_count:]


def adagrad_kernel(me_ref, *refs):
    pieces, (table_ref, accum_ref) = refs[:2], refs[2:4]
    new_table_ref, new_accum_ref = refs[-2:]
    width = table_ref.shape[0]
    for index, piece in enumerate(pieces):

        @pl.when(pl.program_id(0) == index)
        def _(piece=piece):
            grad = piece[...].astype(jnp.float32)
            mean = jnp.sum(grad * grad, axis=0, keepdims=True) * (1.0 / width)
            updated = accum_ref[...] + mean
            new_accum_ref[...] = updated
            new_table_ref[...] = table_ref[...] - grad * (LEARN_RATE / jnp.sqrt(updated))


def update_table(me, pieces, table_down, accum, first, done=()):
    width, table_rows = table_down.shape
    piece = pieces[0].shape[1]

    def moved(rows):
        return pl.BlockSpec((rows, piece), lambda i, me: (0, (first + i) ^ me[0]))

    return pl.pallas_call(
        adagrad_kernel,
        out_shape=(
            jax.ShapeDtypeStruct((width, table_rows), jnp.float32),
            jax.ShapeDtypeStruct((1, table_rows), jnp.float32),
        ),
        grid_spec=pltpu.PrefetchScalarGridSpec(
            num_scalar_prefetch=1,
            grid=(2,),
            in_specs=[pl.BlockSpec(memory_space=pltpu.VMEM)] * 2
            + [moved(width), moved(1)]
            + [pl.BlockSpec(memory_space=pl.ANY)] * len(done),
            out_specs=[moved(width), moved(1)],
        ),
        input_output_aliases={5 + i: i for i in range(len(done))},
        compiler_params=pltpu.CompilerParams(vmem_limit_bytes=16 * 2**20),
        name="update_table",
    )(me, *pieces, table_down, accum, *done)


def swap(values, axis, bit):
    size = lax.axis_size(axis)
    return lax.ppermute(values, axis, [(i, i ^ bit) for i in range(size)])


def add_half(first, second):
    return (first.astype(jnp.float32) + second.astype(jnp.float32)).astype(jnp.bfloat16)


def tree_sum(values):
    while len(values) > 1:
        values = [values[i] + values[i + 1] for i in range(0, len(values), 2)]
    return values[0]


def after(value, *ready):
    return lax.optimization_barrier((value,) + ready)[0]


def stacked(dense, other, side):
    return jnp.where(side == 0, jnp.stack([dense, other]), jnp.stack([other, dense]))


def sum_all(me, keep, send, rows, dense, part, width):
    owners = lax.axis_size("inner")
    outer = lax.axis_index("outer")
    far_count = owners // 2
    first = far_count - len(keep)
    keep = dict(enumerate(keep, first))
    came, parts, kept, sent, rest, second, terms, last = ({} for _ in range(8))
    far_ones, near_ones = list(reversed(range(first, far_count))), list(reversed(range(first)))

    def x_first(far):
        return (far ^ (far >> 1)) % 2 == 0

    def first_stage(far):
        held = keep[far]
        if x_first(far):
            parts[far] = add_half(held[1], came[far][1])
            kept[far] = add_half(held[0], came[far][0])
        else:
            parts[far] = add_half(held[:, 1], came[far][:, 1])
            kept[far] = add_half(held[:, 0], came[far][:, 0])

    def second_stage(far):
        parts[far] = add_half(kept[far][1], sent[far][1])
        rest[far] = add_half(kept[far][0], sent[far][0])
        second[far] = swap(parts[far], *(("outer", 2) if x_first(far) else ("inner", 1)))

    def send_first(far, ready):
        sent[far] = swap(ready, *(("inner", 1) if x_first(far) else ("outer", 2)))

    sides = (outer & 1, outer >> 1)
    for far in far_ones:
        came[far] = swap(send[far - first], "outer", 1)
    others = tuple(swap(dense[bits], "outer", bits) for bits in range(1, len(dense)))
    for far in far_ones:
        first_stage(far)
        send_first(far, parts[far])
    far_parts = [parts[far] for far in far_ones]
    rows = after(rows, *far_parts)
    low_keep, low_send = build_parts(rows, part, width)
    for far in near_ones:
        keep[far] = low_keep[far]
        came[far] = swap(low_send[far], "outer", 1)
    dense = sum_list((dense[0],) + after(others, low_send[0]))
    other = swap(dense, "inner", 1)
    arrived = after(tuple(sent[far] for far in far_ones), dense, low_send[0])
    for far, sent[far] in zip(far_ones, arrived):
        second_stage(far)
    for far in near_ones:
        first_stage(far)
    near_parts = [parts[far] for far in near_ones]
    for far in near_ones:
        send_first(far, parts[far])
    dense = dense + after(other, *near_parts)
    other = swap(dense, "inner", 2)

    def send_last(far, *ready):
        low = far & -far
        value = rest[far].astype(jnp.float32) + second[far].astype(jnp.float32)
        came_far = [terms[far + bit] for bit in (1 << at for at in range(8)) if bit < low]
        if came_far:
            for one in after(tuple(came_far), *ready):
                value = value + one.astype(jnp.float32)
        last[far] = value.astype(jnp.bfloat16)
        terms[far] = swap(last[far], "inner", 2 * low)

    for far in far_ones:
        second[far] = after(second[far], me, dense, *near_parts)
    odd_ones = [far for far in far_ones if far % 2]
    for far in odd_ones:
        send_last(far)
    odd_last = [last[far] for far in odd_ones]
    for bit in range(1, far_count.bit_length() - 1):
        dense = dense + after(other, *odd_last)
        other = swap(dense, "inner", 2 << bit)
    arrived = after(tuple(sent[far] for far in near_ones), *odd_last)
    for far, sent[far] in zip(near_ones, arrived):
        second_stage(far)
    near_parts = [parts[far] for far in near_ones]
    dense = dense + after(other, *near_parts)
    other = swap(dense, "outer", 2)
    for far in far_ones:
        if far % 2 == 0:
            send_last(far, *near_parts)
    even_last = [last[far] for far in far_ones if far % 2 == 0]
    for far in near_ones:
        second[far] = after(second[far], *even_last)
        if far:
            send_last(far)
    dense = stacked(dense, after(other, last[1]), sides[1])
    mine, came_last = after((rest[0], second[0]), dense, last[1])
    total = mine.astype(jnp.float32) + came_last.astype(jnp.float32)
    ends = tuple(terms[1 << bit] for bit in range(far_count.bit_length() - 1))
    for term in after(ends, dense, last[1]):
        total = total + term.astype(jnp.float32)
    total = total.astype(jnp.bfloat16)
    across = swap(total, "outer", 2)
    beside = swap(total, "outer", 1)
    dense = stacked(dense, swap(dense, "outer", 1), sides[0])
    lanes = dense.shape[-1]
    return total, beside, across, jnp.transpose(dense, (1, 0, 2, 3)).reshape(-1, lanes)


def dense_table(
    layer_input,
    out_grad,
    mix_weight,
    lift_weight,
    linear_weight,
    row_ids,
    row_home,
    table,
    row_accum,
):
    owners, outers = lax.axis_size("inner"), lax.axis_size("outer")
    sample_count = layer_input.shape[0]
    table_rows = table.shape[0]
    me = jnp.stack([lax.axis_index("outer"), lax.axis_index("inner")]).astype(jnp.int32)
    width = layer_input.shape[2]
    part = (2, outers // 2, width, table_rows // outers)
    keep, send, rows, dense = local_grads(
        jnp.swapaxes(layer_input, 1, 2),
        jnp.swapaxes(out_grad, 1, 2),
        mix_weight,
        lift_weight.T,
        linear_weight,
        row_ids,
        row_home.reshape(-1, 128),
        owners,
        part,
    )
    total, beside, across, dense = sum_all(me, keep, send, rows, dense, part, width)
    dense = dense * (1.0 / (sample_count * outers * owners))
    feats = layer_input.shape[1]
    linear = [dense[feats * (1 + i) : feats * (2 + i)] for i in range(feats // 128)]
    weights = (
        dense[:feats],
        dense[feats * (1 + feats // 128) :].T,
        jnp.concatenate(linear, axis=1),
    )
    table_down, accum = table.T, row_accum.reshape(1, -1)
    done = update_table(me, (total, beside), table_down, accum, 0)
    across = after(across, done[1], *weights)
    pieces = (across, swap(across, "outer", 1))
    new_table, new_accum = update_table(me, pieces, table_down, accum, 2, done)
    return (new_table.T, new_accum.reshape(-1)) + weights


def power_of_two(number):
    return number & (number - 1) == 0


def on_device(*arrays):
    owners, outers = lax.axis_size("inner"), lax.axis_size("outer")
    layer_input, mix_weight, row_home, table = (arrays[i] for i in (0, 2, 6, 7))
    samples, feats, width = layer_input.shape
    dense_fits = (
        outers == 4
        and owners % 4 == 0
        and power_of_two(owners)
        and row_home.shape[0] <= 2 * samples * feats
        and row_home.shape[0] <= 2**15
        and power_of_two(table.shape[0])
        and 512 <= table.shape[0] <= 4096
        and samples % 16 == 0
        and (feats * (1 + feats // 128) + width) % 64 == 0
        and feats == 256
        and mix_weight.shape[1] == 128
        and 2 * (width - 128) == 128
    )
    return dense_table(*arrays) if dense_fits else routed_rows(*arrays)


def solution(mesh):
    placed = (
        P(("outer", "inner"), None, None),
        P(("outer", "inner"), None, None),
        P(),
        P(),
        P(),
        P(("outer", "inner"), None),
        P(),
        P("inner", None),
        P("inner"),
    )
    return jax.shard_map(
        on_device,
        mesh=mesh,
        in_specs=placed,
        out_specs=(P("inner", None), P("inner"), P(), P(), P()),
        check_vma=False,
    )
```

```python
import functools
import math

import jax
import jax.numpy as jnp
from jax import lax
from jax.experimental import pallas as pl
from jax.experimental.pallas import tpu as pltpu
from jax.sharding import PartitionSpec as P

LEARN_RATE = 0.5


def interaction_grads(inputs, cotangent, mix_weight, lift_weight, linear_weight, scaling):
    compressed = jnp.einsum(
        "bfd,fk->bdk", inputs, mix_weight, preferred_element_type=jnp.float32
    ).astype(jnp.bfloat16)
    products = (
        jnp.einsum("bfd,bdk->bfk", inputs, compressed, preferred_element_type=jnp.float32) * scaling
    ).astype(jnp.bfloat16)
    d_products = jnp.einsum(
        "bfd,kd->bfk", cotangent, lift_weight, preferred_element_type=jnp.float32
    ).astype(jnp.bfloat16)
    d_compressed = (
        jnp.einsum("bfd,bfk->bdk", inputs, d_products, preferred_element_type=jnp.float32) * scaling
    ).astype(jnp.bfloat16)
    d_inputs = cotangent.astype(jnp.float32)
    d_inputs = d_inputs + jnp.einsum(
        "fg,bfd->bgd", linear_weight, cotangent, preferred_element_type=jnp.float32
    )
    d_inputs = d_inputs + scaling * jnp.einsum(
        "bfk,bdk->bfd", d_products, compressed, preferred_element_type=jnp.float32
    )
    d_inputs = d_inputs + jnp.einsum(
        "fk,bdk->bfd", mix_weight, d_compressed, preferred_element_type=jnp.float32
    )
    g_mix = jnp.einsum("bfd,bdk->fk", inputs, d_compressed, preferred_element_type=jnp.float32)
    g_lift = jnp.einsum("bfk,bfd->kd", products, cotangent, preferred_element_type=jnp.float32)
    g_linear = jnp.einsum("bfd,bgd->fg", cotangent, inputs, preferred_element_type=jnp.float32)
    rows_out = d_inputs.astype(jnp.bfloat16).reshape(-1, d_inputs.shape[2])
    return (rows_out, (g_mix, g_lift, g_linear))


def adagrad(weights, history, gradient):
    updated = history + jnp.mean(gradient * gradient, axis=1)
    return (weights - LEARN_RATE * gradient / jnp.sqrt(updated)[:, None], updated)


def owner_ranks(owner_of, owners):
    lookups = owner_of.shape[0]
    width = math.gcd(lookups, 128)
    groups = lookups // width
    hot = (owner_of[:, None] == jnp.arange(owners, dtype=jnp.int32)[None, :]).astype(jnp.bfloat16)
    hot = hot.reshape(groups, width, owners)
    lower = (jnp.arange(width)[:, None] > jnp.arange(width)[None, :]).astype(jnp.bfloat16)
    within = jnp.einsum("ij,gjo->gio", lower, hot, preferred_element_type=jnp.float32)
    totals = jnp.sum(hot.astype(jnp.float32), axis=1)
    before = jnp.cumsum(totals, axis=0) - totals
    counted = jnp.sum(hot.astype(jnp.float32) * (within + before[:, None, :]), axis=2)
    return counted.reshape(-1).astype(jnp.int32)


def add_rows(collected, slots, values):
    count = values.shape[0]
    table_rows = collected.shape[0]
    width = math.gcd(count, 2048)
    columns = jnp.arange(table_rows, dtype=jnp.int32)
    for block_index in range(count // width):
        start = block_index * width
        hot = (slots[start : start + width, None] == columns[None, :]).astype(jnp.bfloat16)
        collected = collected + jnp.einsum(
            "lr,ld->rd", hot, values[start : start + width], preferred_element_type=jnp.float32
        )
    return collected


def routed_rows(
    layer_input,
    out_grad,
    mix_weight,
    lift_weight,
    linear_weight,
    row_ids,
    row_home,
    table,
    row_accum,
):
    owners = lax.axis_size("inner")
    sample_count, feature_count, embed_width = layer_input.shape
    table_rows = table.shape[0]
    half_samples = sample_count // 2
    lookups = sample_count * feature_count
    per_owner = lookups // (2 * owners)
    scaling = 1.0 / math.sqrt(embed_width)
    placed = jnp.take(row_home, row_ids.reshape(-1), axis=0)
    owner_of = placed // table_rows
    target = owner_of * (2 * per_owner) + owner_ranks(owner_of, owners)
    ordering = jnp.zeros((lookups,), jnp.int32).at[target].set(jnp.arange(lookups, dtype=jnp.int32))
    ordering = ordering.reshape(owners, 2, per_owner)
    local_rows = (
        jnp.zeros((lookups,), jnp.int32)
        .at[target]
        .set(placed % table_rows)
        .reshape(owners, 2 * per_owner)
    )
    arrived_rows = lax.all_to_all(
        local_rows, "inner", split_axis=0, concat_axis=0, tiled=True
    ).reshape(owners, 2, per_owner)
    collected = jnp.zeros((table_rows, embed_width), jnp.float32)
    totals = None
    for half_index in range(2):
        first_sample = half_index * half_samples
        rows_out, partial_value = interaction_grads(
            layer_input[first_sample : first_sample + half_samples],
            out_grad[first_sample : first_sample + half_samples],
            mix_weight,
            lift_weight,
            linear_weight,
            scaling,
        )
        picked = ordering[:, half_index, :] - half_index * half_samples * feature_count
        outgoing = jnp.take(rows_out, picked.reshape(-1), axis=0).reshape(
            owners, per_owner, embed_width
        )
        incoming = lax.all_to_all(outgoing, "inner", split_axis=0, concat_axis=0, tiled=True)
        collected = add_rows(
            collected, arrived_rows[:, half_index, :].reshape(-1), incoming.reshape(-1, embed_width)
        )
        if totals is None:
            totals = partial_value
        else:
            totals = tuple((earlier + later for earlier, later in zip(totals, partial_value)))
    batch_total = sample_count * lax.axis_size("outer") * owners
    summed = lax.psum((totals[0], totals[1], totals[2]), ("outer", "inner"))
    mix_grad = summed[0] / batch_total
    lift_grad = summed[1] / batch_total
    linear_grad = summed[2] / batch_total
    complete = lax.psum(collected, "outer")
    new_table, new_accum = adagrad(table, row_accum, complete)
    return (new_table, new_accum, mix_grad, lift_grad, linear_grad)


def matmul(left, right):
    return jnp.dot(left, right, preferred_element_type=jnp.float32)


def matmul_nt(left, right):
    return lax.dot_general(left, right, (((1,), (1,)), ((), ())), preferred_element_type=jnp.float32)


def one_hot(matches):
    return jnp.where(matches, 1.0, 0.0).astype(jnp.bfloat16)


def place_kernel(shift, owners, ids_ref, home_ref, rank_ref, slot_ref, count_ref):
    samples, feats = ids_ref.shape
    high, low = home_ref.shape
    half = low // 2
    home = home_ref[...]
    pieces = []
    for part in (home & 255, home >> 8):
        down = part.astype(jnp.float32).T
        pieces.append(jnp.concatenate([down[:half], down[half:]], axis=1))
    pieces = jnp.concatenate(pieces, axis=0).astype(jnp.bfloat16)
    high_at = lax.broadcasted_iota(jnp.int32, (2 * high, feats), 0)
    low_at = lax.broadcasted_iota(jnp.int32, (half, feats), 0)
    lane = lax.broadcasted_iota(jnp.int32, (1, feats), 1)
    count_lane = lax.broadcasted_iota(jnp.int32, (8, 128), 1)

    @pl.loop(0, samples // 8)
    def _(group):
        first = pl.multiple_of(group * 8, 8)
        ids = ids_ref[pl.ds(first, 8), :]
        every = range(8)
        ones = [ids[row : row + 1] for row in every]
        hots = [one_hot(high_at == ((one >> 6) & 1) * high + (one >> 7)) for one in ones]
        founds = [matmul(pieces, hot) for hot in hots]
        places = []
        for row in every:
            value = founds[row][:half] + 256.0 * founds[row][half:]
            value = jnp.where(low_at == (ones[row] & (half - 1)), value, 0.0)
            places.append(jnp.sum(value, axis=0, keepdims=True))
        place = jnp.concatenate(places, axis=0).astype(jnp.int32)
        owner_all = place >> shift
        slot_ref[pl.ds(first, 8), :] = place & ((1 << shift) - 1)
        keys = (owner_all * feats + lane).astype(jnp.float32)
        downs = [jnp.broadcast_to(keys[row : row + 1], (128, feats)).T for row in every]
        ranks = []
        for row in every:
            parts = []
            for at in range(0, feats, 128):
                less = downs[row] < keys[row : row + 1, at : at + 128]
                parts.append(jnp.sum(jnp.where(less, 1.0, 0.0), axis=0, keepdims=True))
            ranks.append(jnp.concatenate(parts, axis=1))
        rank_ref[pl.ds(first, 8), :] = jnp.concatenate(ranks, axis=0).astype(jnp.int32)
        counts = jnp.zeros((8, 128), jnp.float32)
        for owner_at in range(owners):
            number = jnp.sum(jnp.where(owner_all == owner_at, 1.0, 0.0), axis=1, keepdims=True)
            counts = jnp.where(count_lane == owner_at, number, counts)
        most = jnp.max(counts, axis=1, keepdims=True)
        counts = jnp.where(count_lane == owners, most, counts)
        count_ref[pl.ds(first, 8), :] = counts.astype(jnp.int32)


COPY_ROWS = 56
SCRATCH = 16


def sum_list(values):
    total = values[0]
    for value in values[1:]:
        total = total + value
    return total


def positions():
    return lax.axis_index("outer"), lax.axis_index("inner")


def grads_kernel(
    sizes,
    x_ref,
    g_ref,
    mix_ref,
    lift_ref,
    linear_ref,
    ids_ref,
    home_ref,
    *rest,
):
    group, steps, owners, per_owner, scaling, shift = sizes
    far_count = owners // 4
    keep_refs, send_refs = rest[:far_count], rest[far_count : 2 * far_count]
    rows_ref = rest[2 * far_count]
    dense_refs, scratch = rest[2 * far_count + 1 : -SCRATCH], rest[-SCRATCH:]
    rank_ref, slot_ref, found_ref, count_ref, copied = scratch[:5]
    step = pl.program_id(0)
    outer, inner = positions()

    @pl.when(step == 0)
    def _():
        place_kernel(shift, owners, ids_ref, home_ref, rank_ref, slot_ref, found_ref)
        copy = pltpu.make_async_copy(found_ref, count_ref, copied)
        copy.start()
        copy.wait()

    @pl.when((step > 0) & (step <= steps))
    def _():
        gather_rows(
            step - 1,
            outer,
            sizes,
            count_ref,
            x_ref,
            g_ref,
            mix_ref,
            lift_ref,
            linear_ref,
            rank_ref,
            slot_ref,
            dense_refs,
            *scratch[5:],
        )

    @pl.when(step > steps)
    def _():
        place = owners - 1 - (step - steps - 1)
        row_a, row_b = scratch[-4], scratch[-3]
        near = (step - steps - 1) ^ inner
        rows_ref[0, :, :128] = row_a[near, pl.ds(0, per_owner), :].astype(jnp.bfloat16)
        rows_ref[0, :, 128:] = row_b[near, pl.ds(0, per_owner), :].astype(jnp.bfloat16)
        owner = place ^ inner
        first_rows = row_a[owner, pl.ds(0, per_owner), :]
        second_rows = row_b[owner, pl.ds(0, per_owner), :]
        at = x_ref.shape[1] - 128
        build_rows(at, outer, first_rows, second_rows, place, far_count, keep_refs, send_refs)


def join_rows(count_ref, filled, sorted_a, sorted_b, row_a, row_b, step, group, owners):
    begun = (step >= 0).astype(jnp.int32)
    now = (step + 2) % 2
    first = jnp.maximum(step, 0) * group
    every = range(group)
    numbers = [[count_ref[first + k, owner] * begun for owner in range(owners)] for k in every]
    starts = [filled[owner] for owner in range(owners)]
    ends = list(starts)
    for k in every:
        begin = 0
        for owner in range(owners):
            source, target = pl.ds(begin, COPY_ROWS), pl.ds(ends[owner], COPY_ROWS)
            row_a[owner, target, :] = sorted_a[now, k, source, :]
            row_b[owner, target, :] = sorted_b[now, k, source, :]
            ends[owner] = ends[owner] + numbers[k][owner]
            begin = begin + numbers[k][owner]
    most = count_ref[first, owners] * begun
    for k in range(1, group):
        most = jnp.maximum(most, count_ref[first + k, owners] * begun)

    @pl.when(most > COPY_ROWS)
    def _():
        again = list(starts)
        for k in every:
            begin = 0
            for owner in range(owners):

                def copy(turn, carry, begin=begin, at=again[owner], owner=owner, k=k):
                    off = turn * COPY_ROWS
                    source, target = pl.ds(begin + off, COPY_ROWS), pl.ds(at + off, COPY_ROWS)
                    row_a[owner, target, :] = sorted_a[now, k, source, :]
                    row_b[owner, target, :] = sorted_b[now, k, source, :]
                    return carry

                turns = (numbers[k][owner] + COPY_ROWS - 1) // COPY_ROWS
                lax.fori_loop(0, turns, copy, 0)
                again[owner] = again[owner] + numbers[k][owner]
                begin = begin + numbers[k][owner]

    for owner in range(owners):
        filled[owner] = ends[owner]


def gather_rows(
    step,
    outer,
    sizes,
    count_ref,
    x_ref,
    g_ref,
    mix_ref,
    lift_ref,
    linear_ref,
    rank_ref,
    slot_ref,
    dense_refs,
    mix_down,
    lift_down,
    mix_sum,
    lift_sum,
    linear_sum,
    sorted_a,
    sorted_b,
    row_a,
    row_b,
    dense_ref,
    filled,
):
    group, steps, owners, _, scaling, _ = sizes
    width, feats = x_ref.shape[1:]
    rank = mix_ref.shape[1]

    @pl.when(step == 0)
    def _():
        mix_down[...] = mix_ref[...].astype(jnp.float32).T.astype(jnp.bfloat16)
        lift_down[...] = lift_ref[...].astype(jnp.float32).T.astype(jnp.bfloat16)
        mix_sum[...] = jnp.zeros_like(mix_sum)
        lift_sum[...] = jnp.zeros_like(lift_sum)
        linear_sum[...] = jnp.zeros_like(linear_sum)
        for owner in range(owners):
            filled[owner] = 0

    now = step % 2
    join_rows(count_ref, filled, sorted_a, sorted_b, row_a, row_b, step - 1, group, owners)
    row_at = lax.broadcasted_iota(jnp.int32, (feats, feats), 0)
    extra_at = lax.broadcasted_iota(jnp.int32, (feats - width, feats), 0)
    every = range(group)
    d_prods = [matmul(lift_down[...], g_ref[k]).astype(jnp.bfloat16) for k in every]
    boths = [
        matmul_nt(x_ref[k], jnp.concatenate([mix_down[...], d_prods[k]], axis=0)) for k in every
    ]
    comps = [both[:, :rank].astype(jnp.bfloat16) for both in boths]
    d_comps = [(both[:, rank:] * scaling).astype(jnp.bfloat16) for both in boths]
    x_flat = x_ref[...].reshape(group * width, feats).T
    x_flats = [x_flat[:, k * width : (k + 1) * width] for k in every]
    pairs = [
        matmul(x_flats[k], jnp.concatenate([comps[k], d_comps[k]], axis=1)) for k in every
    ]
    prods = [(pair[:, :rank] * scaling).astype(jnp.bfloat16) for pair in pairs]
    mix_sum[...] += sum_list([pair[:, rank:] for pair in pairs])
    g_all = g_ref[...].reshape(group * width, feats)
    d_all = g_all.astype(jnp.float32) + matmul(g_all, linear_ref[...])
    d_all = d_all + matmul(jnp.concatenate(d_comps, axis=0), mix_down[...])
    d_ins = [
        d_all[k * width : (k + 1) * width] + scaling * matmul(comps[k], d_prods[k]) for k in every
    ]
    moves, rows_downs = [], []
    for k in every:
        slot = slot_ref[pl.ds(step * group + k, 1), :]
        extra = jnp.where(extra_at == 0, slot >> 4, jnp.where(extra_at == 1, slot & 15, 0))
        rows_downs.append(
            jnp.concatenate(
                [d_ins[k].astype(jnp.bfloat16), extra.astype(jnp.float32).astype(jnp.bfloat16)],
                axis=0,
            )
        )
        moves.append(one_hot(row_at == rank_ref[pl.ds(step * group + k, 1), :]))
    for k in every:
        ordered = matmul_nt(moves[k], rows_downs[k])
        sorted_a[now, k, :feats] = ordered[:, :128]
        sorted_b[now, k, :feats] = ordered[:, 128:]
    linear_sum[...] += matmul(x_flat, g_all)
    lift_sum[...] += sum_list([matmul(g_ref[k], prods[k]) for k in every])

    @pl.when(step == steps - 1)
    def _():
        join_rows(count_ref, filled, sorted_a, sorted_b, row_a, row_b, step, group, owners)
        dense_ref[:feats] = mix_sum[...]
        linear = linear_sum[...].T
        for at in range(feats // 128):
            dense_ref[feats * (1 + at) : feats * (2 + at)] = linear[:, 128 * at : 128 * (at + 1)]
        dense_ref[feats * (1 + feats // 128) :] = lift_sum[...]
        piece = dense_refs[0].shape[0]
        for index, ref in enumerate(dense_refs):
            first = pl.multiple_of((index ^ outer) * piece, piece)
            ref[...] = dense_ref[pl.ds(first, piece), :]


def build_rows(at, my_outer, first_rows, second_rows, place, first, keep_refs, send_refs):
    outers, piece = 2 * keep_refs[0].shape[1], keep_refs[0].shape[3]
    per_owner = first_rows.shape[0]
    rows_down = jnp.concatenate([first_rows.T, second_rows.T[:at]], axis=0).astype(jnp.bfloat16)
    slots = second_rows[:, at : at + 1] * 16.0 + second_rows[:, at + 1 : at + 2]
    slots = slots.astype(jnp.int32)
    lanes = lax.broadcasted_iota(jnp.int32, (per_owner, piece), 1)
    totals = []
    for outer in range(outers):
        base = (outer ^ my_outer) * piece
        totals.append(matmul(rows_down, one_hot(lanes == slots - base)).astype(jnp.bfloat16))
    for index in range(len(keep_refs)):

        @pl.when(place // 2 == first + index)
        def _(index=index):
            for outer in range(outers):
                ref = (send_refs if outer % 2 else keep_refs)[index]
                ref[0, outer // 2] = totals[outer]


def part_specs(start, first, count, part):
    def spec(index):
        begin = start + 2 * (count - 1 - index)
        return pl.BlockSpec(
            (1,) + part[1:], lambda i, *_: (jnp.clip(begin + 1 - i, 0, 1), 0, 0, 0)
        )

    return [spec(index) for index in range(count)] * 2


def local_grads(x_down, g_down, mix, lift_down, linear, ids, home, owners, part):
    samples, width, feats = x_down.shape
    rank = mix.shape[1]
    group = 16
    steps = samples // group
    per_owner = samples * feats // owners
    far_count = owners // 4
    shift = (part[1] * 2 * part[3]).bit_length() - 1
    sizes = (group, steps, owners, per_owner, 1.0 / math.sqrt(width), shift)

    def whole(shape):
        return pl.BlockSpec(shape, lambda i, *_: (0,) * len(shape))

    sample_spec = pl.BlockSpec(
        (group, width, feats), lambda i: (jnp.clip(i - 1, 0, steps - 1), 0, 0)
    )
    dense_rows = feats * (1 + feats // 128) + width
    outers = 2 * part[1]
    dense_piece = (dense_rows // outers, 128)
    room = per_owner + 64
    rows_shape = (owners // 2, per_owner, 256)
    scratch = [
        pltpu.VMEM((samples, feats), jnp.int32),
        pltpu.VMEM((samples, feats), jnp.int32),
        pltpu.VMEM((samples, 128), jnp.int32),
        pltpu.SMEM((samples, 128), jnp.int32),
        pltpu.SemaphoreType.DMA,
        pltpu.VMEM((rank, feats), jnp.bfloat16),
        pltpu.VMEM((rank, width), jnp.bfloat16),
        pltpu.VMEM((feats, rank), jnp.float32),
        pltpu.VMEM((width, rank), jnp.float32),
        pltpu.VMEM((feats, feats), jnp.float32),
        pltpu.VMEM((2, group, feats + 64, 128), jnp.float32),
        pltpu.VMEM((2, group, feats + 64, 128), jnp.float32),
        pltpu.VMEM((owners, room, 128), jnp.float32),
        pltpu.VMEM((owners, room, 128), jnp.float32),
        pltpu.VMEM((dense_rows, 128), jnp.float32),
        pltpu.SMEM((owners,), jnp.int32),
    ]
    outs = pl.pallas_call(
        functools.partial(grads_kernel, sizes),
        out_shape=[jax.ShapeDtypeStruct(part, jnp.bfloat16)] * (2 * far_count)
        + [
            jax.ShapeDtypeStruct(rows_shape, jnp.bfloat16),
        ]
        + [jax.ShapeDtypeStruct(dense_piece, jnp.float32)] * outers,
        grid=(1 + steps + owners // 2,),
        in_specs=[
            sample_spec,
            sample_spec,
            whole((feats, rank)),
            whole((width, rank)),
            whole((feats, feats)),
            whole((samples, feats)),
            whole(home.shape),
        ],
        out_specs=part_specs(1 + steps, owners // 2 - far_count, far_count, part)
        + [
            pl.BlockSpec(
                (1,) + rows_shape[1:],
                lambda i: (jnp.clip(i - 1 - steps, 0, owners // 2 - 1), 0, 0),
            )
        ]
        + [whole(dense_piece)] * outers,
        scratch_shapes=scratch,
        compiler_params=pltpu.CompilerParams(vmem_limit_bytes=60 * 2**20),
        cost_estimate=pl.CostEstimate(
            flops=2 * samples * feats * feats * 3072, bytes_accessed=12 * 2**20, transcendentals=0
        ),
        name="local_grads",
    )(x_down, g_down, mix, lift_down, linear, ids, home)
    keep, send = outs[:far_count], outs[far_count : 2 * far_count]
    return keep, send, outs[2 * far_count], outs[2 * far_count + 1 :]


def build_kernel(at, rows_ref, *refs):
    half = len(refs) // 2
    rows = rows_ref[0].astype(jnp.float32)
    place = 2 * half - 1 - pl.program_id(0)
    keep_refs, send_refs = refs[:half], refs[half:]
    outer, _ = positions()
    build_rows(at, outer, rows[:, :128], rows[:, 128:], place, 0, keep_refs, send_refs)


def build_parts(rows, part, width):
    places, per_owner, lanes = rows.shape
    far_count = places // 2
    outs = pl.pallas_call(
        functools.partial(build_kernel, width - 128),
        out_shape=[jax.ShapeDtypeStruct(part, jnp.bfloat16)] * places,
        grid=(places,),
        in_specs=[pl.BlockSpec((1, per_owner, lanes), lambda i: (places - 1 - i, 0, 0))],
        out_specs=part_specs(0, 0, far_count, part),
        compiler_params=pltpu.CompilerParams(vmem_limit_bytes=60 * 2**20),
        cost_estimate=pl.CostEstimate(
            flops=4 * part[3] * part[1] * part[0] * places * per_owner * lanes,
            bytes_accessed=6 * 2**20,
            transcendentals=0,
        ),
        name="build_parts",
    )(rows)
    return outs[:far_count], outs[far_count:]


def adagrad_kernel(me_ref, *refs):
    pieces, (table_ref, accum_ref) = refs[:2], refs[2:4]
    new_table_ref, new_accum_ref = refs[-2:]
    width = table_ref.shape[0]
    for index, piece in enumerate(pieces):

        @pl.when(pl.program_id(0) == index)
        def _(piece=piece):
            grad = piece[...].astype(jnp.float32)
            mean = jnp.sum(grad * grad, axis=0, keepdims=True) * (1.0 / width)
            updated = accum_ref[...] + mean
            new_accum_ref[...] = updated
            new_table_ref[...] = table_ref[...] - grad * (LEARN_RATE / jnp.sqrt(updated))


def update_table(me, pieces, table_down, accum, first, done=()):
    width, table_rows = table_down.shape
    piece = pieces[0].shape[1]

    def moved(rows):
        return pl.BlockSpec((rows, piece), lambda i, me: (0, (first + i) ^ me[0]))

    return pl.pallas_call(
        adagrad_kernel,
        out_shape=(
            jax.ShapeDtypeStruct((width, table_rows), jnp.float32),
            jax.ShapeDtypeStruct((1, table_rows), jnp.float32),
        ),
        grid_spec=pltpu.PrefetchScalarGridSpec(
            num_scalar_prefetch=1,
            grid=(2,),
            in_specs=[pl.BlockSpec(memory_space=pltpu.VMEM)] * 2
            + [moved(width), moved(1)]
            + [pl.BlockSpec(memory_space=pl.ANY)] * len(done),
            out_specs=[moved(width), moved(1)],
        ),
        input_output_aliases={5 + i: i for i in range(len(done))},
        compiler_params=pltpu.CompilerParams(vmem_limit_bytes=16 * 2**20),
        name="update_table",
    )(me, *pieces, table_down, accum, *done)


def swap(values, axis, bit):
    size = lax.axis_size(axis)
    return lax.ppermute(values, axis, [(i, i ^ bit) for i in range(size)])


def add_half(first, second):
    return (first.astype(jnp.float32) + second.astype(jnp.float32)).astype(jnp.bfloat16)


def tree_sum(values):
    while len(values) > 1:
        values = [values[i] + values[i + 1] for i in range(0, len(values), 2)]
    return values[0]


def after(value, *ready):
    return lax.optimization_barrier((value,) + ready)[0]


def halves(dense, side):
    cut = dense.reshape(2, dense.shape[0] // 2, dense.shape[1])
    mine = lax.dynamic_index_in_dim(cut, side, 0, keepdims=False)
    return mine, lax.dynamic_index_in_dim(cut, 1 - side, 0, keepdims=False)


def stacked(dense, other, side):
    return jnp.where(side == 0, jnp.stack([dense, other]), jnp.stack([other, dense]))


def sum_all(me, keep, send, rows, dense, part, width):
    owners = lax.axis_size("inner")
    outer, inner = lax.axis_index("outer"), lax.axis_index("inner")
    far_count = owners // 2
    first = far_count - len(keep)
    keep = dict(enumerate(keep, first))
    came, parts, kept, sent, rest, second, terms, last = ({} for _ in range(8))
    far_ones, near_ones = list(reversed(range(first, far_count))), list(reversed(range(first)))

    def first_stage(far):
        held = keep[far]
        if far % 2:
            parts[far] = add_half(held[1], came[far][1])
            kept[far] = add_half(held[0], came[far][0])
        else:
            parts[far] = add_half(held[:, 1], came[far][:, 1])
            kept[far] = add_half(held[:, 0], came[far][:, 0])

    def second_stage(far):
        parts[far] = add_half(kept[far][1], sent[far][1])
        rest[far] = add_half(kept[far][0], sent[far][0])
        second[far] = swap(parts[far], *(("outer", 2) if far % 2 else ("inner", 1)))

    def send_first(far, ready):
        sent[far] = swap(ready, *(("inner", 1) if far % 2 else ("outer", 2)))

    sides = (outer & 1, outer >> 1, inner & 1)
    for far in far_ones:
        came[far] = swap(send[far - first], "outer", 1)
    others = tuple(swap(dense[bits], "outer", bits) for bits in range(1, len(dense)))
    for far in far_ones:
        first_stage(far)
        send_first(far, parts[far])
    far_parts = [parts[far] for far in far_ones]
    rows = after(rows, *far_parts)
    low_keep, low_send = build_parts(rows, part, width)
    for far in near_ones:
        keep[far] = low_keep[far]
        came[far] = swap(low_send[far], "outer", 1)
    dense = sum_list((dense[0],) + after(others, low_send[0]))
    mine, other = halves(dense, sides[2])
    other = swap(other, "inner", 1)
    for far in far_ones:
        second_stage(far)
    for far in near_ones:
        first_stage(far)
    near_parts = [parts[far] for far in near_ones]
    for far in near_ones:
        send_first(far, parts[far])
    dense = mine + after(other, *near_parts)
    other = swap(dense, "inner", 2)

    def send_last(far, *ready):
        low = far & -far
        value = rest[far].astype(jnp.float32) + second[far].astype(jnp.float32)
        came_far = [terms[far + bit] for bit in (1 << at for at in range(8)) if bit < low]
        if came_far:
            for one in after(tuple(came_far), *ready):
                value = value + one.astype(jnp.float32)
        last[far] = value.astype(jnp.bfloat16)
        terms[far] = swap(last[far], "inner", 2 * low)

    for far in far_ones:
        second[far] = after(second[far], me, dense, *near_parts)
    odd_ones = [far for far in far_ones if far % 2]
    for far in odd_ones:
        send_last(far)
    odd_last = [last[far] for far in odd_ones]
    for bit in range(1, far_count.bit_length() - 1):
        dense = dense + after(other, *odd_last)
        other = swap(dense, "inner", 2 << bit)
    arrived = after(tuple(sent[far] for far in near_ones), *odd_last)
    for far, sent[far] in zip(near_ones, arrived):
        second_stage(far)
    near_parts = [parts[far] for far in near_ones]
    dense = dense + after(other, *near_parts)
    other = swap(dense, "inner", 1)
    for far in far_ones:
        if far % 2 == 0:
            send_last(far, *near_parts)
    even_last = [last[far] for far in far_ones if far % 2 == 0]
    for far in near_ones:
        second[far] = after(second[far], *even_last)
        if far:
            send_last(far)
    dense = stacked(dense, after(other, last[1]), sides[2])
    other = swap(dense, "outer", 2)
    dense = stacked(dense, after(other, second[0], terms[2]), sides[1])
    mine, came_last = after((rest[0], second[0]), dense, last[1])
    total = mine.astype(jnp.float32) + came_last.astype(jnp.float32)
    ends = tuple(terms[1 << bit] for bit in range(far_count.bit_length() - 1))
    for term in after(ends, dense, last[1]):
        total = total + term.astype(jnp.float32)
    total = total.astype(jnp.bfloat16)
    across = swap(total, "outer", 2)
    beside = swap(total, "outer", 1)
    dense = stacked(dense, swap(dense, "outer", 1), sides[0])
    lanes = dense.shape[-1]
    return total, beside, across, jnp.transpose(dense, (1, 0, 2, 3, 4)).reshape(-1, lanes)


def dense_table(
    layer_input,
    out_grad,
    mix_weight,
    lift_weight,
    linear_weight,
    row_ids,
    row_home,
    table,
    row_accum,
):
    owners, outers = lax.axis_size("inner"), lax.axis_size("outer")
    sample_count = layer_input.shape[0]
    table_rows = table.shape[0]
    me = jnp.stack([lax.axis_index("outer"), lax.axis_index("inner")]).astype(jnp.int32)
    width = layer_input.shape[2]
    part = (2, outers // 2, width, table_rows // outers)
    keep, send, rows, dense = local_grads(
        jnp.swapaxes(layer_input, 1, 2),
        jnp.swapaxes(out_grad, 1, 2),
        mix_weight,
        lift_weight.T,
        linear_weight,
        row_ids,
        row_home.reshape(-1, 128),
        owners,
        part,
    )
    total, beside, across, dense = sum_all(me, keep, send, rows, dense, part, width)
    dense = dense * (1.0 / (sample_count * outers * owners))
    feats = layer_input.shape[1]
    linear = [dense[feats * (1 + i) : feats * (2 + i)] for i in range(feats // 128)]
    weights = (
        dense[:feats],
        dense[feats * (1 + feats // 128) :].T,
        jnp.concatenate(linear, axis=1),
    )
    table_down, accum = table.T, row_accum.reshape(1, -1)
    done = update_table(me, (total, beside), table_down, accum, 0)
    across = after(across, done[1], *weights)
    pieces = (across, swap(across, "outer", 1))
    new_table, new_accum = update_table(me, pieces, table_down, accum, 2, done)
    return (new_table.T, new_accum.reshape(-1)) + weights


def power_of_two(number):
    return number & (number - 1) == 0


def on_device(*arrays):
    owners, outers = lax.axis_size("inner"), lax.axis_size("outer")
    layer_input, mix_weight, row_home, table = (arrays[i] for i in (0, 2, 6, 7))
    samples, feats, width = layer_input.shape
    dense_fits = (
        outers == 4
        and owners % 4 == 0
        and power_of_two(owners)
        and row_home.shape[0] <= 2 * samples * feats
        and row_home.shape[0] <= 2**15
        and power_of_two(table.shape[0])
        and 512 <= table.shape[0] <= 4096
        and samples % 16 == 0
        and (feats * (1 + feats // 128) + width) % 64 == 0
        and feats == 256
        and mix_weight.shape[1] == 128
        and 2 * (width - 128) == 128
    )
    return dense_table(*arrays) if dense_fits else routed_rows(*arrays)


def solution(mesh):
    placed = (
        P(("outer", "inner"), None, None),
        P(("outer", "inner"), None, None),
        P(),
        P(),
        P(),
        P(("outer", "inner"), None),
        P(),
        P("inner", None),
        P("inner"),
    )
    return jax.shard_map(
        on_device,
        mesh=mesh,
        in_specs=placed,
        out_specs=(P("inner", None), P("inner"), P(), P(), P()),
        check_vma=False,
    )
```

```python
import functools
import math

import jax
import jax.numpy as jnp
from jax import lax
from jax.experimental import pallas as pl
from jax.experimental.pallas import tpu as pltpu
from jax.sharding import PartitionSpec as P

LEARN_RATE = 0.5


def interaction_grads(inputs, cotangent, mix_weight, lift_weight, linear_weight, scaling):
    compressed = jnp.einsum(
        "bfd,fk->bdk", inputs, mix_weight, preferred_element_type=jnp.float32
    ).astype(jnp.bfloat16)
    products = (
        jnp.einsum("bfd,bdk->bfk", inputs, compressed, preferred_element_type=jnp.float32) * scaling
    ).astype(jnp.bfloat16)
    d_products = jnp.einsum(
        "bfd,kd->bfk", cotangent, lift_weight, preferred_element_type=jnp.float32
    ).astype(jnp.bfloat16)
    d_compressed = (
        jnp.einsum("bfd,bfk->bdk", inputs, d_products, preferred_element_type=jnp.float32) * scaling
    ).astype(jnp.bfloat16)
    d_inputs = cotangent.astype(jnp.float32)
    d_inputs = d_inputs + jnp.einsum(
        "fg,bfd->bgd", linear_weight, cotangent, preferred_element_type=jnp.float32
    )
    d_inputs = d_inputs + scaling * jnp.einsum(
        "bfk,bdk->bfd", d_products, compressed, preferred_element_type=jnp.float32
    )
    d_inputs = d_inputs + jnp.einsum(
        "fk,bdk->bfd", mix_weight, d_compressed, preferred_element_type=jnp.float32
    )
    g_mix = jnp.einsum("bfd,bdk->fk", inputs, d_compressed, preferred_element_type=jnp.float32)
    g_lift = jnp.einsum("bfk,bfd->kd", products, cotangent, preferred_element_type=jnp.float32)
    g_linear = jnp.einsum("bfd,bgd->fg", cotangent, inputs, preferred_element_type=jnp.float32)
    rows_out = d_inputs.astype(jnp.bfloat16).reshape(-1, d_inputs.shape[2])
    return (rows_out, (g_mix, g_lift, g_linear))


def adagrad(weights, history, gradient):
    updated = history + jnp.mean(gradient * gradient, axis=1)
    return (weights - LEARN_RATE * gradient / jnp.sqrt(updated)[:, None], updated)


def owner_ranks(owner_of, owners):
    lookups = owner_of.shape[0]
    width = math.gcd(lookups, 128)
    groups = lookups // width
    hot = (owner_of[:, None] == jnp.arange(owners, dtype=jnp.int32)[None, :]).astype(jnp.bfloat16)
    hot = hot.reshape(groups, width, owners)
    lower = (jnp.arange(width)[:, None] > jnp.arange(width)[None, :]).astype(jnp.bfloat16)
    within = jnp.einsum("ij,gjo->gio", lower, hot, preferred_element_type=jnp.float32)
    totals = jnp.sum(hot.astype(jnp.float32), axis=1)
    before = jnp.cumsum(totals, axis=0) - totals
    counted = jnp.sum(hot.astype(jnp.float32) * (within + before[:, None, :]), axis=2)
    return counted.reshape(-1).astype(jnp.int32)


def add_rows(collected, slots, values):
    count = values.shape[0]
    table_rows = collected.shape[0]
    width = math.gcd(count, 2048)
    columns = jnp.arange(table_rows, dtype=jnp.int32)
    for block_index in range(count // width):
        start = block_index * width
        hot = (slots[start : start + width, None] == columns[None, :]).astype(jnp.bfloat16)
        collected = collected + jnp.einsum(
            "lr,ld->rd", hot, values[start : start + width], preferred_element_type=jnp.float32
        )
    return collected


def routed_rows(
    layer_input,
    out_grad,
    mix_weight,
    lift_weight,
    linear_weight,
    row_ids,
    row_home,
    table,
    row_accum,
):
    owners = lax.axis_size("inner")
    sample_count, feature_count, embed_width = layer_input.shape
    table_rows = table.shape[0]
    half_samples = sample_count // 2
    lookups = sample_count * feature_count
    per_owner = lookups // (2 * owners)
    scaling = 1.0 / math.sqrt(embed_width)
    placed = jnp.take(row_home, row_ids.reshape(-1), axis=0)
    owner_of = placed // table_rows
    target = owner_of * (2 * per_owner) + owner_ranks(owner_of, owners)
    ordering = jnp.zeros((lookups,), jnp.int32).at[target].set(jnp.arange(lookups, dtype=jnp.int32))
    ordering = ordering.reshape(owners, 2, per_owner)
    local_rows = (
        jnp.zeros((lookups,), jnp.int32)
        .at[target]
        .set(placed % table_rows)
        .reshape(owners, 2 * per_owner)
    )
    arrived_rows = lax.all_to_all(
        local_rows, "inner", split_axis=0, concat_axis=0, tiled=True
    ).reshape(owners, 2, per_owner)
    collected = jnp.zeros((table_rows, embed_width), jnp.float32)
    totals = None
    for half_index in range(2):
        first_sample = half_index * half_samples
        rows_out, partial_value = interaction_grads(
            layer_input[first_sample : first_sample + half_samples],
            out_grad[first_sample : first_sample + half_samples],
            mix_weight,
            lift_weight,
            linear_weight,
            scaling,
        )
        picked = ordering[:, half_index, :] - half_index * half_samples * feature_count
        outgoing = jnp.take(rows_out, picked.reshape(-1), axis=0).reshape(
            owners, per_owner, embed_width
        )
        incoming = lax.all_to_all(outgoing, "inner", split_axis=0, concat_axis=0, tiled=True)
        collected = add_rows(
            collected, arrived_rows[:, half_index, :].reshape(-1), incoming.reshape(-1, embed_width)
        )
        if totals is None:
            totals = partial_value
        else:
            totals = tuple((earlier + later for earlier, later in zip(totals, partial_value)))
    batch_total = sample_count * lax.axis_size("outer") * owners
    summed = lax.psum((totals[0], totals[1], totals[2]), ("outer", "inner"))
    mix_grad = summed[0] / batch_total
    lift_grad = summed[1] / batch_total
    linear_grad = summed[2] / batch_total
    complete = lax.psum(collected, "outer")
    new_table, new_accum = adagrad(table, row_accum, complete)
    return (new_table, new_accum, mix_grad, lift_grad, linear_grad)


def matmul(left, right):
    return jnp.dot(left, right, preferred_element_type=jnp.float32)


def matmul_nt(left, right):
    return lax.dot_general(left, right, (((1,), (1,)), ((), ())), preferred_element_type=jnp.float32)


def one_hot(matches):
    return jnp.where(matches, 1.0, 0.0).astype(jnp.bfloat16)


def place_group(shift, owners, group, ids_ref, home_ref, rank_ref, slot_ref, count_ref):
    feats = ids_ref.shape[1]
    high, low = home_ref.shape
    half = low // 2
    home = home_ref[...]
    pieces = []
    for piece in (home & 255, home >> 8):
        down = piece.astype(jnp.float32).T
        pieces.append(jnp.concatenate([down[:half], down[half:]], axis=1))
    pieces = jnp.concatenate(pieces, axis=0).astype(jnp.bfloat16)
    high_at = lax.broadcasted_iota(jnp.int32, (2 * high, feats), 0)
    low_at = lax.broadcasted_iota(jnp.int32, (half, feats), 0)
    lane = lax.broadcasted_iota(jnp.int32, (1, feats), 1)
    count_lane = lax.broadcasted_iota(jnp.int32, (8, 128), 1)

    for part in range(SAMPLES // 8):
        first = pl.multiple_of(group * SAMPLES + part * 8, 8)
        ids = ids_ref[pl.ds(first, 8), :]
        every = range(8)
        ones = [ids[row : row + 1] for row in every]
        hots = [one_hot(high_at == ((one >> 6) & 1) * high + (one >> 7)) for one in ones]
        founds = [matmul(pieces, hot) for hot in hots]
        places = []
        for row in every:
            value = founds[row][:half] + 256.0 * founds[row][half:]
            value = jnp.where(low_at == (ones[row] & (half - 1)), value, 0.0)
            places.append(jnp.sum(value, axis=0, keepdims=True))
        place = jnp.concatenate(places, axis=0).astype(jnp.int32)
        owner_all = place >> shift
        slot_ref[pl.ds(first, 8), :] = place & ((1 << shift) - 1)
        keys = (owner_all * feats + lane).astype(jnp.float32)
        downs = [jnp.broadcast_to(keys[row : row + 1], (128, feats)).T for row in every]
        ranks = []
        for row in every:
            parts = []
            for at in range(0, feats, 128):
                less = downs[row] < keys[row : row + 1, at : at + 128]
                parts.append(jnp.sum(jnp.where(less, 1.0, 0.0), axis=0, keepdims=True))
            ranks.append(jnp.concatenate(parts, axis=1))
        rank_ref[pl.ds(first, 8), :] = jnp.concatenate(ranks, axis=0).astype(jnp.int32)
        counts = jnp.zeros((8, 128), jnp.float32)
        for owner_at in range(owners):
            number = jnp.sum(jnp.where(owner_all == owner_at, 1.0, 0.0), axis=1, keepdims=True)
            counts = jnp.where(count_lane == owner_at, number, counts)
        most = jnp.max(counts, axis=1, keepdims=True)
        counts = jnp.where(count_lane == owners, most, counts)
        count_ref[pl.ds(first, 8), :] = counts.astype(jnp.int32)


COPY_ROWS = 56
SAMPLES = 8
SCRATCH = 16


def sum_list(values):
    total = values[0]
    for value in values[1:]:
        total = total + value
    return total


def positions():
    return lax.axis_index("outer"), lax.axis_index("inner")


def grads_kernel(
    sizes,
    x_ref,
    g_ref,
    mix_ref,
    lift_ref,
    linear_ref,
    ids_ref,
    home_ref,
    *rest,
):
    group, steps, owners, per_owner, scaling, shift = sizes
    far_count = owners // 4
    keep_refs, send_refs = rest[:far_count], rest[far_count : 2 * far_count]
    rows_ref = rest[2 * far_count]
    dense_refs, scratch = rest[2 * far_count + 1 : -SCRATCH], rest[-SCRATCH:]
    rank_ref, slot_ref, found_ref, count_ref, copied = scratch[:5]
    step = pl.program_id(0)
    outer, inner = positions()

    def place(index):
        place_group(shift, owners, index, ids_ref, home_ref, rank_ref, slot_ref, found_ref)

    def counts(index):
        samples = pl.ds(pl.multiple_of(index * group, group), group)
        return pltpu.make_async_copy(found_ref.at[samples], count_ref.at[samples], copied)

    @pl.when(step == 0)
    def _():
        place(0)
        counts(0).start()

    @pl.when((step > 0) & (step <= steps))
    def _():
        counts(step - 1).wait()
        now = pl.ds(pl.multiple_of((step - 1) * group, group), group)
        ranks, slots = rank_ref[now, :], slot_ref[now, :]
        place(jnp.minimum(step, steps - 1))
        gather_rows(
            step - 1,
            outer,
            sizes,
            count_ref,
            x_ref,
            g_ref,
            mix_ref,
            lift_ref,
            linear_ref,
            ranks,
            slots,
            dense_refs,
            *scratch[5:],
        )

        @pl.when(step < steps)
        def _():
            counts(step).start()

    @pl.when(step > steps)
    def _():
        place = owners - 1 - (step - steps - 1)
        row_a, row_b = scratch[-4], scratch[-3]
        near = (step - steps - 1) ^ inner
        rows_ref[0, :, :128] = row_a[near, pl.ds(0, per_owner), :].astype(jnp.bfloat16)
        rows_ref[0, :, 128:] = row_b[near, pl.ds(0, per_owner), :].astype(jnp.bfloat16)
        owner = place ^ inner
        first_rows = row_a[owner, pl.ds(0, per_owner), :]
        second_rows = row_b[owner, pl.ds(0, per_owner), :]
        at = x_ref.shape[1] - 128
        build_rows(at, outer, first_rows, second_rows, place, far_count, keep_refs, send_refs)


def join_rows(count_ref, filled, sorted_a, sorted_b, row_a, row_b, step, group, owners):
    begun = (step >= 0).astype(jnp.int32)
    now = (step + 2) % 2
    first = jnp.maximum(step, 0) * group
    every = range(group)
    numbers = [[count_ref[first + k, owner] * begun for owner in range(owners)] for k in every]
    starts = [filled[owner] for owner in range(owners)]
    ends = list(starts)
    for k in every:
        begin = 0
        for owner in range(owners):
            source, target = pl.ds(begin, COPY_ROWS), pl.ds(ends[owner], COPY_ROWS)
            row_a[owner, target, :] = sorted_a[now, k, source, :]
            row_b[owner, target, :] = sorted_b[now, k, source, :]
            ends[owner] = ends[owner] + numbers[k][owner]
            begin = begin + numbers[k][owner]
    most = count_ref[first, owners] * begun
    for k in range(1, group):
        most = jnp.maximum(most, count_ref[first + k, owners] * begun)

    @pl.when(most > COPY_ROWS)
    def _():
        again = list(starts)
        for k in every:
            begin = 0
            for owner in range(owners):

                def copy(turn, carry, begin=begin, at=again[owner], owner=owner, k=k):
                    off = turn * COPY_ROWS
                    source, target = pl.ds(begin + off, COPY_ROWS), pl.ds(at + off, COPY_ROWS)
                    row_a[owner, target, :] = sorted_a[now, k, source, :]
                    row_b[owner, target, :] = sorted_b[now, k, source, :]
                    return carry

                turns = (numbers[k][owner] + COPY_ROWS - 1) // COPY_ROWS
                lax.fori_loop(0, turns, copy, 0)
                again[owner] = again[owner] + numbers[k][owner]
                begin = begin + numbers[k][owner]

    for owner in range(owners):
        filled[owner] = ends[owner]


def gather_rows(
    step,
    outer,
    sizes,
    count_ref,
    x_ref,
    g_ref,
    mix_ref,
    lift_ref,
    linear_ref,
    ranks,
    slots,
    dense_refs,
    mix_down,
    lift_down,
    mix_sum,
    lift_sum,
    linear_sum,
    sorted_a,
    sorted_b,
    row_a,
    row_b,
    dense_ref,
    filled,
):
    group, steps, owners, _, scaling, _ = sizes
    width, feats = x_ref.shape[1:]
    rank = mix_ref.shape[1]

    @pl.when(step == 0)
    def _():
        mix_down[...] = mix_ref[...].astype(jnp.float32).T.astype(jnp.bfloat16)
        lift_down[...] = lift_ref[...].astype(jnp.float32).T.astype(jnp.bfloat16)
        mix_sum[...] = jnp.zeros_like(mix_sum)
        lift_sum[...] = jnp.zeros_like(lift_sum)
        linear_sum[...] = jnp.zeros_like(linear_sum)
        for owner in range(owners):
            filled[owner] = 0

    now = step % 2
    join_rows(count_ref, filled, sorted_a, sorted_b, row_a, row_b, step - 1, group, owners)
    row_at = lax.broadcasted_iota(jnp.int32, (feats, feats), 0)
    extra_at = lax.broadcasted_iota(jnp.int32, (feats - width, feats), 0)
    every = range(group)
    d_prods = [matmul(lift_down[...], g_ref[k]).astype(jnp.bfloat16) for k in every]
    boths = [
        matmul_nt(x_ref[k], jnp.concatenate([mix_down[...], d_prods[k]], axis=0)) for k in every
    ]
    comps = [both[:, :rank].astype(jnp.bfloat16) for both in boths]
    d_comps = [(both[:, rank:] * scaling).astype(jnp.bfloat16) for both in boths]
    x_flat = x_ref[...].reshape(group * width, feats).T
    x_flats = [x_flat[:, k * width : (k + 1) * width] for k in every]
    pairs = [
        matmul(x_flats[k], jnp.concatenate([comps[k], d_comps[k]], axis=1)) for k in every
    ]
    prods = [(pair[:, :rank] * scaling).astype(jnp.bfloat16) for pair in pairs]
    mix_sum[...] += sum_list([pair[:, rank:] for pair in pairs])
    g_all = g_ref[...].reshape(group * width, feats)
    d_all = g_all.astype(jnp.float32) + matmul(g_all, linear_ref[...])
    d_all = d_all + matmul(jnp.concatenate(d_comps, axis=0), mix_down[...])
    d_ins = [
        d_all[k * width : (k + 1) * width] + scaling * matmul(comps[k], d_prods[k]) for k in every
    ]
    moves, rows_downs = [], []
    for k in every:
        slot = slots[k : k + 1]
        extra = jnp.where(extra_at == 0, slot >> 4, jnp.where(extra_at == 1, slot & 15, 0))
        rows_downs.append(
            jnp.concatenate(
                [d_ins[k].astype(jnp.bfloat16), extra.astype(jnp.float32).astype(jnp.bfloat16)],
                axis=0,
            )
        )
        moves.append(one_hot(row_at == ranks[k : k + 1]))
    for k in every:
        ordered = matmul_nt(moves[k], rows_downs[k])
        sorted_a[now, k, :feats] = ordered[:, :128]
        sorted_b[now, k, :feats] = ordered[:, 128:]
    linear_sum[...] += matmul(x_flat, g_all)
    lift_sum[...] += sum_list([matmul(g_ref[k], prods[k]) for k in every])

    @pl.when(step == steps - 1)
    def _():
        join_rows(count_ref, filled, sorted_a, sorted_b, row_a, row_b, step, group, owners)
        dense_ref[:feats] = mix_sum[...]
        linear = linear_sum[...].T
        for at in range(feats // 128):
            dense_ref[feats * (1 + at) : feats * (2 + at)] = linear[:, 128 * at : 128 * (at + 1)]
        dense_ref[feats * (1 + feats // 128) :] = lift_sum[...]
        piece = dense_refs[0].shape[0]
        for index, ref in enumerate(dense_refs):
            first = pl.multiple_of((index ^ outer) * piece, piece)
            ref[...] = dense_ref[pl.ds(first, piece), :]


def build_rows(at, my_outer, first_rows, second_rows, place, first, keep_refs, send_refs):
    outers, piece = 2 * keep_refs[0].shape[1], keep_refs[0].shape[3]
    per_owner = first_rows.shape[0]
    rows_down = jnp.concatenate([first_rows.T, second_rows.T[:at]], axis=0).astype(jnp.bfloat16)
    slots = second_rows[:, at : at + 1] * 16.0 + second_rows[:, at + 1 : at + 2]
    slots = slots.astype(jnp.int32)
    lanes = lax.broadcasted_iota(jnp.int32, (per_owner, piece), 1)
    totals = []
    for outer in range(outers):
        base = (outer ^ my_outer) * piece
        totals.append(matmul(rows_down, one_hot(lanes == slots - base)).astype(jnp.bfloat16))
    for index in range(len(keep_refs)):

        @pl.when(place // 2 == first + index)
        def _(index=index):
            for outer in range(outers):
                ref = (send_refs if outer % 2 else keep_refs)[index]
                ref[0, outer // 2] = totals[outer]


def part_specs(start, first, count, part):
    def spec(index):
        begin = start + 2 * (count - 1 - index)
        return pl.BlockSpec(
            (1,) + part[1:], lambda i, *_: (jnp.clip(begin + 1 - i, 0, 1), 0, 0, 0)
        )

    return [spec(index) for index in range(count)] * 2


def local_grads(x_down, g_down, mix, lift_down, linear, ids, home, owners, part):
    samples, width, feats = x_down.shape
    rank = mix.shape[1]
    group = SAMPLES
    steps = samples // group
    per_owner = samples * feats // owners
    far_count = owners // 4
    shift = (part[1] * 2 * part[3]).bit_length() - 1
    sizes = (group, steps, owners, per_owner, 1.0 / math.sqrt(width), shift)

    def whole(shape):
        return pl.BlockSpec(shape, lambda i, *_: (0,) * len(shape))

    sample_spec = pl.BlockSpec(
        (group, width, feats), lambda i: (jnp.clip(i - 1, 0, steps - 1), 0, 0)
    )
    dense_rows = feats * (1 + feats // 128) + width
    outers = 2 * part[1]
    dense_piece = (dense_rows // outers, 128)
    room = per_owner + 64
    rows_shape = (owners // 2, per_owner, 256)
    scratch = [
        pltpu.VMEM((samples, feats), jnp.int32),
        pltpu.VMEM((samples, feats), jnp.int32),
        pltpu.VMEM((samples, 128), jnp.int32),
        pltpu.SMEM((samples, 128), jnp.int32),
        pltpu.SemaphoreType.DMA,
        pltpu.VMEM((rank, feats), jnp.bfloat16),
        pltpu.VMEM((rank, width), jnp.bfloat16),
        pltpu.VMEM((feats, rank), jnp.float32),
        pltpu.VMEM((width, rank), jnp.float32),
        pltpu.VMEM((feats, feats), jnp.float32),
        pltpu.VMEM((2, group, feats + 64, 128), jnp.float32),
        pltpu.VMEM((2, group, feats + 64, 128), jnp.float32),
        pltpu.VMEM((owners, room, 128), jnp.float32),
        pltpu.VMEM((owners, room, 128), jnp.float32),
        pltpu.VMEM((dense_rows, 128), jnp.float32),
        pltpu.SMEM((owners,), jnp.int32),
    ]
    outs = pl.pallas_call(
        functools.partial(grads_kernel, sizes),
        out_shape=[jax.ShapeDtypeStruct(part, jnp.bfloat16)] * (2 * far_count)
        + [
            jax.ShapeDtypeStruct(rows_shape, jnp.bfloat16),
        ]
        + [jax.ShapeDtypeStruct(dense_piece, jnp.float32)] * outers,
        grid=(1 + steps + owners // 2,),
        in_specs=[
            sample_spec,
            sample_spec,
            whole((feats, rank)),
            whole((width, rank)),
            whole((feats, feats)),
            whole((samples, feats)),
            whole(home.shape),
        ],
        out_specs=part_specs(1 + steps, owners // 2 - far_count, far_count, part)
        + [
            pl.BlockSpec(
                (1,) + rows_shape[1:],
                lambda i: (jnp.clip(i - 1 - steps, 0, owners // 2 - 1), 0, 0),
            )
        ]
        + [whole(dense_piece)] * outers,
        scratch_shapes=scratch,
        compiler_params=pltpu.CompilerParams(vmem_limit_bytes=60 * 2**20),
        cost_estimate=pl.CostEstimate(
            flops=2 * samples * feats * feats * 3072, bytes_accessed=12 * 2**20, transcendentals=0
        ),
        name="local_grads",
    )(x_down, g_down, mix, lift_down, linear, ids, home)
    keep, send = outs[:far_count], outs[far_count : 2 * far_count]
    return keep, send, outs[2 * far_count], outs[2 * far_count + 1 :]


def build_kernel(at, rows_ref, *refs):
    half = len(refs) // 2
    rows = rows_ref[0].astype(jnp.float32)
    place = 2 * half - 1 - pl.program_id(0)
    keep_refs, send_refs = refs[:half], refs[half:]
    outer, _ = positions()
    build_rows(at, outer, rows[:, :128], rows[:, 128:], place, 0, keep_refs, send_refs)


def build_parts(rows, part, width):
    places, per_owner, lanes = rows.shape
    far_count = places // 2
    outs = pl.pallas_call(
        functools.partial(build_kernel, width - 128),
        out_shape=[jax.ShapeDtypeStruct(part, jnp.bfloat16)] * places,
        grid=(places,),
        in_specs=[pl.BlockSpec((1, per_owner, lanes), lambda i: (places - 1 - i, 0, 0))],
        out_specs=part_specs(0, 0, far_count, part),
        compiler_params=pltpu.CompilerParams(vmem_limit_bytes=60 * 2**20),
        cost_estimate=pl.CostEstimate(
            flops=4 * part[3] * part[1] * part[0] * places * per_owner * lanes,
            bytes_accessed=6 * 2**20,
            transcendentals=0,
        ),
        name="build_parts",
    )(rows)
    return outs[:far_count], outs[far_count:]


def adagrad_kernel(me_ref, *refs):
    pieces, (table_ref, accum_ref) = refs[:2], refs[2:4]
    new_table_ref, new_accum_ref = refs[-2:]
    width = table_ref.shape[0]
    for index, piece in enumerate(pieces):

        @pl.when(pl.program_id(0) == index)
        def _(piece=piece):
            grad = piece[...].astype(jnp.float32)
            mean = jnp.sum(grad * grad, axis=0, keepdims=True) * (1.0 / width)
            updated = accum_ref[...] + mean
            new_accum_ref[...] = updated
            new_table_ref[...] = table_ref[...] - grad * (LEARN_RATE / jnp.sqrt(updated))


def update_table(me, pieces, table_down, accum, first, done=()):
    width, table_rows = table_down.shape
    piece = pieces[0].shape[1]

    def moved(rows):
        return pl.BlockSpec((rows, piece), lambda i, me: (0, (first + i) ^ me[0]))

    return pl.pallas_call(
        adagrad_kernel,
        out_shape=(
            jax.ShapeDtypeStruct((width, table_rows), jnp.float32),
            jax.ShapeDtypeStruct((1, table_rows), jnp.float32),
        ),
        grid_spec=pltpu.PrefetchScalarGridSpec(
            num_scalar_prefetch=1,
            grid=(2,),
            in_specs=[pl.BlockSpec(memory_space=pltpu.VMEM)] * 2
            + [moved(width), moved(1)]
            + [pl.BlockSpec(memory_space=pl.ANY)] * len(done),
            out_specs=[moved(width), moved(1)],
        ),
        input_output_aliases={5 + i: i for i in range(len(done))},
        compiler_params=pltpu.CompilerParams(vmem_limit_bytes=16 * 2**20),
        name="update_table",
    )(me, *pieces, table_down, accum, *done)


def swap(values, axis, bit):
    size = lax.axis_size(axis)
    return lax.ppermute(values, axis, [(i, i ^ bit) for i in range(size)])


def add_half(first, second):
    return (first.astype(jnp.float32) + second.astype(jnp.float32)).astype(jnp.bfloat16)


def tree_sum(values):
    while len(values) > 1:
        values = [values[i] + values[i + 1] for i in range(0, len(values), 2)]
    return values[0]


def after(value, *ready):
    return lax.optimization_barrier((value,) + ready)[0]


def halves(dense, side):
    cut = dense.reshape(2, dense.shape[0] // 2, dense.shape[1])
    mine = lax.dynamic_index_in_dim(cut, side, 0, keepdims=False)
    return mine, lax.dynamic_index_in_dim(cut, 1 - side, 0, keepdims=False)


def stacked(dense, other, side):
    return jnp.where(side == 0, jnp.stack([dense, other]), jnp.stack([other, dense]))


def sum_all(me, keep, send, rows, dense, part, width):
    owners = lax.axis_size("inner")
    outer, inner = lax.axis_index("outer"), lax.axis_index("inner")
    far_count = owners // 2
    first = far_count - len(keep)
    keep = dict(enumerate(keep, first))
    came, parts, kept, sent, rest, second, terms, last = ({} for _ in range(8))
    far_ones, near_ones = list(reversed(range(first, far_count))), list(reversed(range(first)))

    def first_stage(far):
        held = keep[far]
        if far % 2:
            parts[far] = add_half(held[1], came[far][1])
            kept[far] = add_half(held[0], came[far][0])
        else:
            parts[far] = add_half(held[:, 1], came[far][:, 1])
            kept[far] = add_half(held[:, 0], came[far][:, 0])

    def second_stage(far):
        parts[far] = add_half(kept[far][1], sent[far][1])
        rest[far] = add_half(kept[far][0], sent[far][0])
        second[far] = swap(parts[far], *(("outer", 2) if far % 2 else ("inner", 1)))

    def send_first(far, ready):
        sent[far] = swap(ready, *(("inner", 1) if far % 2 else ("outer", 2)))

    sides = (outer & 1, outer >> 1, inner & 1)
    for far in far_ones:
        came[far] = swap(send[far - first], "outer", 1)
    others = tuple(swap(dense[bits], "outer", bits) for bits in range(1, len(dense)))
    for far in far_ones:
        first_stage(far)
        send_first(far, parts[far])
    far_parts = [parts[far] for far in far_ones]
    rows = after(rows, *far_parts)
    low_keep, low_send = build_parts(rows, part, width)
    for far in near_ones:
        keep[far] = low_keep[far]
        came[far] = swap(low_send[far], "outer", 1)
    dense = sum_list((dense[0],) + after(others, low_send[0]))
    mine, other = halves(dense, sides[2])
    other = swap(other, "inner", 1)
    for far in far_ones:
        second_stage(far)
    for far in near_ones:
        first_stage(far)
    near_parts = [parts[far] for far in near_ones]
    for far in near_ones:
        send_first(far, parts[far])
    dense = mine + after(other, *near_parts)
    other = swap(dense, "inner", 2)

    def send_last(far, *ready):
        low = far & -far
        value = rest[far].astype(jnp.float32) + second[far].astype(jnp.float32)
        came_far = [terms[far + bit] for bit in (1 << at for at in range(8)) if bit < low]
        if came_far:
            for one in after(tuple(came_far), *ready):
                value = value + one.astype(jnp.float32)
        last[far] = value.astype(jnp.bfloat16)
        terms[far] = swap(last[far], "inner", 2 * low)

    for far in far_ones:
        second[far] = after(second[far], me, dense, *near_parts)
    odd_ones = [far for far in far_ones if far % 2]
    for far in odd_ones:
        send_last(far)
    odd_last = [last[far] for far in odd_ones]
    for bit in range(1, far_count.bit_length() - 1):
        dense = dense + after(other, *odd_last)
        other = swap(dense, "inner", 2 << bit)
    arrived = after(tuple(sent[far] for far in near_ones), *odd_last)
    for far, sent[far] in zip(near_ones, arrived):
        second_stage(far)
    near_parts = [parts[far] for far in near_ones]
    dense = dense + after(other, *near_parts)
    other = swap(dense, "inner", 1)
    for far in far_ones:
        if far % 2 == 0:
            send_last(far, *near_parts)
    even_last = [last[far] for far in far_ones if far % 2 == 0]
    for far in near_ones:
        second[far] = after(second[far], *even_last)
        if far:
            send_last(far)
    dense = stacked(dense, after(other, last[1]), sides[2])
    other = swap(dense, "outer", 2)
    dense = stacked(dense, after(other, second[0], terms[2]), sides[1])
    mine, came_last = after((rest[0], second[0]), dense, last[1])
    total = mine.astype(jnp.float32) + came_last.astype(jnp.float32)
    ends = tuple(terms[1 << bit] for bit in range(far_count.bit_length() - 1))
    for term in after(ends, dense, last[1]):
        total = total + term.astype(jnp.float32)
    total = total.astype(jnp.bfloat16)
    across = swap(total, "outer", 2)
    beside = swap(total, "outer", 1)
    dense = stacked(dense, swap(dense, "outer", 1), sides[0])
    lanes = dense.shape[-1]
    return total, beside, across, jnp.transpose(dense, (1, 0, 2, 3, 4)).reshape(-1, lanes)


def dense_table(
    layer_input,
    out_grad,
    mix_weight,
    lift_weight,
    linear_weight,
    row_ids,
    row_home,
    table,
    row_accum,
):
    owners, outers = lax.axis_size("inner"), lax.axis_size("outer")
    sample_count = layer_input.shape[0]
    table_rows = table.shape[0]
    me = jnp.stack([lax.axis_index("outer"), lax.axis_index("inner")]).astype(jnp.int32)
    width = layer_input.shape[2]
    part = (2, outers // 2, width, table_rows // outers)
    keep, send, rows, dense = local_grads(
        jnp.swapaxes(layer_input, 1, 2),
        jnp.swapaxes(out_grad, 1, 2),
        mix_weight,
        lift_weight.T,
        linear_weight,
        row_ids,
        row_home.reshape(-1, 128),
        owners,
        part,
    )
    total, beside, across, dense = sum_all(me, keep, send, rows, dense, part, width)
    dense = dense * (1.0 / (sample_count * outers * owners))
    feats = layer_input.shape[1]
    linear = [dense[feats * (1 + i) : feats * (2 + i)] for i in range(feats // 128)]
    weights = (
        dense[:feats],
        dense[feats * (1 + feats // 128) :].T,
        jnp.concatenate(linear, axis=1),
    )
    table_down, accum = table.T, row_accum.reshape(1, -1)
    done = update_table(me, (total, beside), table_down, accum, 0)
    across = after(across, done[1], *weights)
    pieces = (across, swap(across, "outer", 1))
    new_table, new_accum = update_table(me, pieces, table_down, accum, 2, done)
    return (new_table.T, new_accum.reshape(-1)) + weights


def power_of_two(number):
    return number & (number - 1) == 0


def on_device(*arrays):
    owners, outers = lax.axis_size("inner"), lax.axis_size("outer")
    layer_input, mix_weight, row_home, table = (arrays[i] for i in (0, 2, 6, 7))
    samples, feats, width = layer_input.shape
    dense_fits = (
        outers == 4
        and owners % 4 == 0
        and power_of_two(owners)
        and row_home.shape[0] <= 2 * samples * feats
        and row_home.shape[0] <= 2**15
        and power_of_two(table.shape[0])
        and 512 <= table.shape[0] <= 4096
        and samples % 16 == 0
        and (feats * (1 + feats // 128) + width) % 64 == 0
        and feats == 256
        and mix_weight.shape[1] == 128
        and 2 * (width - 128) == 128
    )
    return dense_table(*arrays) if dense_fits else routed_rows(*arrays)


def solution(mesh):
    placed = (
        P(("outer", "inner"), None, None),
        P(("outer", "inner"), None, None),
        P(),
        P(),
        P(),
        P(("outer", "inner"), None),
        P(),
        P("inner", None),
        P("inner"),
    )
    return jax.shard_map(
        on_device,
        mesh=mesh,
        in_specs=placed,
        out_specs=(P("inner", None), P("inner"), P(), P(), P()),
        check_vma=False,
    )
```

```python
import functools
import math

import jax
import jax.numpy as jnp
from jax import lax
from jax.experimental import pallas as pl
from jax.experimental.pallas import tpu as pltpu
from jax.sharding import PartitionSpec as P

LEARN_RATE = 0.5


def interaction_grads(inputs, cotangent, mix_weight, lift_weight, linear_weight, scaling):
    compressed = jnp.einsum(
        "bfd,fk->bdk", inputs, mix_weight, preferred_element_type=jnp.float32
    ).astype(jnp.bfloat16)
    products = (
        jnp.einsum("bfd,bdk->bfk", inputs, compressed, preferred_element_type=jnp.float32) * scaling
    ).astype(jnp.bfloat16)
    d_products = jnp.einsum(
        "bfd,kd->bfk", cotangent, lift_weight, preferred_element_type=jnp.float32
    ).astype(jnp.bfloat16)
    d_compressed = (
        jnp.einsum("bfd,bfk->bdk", inputs, d_products, preferred_element_type=jnp.float32) * scaling
    ).astype(jnp.bfloat16)
    d_inputs = cotangent.astype(jnp.float32)
    d_inputs = d_inputs + jnp.einsum(
        "fg,bfd->bgd", linear_weight, cotangent, preferred_element_type=jnp.float32
    )
    d_inputs = d_inputs + scaling * jnp.einsum(
        "bfk,bdk->bfd", d_products, compressed, preferred_element_type=jnp.float32
    )
    d_inputs = d_inputs + jnp.einsum(
        "fk,bdk->bfd", mix_weight, d_compressed, preferred_element_type=jnp.float32
    )
    g_mix = jnp.einsum("bfd,bdk->fk", inputs, d_compressed, preferred_element_type=jnp.float32)
    g_lift = jnp.einsum("bfk,bfd->kd", products, cotangent, preferred_element_type=jnp.float32)
    g_linear = jnp.einsum("bfd,bgd->fg", cotangent, inputs, preferred_element_type=jnp.float32)
    rows_out = d_inputs.astype(jnp.bfloat16).reshape(-1, d_inputs.shape[2])
    return (rows_out, (g_mix, g_lift, g_linear))


def adagrad(weights, history, gradient):
    updated = history + jnp.mean(gradient * gradient, axis=1)
    return (weights - LEARN_RATE * gradient / jnp.sqrt(updated)[:, None], updated)


def owner_ranks(owner_of, owners):
    lookups = owner_of.shape[0]
    width = math.gcd(lookups, 128)
    groups = lookups // width
    hot = (owner_of[:, None] == jnp.arange(owners, dtype=jnp.int32)[None, :]).astype(jnp.bfloat16)
    hot = hot.reshape(groups, width, owners)
    lower = (jnp.arange(width)[:, None] > jnp.arange(width)[None, :]).astype(jnp.bfloat16)
    within = jnp.einsum("ij,gjo->gio", lower, hot, preferred_element_type=jnp.float32)
    totals = jnp.sum(hot.astype(jnp.float32), axis=1)
    before = jnp.cumsum(totals, axis=0) - totals
    counted = jnp.sum(hot.astype(jnp.float32) * (within + before[:, None, :]), axis=2)
    return counted.reshape(-1).astype(jnp.int32)


def add_rows(collected, slots, values):
    count = values.shape[0]
    table_rows = collected.shape[0]
    width = math.gcd(count, 2048)
    columns = jnp.arange(table_rows, dtype=jnp.int32)
    for block_index in range(count // width):
        start = block_index * width
        hot = (slots[start : start + width, None] == columns[None, :]).astype(jnp.bfloat16)
        collected = collected + jnp.einsum(
            "lr,ld->rd", hot, values[start : start + width], preferred_element_type=jnp.float32
        )
    return collected


def routed_rows(
    layer_input,
    out_grad,
    mix_weight,
    lift_weight,
    linear_weight,
    row_ids,
    row_home,
    table,
    row_accum,
):
    owners = lax.axis_size("inner")
    sample_count, feature_count, embed_width = layer_input.shape
    table_rows = table.shape[0]
    half_samples = sample_count // 2
    lookups = sample_count * feature_count
    per_owner = lookups // (2 * owners)
    scaling = 1.0 / math.sqrt(embed_width)
    placed = jnp.take(row_home, row_ids.reshape(-1), axis=0)
    owner_of = placed // table_rows
    target = owner_of * (2 * per_owner) + owner_ranks(owner_of, owners)
    ordering = jnp.zeros((lookups,), jnp.int32).at[target].set(jnp.arange(lookups, dtype=jnp.int32))
    ordering = ordering.reshape(owners, 2, per_owner)
    local_rows = (
        jnp.zeros((lookups,), jnp.int32)
        .at[target]
        .set(placed % table_rows)
        .reshape(owners, 2 * per_owner)
    )
    arrived_rows = lax.all_to_all(
        local_rows, "inner", split_axis=0, concat_axis=0, tiled=True
    ).reshape(owners, 2, per_owner)
    collected = jnp.zeros((table_rows, embed_width), jnp.float32)
    totals = None
    for half_index in range(2):
        first_sample = half_index * half_samples
        rows_out, partial_value = interaction_grads(
            layer_input[first_sample : first_sample + half_samples],
            out_grad[first_sample : first_sample + half_samples],
            mix_weight,
            lift_weight,
            linear_weight,
            scaling,
        )
        picked = ordering[:, half_index, :] - half_index * half_samples * feature_count
        outgoing = jnp.take(rows_out, picked.reshape(-1), axis=0).reshape(
            owners, per_owner, embed_width
        )
        incoming = lax.all_to_all(outgoing, "inner", split_axis=0, concat_axis=0, tiled=True)
        collected = add_rows(
            collected, arrived_rows[:, half_index, :].reshape(-1), incoming.reshape(-1, embed_width)
        )
        if totals is None:
            totals = partial_value
        else:
            totals = tuple((earlier + later for earlier, later in zip(totals, partial_value)))
    batch_total = sample_count * lax.axis_size("outer") * owners
    summed = lax.psum((totals[0], totals[1], totals[2]), ("outer", "inner"))
    mix_grad = summed[0] / batch_total
    lift_grad = summed[1] / batch_total
    linear_grad = summed[2] / batch_total
    complete = lax.psum(collected, "outer")
    new_table, new_accum = adagrad(table, row_accum, complete)
    return (new_table, new_accum, mix_grad, lift_grad, linear_grad)


def matmul(left, right):
    return jnp.dot(left, right, preferred_element_type=jnp.float32)


def matmul_nt(left, right):
    return lax.dot_general(left, right, (((1,), (1,)), ((), ())), preferred_element_type=jnp.float32)


def one_hot(matches):
    return jnp.where(matches, 1.0, 0.0).astype(jnp.bfloat16)


def place_kernel(shift, owners, ids_ref, home_ref, rank_ref, slot_ref, count_ref):
    samples, feats = ids_ref.shape
    high, low = home_ref.shape
    half = low // 2
    home = home_ref[...]
    pieces = []
    for part in (home & 255, home >> 8):
        down = part.astype(jnp.float32).T
        pieces.append(jnp.concatenate([down[:half], down[half:]], axis=1))
    pieces = jnp.concatenate(pieces, axis=0).astype(jnp.bfloat16)
    high_at = lax.broadcasted_iota(jnp.int32, (2 * high, feats), 0)
    low_at = lax.broadcasted_iota(jnp.int32, (half, feats), 0)
    lane = lax.broadcasted_iota(jnp.int32, (1, feats), 1)
    count_lane = lax.broadcasted_iota(jnp.int32, (8, 128), 1)

    @pl.loop(0, samples // 8)
    def _(group):
        first = pl.multiple_of(group * 8, 8)
        ids = ids_ref[pl.ds(first, 8), :]
        every = range(8)
        ones = [ids[row : row + 1] for row in every]
        hots = [one_hot(high_at == ((one >> 6) & 1) * high + (one >> 7)) for one in ones]
        founds = [matmul(pieces, hot) for hot in hots]
        places = []
        for row in every:
            value = founds[row][:half] + 256.0 * founds[row][half:]
            value = jnp.where(low_at == (ones[row] & (half - 1)), value, 0.0)
            places.append(jnp.sum(value, axis=0, keepdims=True))
        place = jnp.concatenate(places, axis=0).astype(jnp.int32)
        owner_all = place >> shift
        slot_ref[pl.ds(first, 8), :] = place & ((1 << shift) - 1)
        keys = (owner_all * feats + lane).astype(jnp.float32)
        downs = [jnp.broadcast_to(keys[row : row + 1], (128, feats)).T for row in every]
        ranks = []
        for row in every:
            parts = []
            for at in range(0, feats, 128):
                less = downs[row] < keys[row : row + 1, at : at + 128]
                parts.append(jnp.sum(jnp.where(less, 1.0, 0.0), axis=0, keepdims=True))
            ranks.append(jnp.concatenate(parts, axis=1))
        rank_ref[pl.ds(first, 8), :] = jnp.concatenate(ranks, axis=0).astype(jnp.int32)
        counts = jnp.zeros((8, 128), jnp.float32)
        for owner_at in range(owners):
            number = jnp.sum(jnp.where(owner_all == owner_at, 1.0, 0.0), axis=1, keepdims=True)
            counts = jnp.where(count_lane == owner_at, number, counts)
        most = jnp.max(counts, axis=1, keepdims=True)
        counts = jnp.where(count_lane == owners, most, counts)
        count_ref[pl.ds(first, 8), :] = counts.astype(jnp.int32)


COPY_ROWS = 56
SCRATCH = 16


def sum_list(values):
    total = values[0]
    for value in values[1:]:
        total = total + value
    return total


def positions():
    return lax.axis_index("outer"), lax.axis_index("inner")


def grads_kernel(
    sizes,
    x_ref,
    g_ref,
    mix_ref,
    lift_ref,
    linear_ref,
    ids_ref,
    home_ref,
    *rest,
):
    group, steps, owners, per_owner, scaling, shift = sizes
    far_count = owners // 4
    keep_refs, send_refs = rest[:far_count], rest[far_count : 2 * far_count]
    rows_ref = rest[2 * far_count]
    dense_refs, scratch = rest[2 * far_count + 1 : -SCRATCH], rest[-SCRATCH:]
    rank_ref, slot_ref, found_ref, count_ref, copied = scratch[:5]
    step = pl.program_id(0)
    outer, inner = positions()

    @pl.when(step == 0)
    def _():
        place_kernel(shift, owners, ids_ref, home_ref, rank_ref, slot_ref, found_ref)
        copy = pltpu.make_async_copy(found_ref, count_ref, copied)
        copy.start()
        copy.wait()

    @pl.when((step > 0) & (step <= steps))
    def _():
        gather_rows(
            step - 1,
            outer,
            sizes,
            count_ref,
            x_ref,
            g_ref,
            mix_ref,
            lift_ref,
            linear_ref,
            rank_ref,
            slot_ref,
            dense_refs,
            *scratch[5:],
        )

    @pl.when(step > steps)
    def _():
        place = owners - 1 - (step - steps - 1)
        row_a, row_b = scratch[-4], scratch[-3]
        near = (step - steps - 1) ^ inner
        rows_ref[0, :, :128] = row_a[near, pl.ds(0, per_owner), :].astype(jnp.bfloat16)
        rows_ref[0, :, 128:] = row_b[near, pl.ds(0, per_owner), :].astype(jnp.bfloat16)
        owner = place ^ inner
        first_rows = row_a[owner, pl.ds(0, per_owner), :]
        second_rows = row_b[owner, pl.ds(0, per_owner), :]
        at = x_ref.shape[1] - 128
        build_rows(at, outer, first_rows, second_rows, place, far_count, keep_refs, send_refs)


def join_rows(count_ref, filled, sorted_a, sorted_b, row_a, row_b, step, group, owners):
    begun = (step >= 0).astype(jnp.int32)
    now = (step + 2) % 2
    first = jnp.maximum(step, 0) * group
    every = range(group)
    numbers = [[count_ref[first + k, owner] * begun for owner in range(owners)] for k in every]
    starts = [filled[owner] for owner in range(owners)]
    ends = list(starts)
    for k in every:
        begin = 0
        for owner in range(owners):
            source, target = pl.ds(begin, COPY_ROWS), pl.ds(ends[owner], COPY_ROWS)
            row_a[owner, target, :] = sorted_a[now, k, source, :]
            row_b[owner, target, :] = sorted_b[now, k, source, :]
            ends[owner] = ends[owner] + numbers[k][owner]
            begin = begin + numbers[k][owner]
    most = count_ref[first, owners] * begun
    for k in range(1, group):
        most = jnp.maximum(most, count_ref[first + k, owners] * begun)

    @pl.when(most > COPY_ROWS)
    def _():
        again = list(starts)
        for k in every:
            begin = 0
            for owner in range(owners):

                def copy(turn, carry, begin=begin, at=again[owner], owner=owner, k=k):
                    off = turn * COPY_ROWS
                    source, target = pl.ds(begin + off, COPY_ROWS), pl.ds(at + off, COPY_ROWS)
                    row_a[owner, target, :] = sorted_a[now, k, source, :]
                    row_b[owner, target, :] = sorted_b[now, k, source, :]
                    return carry

                turns = (numbers[k][owner] + COPY_ROWS - 1) // COPY_ROWS
                lax.fori_loop(0, turns, copy, 0)
                again[owner] = again[owner] + numbers[k][owner]
                begin = begin + numbers[k][owner]

    for owner in range(owners):
        filled[owner] = ends[owner]


def gather_rows(
    step,
    outer,
    sizes,
    count_ref,
    x_ref,
    g_ref,
    mix_ref,
    lift_ref,
    linear_ref,
    rank_ref,
    slot_ref,
    dense_refs,
    mix_down,
    lift_down,
    mix_sum,
    lift_sum,
    linear_sum,
    sorted_a,
    sorted_b,
    row_a,
    row_b,
    dense_ref,
    filled,
):
    group, steps, owners, _, scaling, _ = sizes
    width, feats = x_ref.shape[1:]
    rank = mix_ref.shape[1]

    @pl.when(step == 0)
    def _():
        mix_down[...] = mix_ref[...].astype(jnp.float32).T.astype(jnp.bfloat16)
        lift_down[...] = lift_ref[...].astype(jnp.float32).T.astype(jnp.bfloat16)
        mix_sum[...] = jnp.zeros_like(mix_sum)
        lift_sum[...] = jnp.zeros_like(lift_sum)
        linear_sum[...] = jnp.zeros_like(linear_sum)
        for owner in range(owners):
            filled[owner] = 0

    now = step % 2
    join_rows(count_ref, filled, sorted_a, sorted_b, row_a, row_b, step - 1, group, owners)
    row_at = lax.broadcasted_iota(jnp.int32, (feats, feats), 0)
    extra_at = lax.broadcasted_iota(jnp.int32, (feats - width, feats), 0)
    every = range(group)
    d_prods = [matmul(lift_down[...], g_ref[k]).astype(jnp.bfloat16) for k in every]
    boths = [
        matmul_nt(x_ref[k], jnp.concatenate([mix_down[...], d_prods[k]], axis=0)) for k in every
    ]
    comps = [both[:, :rank].astype(jnp.bfloat16) for both in boths]
    d_comps = [(both[:, rank:] * scaling).astype(jnp.bfloat16) for both in boths]
    x_flat = x_ref[...].reshape(group * width, feats).T
    x_flats = [x_flat[:, k * width : (k + 1) * width] for k in every]
    pairs = [
        matmul(x_flats[k], jnp.concatenate([comps[k], d_comps[k]], axis=1)) for k in every
    ]
    prods = [(pair[:, :rank] * scaling).astype(jnp.bfloat16) for pair in pairs]
    mix_sum[...] += sum_list([pair[:, rank:] for pair in pairs])
    g_all = g_ref[...].reshape(group * width, feats)
    d_all = g_all.astype(jnp.float32) + matmul(g_all, linear_ref[...])
    d_all = d_all + matmul(jnp.concatenate(d_comps, axis=0), mix_down[...])
    d_ins = [
        d_all[k * width : (k + 1) * width] + scaling * matmul(comps[k], d_prods[k]) for k in every
    ]
    moves, rows_downs = [], []
    for k in every:
        slot = slot_ref[pl.ds(step * group + k, 1), :]
        extra = jnp.where(extra_at == 0, slot >> 4, jnp.where(extra_at == 1, slot & 15, 0))
        rows_downs.append(
            jnp.concatenate(
                [d_ins[k].astype(jnp.bfloat16), extra.astype(jnp.float32).astype(jnp.bfloat16)],
                axis=0,
            )
        )
        moves.append(one_hot(row_at == rank_ref[pl.ds(step * group + k, 1), :]))
    for k in every:
        ordered = matmul_nt(moves[k], rows_downs[k])
        sorted_a[now, k, :feats] = ordered[:, :128]
        sorted_b[now, k, :feats] = ordered[:, 128:]
    linear_sum[...] += matmul(x_flat, g_all)
    lift_sum[...] += sum_list([matmul(g_ref[k], prods[k]) for k in every])

    @pl.when(step == steps - 1)
    def _():
        join_rows(count_ref, filled, sorted_a, sorted_b, row_a, row_b, step, group, owners)
        dense_ref[:feats] = mix_sum[...]
        linear = linear_sum[...].T
        for at in range(feats // 128):
            dense_ref[feats * (1 + at) : feats * (2 + at)] = linear[:, 128 * at : 128 * (at + 1)]
        dense_ref[feats * (1 + feats // 128) :] = lift_sum[...]
        piece = dense_refs[0].shape[0]
        for index, ref in enumerate(dense_refs):
            first = pl.multiple_of((index ^ outer) * piece, piece)
            ref[...] = dense_ref[pl.ds(first, piece), :]


def build_rows(at, my_outer, first_rows, second_rows, place, first, keep_refs, send_refs):
    outers, piece = 2 * keep_refs[0].shape[1], keep_refs[0].shape[3]
    per_owner = first_rows.shape[0]
    rows_down = jnp.concatenate([first_rows.T, second_rows.T[:at]], axis=0).astype(jnp.bfloat16)
    slots = second_rows[:, at : at + 1] * 16.0 + second_rows[:, at + 1 : at + 2]
    slots = slots.astype(jnp.int32)
    lanes = lax.broadcasted_iota(jnp.int32, (per_owner, piece), 1)
    totals = []
    for outer in range(outers):
        base = (outer ^ my_outer) * piece
        totals.append(matmul(rows_down, one_hot(lanes == slots - base)).astype(jnp.bfloat16))
    for index in range(len(keep_refs)):

        @pl.when(place // 2 == first + index)
        def _(index=index):
            for outer in range(outers):
                ref = (send_refs if outer % 2 else keep_refs)[index]
                ref[0, outer // 2] = totals[outer]


def part_specs(start, first, count, part):
    def spec(index):
        begin = start + 2 * (count - 1 - index)
        return pl.BlockSpec(
            (1,) + part[1:], lambda i, *_: (jnp.clip(begin + 1 - i, 0, 1), 0, 0, 0)
        )

    return [spec(index) for index in range(count)] * 2


def local_grads(x_down, g_down, mix, lift_down, linear, ids, home, owners, part):
    samples, width, feats = x_down.shape
    rank = mix.shape[1]
    group = 8
    steps = samples // group
    per_owner = samples * feats // owners
    far_count = owners // 4
    shift = (part[1] * 2 * part[3]).bit_length() - 1
    sizes = (group, steps, owners, per_owner, 1.0 / math.sqrt(width), shift)

    def whole(shape):
        return pl.BlockSpec(shape, lambda i, *_: (0,) * len(shape))

    sample_spec = pl.BlockSpec(
        (group, width, feats), lambda i: (jnp.clip(i - 1, 0, steps - 1), 0, 0)
    )
    dense_rows = feats * (1 + feats // 128) + width
    outers = 2 * part[1]
    dense_piece = (dense_rows // outers, 128)
    room = per_owner + 64
    rows_shape = (owners // 2, per_owner, 256)
    scratch = [
        pltpu.VMEM((samples, feats), jnp.int32),
        pltpu.VMEM((samples, feats), jnp.int32),
        pltpu.VMEM((samples, 128), jnp.int32),
        pltpu.SMEM((samples, 128), jnp.int32),
        pltpu.SemaphoreType.DMA,
        pltpu.VMEM((rank, feats), jnp.bfloat16),
        pltpu.VMEM((rank, width), jnp.bfloat16),
        pltpu.VMEM((feats, rank), jnp.float32),
        pltpu.VMEM((width, rank), jnp.float32),
        pltpu.VMEM((feats, feats), jnp.float32),
        pltpu.VMEM((2, group, feats + 64, 128), jnp.float32),
        pltpu.VMEM((2, group, feats + 64, 128), jnp.float32),
        pltpu.VMEM((owners, room, 128), jnp.float32),
        pltpu.VMEM((owners, room, 128), jnp.float32),
        pltpu.VMEM((dense_rows, 128), jnp.float32),
        pltpu.SMEM((owners,), jnp.int32),
    ]
    outs = pl.pallas_call(
        functools.partial(grads_kernel, sizes),
        out_shape=[jax.ShapeDtypeStruct(part, jnp.bfloat16)] * (2 * far_count)
        + [
            jax.ShapeDtypeStruct(rows_shape, jnp.bfloat16),
        ]
        + [jax.ShapeDtypeStruct(dense_piece, jnp.float32)] * outers,
        grid=(1 + steps + owners // 2,),
        in_specs=[
            sample_spec,
            sample_spec,
            whole((feats, rank)),
            whole((width, rank)),
            whole((feats, feats)),
            whole((samples, feats)),
            whole(home.shape),
        ],
        out_specs=part_specs(1 + steps, owners // 2 - far_count, far_count, part)
        + [
            pl.BlockSpec(
                (1,) + rows_shape[1:],
                lambda i: (jnp.clip(i - 1 - steps, 0, owners // 2 - 1), 0, 0),
            )
        ]
        + [whole(dense_piece)] * outers,
        scratch_shapes=scratch,
        compiler_params=pltpu.CompilerParams(vmem_limit_bytes=60 * 2**20),
        cost_estimate=pl.CostEstimate(
            flops=2 * samples * feats * feats * 3072, bytes_accessed=12 * 2**20, transcendentals=0
        ),
        name="local_grads",
    )(x_down, g_down, mix, lift_down, linear, ids, home)
    keep, send = outs[:far_count], outs[far_count : 2 * far_count]
    return keep, send, outs[2 * far_count], outs[2 * far_count + 1 :]


def build_kernel(at, rows_ref, *refs):
    half = len(refs) // 2
    rows = rows_ref[0].astype(jnp.float32)
    place = 2 * half - 1 - pl.program_id(0)
    keep_refs, send_refs = refs[:half], refs[half:]
    outer, _ = positions()
    build_rows(at, outer, rows[:, :128], rows[:, 128:], place, 0, keep_refs, send_refs)


def build_parts(rows, part, width):
    places, per_owner, lanes = rows.shape
    far_count = places // 2
    outs = pl.pallas_call(
        functools.partial(build_kernel, width - 128),
        out_shape=[jax.ShapeDtypeStruct(part, jnp.bfloat16)] * places,
        grid=(places,),
        in_specs=[pl.BlockSpec((1, per_owner, lanes), lambda i: (places - 1 - i, 0, 0))],
        out_specs=part_specs(0, 0, far_count, part),
        compiler_params=pltpu.CompilerParams(vmem_limit_bytes=60 * 2**20),
        cost_estimate=pl.CostEstimate(
            flops=4 * part[3] * part[1] * part[0] * places * per_owner * lanes,
            bytes_accessed=6 * 2**20,
            transcendentals=0,
        ),
        name="build_parts",
    )(rows)
    return outs[:far_count], outs[far_count:]


def adagrad_kernel(me_ref, *refs):
    pieces, (table_ref, accum_ref) = refs[:2], refs[2:4]
    new_table_ref, new_accum_ref = refs[-2:]
    width = table_ref.shape[0]
    for index, piece in enumerate(pieces):

        @pl.when(pl.program_id(0) == index)
        def _(piece=piece):
            grad = piece[...].astype(jnp.float32)
            mean = jnp.sum(grad * grad, axis=0, keepdims=True) * (1.0 / width)
            updated = accum_ref[...] + mean
            new_accum_ref[...] = updated
            new_table_ref[...] = table_ref[...] - grad * (LEARN_RATE / jnp.sqrt(updated))


def update_table(me, pieces, table_down, accum, first, done=()):
    width, table_rows = table_down.shape
    piece = pieces[0].shape[1]

    def moved(rows):
        return pl.BlockSpec((rows, piece), lambda i, me: (0, (first + i) ^ me[0]))

    return pl.pallas_call(
        adagrad_kernel,
        out_shape=(
            jax.ShapeDtypeStruct((width, table_rows), jnp.float32),
            jax.ShapeDtypeStruct((1, table_rows), jnp.float32),
        ),
        grid_spec=pltpu.PrefetchScalarGridSpec(
            num_scalar_prefetch=1,
            grid=(2,),
            in_specs=[pl.BlockSpec(memory_space=pltpu.VMEM)] * 2
            + [moved(width), moved(1)]
            + [pl.BlockSpec(memory_space=pl.ANY)] * len(done),
            out_specs=[moved(width), moved(1)],
        ),
        input_output_aliases={5 + i: i for i in range(len(done))},
        compiler_params=pltpu.CompilerParams(vmem_limit_bytes=16 * 2**20),
        name="update_table",
    )(me, *pieces, table_down, accum, *done)


def swap(values, axis, bit):
    size = lax.axis_size(axis)
    return lax.ppermute(values, axis, [(i, i ^ bit) for i in range(size)])


def add_half(first, second):
    return (first.astype(jnp.float32) + second.astype(jnp.float32)).astype(jnp.bfloat16)


def tree_sum(values):
    while len(values) > 1:
        values = [values[i] + values[i + 1] for i in range(0, len(values), 2)]
    return values[0]


def after(value, *ready):
    return lax.optimization_barrier((value,) + ready)[0]


def halves(dense, side):
    cut = dense.reshape(2, dense.shape[0] // 2, dense.shape[1])
    mine = lax.dynamic_index_in_dim(cut, side, 0, keepdims=False)
    return mine, lax.dynamic_index_in_dim(cut, 1 - side, 0, keepdims=False)


def stacked(dense, other, side):
    return jnp.where(side == 0, jnp.stack([dense, other]), jnp.stack([other, dense]))


def sum_all(me, keep, send, rows, dense, part, width):
    owners = lax.axis_size("inner")
    outer, inner = lax.axis_index("outer"), lax.axis_index("inner")
    far_count = owners // 2
    first = far_count - len(keep)
    keep = dict(enumerate(keep, first))
    came, parts, kept, sent, rest, second, terms, last = ({} for _ in range(8))
    far_ones, near_ones = list(reversed(range(first, far_count))), list(reversed(range(first)))

    def first_stage(far):
        held = keep[far]
        parts[far] = (
            add_half(held[1], came[far][1]) if far % 2 else add_half(held[:, 1], came[far][:, 1])
        )
        held, arrived = after((held, came[far]), parts[far])
        kept[far] = add_half(held[0], arrived[0]) if far % 2 else add_half(held[:, 0], arrived[:, 0])

    def second_stage(far):
        parts[far] = add_half(kept[far][1], sent[far][1])
        rest[far] = add_half(kept[far][0], sent[far][0])
        second[far] = swap(parts[far], *(("outer", 2) if far % 2 else ("inner", 1)))

    def send_first(far, ready):
        sent[far] = swap(ready, *(("inner", 1) if far % 2 else ("outer", 2)))

    sides = (outer & 1, outer >> 1, inner & 1)
    for far in far_ones:
        came[far] = swap(send[far - first], "outer", 1)
    others = tuple(swap(dense[bits], "outer", bits) for bits in range(1, len(dense)))
    for far in far_ones:
        first_stage(far)
        send_first(far, parts[far])
    far_parts = [parts[far] for far in far_ones]
    rows = after(rows, *far_parts)
    low_keep, low_send = build_parts(rows, part, width)
    for far in near_ones:
        keep[far] = low_keep[far]
        came[far] = swap(low_send[far], "outer", 1)
    dense = sum_list((dense[0],) + after(others, low_send[0]))
    mine, other = halves(dense, sides[2])
    other = swap(other, "inner", 1)
    for far in far_ones:
        second_stage(far)
    for far in near_ones:
        first_stage(far)
    near_parts = [parts[far] for far in near_ones]
    for far in near_ones:
        send_first(far, parts[far])
    dense = mine + after(other, *near_parts)
    other = swap(dense, "inner", 2)

    def send_last(far, *ready):
        low = far & -far
        value = rest[far].astype(jnp.float32) + second[far].astype(jnp.float32)
        came_far = [terms[far + bit] for bit in (1 << at for at in range(8)) if bit < low]
        if came_far:
            for one in after(tuple(came_far), *ready):
                value = value + one.astype(jnp.float32)
        last[far] = value.astype(jnp.bfloat16)
        terms[far] = swap(last[far], "inner", 2 * low)

    for far in far_ones:
        second[far] = after(second[far], me, dense, *near_parts)
    odd_ones = [far for far in far_ones if far % 2]
    for far in odd_ones:
        send_last(far)
    odd_last = [last[far] for far in odd_ones]
    for bit in range(1, far_count.bit_length() - 1):
        dense = dense + after(other, *odd_last)
        other = swap(dense, "inner", 2 << bit)
    arrived = after(tuple(sent[far] for far in near_ones), *odd_last)
    for far, sent[far] in zip(near_ones, arrived):
        second_stage(far)
    near_parts = [parts[far] for far in near_ones]
    dense = dense + after(other, *near_parts)
    other = swap(dense, "inner", 1)
    for far in far_ones:
        if far % 2 == 0:
            send_last(far, *near_parts)
    even_last = [last[far] for far in far_ones if far % 2 == 0]
    for far in near_ones:
        second[far] = after(second[far], *even_last)
        if far:
            send_last(far)
    dense = stacked(dense, after(other, last[1]), sides[2])
    other = swap(dense, "outer", 2)
    dense = stacked(dense, after(other, second[0], terms[2]), sides[1])
    mine, came_last = after((rest[0], second[0]), dense, last[1])
    total = mine.astype(jnp.float32) + came_last.astype(jnp.float32)
    ends = tuple(terms[1 << bit] for bit in range(far_count.bit_length() - 1))
    for term in after(ends, dense, last[1]):
        total = total + term.astype(jnp.float32)
    total = total.astype(jnp.bfloat16)
    across = swap(total, "outer", 2)
    beside = swap(total, "outer", 1)
    dense = stacked(dense, swap(dense, "outer", 1), sides[0])
    lanes = dense.shape[-1]
    return total, beside, across, jnp.transpose(dense, (1, 0, 2, 3, 4)).reshape(-1, lanes)


def dense_table(
    layer_input,
    out_grad,
    mix_weight,
    lift_weight,
    linear_weight,
    row_ids,
    row_home,
    table,
    row_accum,
):
    owners, outers = lax.axis_size("inner"), lax.axis_size("outer")
    sample_count = layer_input.shape[0]
    table_rows = table.shape[0]
    me = jnp.stack([lax.axis_index("outer"), lax.axis_index("inner")]).astype(jnp.int32)
    width = layer_input.shape[2]
    part = (2, outers // 2, width, table_rows // outers)
    keep, send, rows, dense = local_grads(
        jnp.swapaxes(layer_input, 1, 2),
        jnp.swapaxes(out_grad, 1, 2),
        mix_weight,
        lift_weight.T,
        linear_weight,
        row_ids,
        row_home.reshape(-1, 128),
        owners,
        part,
    )
    total, beside, across, dense = sum_all(me, keep, send, rows, dense, part, width)
    dense = dense * (1.0 / (sample_count * outers * owners))
    feats = layer_input.shape[1]
    linear = [dense[feats * (1 + i) : feats * (2 + i)] for i in range(feats // 128)]
    weights = (
        dense[:feats],
        dense[feats * (1 + feats // 128) :].T,
        jnp.concatenate(linear, axis=1),
    )
    table_down, accum = table.T, row_accum.reshape(1, -1)
    done = update_table(me, (total, beside), table_down, accum, 0)
    across = after(across, done[1], *weights)
    pieces = (across, swap(across, "outer", 1))
    new_table, new_accum = update_table(me, pieces, table_down, accum, 2, done)
    return (new_table.T, new_accum.reshape(-1)) + weights


def power_of_two(number):
    return number & (number - 1) == 0


def on_device(*arrays):
    owners, outers = lax.axis_size("inner"), lax.axis_size("outer")
    layer_input, mix_weight, row_home, table = (arrays[i] for i in (0, 2, 6, 7))
    samples, feats, width = layer_input.shape
    dense_fits = (
        outers == 4
        and owners % 4 == 0
        and power_of_two(owners)
        and row_home.shape[0] <= 2 * samples * feats
        and row_home.shape[0] <= 2**15
        and power_of_two(table.shape[0])
        and 512 <= table.shape[0] <= 4096
        and samples % 16 == 0
        and (feats * (1 + feats // 128) + width) % 64 == 0
        and feats == 256
        and mix_weight.shape[1] == 128
        and 2 * (width - 128) == 128
    )
    return dense_table(*arrays) if dense_fits else routed_rows(*arrays)


def solution(mesh):
    placed = (
        P(("outer", "inner"), None, None),
        P(("outer", "inner"), None, None),
        P(),
        P(),
        P(),
        P(("outer", "inner"), None),
        P(),
        P("inner", None),
        P("inner"),
    )
    return jax.shard_map(
        on_device,
        mesh=mesh,
        in_specs=placed,
        out_specs=(P("inner", None), P("inner"), P(), P(), P()),
        check_vma=False,
    )
```

```python
import functools
import math

import jax
import jax.numpy as jnp
from jax import lax
from jax.experimental import pallas as pl
from jax.experimental.pallas import tpu as pltpu
from jax.sharding import PartitionSpec as P

LEARN_RATE = 0.5


def interaction_grads(inputs, cotangent, mix_weight, lift_weight, linear_weight, scaling):
    compressed = jnp.einsum(
        "bfd,fk->bdk", inputs, mix_weight, preferred_element_type=jnp.float32
    ).astype(jnp.bfloat16)
    products = (
        jnp.einsum("bfd,bdk->bfk", inputs, compressed, preferred_element_type=jnp.float32) * scaling
    ).astype(jnp.bfloat16)
    d_products = jnp.einsum(
        "bfd,kd->bfk", cotangent, lift_weight, preferred_element_type=jnp.float32
    ).astype(jnp.bfloat16)
    d_compressed = (
        jnp.einsum("bfd,bfk->bdk", inputs, d_products, preferred_element_type=jnp.float32) * scaling
    ).astype(jnp.bfloat16)
    d_inputs = cotangent.astype(jnp.float32)
    d_inputs = d_inputs + jnp.einsum(
        "fg,bfd->bgd", linear_weight, cotangent, preferred_element_type=jnp.float32
    )
    d_inputs = d_inputs + scaling * jnp.einsum(
        "bfk,bdk->bfd", d_products, compressed, preferred_element_type=jnp.float32
    )
    d_inputs = d_inputs + jnp.einsum(
        "fk,bdk->bfd", mix_weight, d_compressed, preferred_element_type=jnp.float32
    )
    g_mix = jnp.einsum("bfd,bdk->fk", inputs, d_compressed, preferred_element_type=jnp.float32)
    g_lift = jnp.einsum("bfk,bfd->kd", products, cotangent, preferred_element_type=jnp.float32)
    g_linear = jnp.einsum("bfd,bgd->fg", cotangent, inputs, preferred_element_type=jnp.float32)
    rows_out = d_inputs.astype(jnp.bfloat16).reshape(-1, d_inputs.shape[2])
    return (rows_out, (g_mix, g_lift, g_linear))


def adagrad(weights, history, gradient):
    updated = history + jnp.mean(gradient * gradient, axis=1)
    return (weights - LEARN_RATE * gradient / jnp.sqrt(updated)[:, None], updated)


def owner_ranks(owner_of, owners):
    lookups = owner_of.shape[0]
    width = math.gcd(lookups, 128)
    groups = lookups // width
    hot = (owner_of[:, None] == jnp.arange(owners, dtype=jnp.int32)[None, :]).astype(jnp.bfloat16)
    hot = hot.reshape(groups, width, owners)
    lower = (jnp.arange(width)[:, None] > jnp.arange(width)[None, :]).astype(jnp.bfloat16)
    within = jnp.einsum("ij,gjo->gio", lower, hot, preferred_element_type=jnp.float32)
    totals = jnp.sum(hot.astype(jnp.float32), axis=1)
    before = jnp.cumsum(totals, axis=0) - totals
    counted = jnp.sum(hot.astype(jnp.float32) * (within + before[:, None, :]), axis=2)
    return counted.reshape(-1).astype(jnp.int32)


def add_rows(collected, slots, values):
    count = values.shape[0]
    table_rows = collected.shape[0]
    width = math.gcd(count, 2048)
    columns = jnp.arange(table_rows, dtype=jnp.int32)
    for block_index in range(count // width):
        start = block_index * width
        hot = (slots[start : start + width, None] == columns[None, :]).astype(jnp.bfloat16)
        collected = collected + jnp.einsum(
            "lr,ld->rd", hot, values[start : start + width], preferred_element_type=jnp.float32
        )
    return collected


def routed_rows(
    layer_input,
    out_grad,
    mix_weight,
    lift_weight,
    linear_weight,
    row_ids,
    row_home,
    table,
    row_accum,
):
    owners = lax.axis_size("inner")
    sample_count, feature_count, embed_width = layer_input.shape
    table_rows = table.shape[0]
    half_samples = sample_count // 2
    lookups = sample_count * feature_count
    per_owner = lookups // (2 * owners)
    scaling = 1.0 / math.sqrt(embed_width)
    placed = jnp.take(row_home, row_ids.reshape(-1), axis=0)
    owner_of = placed // table_rows
    target = owner_of * (2 * per_owner) + owner_ranks(owner_of, owners)
    ordering = jnp.zeros((lookups,), jnp.int32).at[target].set(jnp.arange(lookups, dtype=jnp.int32))
    ordering = ordering.reshape(owners, 2, per_owner)
    local_rows = (
        jnp.zeros((lookups,), jnp.int32)
        .at[target]
        .set(placed % table_rows)
        .reshape(owners, 2 * per_owner)
    )
    arrived_rows = lax.all_to_all(
        local_rows, "inner", split_axis=0, concat_axis=0, tiled=True
    ).reshape(owners, 2, per_owner)
    collected = jnp.zeros((table_rows, embed_width), jnp.float32)
    totals = None
    for half_index in range(2):
        first_sample = half_index * half_samples
        rows_out, partial_value = interaction_grads(
            layer_input[first_sample : first_sample + half_samples],
            out_grad[first_sample : first_sample + half_samples],
            mix_weight,
            lift_weight,
            linear_weight,
            scaling,
        )
        picked = ordering[:, half_index, :] - half_index * half_samples * feature_count
        outgoing = jnp.take(rows_out, picked.reshape(-1), axis=0).reshape(
            owners, per_owner, embed_width
        )
        incoming = lax.all_to_all(outgoing, "inner", split_axis=0, concat_axis=0, tiled=True)
        collected = add_rows(
            collected, arrived_rows[:, half_index, :].reshape(-1), incoming.reshape(-1, embed_width)
        )
        if totals is None:
            totals = partial_value
        else:
            totals = tuple((earlier + later for earlier, later in zip(totals, partial_value)))
    batch_total = sample_count * lax.axis_size("outer") * owners
    summed = lax.psum((totals[0], totals[1], totals[2]), ("outer", "inner"))
    mix_grad = summed[0] / batch_total
    lift_grad = summed[1] / batch_total
    linear_grad = summed[2] / batch_total
    complete = lax.psum(collected, "outer")
    new_table, new_accum = adagrad(table, row_accum, complete)
    return (new_table, new_accum, mix_grad, lift_grad, linear_grad)


def matmul(left, right):
    return jnp.dot(left, right, preferred_element_type=jnp.float32)


def matmul_nt(left, right):
    return lax.dot_general(left, right, (((1,), (1,)), ((), ())), preferred_element_type=jnp.float32)


def one_hot(matches):
    return jnp.where(matches, 1.0, 0.0).astype(jnp.bfloat16)


def place_kernel(shift, owners, ids_ref, home_ref, rank_ref, slot_ref, count_ref):
    samples, feats = ids_ref.shape
    high, low = home_ref.shape
    half = low // 2
    home = home_ref[...]
    pieces = []
    for part in (home & 255, home >> 8):
        down = part.astype(jnp.float32).T
        pieces.append(jnp.concatenate([down[:half], down[half:]], axis=1))
    pieces = jnp.concatenate(pieces, axis=0).astype(jnp.bfloat16)
    high_at = lax.broadcasted_iota(jnp.int32, (2 * high, feats), 0)
    low_at = lax.broadcasted_iota(jnp.int32, (half, feats), 0)
    lane = lax.broadcasted_iota(jnp.int32, (1, feats), 1)
    count_lane = lax.broadcasted_iota(jnp.int32, (8, 128), 1)

    @pl.loop(0, samples // 8)
    def _(group):
        first = pl.multiple_of(group * 8, 8)
        ids = ids_ref[pl.ds(first, 8), :]
        every = range(8)
        ones = [ids[row : row + 1] for row in every]
        hots = [one_hot(high_at == ((one >> 6) & 1) * high + (one >> 7)) for one in ones]
        founds = [matmul(pieces, hot) for hot in hots]
        places = []
        for row in every:
            value = founds[row][:half] + 256.0 * founds[row][half:]
            value = jnp.where(low_at == (ones[row] & (half - 1)), value, 0.0)
            places.append(jnp.sum(value, axis=0, keepdims=True))
        place = jnp.concatenate(places, axis=0).astype(jnp.int32)
        owner_all = place >> shift
        slot_ref[pl.ds(first, 8), :] = place & ((1 << shift) - 1)
        keys = (owner_all * feats + lane).astype(jnp.float32)
        downs = [jnp.broadcast_to(keys[row : row + 1], (128, feats)).T for row in every]
        ranks = []
        for row in every:
            parts = []
            for at in range(0, feats, 128):
                less = downs[row] < keys[row : row + 1, at : at + 128]
                parts.append(jnp.sum(jnp.where(less, 1.0, 0.0), axis=0, keepdims=True))
            ranks.append(jnp.concatenate(parts, axis=1))
        rank_ref[pl.ds(first, 8), :] = jnp.concatenate(ranks, axis=0).astype(jnp.int32)
        counts = jnp.zeros((8, 128), jnp.float32)
        for owner_at in range(owners):
            number = jnp.sum(jnp.where(owner_all == owner_at, 1.0, 0.0), axis=1, keepdims=True)
            counts = jnp.where(count_lane == owner_at, number, counts)
        most = jnp.max(counts, axis=1, keepdims=True)
        counts = jnp.where(count_lane == owners, most, counts)
        count_ref[pl.ds(first, 8), :] = counts.astype(jnp.int32)


COPY_ROWS = 56
SCRATCH = 19


def sum_list(values):
    total = values[0]
    for value in values[1:]:
        total = total + value
    return total


def positions():
    return lax.axis_index("outer"), lax.axis_index("inner")


def grads_kernel(
    sizes,
    x_ref,
    g_ref,
    mix_ref,
    lift_ref,
    linear_ref,
    ids_ref,
    home_ref,
    *rest,
):
    group, steps, owners, per_owner, scaling, shift = sizes
    far_count = owners // 4
    keep_refs, send_refs = rest[:far_count], rest[far_count : 2 * far_count]
    rows_ref = rest[2 * far_count]
    dense_refs, scratch = rest[2 * far_count + 1 : -SCRATCH], rest[-SCRATCH:]
    rank_ref, slot_ref, found_ref, count_ref, copied, x_held, g_held, landed = scratch[:8]
    step = pl.program_id(0)
    outer, inner = positions()

    def fetch(index):
        samples, slot = pl.ds(pl.multiple_of(index * group, group), group), index % 2
        return [
            pltpu.make_async_copy(ref.at[samples], held.at[slot], landed.at[at, slot])
            for at, (ref, held) in enumerate(((x_ref, x_held), (g_ref, g_held)))
        ]

    @pl.when(step == 0)
    def _():
        for copy in fetch(0):
            copy.start()
        place_kernel(shift, owners, ids_ref, home_ref, rank_ref, slot_ref, found_ref)
        copy = pltpu.make_async_copy(found_ref, count_ref, copied)
        copy.start()
        copy.wait()

    @pl.when((step > 0) & (step < steps))
    def _():
        for copy in fetch(step):
            copy.start()

    @pl.when((step > 0) & (step <= steps))
    def _():
        for copy in fetch(step - 1):
            copy.wait()
        slot = (step - 1) % 2
        gather_rows(
            step - 1,
            outer,
            sizes,
            count_ref,
            x_held.at[slot],
            g_held.at[slot],
            mix_ref,
            lift_ref,
            linear_ref,
            rank_ref,
            slot_ref,
            dense_refs,
            *scratch[8:],
        )

    @pl.when(step > steps)
    def _():
        place = owners - 1 - (step - steps - 1)
        row_a, row_b = scratch[-4], scratch[-3]
        near = (step - steps - 1) ^ inner
        rows_ref[0, :, :128] = row_a[near, pl.ds(0, per_owner), :].astype(jnp.bfloat16)
        rows_ref[0, :, 128:] = row_b[near, pl.ds(0, per_owner), :].astype(jnp.bfloat16)
        owner = place ^ inner
        first_rows = row_a[owner, pl.ds(0, per_owner), :].astype(jnp.bfloat16)
        second_rows = row_b[owner, pl.ds(0, per_owner), :].astype(jnp.bfloat16)
        at = x_held.shape[2] - 128
        build_rows(at, outer, first_rows, second_rows, place, far_count, keep_refs, send_refs)


def join_rows(count_ref, filled, sorted_a, sorted_b, row_a, row_b, step, group, owners):
    begun = (step >= 0).astype(jnp.int32)
    now = (step + 2) % 2
    first = jnp.maximum(step, 0) * group
    every = range(group)
    numbers = [[count_ref[first + k, owner] * begun for owner in range(owners)] for k in every]
    starts = [filled[owner] for owner in range(owners)]
    ends = list(starts)
    for k in every:
        begin = 0
        for owner in range(owners):
            source, target = pl.ds(begin, COPY_ROWS), pl.ds(ends[owner], COPY_ROWS)
            row_a[owner, target, :] = sorted_a[now, k, source, :]
            row_b[owner, target, :] = sorted_b[now, k, source, :]
            ends[owner] = ends[owner] + numbers[k][owner]
            begin = begin + numbers[k][owner]
    most = count_ref[first, owners] * begun
    for k in range(1, group):
        most = jnp.maximum(most, count_ref[first + k, owners] * begun)

    @pl.when(most > COPY_ROWS)
    def _():
        again = list(starts)
        for k in every:
            begin = 0
            for owner in range(owners):

                def copy(turn, carry, begin=begin, at=again[owner], owner=owner, k=k):
                    off = turn * COPY_ROWS
                    source, target = pl.ds(begin + off, COPY_ROWS), pl.ds(at + off, COPY_ROWS)
                    row_a[owner, target, :] = sorted_a[now, k, source, :]
                    row_b[owner, target, :] = sorted_b[now, k, source, :]
                    return carry

                turns = (numbers[k][owner] + COPY_ROWS - 1) // COPY_ROWS
                lax.fori_loop(0, turns, copy, 0)
                again[owner] = again[owner] + numbers[k][owner]
                begin = begin + numbers[k][owner]

    for owner in range(owners):
        filled[owner] = ends[owner]


def gather_rows(
    step,
    outer,
    sizes,
    count_ref,
    x_ref,
    g_ref,
    mix_ref,
    lift_ref,
    linear_ref,
    rank_ref,
    slot_ref,
    dense_refs,
    mix_down,
    lift_down,
    mix_sum,
    lift_sum,
    linear_sum,
    sorted_a,
    sorted_b,
    row_a,
    row_b,
    dense_ref,
    filled,
):
    group, steps, owners, _, scaling, _ = sizes
    width, feats = x_ref.shape[1:]
    rank = mix_ref.shape[1]

    @pl.when(step == 0)
    def _():
        mix_down[...] = mix_ref[...].astype(jnp.float32).T.astype(jnp.bfloat16)
        lift_down[...] = lift_ref[...].astype(jnp.float32).T.astype(jnp.bfloat16)
        mix_sum[...] = jnp.zeros_like(mix_sum)
        lift_sum[...] = jnp.zeros_like(lift_sum)
        linear_sum[...] = jnp.zeros_like(linear_sum)
        for owner in range(owners):
            filled[owner] = 0

    now = step % 2
    join_rows(count_ref, filled, sorted_a, sorted_b, row_a, row_b, step - 1, group, owners)
    row_at = lax.broadcasted_iota(jnp.int32, (feats, feats), 0)
    extra_at = lax.broadcasted_iota(jnp.int32, (feats - width, feats), 0)
    every = range(group)
    d_prods = [matmul(lift_down[...], g_ref[k]).astype(jnp.bfloat16) for k in every]
    boths = [
        matmul_nt(x_ref[k], jnp.concatenate([mix_down[...], d_prods[k]], axis=0)) for k in every
    ]
    comps = [both[:, :rank].astype(jnp.bfloat16) for both in boths]
    d_comps = [(both[:, rank:] * scaling).astype(jnp.bfloat16) for both in boths]
    x_flat = x_ref[...].reshape(group * width, feats).T
    x_flats = [x_flat[:, k * width : (k + 1) * width] for k in every]
    pairs = [
        matmul(x_flats[k], jnp.concatenate([comps[k], d_comps[k]], axis=1)) for k in every
    ]
    prods = [(pair[:, :rank] * scaling).astype(jnp.bfloat16) for pair in pairs]
    mix_sum[...] += sum_list([pair[:, rank:] for pair in pairs])
    g_all = g_ref[...].reshape(group * width, feats)
    d_all = g_all.astype(jnp.float32) + matmul(g_all, linear_ref[...])
    d_all = d_all + matmul(jnp.concatenate(d_comps, axis=0), mix_down[...])
    d_ins = [
        d_all[k * width : (k + 1) * width] + scaling * matmul(comps[k], d_prods[k]) for k in every
    ]
    moves, rows_downs = [], []
    for k in every:
        slot = slot_ref[pl.ds(step * group + k, 1), :]
        extra = jnp.where(extra_at == 0, slot >> 4, jnp.where(extra_at == 1, slot & 15, 0))
        rows_downs.append(
            jnp.concatenate(
                [d_ins[k].astype(jnp.bfloat16), extra.astype(jnp.float32).astype(jnp.bfloat16)],
                axis=0,
            )
        )
        moves.append(one_hot(row_at == rank_ref[pl.ds(step * group + k, 1), :]))
    for k in every:
        ordered = matmul_nt(moves[k], rows_downs[k])
        sorted_a[now, k, :feats] = ordered[:, :128]
        sorted_b[now, k, :feats] = ordered[:, 128:]
    linear_sum[...] += matmul(x_flat, g_all)
    lift_sum[...] += sum_list([matmul(g_ref[k], prods[k]) for k in every])

    @pl.when(step == steps - 1)
    def _():
        join_rows(count_ref, filled, sorted_a, sorted_b, row_a, row_b, step, group, owners)
        dense_ref[:feats] = mix_sum[...]
        linear = linear_sum[...].T
        for at in range(feats // 128):
            dense_ref[feats * (1 + at) : feats * (2 + at)] = linear[:, 128 * at : 128 * (at + 1)]
        dense_ref[feats * (1 + feats // 128) :] = lift_sum[...]
        piece = dense_refs[0].shape[0]
        for index, ref in enumerate(dense_refs):
            first = pl.multiple_of((index ^ outer) * piece, piece)
            ref[...] = dense_ref[pl.ds(first, piece), :]


def build_rows(at, my_outer, first_rows, second_rows, place, first, keep_refs, send_refs):
    outers, piece = 2 * keep_refs[0].shape[1], keep_refs[0].shape[3]
    per_owner = first_rows.shape[0]
    rows_down = jnp.concatenate([first_rows.T, second_rows.T[:at]], axis=0)
    slots = second_rows.astype(jnp.float32)
    slots = slots[:, at : at + 1] * 16.0 + slots[:, at + 1 : at + 2]
    slots = slots.astype(jnp.int32)
    lanes = lax.broadcasted_iota(jnp.int32, (per_owner, piece), 1)
    totals = []
    for outer in range(outers):
        base = (outer ^ my_outer) * piece
        totals.append(matmul(rows_down, one_hot(lanes == slots - base)).astype(jnp.bfloat16))
    for index in range(len(keep_refs)):

        @pl.when(place // 2 == first + index)
        def _(index=index):
            for outer in range(outers):
                ref = (send_refs if outer % 2 else keep_refs)[index]
                ref[0, outer // 2] = totals[outer]


def part_specs(start, first, count, part):
    def spec(index):
        begin = start + 2 * (count - 1 - index)
        return pl.BlockSpec(
            (1,) + part[1:], lambda i, *_: (jnp.clip(begin + 1 - i, 0, 1), 0, 0, 0)
        )

    return [spec(index) for index in range(count)] * 2


def local_grads(x_down, g_down, mix, lift_down, linear, ids, home, owners, part):
    samples, width, feats = x_down.shape
    rank = mix.shape[1]
    group = 16
    steps = samples // group
    per_owner = samples * feats // owners
    far_count = owners // 4
    shift = (part[1] * 2 * part[3]).bit_length() - 1
    sizes = (group, steps, owners, per_owner, 1.0 / math.sqrt(width), shift)

    def whole(shape):
        return pl.BlockSpec(shape, lambda i, *_: (0,) * len(shape))

    sample_spec = pl.BlockSpec(memory_space=pl.ANY)
    dense_rows = feats * (1 + feats // 128) + width
    outers = 2 * part[1]
    dense_piece = (dense_rows // outers, 128)
    room = per_owner + 64
    rows_shape = (owners // 2, per_owner, 256)
    scratch = [
        pltpu.VMEM((samples, feats), jnp.int32),
        pltpu.VMEM((samples, feats), jnp.int32),
        pltpu.VMEM((samples, 128), jnp.int32),
        pltpu.SMEM((samples, 128), jnp.int32),
        pltpu.SemaphoreType.DMA,
        pltpu.VMEM((2, group, width, feats), jnp.bfloat16),
        pltpu.VMEM((2, group, width, feats), jnp.bfloat16),
        pltpu.SemaphoreType.DMA((2, 2)),
        pltpu.VMEM((rank, feats), jnp.bfloat16),
        pltpu.VMEM((rank, width), jnp.bfloat16),
        pltpu.VMEM((feats, rank), jnp.float32),
        pltpu.VMEM((width, rank), jnp.float32),
        pltpu.VMEM((feats, feats), jnp.float32),
        pltpu.VMEM((2, group, feats + 64, 128), jnp.float32),
        pltpu.VMEM((2, group, feats + 64, 128), jnp.float32),
        pltpu.VMEM((owners, room, 128), jnp.float32),
        pltpu.VMEM((owners, room, 128), jnp.float32),
        pltpu.VMEM((dense_rows, 128), jnp.float32),
        pltpu.SMEM((owners,), jnp.int32),
    ]
    outs = pl.pallas_call(
        functools.partial(grads_kernel, sizes),
        out_shape=[jax.ShapeDtypeStruct(part, jnp.bfloat16)] * (2 * far_count)
        + [
            jax.ShapeDtypeStruct(rows_shape, jnp.bfloat16),
        ]
        + [jax.ShapeDtypeStruct(dense_piece, jnp.float32)] * outers,
        grid=(1 + steps + owners // 2,),
        in_specs=[
            sample_spec,
            sample_spec,
            whole((feats, rank)),
            whole((width, rank)),
            whole((feats, feats)),
            whole((samples, feats)),
            whole(home.shape),
        ],
        out_specs=part_specs(1 + steps, owners // 2 - far_count, far_count, part)
        + [
            pl.BlockSpec(
                (1,) + rows_shape[1:],
                lambda i: (jnp.clip(i - 1 - steps, 0, owners // 2 - 1), 0, 0),
            )
        ]
        + [whole(dense_piece)] * outers,
        scratch_shapes=scratch,
        compiler_params=pltpu.CompilerParams(vmem_limit_bytes=60 * 2**20),
        cost_estimate=pl.CostEstimate(
            flops=2 * samples * feats * feats * 3072, bytes_accessed=12 * 2**20, transcendentals=0
        ),
        name="local_grads",
    )(x_down, g_down, mix, lift_down, linear, ids, home)
    keep, send = outs[:far_count], outs[far_count : 2 * far_count]
    return keep, send, outs[2 * far_count], outs[2 * far_count + 1 :]


def build_kernel(at, rows_ref, *refs):
    half = len(refs) // 2
    rows = rows_ref[0]
    place = 2 * half - 1 - pl.program_id(0)
    keep_refs, send_refs = refs[:half], refs[half:]
    outer, _ = positions()
    build_rows(at, outer, rows[:, :128], rows[:, 128:], place, 0, keep_refs, send_refs)


def build_parts(rows, part, width):
    places, per_owner, lanes = rows.shape
    far_count = places // 2
    outs = pl.pallas_call(
        functools.partial(build_kernel, width - 128),
        out_shape=[jax.ShapeDtypeStruct(part, jnp.bfloat16)] * places,
        grid=(places,),
        in_specs=[pl.BlockSpec((1, per_owner, lanes), lambda i: (places - 1 - i, 0, 0))],
        out_specs=part_specs(0, 0, far_count, part),
        compiler_params=pltpu.CompilerParams(vmem_limit_bytes=60 * 2**20),
        cost_estimate=pl.CostEstimate(
            flops=4 * part[3] * part[1] * part[0] * places * per_owner * lanes,
            bytes_accessed=6 * 2**20,
            transcendentals=0,
        ),
        name="build_parts",
    )(rows)
    return outs[:far_count], outs[far_count:]


def adagrad_kernel(me_ref, *refs):
    pieces, (table_ref, accum_ref) = refs[:2], refs[2:4]
    new_table_ref, new_accum_ref = refs[-2:]
    width = table_ref.shape[0]
    for index, piece in enumerate(pieces):

        @pl.when(pl.program_id(0) == index)
        def _(piece=piece):
            grad = piece[...].astype(jnp.float32)
            mean = jnp.sum(grad * grad, axis=0, keepdims=True) * (1.0 / width)
            updated = accum_ref[...] + mean
            new_accum_ref[...] = updated
            new_table_ref[...] = table_ref[...] - grad * (LEARN_RATE / jnp.sqrt(updated))


def update_table(me, pieces, table_down, accum, first, done=()):
    width, table_rows = table_down.shape
    piece = pieces[0].shape[1]

    def moved(rows):
        return pl.BlockSpec((rows, piece), lambda i, me: (0, (first + i) ^ me[0]))

    return pl.pallas_call(
        adagrad_kernel,
        out_shape=(
            jax.ShapeDtypeStruct((width, table_rows), jnp.float32),
            jax.ShapeDtypeStruct((1, table_rows), jnp.float32),
        ),
        grid_spec=pltpu.PrefetchScalarGridSpec(
            num_scalar_prefetch=1,
            grid=(2,),
            in_specs=[pl.BlockSpec(memory_space=pltpu.VMEM)] * 2
            + [moved(width), moved(1)]
            + [pl.BlockSpec(memory_space=pl.ANY)] * len(done),
            out_specs=[moved(width), moved(1)],
        ),
        input_output_aliases={5 + i: i for i in range(len(done))},
        compiler_params=pltpu.CompilerParams(vmem_limit_bytes=16 * 2**20),
        name="update_table",
    )(me, *pieces, table_down, accum, *done)


def swap(values, axis, bit):
    size = lax.axis_size(axis)
    return lax.ppermute(values, axis, [(i, i ^ bit) for i in range(size)])


def add_half(first, second):
    return (first.astype(jnp.float32) + second.astype(jnp.float32)).astype(jnp.bfloat16)


def tree_sum(values):
    while len(values) > 1:
        values = [values[i] + values[i + 1] for i in range(0, len(values), 2)]
    return values[0]


def after(value, *ready):
    return lax.optimization_barrier((value,) + ready)[0]


def halves(dense, side):
    cut = dense.reshape(2, dense.shape[0] // 2, dense.shape[1])
    mine = lax.dynamic_index_in_dim(cut, side, 0, keepdims=False)
    return mine, lax.dynamic_index_in_dim(cut, 1 - side, 0, keepdims=False)


def stacked(dense, other, side):
    return jnp.where(side == 0, jnp.stack([dense, other]), jnp.stack([other, dense]))


def sum_all(me, keep, send, rows, dense, part, width):
    owners = lax.axis_size("inner")
    outer, inner = lax.axis_index("outer"), lax.axis_index("inner")
    far_count = owners // 2
    first = far_count - len(keep)
    keep = dict(enumerate(keep, first))
    came, parts, kept, sent, rest, second, terms, last = ({} for _ in range(8))
    far_ones, near_ones = list(reversed(range(first, far_count))), list(reversed(range(first)))

    def first_stage(far):
        held = keep[far]
        if far % 2:
            parts[far] = add_half(held[1], came[far][1])
            kept[far] = add_half(held[0], came[far][0])
        else:
            parts[far] = add_half(held[:, 1], came[far][:, 1])
            kept[far] = add_half(held[:, 0], came[far][:, 0])

    def second_stage(far):
        parts[far] = add_half(kept[far][1], sent[far][1])
        rest[far] = add_half(kept[far][0], sent[far][0])
        second[far] = swap(parts[far], *(("outer", 2) if far % 2 else ("inner", 1)))

    def send_first(far, ready):
        sent[far] = swap(ready, *(("inner", 1) if far % 2 else ("outer", 2)))

    sides = (outer & 1, outer >> 1, inner & 1)
    for far in far_ones:
        came[far] = swap(send[far - first], "outer", 1)
    others = tuple(swap(dense[bits], "outer", bits) for bits in range(1, len(dense)))
    for far in far_ones:
        first_stage(far)
        send_first(far, parts[far])
    far_parts = [parts[far] for far in far_ones]
    rows = after(rows, *far_parts)
    low_keep, low_send = build_parts(rows, part, width)
    for far in near_ones:
        keep[far] = low_keep[far]
        came[far] = swap(low_send[far], "outer", 1)
    dense = sum_list((dense[0],) + after(others, low_send[0]))
    mine, other = halves(dense, sides[2])
    other = swap(other, "inner", 1)
    for far in far_ones:
        second_stage(far)
    for far in near_ones:
        first_stage(far)
    near_parts = [parts[far] for far in near_ones]
    for far in near_ones:
        send_first(far, parts[far])
    dense = mine + after(other, *near_parts)
    other = swap(dense, "inner", 2)

    def send_last(far, *ready):
        low = far & -far
        value = rest[far].astype(jnp.float32) + second[far].astype(jnp.float32)
        came_far = [terms[far + bit] for bit in (1 << at for at in range(8)) if bit < low]
        if came_far:
            for one in after(tuple(came_far), *ready):
                value = value + one.astype(jnp.float32)
        last[far] = value.astype(jnp.bfloat16)
        terms[far] = swap(last[far], "inner", 2 * low)

    for far in far_ones:
        second[far] = after(second[far], me, dense, *near_parts)
    odd_ones = [far for far in far_ones if far % 2]
    for far in odd_ones:
        send_last(far)
    odd_last = [last[far] for far in odd_ones]
    for bit in range(1, far_count.bit_length() - 1):
        dense = dense + after(other, *odd_last)
        other = swap(dense, "inner", 2 << bit)
    arrived = after(tuple(sent[far] for far in near_ones), *odd_last)
    for far, sent[far] in zip(near_ones, arrived):
        second_stage(far)
    near_parts = [parts[far] for far in near_ones]
    dense = dense + after(other, *near_parts)
    other = swap(dense, "inner", 1)
    for far in far_ones:
        if far % 2 == 0:
            send_last(far, *near_parts)
    even_last = [last[far] for far in far_ones if far % 2 == 0]
    for far in near_ones:
        second[far] = after(second[far], *even_last)
        if far:
            send_last(far)
    dense = stacked(dense, after(other, last[1]), sides[2])
    other = swap(dense, "outer", 2)
    dense = stacked(dense, after(other, second[0], terms[2]), sides[1])
    mine, came_last = after((rest[0], second[0]), dense, last[1])
    total = mine.astype(jnp.float32) + came_last.astype(jnp.float32)
    ends = tuple(terms[1 << bit] for bit in range(far_count.bit_length() - 1))
    for term in after(ends, dense, last[1]):
        total = total + term.astype(jnp.float32)
    total = total.astype(jnp.bfloat16)
    across = swap(total, "outer", 2)
    beside = swap(total, "outer", 1)
    dense = stacked(dense, swap(dense, "outer", 1), sides[0])
    lanes = dense.shape[-1]
    return total, beside, across, jnp.transpose(dense, (1, 0, 2, 3, 4)).reshape(-1, lanes)


def dense_table(
    layer_input,
    out_grad,
    mix_weight,
    lift_weight,
    linear_weight,
    row_ids,
    row_home,
    table,
    row_accum,
):
    owners, outers = lax.axis_size("inner"), lax.axis_size("outer")
    sample_count = layer_input.shape[0]
    table_rows = table.shape[0]
    me = jnp.stack([lax.axis_index("outer"), lax.axis_index("inner")]).astype(jnp.int32)
    width = layer_input.shape[2]
    part = (2, outers // 2, width, table_rows // outers)
    keep, send, rows, dense = local_grads(
        jnp.swapaxes(layer_input, 1, 2),
        jnp.swapaxes(out_grad, 1, 2),
        mix_weight,
        lift_weight.T,
        linear_weight,
        row_ids,
        row_home.reshape(-1, 128),
        owners,
        part,
    )
    total, beside, across, dense = sum_all(me, keep, send, rows, dense, part, width)
    dense = dense * (1.0 / (sample_count * outers * owners))
    feats = layer_input.shape[1]
    linear = [dense[feats * (1 + i) : feats * (2 + i)] for i in range(feats // 128)]
    weights = (
        dense[:feats],
        dense[feats * (1 + feats // 128) :].T,
        jnp.concatenate(linear, axis=1),
    )
    table_down, accum = table.T, row_accum.reshape(1, -1)
    done = update_table(me, (total, beside), table_down, accum, 0)
    across = after(across, done[1], *weights)
    pieces = (across, swap(across, "outer", 1))
    new_table, new_accum = update_table(me, pieces, table_down, accum, 2, done)
    return (new_table.T, new_accum.reshape(-1)) + weights


def power_of_two(number):
    return number & (number - 1) == 0


def on_device(*arrays):
    owners, outers = lax.axis_size("inner"), lax.axis_size("outer")
    layer_input, mix_weight, row_home, table = (arrays[i] for i in (0, 2, 6, 7))
    samples, feats, width = layer_input.shape
    dense_fits = (
        outers == 4
        and owners % 4 == 0
        and power_of_two(owners)
        and row_home.shape[0] <= 2 * samples * feats
        and row_home.shape[0] <= 2**15
        and power_of_two(table.shape[0])
        and 512 <= table.shape[0] <= 4096
        and samples % 16 == 0
        and (feats * (1 + feats // 128) + width) % 64 == 0
        and feats == 256
        and mix_weight.shape[1] == 128
        and 2 * (width - 128) == 128
    )
    return dense_table(*arrays) if dense_fits else routed_rows(*arrays)


def solution(mesh):
    placed = (
        P(("outer", "inner"), None, None),
        P(("outer", "inner"), None, None),
        P(),
        P(),
        P(),
        P(("outer", "inner"), None),
        P(),
        P("inner", None),
        P("inner"),
    )
    return jax.shard_map(
        on_device,
        mesh=mesh,
        in_specs=placed,
        out_specs=(P("inner", None), P("inner"), P(), P(), P()),
        check_vma=False,
    )
```
